32 devices in a mesh: groups: 2 (over x), section: 8 (over z, y), tensor: 2 (over core).
Axes of the slice: x: 2, y: 2, z: 4, core: 2. Of those that a mesh axis runs over, the one named last changes fastest.
Arguments:
- text_rows: bfloat16 [4096, 8192], P(('groups', 'section'), 'tensor'), parts along dimension 0, may hold values from -6 to 6
- vis_rows: bfloat16 [1024, 8192], P(('groups', 'section'), 'tensor'), parts along dimension 0, may hold values from -6 to 6
- img_route: int32 [1024, 1], P('groups'), parts along dimension 0, may hold values from 0 to 7; in each aligned block of 64 rows (0 to 63, 64 to 127, ...) at most 16 rows name the same one
- norm_gain: float32 [8192], replicated, may hold values from 0.1 to 1.9
- w_key: bfloat16 [8192, 512], P(None, 'tensor'), may hold values from -0.0625 to 0.0625
- w_value: bfloat16 [8192, 512], P(None, 'tensor'), may hold values from -0.0625 to 0.0625
- page_count: int32 [16], P('groups'), parts along dimension 0, may hold values from 1 to 32, 128 in all
- tail_len: int32 [16], P('groups'), parts along dimension 0, may hold values from 1 to 16
- page_dest: int32 [256, 1], P('groups'), parts along dimension 0, may hold values from 0 to 7; in each aligned block of 16 rows (0 to 15, 16 to 31, ...) at most 2 rows name the same one
- dec_req: int32 [16], P('groups'), parts along dimension 0, may hold values from 0 to 7, each once
- dec_query: bfloat16 [16, 4, 4096], P(('groups', 'section'), None, 'tensor'), parts along dimension 0, may hold values from -90 to 90
- dec_key: bfloat16 [16, 4, 512], P(('groups', 'section'), None, 'tensor'), parts along dimension 0, may hold values from -3.1 to 3.1
- dec_value: bfloat16 [16, 4, 512], P(('groups', 'section'), None, 'tensor'), parts along dimension 0, may hold values from -6 to 6
Outputs:
- attended: bfloat16 [16, 4, 4096], P(('groups', 'section'), None, 'tensor'), parts along dimension 0
- cache_key: bfloat16 [256, 16, 512], P(('groups', 'section'), None, 'tensor'), parts along dimension 0
- cache_value: bfloat16 [256, 16, 512], P(('groups', 'section'), None, 'tensor'), parts along dimension 0
The draws below stay inside these ranges and needn't reach their ends.
There are 2 independent parts, one for each index of `groups`. The reference program is written for one: setup_inputs(seed, part) draws one part's arguments, and reference() takes and returns one part's arrays. A program takes and returns all parts, laid end to end along the dimension named above; an argument that names none is the same for every part. Nothing has to cross between parts.
Inputs may be any that keep to these rules, and one draw needn't show every extreme that they name: `img_route`: of the rows of one encoder device (aligned blocks of 64 rows) at most 16 go to one prefill device. `page_count`: they sum to 128. `page_dest`: of the pages of one prefill device (aligned blocks of 16 pages) at most 2 go to one decode device. `dec_req`: each request is served by exactly one slot.
All inputs are finite; a program needn't handle non-finite values.
Results may differ from the reference program's by a relative error of at most 0.0061.
Values may be sent and summed in bfloat16 or wider, within the bound.
No kernel may reach another device: no remote copies, remote signals or barrier semaphores. Data moves between devices by JAX's collectives and lax.ppermute only.
A program may use at most 128 MiB of HBM per device.

```python
import math
import jax
import jax.numpy as jnp
import numpy as np
from jax import lax

D = 8192
HD = 128
KVH = 4
QH = 32
PAGE = 16
STEPS = 4
MAXP = 32
TOK_DEV = 256
KVD = 512
QD = 4096
BLK_DEV = 16
PCAP = 2
IMG_DEV = 64
ICAP = 16
TOKENS = 2048
IMG = 512
PAGES = 128
SEQS = 8
SLOTS = 128
N_SECTION = 8


def base_keys(key):
    return jnp.clip(jax.random.normal(jax.random.fold_in(key, 101), (SEQS, STEPS, KVD), jnp.float32), -3.0, 3.0)


def draw_dec_key(key, part):
    shared = base_keys(key)
    result = shared
    return result.astype(jnp.bfloat16)


def draw_dec_query(key, part):
    key = jax.random.fold_in(key, 5)
    own_draw = jnp.clip(jax.random.normal(key, (SEQS, STEPS, QD), jnp.float32), -3.0, 3.0)
    return own_draw.astype(jnp.bfloat16)


def with_ends(entries, own_key, smallest, high):
    shape = entries.shape
    place = [jax.random.randint(jax.random.fold_in(own_key, axis), (), 0, shape[axis]) for axis in range(len(shape))]
    entries = entries.at[tuple(place)].set(smallest)
    longest = shape.index(max(shape))
    place[longest] = (place[longest] + 1) % shape[longest]
    return entries.at[tuple(place)].set(high)


def steps_of(stream_key, shape, split, least, high):
    def one(position, shards_of):
        heights = jax.random.uniform(jax.random.fold_in(jax.random.fold_in(stream_key, 6), position), (shards_of,), jnp.float32, least / len(split), high / len(split))
        return jnp.repeat(jnp.exp(heights), shape[position] // shards_of).reshape((-1,) + (1,) * (len(shape) - position - 1))

    level = one(*split[0])
    for cut in split[1:]:
        level = level * one(*cut)
    return level


def length_profile(number_of, total, limit, slope):
    loads = [(1 << 20) // math.isqrt(rank ** slope) + 1 for rank in range(2, number_of + 1)]
    surplus, holding = total - limit - (number_of - 1), [1] * (number_of - 1)
    while surplus > 0:
        free = [i for i in range(number_of - 1) if holding[i] < limit]
        pool, left = sum([loads[i] for i in free]), surplus
        for i in free:
            more = min(limit - holding[i], max(1, left * loads[i] // pool), surplus)
            holding[i] = holding[i] + more
            surplus = surplus - more
    return np.array([limit] + holding)


def ragged_sizes(own_key, count, total, reach, lean):
    if count == 2:
        one = jax.random.randint(own_key, (), max(1, total - reach), min(reach, total - 1) + 1)
        return jnp.stack([one, total - one])
    sizes = jnp.asarray(length_profile(count, total, reach, lean), jnp.int32)
    twos = (count - 1) // 2
    giver, receiver = sizes[1:1 + 2 * twos:2], sizes[2:2 + 2 * twos:2]
    room = jnp.minimum(giver - 1, reach - receiver)
    shifted = jax.random.randint(jax.random.fold_in(own_key, 1), (twos,), 0, 1 << 20) % (room + 1)
    sizes = sizes.at[1:1 + 2 * twos:2].set(giver - shifted).at[2:2 + 2 * twos:2].set(receiver + shifted)
    return sizes[jax.random.permutation(jax.random.fold_in(own_key, 2), count)]


def assign_block(key, own, number, rows, count, top, limit, skew):
    ranking = jax.random.permutation(key, count)
    crowded, ordinary = portions_of(count, rows * top, limit, skew, True), portions_of(count, rows * top, limit, skew, False)
    places = jnp.arange(count)

    def named(sizes, rotation):
        used = int((sizes > 0).sum())
        fixed = max(1, used // 4)
        moved = fixed + (places - fixed + rotation * (used - fixed)) % max(1, count - fixed)
        return jnp.zeros((count,), jnp.int32).at[ranking[jnp.where(places < fixed, places, moved)]].set(jnp.asarray(sizes, jnp.int32))

    sizes = jnp.where(number % 4 == 0, named(crowded, number // 4), named(ordinary, number - number // 4 - 1))
    mixed = jax.random.permutation(jax.random.fold_in(own, 3), count)
    giver, sink = mixed[0:count // 2 * 2:2], mixed[1:count // 2 * 2:2]
    room = jnp.minimum(sizes[giver] - 1, limit - sizes[sink]) // 2
    room = jnp.where((giver == ranking[0]) | (sink == ranking[0]) | (sizes[sink] == 0), 0, jnp.maximum(room, 0))
    moved = jax.random.randint(jax.random.fold_in(own, 4), (count // 2,), 0, 1 << 20) % (room + 1)
    sizes = sizes.at[giver].add(-moved).at[sink].add(moved)
    labels = jnp.searchsorted(jnp.cumsum(sizes), jnp.arange(rows * top), side="right").astype(jnp.int32)
    table = labels.reshape(top, rows).T
    table = table[jax.random.permutation(jax.random.fold_in(own, 1), rows)]
    rotation = jax.random.randint(jax.random.fold_in(own, 2), (rows, 1), 0, top)
    return jnp.take_along_axis(table, (jnp.arange(top)[None, :] + rotation) % top, axis=1)


def portions_of(amount, total, bound, skew, full):
    loads = [(1 << 20) // math.isqrt(rank ** skew) + 1 for rank in range(1, amount + 1)]
    largest = bound if full else min(bound, max(-(-total // amount), total * loads[0] // sum(loads)))
    least = 1 if total - largest >= amount - 1 else 0
    counts, rest = [largest] + [least] * (amount - 1), total - largest - least * (amount - 1)
    while rest > 0:
        free = [i for i in range(1, amount) if counts[i] < largest] or [i for i in range(1, amount) if counts[i] < bound]
        pool, remaining = sum([loads[i] for i in free]), rest
        for i in free:
            more = min(bound - counts[i], max(1, remaining * loads[i] // pool), rest)
            counts[i] = counts[i] + more
            rest = rest - more
    return np.array(counts)


def bell_draw(own_key, dims, width, reach, pieces=(), kind=jnp.bfloat16):
    array = jax.random.normal(own_key, dims, jnp.float32) * width
    if len(pieces) > 0:
        array = steps_of(own_key, dims, pieces, -0.22, 0.18) * array
    return jnp.clip(array, min=-reach, max=reach).astype(kind)


def setup_inputs(seed: int = 0, part: int = 0) -> dict:
    streams_of = jax.random.split(jax.random.key(seed), 14)
    part_keys = jax.random.split(jax.random.fold_in(streams_of[13], part), 14)
    text_rows = bell_draw(part_keys[0], (TOKENS, D), 1.0, 6.0, ((0, 8), (1, 2)))
    vis_rows = bell_draw(part_keys[1], (IMG, D), 1.0, 6.0, ((0, 8), (1, 2)))
    img_route_keys = jax.random.split(jax.random.fold_in(part_keys[2], 1), IMG // IMG_DEV)
    img_route_turns = jax.random.permutation(jax.random.fold_in(part_keys[2], 3), IMG // IMG_DEV)
    img_route = jax.vmap(lambda own, number: assign_block(jax.random.fold_in(part_keys[2], 2), own, number, IMG_DEV, N_SECTION, 1, ICAP, 2))(img_route_keys, img_route_turns).reshape((IMG, 1))
    norm_gain = jnp.clip(1.0 + 0.18 * jax.random.normal(streams_of[3], (D,), jnp.float32), 0.1, 1.9)
    w_key = bell_draw(streams_of[4], (D, KVD), D ** -0.5, 0.0625, ((1, 2),))
    w_value = bell_draw(streams_of[5], (D, KVD), D ** -0.5, 0.0625, ((1, 2),))
    page_count = ragged_sizes(part_keys[6], SEQS, PAGES, MAXP, 2).astype(jnp.int32)
    tail_len = with_ends(jax.random.randint(part_keys[7], (SEQS,), 1, PAGE + 1), jax.random.fold_in(part_keys[7], 1), 1, PAGE).astype(jnp.int32)
    page_dest_keys = jax.random.split(jax.random.fold_in(part_keys[8], 1), PAGES // BLK_DEV)
    page_dest_turns = jax.random.permutation(jax.random.fold_in(part_keys[8], 3), PAGES // BLK_DEV)
    page_dest = jax.vmap(lambda own, number: assign_block(jax.random.fold_in(part_keys[8], 2), own, number, BLK_DEV, N_SECTION, 1, PCAP, 2))(page_dest_keys, page_dest_turns).reshape((PAGES, 1))
    dec_req = jax.random.permutation(part_keys[9], SEQS).astype(jnp.int32)
    dec_query = draw_dec_query(jax.random.fold_in(jax.random.fold_in(streams_of[13], part), 71), part)
    dec_key = draw_dec_key(jax.random.fold_in(jax.random.fold_in(streams_of[13], part), 71), part)
    dec_value = bell_draw(part_keys[12], (SEQS, STEPS, KVD), 1.0, 6.0, ((0, 8), (2, 2)))
    return dict(text_rows=text_rows, vis_rows=vis_rows, img_route=img_route, norm_gain=norm_gain, w_key=w_key, w_value=w_value, page_count=page_count, tail_len=tail_len, page_dest=page_dest, dec_req=dec_req, dec_query=dec_query, dec_key=dec_key, dec_value=dec_value)


lowest_score = -1e+30

def prior_rank(marked, axis_number):
    earlier = jnp.cumsum(marked, axis=axis_number) - marked
    return lax.optimization_barrier(jnp.sum(earlier * marked, axis=-1))

def reference(text_rows, vis_rows, img_route, norm_gain, w_key, w_value, page_count, tail_len, page_dest, dec_req, dec_query, dec_key, dec_value):
    station = jnp.arange(N_SECTION, dtype=jnp.int32)
    targets = img_route[:, 0]
    target_marks = (targets[:, None] == station[None, :]).astype(jnp.int32)
    row_ranks = prior_rank(target_marks, 0)
    places = (targets * TOK_DEV + row_ranks).astype(jnp.int32)
    hidden = text_rows.at[places].set(vis_rows)
    widened = hidden.astype(jnp.float32)
    mean_square = lax.optimization_barrier(jnp.mean(widened * widened, axis=1, keepdims=True))
    normed = (widened * lax.rsqrt(mean_square + 1e-06) * norm_gain[None, :]).astype(jnp.bfloat16)
    keys_all = jnp.dot(normed, w_key, preferred_element_type=jnp.float32).astype(jnp.bfloat16)
    values_all = jnp.dot(normed, w_value, preferred_element_type=jnp.float32).astype(jnp.bfloat16)
    holders = page_dest[:, 0]
    holder_marks = (holders[:, None] == station[None, :]).astype(jnp.int32).reshape(N_SECTION, BLK_DEV, N_SECTION)
    page_rank = prior_rank(holder_marks, 1).reshape(-1)
    sources = jnp.arange(PAGES, dtype=jnp.int32) // BLK_DEV
    cache_slots = (holders * (N_SECTION * PCAP) + sources * PCAP + page_rank).astype(jnp.int32)
    cache_key = jnp.zeros((SLOTS, PAGE, KVD), jnp.bfloat16).at[cache_slots].set(keys_all.reshape(PAGES, PAGE, KVD))
    cache_value = jnp.zeros((SLOTS, PAGE, KVD), jnp.bfloat16).at[cache_slots].set(values_all.reshape(PAGES, PAGE, KVD))
    starts = jnp.cumsum(page_count) - page_count
    lengths = (page_count - 1) * PAGE + tail_len
    window = MAXP * PAGE
    keys_long = jnp.concatenate([keys_all, jnp.zeros((window, KVD), jnp.bfloat16)], axis=0)
    values_long = jnp.concatenate([values_all, jnp.zeros((window, KVD), jnp.bfloat16)], axis=0)
    head_group = QH // KVH
    score_scale = HD ** (-0.5)

    def one_slot(slot_number):
        request = dec_req[slot_number]
        beginning = (starts[request] * PAGE).astype(jnp.int32)
        nearby_keys = lax.dynamic_slice_in_dim(keys_long, beginning, window, 0).astype(jnp.float32).reshape(window, KVH, HD)
        nearby_values = lax.dynamic_slice_in_dim(values_long, beginning, window, 0).astype(jnp.float32).reshape(window, KVH, HD)
        queries_here = dec_query[slot_number].astype(jnp.float32).reshape(STEPS, KVH, head_group, HD)
        fresh_keys = dec_key[slot_number].astype(jnp.float32).reshape(STEPS, KVH, HD)
        fresh_values = dec_value[slot_number].astype(jnp.float32).reshape(STEPS, KVH, HD)
        prompt_scores = jnp.einsum('sghd,jgd->sghj', queries_here, nearby_keys, precision=lax.Precision.HIGHEST) * score_scale
        fresh_scores = jnp.einsum('sghd,tgd->sght', queries_here, fresh_keys, precision=lax.Precision.HIGHEST) * score_scale
        prompt_usable = (jnp.arange(window, dtype=jnp.int32) < lengths[request])[None, None, None, :]
        fresh_usable = (jnp.arange(STEPS)[None, :] <= jnp.arange(STEPS)[:, None])[:, None, None, :]
        prompt_scores = jnp.where(prompt_usable, prompt_scores, lowest_score)
        fresh_scores = jnp.where(fresh_usable, fresh_scores, lowest_score)
        highest = jnp.maximum(lax.optimization_barrier(jnp.max(prompt_scores, axis=-1)), lax.optimization_barrier(jnp.max(fresh_scores, axis=-1)))
        prompt_weights = jnp.where(prompt_usable, jnp.exp(prompt_scores - highest[..., None]), 0.0)
        fresh_weights = jnp.where(fresh_usable, jnp.exp(fresh_scores - highest[..., None]), 0.0)
        denominator = lax.optimization_barrier(jnp.sum(prompt_weights, axis=-1)) + lax.optimization_barrier(jnp.sum(fresh_weights, axis=-1))
        rounded_prompt = lax.optimization_barrier(prompt_weights.astype(jnp.bfloat16)).astype(jnp.float32)
        rounded_fresh = lax.optimization_barrier(fresh_weights.astype(jnp.bfloat16)).astype(jnp.float32)
        numerator = jnp.einsum('sghj,jgd->sghd', rounded_prompt, nearby_values, precision=lax.Precision.HIGHEST)
        numerator = numerator + jnp.einsum('sght,tgd->sghd', rounded_fresh, fresh_values, precision=lax.Precision.HIGHEST)
        return (numerator / denominator[..., None]).reshape(STEPS, QD).astype(jnp.bfloat16)
    attended = lax.map(one_slot, jnp.arange(SEQS, dtype=jnp.int32))
    return (attended, cache_key, cache_value)
```

```python
import jax
import jax.numpy as jnp
from jax import lax
from jax.experimental import pallas as pl
from jax.experimental.pallas import tpu as pltpu
from jax.sharding import PartitionSpec as P

HD = 128
PAGE = 16
LOWEST = -1e30
EPS = 1e-06
STAT = 8
F32 = jnp.float32
BF16 = jnp.bfloat16
I32 = jnp.int32

VM = pl.BlockSpec(memory_space=pltpu.VMEM)
SM = pl.BlockSpec(memory_space=pltpu.SMEM)
MIB = 1 << 20


def call(kernel, out_shape, in_specs, out_specs, scratch=(), limit=16, flops=0, traffic=0):
    return pl.pallas_call(
        kernel,
        out_shape=out_shape,
        in_specs=in_specs,
        out_specs=out_specs,
        scratch_shapes=list(scratch),
        compiler_params=pltpu.CompilerParams(vmem_limit_bytes=limit * MIB),
        cost_estimate=pl.CostEstimate(flops=flops, bytes_accessed=traffic, transcendentals=0),
    )


def dot(a, b):
    return jnp.dot(a, b, preferred_element_type=F32)


def dot_t(a, b):
    return lax.dot_general(a, b, (((1,), (1,)), ((), ())), preferred_element_type=F32)


def diagonal(shape):
    return lax.broadcasted_iota(I32, shape, 0) == lax.broadcasted_iota(I32, shape, 1)


def column_to_row(column):
    rows = column.shape[0]
    return jnp.sum(jnp.where(diagonal((rows, rows)), column, 0.0), axis=0, keepdims=True)


def row_to_column(row):
    lanes = row.shape[1]
    return jnp.sum(jnp.where(diagonal((lanes, lanes)), row, 0.0), axis=1, keepdims=True)


def put_partial(out, kv_heads, numerators, tops, totals):
    rows = numerators[0].shape[0]
    for g in range(kv_heads):
        out[g * rows : (g + 1) * rows, :] = numerators[g]
    stats = column_to_row(jnp.concatenate(list(tops) + list(totals), axis=0))
    out[kv_heads * rows :, :] = jnp.broadcast_to(stats, (STAT, stats.shape[1]))


def meta_kernel(sizes, route, pages, count, tail, req, query, key, value, info, slots, fresh, starts):
    n, img, tok, blocks, cap, page_cap, kv_heads, steps = sizes
    pos = lax.axis_index("section")
    own = route[pl.ds(pos, 1), :]
    table = route[...]
    stations = lax.broadcasted_iota(I32, (n, img), 0)
    marks = own == stations
    ones = jnp.where(marks, 1.0, 0.0).astype(BF16)
    earlier = lax.broadcasted_iota(I32, (img, img), 0) < lax.broadcasted_iota(I32, (img, img), 1)
    prefix = dot(ones, jnp.where(earlier, 1.0, 0.0).astype(BF16))
    before = jnp.zeros((n, 1), I32)
    for e in range(n):
        here = jnp.sum((table[e : e + 1, :] == stations).astype(I32), axis=1, keepdims=True)
        before = before + jnp.where(e < pos, here, 0)
    local = jnp.sum(jnp.where(marks, prefix, 0.0), axis=0, keepdims=True).astype(I32)
    rank = local + jnp.sum(jnp.where(marks, before, 0), axis=0, keepdims=True)
    send = jnp.bitwise_xor(own, pos) * cap + local
    place = own * tok + rank
    arriving = jnp.sum((table == pos).astype(I32), axis=1, keepdims=True)
    lanes = lax.broadcasted_iota(I32, (n, n * cap), 1)
    source = jnp.bitwise_xor(lanes // cap, pos)
    number = lax.broadcasted_iota(I32, (n, n * cap), 0)
    fits = jnp.sum(jnp.where(number == source, arriving, 0), axis=0, keepdims=True)
    offset = jnp.sum(jnp.where(number < source, arriving, 0), axis=0, keepdims=True)
    inner = lanes[:1] % cap
    target = jnp.where(inner < fits, offset + inner, -1)
    replaced = jnp.sum(arriving, axis=0, keepdims=True)
    total = jnp.int32(0)
    for r in range(n):
        starts[r] = total
        total = total + count[r]
    inside = lax.broadcasted_iota(I32, (1, tok), 1)
    text = inside + pos * tok
    text_slot = jnp.full((1, tok), -1, I32)
    vis_slot = jnp.full((1, img), -1, I32)
    for b in range(n):
        r = req[b]
        first = starts[r] * PAGE
        last = first + (count[r] - 1) * PAGE + tail[r]
        text_slot = jnp.where((text >= first) & (text < last), b, text_slot)
        vis_slot = jnp.where((place >= first) & (place < last), b, vis_slot)
    text_slot = jnp.where(inside < replaced, -1, text_slot)
    info[0:1, :img] = send
    info[1:2, :img] = vis_slot
    info[2:3, :tok] = text_slot
    info[3:4, : n * cap] = target
    for g in range(blocks):
        holder = pages[pos * blocks + g]
        slot = jnp.bitwise_xor(holder, pos) * page_cap
        for e in range(g):
            slot = slot + (pages[pos * blocks + e] == holder).astype(I32)
        slots[g] = slot
    rows = query.shape[0] // kv_heads
    row = lax.broadcasted_iota(I32, (rows, steps), 0)
    causal = lax.broadcasted_iota(I32, (rows, steps), 1) <= row % steps
    parts = ([], [], [])
    for g in range(kv_heads):
        cols = slice(g * HD, (g + 1) * HD)
        scores = dot_t(query[g * rows : (g + 1) * rows, :], key[:, cols]) * HD**-0.5
        scores = jnp.where(causal, scores, LOWEST)
        top = jnp.max(scores, axis=1, keepdims=True)
        weights = jnp.where(causal, jnp.exp(scores - top), 0.0)
        numerator = dot(weights.astype(BF16), value[:, cols])
        for held, new in zip(parts, (numerator, top, jnp.sum(weights, axis=1, keepdims=True))):
            held.append(new)
    put_partial(fresh, kv_heads, *parts)


def project_kernel(sizes, text, text_far, vis, vis_far, gain, w_key, w_value, info, kv_text, kv_vis, *rest):
    n, cap, step = sizes
    packed, (total, ) = rest[:-1], rest[-1:]
    tok, half = text.shape
    img = vis.shape[0]
    kvw = w_key.shape[1]
    me = lax.axis_index("tensor")
    squares = [jnp.zeros((tok, 1), F32), jnp.zeros((img, 1), F32)]
    for number, pair in enumerate(((text, text_far), (vis, vis_far))):
        for half_rows in pair:
            for c in range(0, half, step):
                wide = half_rows[:, c : c + step].astype(F32)
                squares[number] += jnp.sum(wide * wide, axis=1, keepdims=True)
    scales = [lax.rsqrt(s / (2.0 * half) + EPS) for s in squares]
    for side in range(2):
        text_side, vis_side = (text, vis) if side == 0 else (text_far, vis_far)
        base = (me if side == 0 else 1 - me) * half
        for c in range(0, half, step):
            columns = pl.ds(pl.multiple_of(base + c, step), step)
            scaled = gain[:, columns]
            wk = w_key[columns, :]
            wv = w_value[columns, :]
            for scale, rows, lo in ((scales[0], text_side, 0), (scales[1], vis_side, tok)):
                size = rows.shape[0]
                normed = (rows[:, c : c + step].astype(F32) * scale * scaled).astype(BF16)
                for w, at in ((wk, 0), (wv, kvw)):
                    part = dot(normed, w)
                    if side == 0 and c == 0:
                        total[lo : lo + size, at : at + kvw] = part
                    else:
                        total[lo : lo + size, at : at + kvw] += part
    kv_text[...] = total[:tok, :].astype(BF16)
    own = total[tok : tok + img, :].astype(BF16)
    kv_vis[...] = own
    slot = lax.broadcasted_iota(I32, (n * cap, img), 0)
    chosen = jnp.where(slot == info[0:1, :img], 1.0, 0.0).astype(BF16)
    outgoing = dot(chosen, own).astype(BF16)
    for k in range(n):
        packed[k][...] = outgoing[k * cap : (k + 1) * cap, :]


def attend_kernel(n, kv_heads, query, kv_text, kv_vis, info, *out):
    pos = lax.axis_index("section")
    tok, img = kv_text.shape[0], kv_vis.shape[0]
    kvw = kv_heads * HD
    rows = query.shape[1] // kv_heads
    number = lax.broadcasted_iota(I32, (n * rows, 1), 0) // rows
    slot = jnp.bitwise_xor(number, pos)
    text_ok = slot == info[2:3, :tok]
    vis_ok = slot == info[1:2, :img]
    parts = []
    for g in range(kv_heads):
        q = query[:, g * rows : (g + 1) * rows, :].reshape(n * rows, HD)
        cols = slice(g * HD, (g + 1) * HD)
        vcols = slice(kvw + g * HD, kvw + (g + 1) * HD)
        s_text = jnp.where(text_ok, dot_t(q, kv_text[:, cols]) * HD**-0.5, LOWEST)
        s_vis = jnp.where(vis_ok, dot_t(q, kv_vis[:, cols]) * HD**-0.5, LOWEST)
        top = jnp.maximum(jnp.max(s_text, axis=1, keepdims=True), jnp.max(s_vis, axis=1, keepdims=True))
        w_text = jnp.where(text_ok, jnp.exp(s_text - top), 0.0)
        w_vis = jnp.where(vis_ok, jnp.exp(s_vis - top), 0.0)
        total = jnp.sum(w_text, axis=1, keepdims=True) + jnp.sum(w_vis, axis=1, keepdims=True)
        numerator = dot(w_text.astype(BF16), kv_text[:, vcols]) + dot(w_vis.astype(BF16), kv_vis[:, vcols])
        parts.append((numerator, top, total))
    for k in range(n):
        at = slice(k * rows, (k + 1) * rows)
        put_partial(out[k], kv_heads, *zip(*[tuple(x[at] for x in p) for p in parts]))


def pack_kernel(n, cap, page_cap, slots, info, kv_text, *rest):
    pieces, out, (incoming, staged) = rest[:n], rest[n : 2 * n], rest[2 * n :]
    tok = kv_text.shape[0]
    blocks = tok // PAGE
    for k in range(n):
        incoming[k * cap : (k + 1) * cap, :] = pieces[k][...]
    reach = min(tok, n * cap)
    hit = lax.broadcasted_iota(I32, (reach, n * cap), 0) == info[3:4, : n * cap]
    hot = jnp.where(hit, 1.0, 0.0)
    covered = jnp.sum(hot, axis=1, keepdims=True) > 0.0
    placed = dot(hot.astype(BF16), incoming[...])
    mixed = jnp.where(covered, placed, kv_text[:reach, :].astype(F32)).astype(BF16)
    staged[...] = jnp.zeros(staged.shape, BF16)
    for g in range(blocks):
        if (g + 1) * PAGE <= reach:
            rows = mixed[g * PAGE : (g + 1) * PAGE, :]
        else:
            rows = kv_text[g * PAGE : (g + 1) * PAGE, :]
        staged[slots[g]] = rows
    for k in range(n):
        out[k][...] = staged[k * page_cap : (k + 1) * page_cap]


def store_kernel(n, page_cap, *refs):
    pieces, (keys, values) = refs[:n], refs[n:]
    pos = lax.axis_index("section")
    kvw = keys.shape[2]
    for k in range(n):
        at = pl.ds(jnp.bitwise_xor(pos, k) * page_cap, page_cap)
        keys[at] = pieces[k][:, :, :kvw]
        values[at] = pieces[k][:, :, kvw:]


def join_kernel(kv_heads, steps, *refs):
    pieces, attended = refs[:-1], refs[-1]
    rows = pieces[0].shape[0] - STAT
    stats = [row_to_column(p[rows : rows + 1, :]) for p in pieces]
    tops = [s[:rows] for s in stats]
    highest = tops[0]
    for t in tops[1:]:
        highest = jnp.maximum(highest, t)
    numerator = jnp.zeros((rows, HD), F32)
    total = jnp.zeros((rows, 1), F32)
    for piece, s, t in zip(pieces, stats, tops):
        scale = jnp.exp(t - highest)
        numerator = numerator + piece[:rows, :] * scale
        total = total + s[rows:] * scale
    result = (numerator / total).astype(BF16)
    for h in range(rows // steps):
        attended[0, :, h * HD : (h + 1) * HD] = result[h * steps : (h + 1) * steps, :]


def body(
    text_rows,
    vis_rows,
    img_route,
    norm_gain,
    w_key,
    w_value,
    page_count,
    tail_len,
    page_dest,
    dec_req,
    dec_query,
    dec_key,
    dec_value,
):
    n = lax.axis_size("section")
    tok, half = text_rows.shape
    img = vis_rows.shape[0]
    kvw = w_key.shape[1]
    kv_heads = kvw // HD
    _, steps, q_width = dec_query.shape
    heads = q_width // HD
    q_rows = heads * steps
    blocks = tok // PAGE
    cap = max(2, (2 * img + n - 1) // n)
    page_cap = max(1, (blocks + n - 1) // n)

    def across(array):
        return lax.ppermute(array, "tensor", [(0, 1), (1, 0)])

    def swap(array, k):
        return lax.ppermute(array, "section", [(i, i ^ k) for i in range(n)])

    vis_far = across(vis_rows)
    text_far = across(text_rows)
    query = dec_query.reshape(steps, heads, HD).transpose(1, 0, 2).reshape(1, q_rows, HD)
    queries = query
    k = 1
    while k < n:
        queries = jnp.concatenate([queries, swap(queries, k)], axis=0)
        k *= 2

    width = max(tok, n * cap)
    info, slots, fresh = call(
        lambda *refs: meta_kernel((n, img, tok, blocks, cap, page_cap, kv_heads, steps), *refs),
        (
            jax.ShapeDtypeStruct((8, width), I32),
            jax.ShapeDtypeStruct((blocks,), I32),
            jax.ShapeDtypeStruct((q_rows + STAT, HD), F32),
        ),
        [VM, SM, SM, SM, SM, VM, VM, VM],
        (VM, SM, VM),
        [pltpu.SMEM((n,), I32)],
    )(
        img_route.reshape(n, img),
        page_dest.reshape(n * blocks),
        page_count,
        tail_len,
        dec_req,
        query[0],
        dec_key[0],
        dec_value[0],
    )

    kv_text, kv_vis, *packed = call(
        lambda *refs: project_kernel((n, cap, min(1024, half)), *refs),
        (
            jax.ShapeDtypeStruct((tok, 2 * kvw), BF16),
            jax.ShapeDtypeStruct((img, 2 * kvw), BF16),
            *[jax.ShapeDtypeStruct((cap, 2 * kvw), BF16)] * n,
        ),
        [VM] * 8,
        (VM,) * (2 + n),
        [pltpu.VMEM((tok + img, 2 * kvw), F32)],
        limit=32,
        flops=2 * (tok + img) * 2 * half * 2 * kvw,
        traffic=2 * (tok + img) * 2 * half + 8 * half * kvw,
    )(text_rows, text_far, vis_rows, vis_far, norm_gain.reshape(1, 2 * half), w_key, w_value, info)

    arrived = [packed[0]] + [swap(packed[k], k) for k in range(1, n)]

    partials = call(
        lambda *refs: attend_kernel(n, kv_heads, *refs),
        (jax.ShapeDtypeStruct((q_rows + STAT, HD), F32),) * n,
        [VM] * 4,
        (VM,) * n,
        limit=24,
        flops=4 * n * q_rows * (tok + img) * HD,
        traffic=n * (q_rows + STAT) * HD * 4,
    )(queries, kv_text, kv_vis, info)
    shares = [partials[0]] + [swap(partials[k], k) for k in range(1, n)]

    sent = call(
        lambda *refs: pack_kernel(n, cap, page_cap, *refs),
        (jax.ShapeDtypeStruct((page_cap, PAGE, 2 * kvw), BF16),) * n,
        [SM, VM, VM] + [VM] * n,
        (VM,) * n,
        [pltpu.VMEM((n * cap, 2 * kvw), BF16), pltpu.VMEM((n * page_cap, PAGE, 2 * kvw), BF16)],
        traffic=4 * tok * 2 * kvw,
    )(slots, info, kv_text, *arrived)
    stored = [sent[0]] + [swap(sent[k], k) for k in range(1, n)]

    attended = call(
        lambda *refs: join_kernel(kv_heads, steps, *refs),
        jax.ShapeDtypeStruct(dec_query.shape, BF16),
        [VM] * (n + 1),
        VM,
        traffic=(n + 1) * (q_rows + STAT) * HD * 4,
    )(*shares, fresh)

    cache_key, cache_value = call(
        lambda *refs: store_kernel(n, page_cap, *refs),
        (jax.ShapeDtypeStruct((n * page_cap, PAGE, kvw), BF16),) * 2,
        [VM] * n,
        (VM, VM),
        traffic=4 * tok * 2 * kvw,
    )(*stored)
    return (attended, cache_key, cache_value)


def solution(mesh):
    return jax.shard_map(
        body,
        mesh=mesh,
        in_specs=(
            P(("groups", "section"), "tensor"),
            P(("groups", "section"), "tensor"),
            P("groups", None),
            P(),
            P(None, "tensor"),
            P(None, "tensor"),
            P("groups"),
            P("groups"),
            P("groups", None),
            P("groups"),
            P(("groups", "section"), None, "tensor"),
            P(("groups", "section"), None, "tensor"),
            P(("groups", "section"), None, "tensor"),
        ),
        out_specs=(
            P(("groups", "section"), None, "tensor"),
            P(("groups", "section"), None, "tensor"),
            P(("groups", "section"), None, "tensor"),
        ),
        check_vma=False,
    )
```

```python
import jax
import jax.numpy as jnp
from jax import lax
from jax.experimental import pallas as pl
from jax.experimental.pallas import tpu as pltpu
from jax.sharding import PartitionSpec as P

HD = 128
PAGE = 16
LOWEST = -1e30
EPS = 1e-06
STAT = 8
F32 = jnp.float32
BF16 = jnp.bfloat16
I32 = jnp.int32

VM = pl.BlockSpec(memory_space=pltpu.VMEM)
SM = pl.BlockSpec(memory_space=pltpu.SMEM)
ANY = pl.BlockSpec(memory_space=pl.ANY)
MIB = 1 << 20


def call(kernel, out_shape, in_specs, out_specs, scratch=(), limit=16, flops=0, traffic=0):
    return pl.pallas_call(
        kernel,
        out_shape=out_shape,
        in_specs=in_specs,
        out_specs=out_specs,
        scratch_shapes=list(scratch),
        compiler_params=pltpu.CompilerParams(vmem_limit_bytes=limit * MIB),
        cost_estimate=pl.CostEstimate(flops=flops, bytes_accessed=traffic, transcendentals=0),
    )


def dot(a, b):
    return jnp.dot(a, b, preferred_element_type=F32)


def dot_t(a, b):
    return lax.dot_general(a, b, (((1,), (1,)), ((), ())), preferred_element_type=F32)


def diagonal(shape):
    return lax.broadcasted_iota(I32, shape, 0) == lax.broadcasted_iota(I32, shape, 1)


def column_to_row(column):
    rows = column.shape[0]
    return jnp.sum(jnp.where(diagonal((rows, rows)), column, 0.0), axis=0, keepdims=True)


def row_to_column(row):
    lanes = row.shape[1]
    return jnp.sum(jnp.where(diagonal((lanes, lanes)), row, 0.0), axis=1, keepdims=True)


def put_partial(out, kv_heads, numerators, tops, totals):
    rows = numerators[0].shape[0]
    for g in range(kv_heads):
        out[g * rows : (g + 1) * rows, :] = numerators[g]
    stats = column_to_row(jnp.concatenate(list(tops) + list(totals), axis=0))
    out[kv_heads * rows :, :] = jnp.broadcast_to(stats, (STAT, stats.shape[1]))


def prepare_kernel(sizes, *refs):
    n, img, tok, blocks, cap, page_cap, kv_heads, steps = sizes
    far, (info, slots, fresh, square), near, small, (starts, sems) = (
        refs[:12],
        refs[12:16],
        refs[16:20],
        refs[20:28],
        refs[28:],
    )
    copies = [pltpu.make_async_copy(a, b, sems.at[i]) for i, (a, b) in enumerate(zip(far, small + near))]
    for c in copies:
        c.start()
    route, pages, count, tail, req, query, key, value = small
    text, vis, w_key, w_value = near
    for c in copies[: len(small)]:
        c.wait()
    pos = lax.axis_index("section")
    table = [route[:, e * img : (e + 1) * img] for e in range(n)]
    own = jnp.zeros((1, img), I32)
    for e in range(n):
        own = jnp.where(pos == e, table[e], own)
    stations = lax.broadcasted_iota(I32, (n, img), 0)
    marks = own == stations
    ones = jnp.where(marks, 1.0, 0.0).astype(BF16)
    earlier = lax.broadcasted_iota(I32, (img, img), 0) < lax.broadcasted_iota(I32, (img, img), 1)
    prefix = dot(ones, jnp.where(earlier, 1.0, 0.0).astype(BF16))
    before = jnp.zeros((n, 1), I32)
    lanes = lax.broadcasted_iota(I32, (1, n * cap), 1)
    source, inner = lanes // cap, lanes % cap
    fits = jnp.zeros((1, n * cap), I32)
    offset = jnp.zeros((1, n * cap), I32)
    for e in range(n):
        here = jnp.sum((table[e] == stations).astype(I32), axis=1, keepdims=True)
        before = before + jnp.where(e < pos, here, 0)
        arriving = jnp.sum((table[e] == pos).astype(I32), axis=1, keepdims=True)
        fits = fits + jnp.where(source == e, arriving, 0)
        offset = offset + jnp.where(source > e, arriving, 0)
    local = jnp.sum(jnp.where(marks, prefix, 0.0), axis=0, keepdims=True).astype(I32)
    rank = local + jnp.sum(jnp.where(marks, before, 0), axis=0, keepdims=True)
    send = own * cap + local
    place = own * tok + rank
    target = jnp.where(inner < fits, offset + inner, -1)
    replaced = jnp.sum(jnp.where(inner == 0, fits, 0), axis=1, keepdims=True)
    total = jnp.int32(0)
    for r in range(n):
        starts[r] = total
        total = total + count[r]
    inside = lax.broadcasted_iota(I32, (1, tok), 1)
    text_at = inside + pos * tok
    text_slot = jnp.full((1, tok), -1, I32)
    vis_slot = jnp.full((1, img), -1, I32)
    for b in range(n):
        r = req[b]
        first = starts[r] * PAGE
        last = first + (count[r] - 1) * PAGE + tail[r]
        text_slot = jnp.where((text_at >= first) & (text_at < last), b, text_slot)
        vis_slot = jnp.where((place >= first) & (place < last), b, vis_slot)
    text_slot = jnp.where(inside < replaced, -1, text_slot)
    info[0:1, :img] = send
    info[1:2, :img] = vis_slot
    info[2:3, :tok] = text_slot
    info[3:4, : n * cap] = target
    for g in range(blocks):
        holder = pages[0, pos * blocks + g]
        slot = holder * page_cap
        for e in range(g):
            slot = slot + (pages[0, pos * blocks + e] == holder).astype(I32)
        slots[g] = slot
    rows = query.shape[0] // kv_heads
    row = lax.broadcasted_iota(I32, (rows, steps), 0)
    causal = lax.broadcasted_iota(I32, (rows, steps), 1) <= row % steps
    parts = ([], [], [])
    for g in range(kv_heads):
        cols = slice(g * HD, (g + 1) * HD)
        scores = dot_t(query[g * rows : (g + 1) * rows, :], key[:, cols]) * HD**-0.5
        scores = jnp.where(causal, scores, LOWEST)
        top = jnp.max(scores, axis=1, keepdims=True)
        weights = jnp.where(causal, jnp.exp(scores - top), 0.0)
        numerator = dot(weights.astype(BF16), value[:, cols])
        for held, new in zip(parts, (numerator, top, jnp.sum(weights, axis=1, keepdims=True))):
            held.append(new)
    put_partial(fresh, kv_heads, *parts)
    for c in copies[len(small) : len(small) + 2]:
        c.wait()
    square[:tok, :] = squares_of(text)
    square[tok:, :] = squares_of(vis)
    for c in copies[len(small) + 2 :]:
        c.wait()


def squares_of(rows):
    total = jnp.zeros((rows.shape[0], HD), F32)
    for c in range(0, rows.shape[1], HD):
        wide = rows[:, c : c + HD].astype(F32)
        total = total + wide * wide
    return total


def project_kernel(sizes, text, text_far, vis, vis_far, gain, w_key, w_value, square, info, kv_text, kv_vis, packed, total):
    n, cap, step = sizes
    tok, half = text.shape
    img = vis.shape[0]
    kvw = w_key.shape[1]
    me = lax.axis_index("tensor")
    scales = []
    for far, lo in ((text_far, 0), (vis_far, tok)):
        size = far.shape[0]
        sums = jnp.sum(square[lo : lo + size, :] + squares_of(far), axis=1, keepdims=True)
        scales.append(lax.rsqrt(sums / (2.0 * half) + EPS))
    for side in range(2):
        text_side, vis_side = (text, vis) if side == 0 else (text_far, vis_far)
        base = (me if side == 0 else 1 - me) * half
        for c in range(0, half, step):
            columns = pl.ds(pl.multiple_of(base + c, step), step)
            scaled = gain[:, columns]
            wk = w_key[columns, :]
            wv = w_value[columns, :]
            for scale, rows, lo in ((scales[0], text_side, 0), (scales[1], vis_side, tok)):
                size = rows.shape[0]
                normed = (rows[:, c : c + step].astype(F32) * scale * scaled).astype(BF16)
                for w, at in ((wk, 0), (wv, kvw)):
                    part = dot(normed, w)
                    if side == 0 and c == 0:
                        total[lo : lo + size, at : at + kvw] = part
                    else:
                        total[lo : lo + size, at : at + kvw] += part
    kv_text[...] = total[:tok, :].astype(BF16)
    own = total[tok : tok + img, :].astype(BF16)
    kv_vis[...] = own
    slot = lax.broadcasted_iota(I32, (n * cap, img), 0)
    chosen = jnp.where(slot == info[0:1, :img], 1.0, 0.0).astype(BF16)
    packed[...] = dot(chosen, own).astype(BF16)


def attend_kernel(n, kv_heads, query, kv_text, kv_vis, info, out):
    tok, img = kv_text.shape[0], kv_vis.shape[0]
    kvw = kv_heads * HD
    rows = query.shape[1] // kv_heads
    slot = lax.broadcasted_iota(I32, (n * rows, 1), 0) // rows
    text_ok = slot == info[2:3, :tok]
    vis_ok = slot == info[1:2, :img]
    parts = []
    for g in range(kv_heads):
        q = query[:, g * rows : (g + 1) * rows, :].reshape(n * rows, HD)
        cols = slice(g * HD, (g + 1) * HD)
        vcols = slice(kvw + g * HD, kvw + (g + 1) * HD)
        s_text = jnp.where(text_ok, dot_t(q, kv_text[:, cols]) * HD**-0.5, LOWEST)
        s_vis = jnp.where(vis_ok, dot_t(q, kv_vis[:, cols]) * HD**-0.5, LOWEST)
        top = jnp.maximum(jnp.max(s_text, axis=1, keepdims=True), jnp.max(s_vis, axis=1, keepdims=True))
        w_text = jnp.where(text_ok, jnp.exp(s_text - top), 0.0)
        w_vis = jnp.where(vis_ok, jnp.exp(s_vis - top), 0.0)
        total = jnp.sum(w_text, axis=1, keepdims=True) + jnp.sum(w_vis, axis=1, keepdims=True)
        numerator = dot(w_text.astype(BF16), kv_text[:, vcols]) + dot(w_vis.astype(BF16), kv_vis[:, vcols])
        parts.append((numerator, top, total))
    for k in range(n):
        at = slice(k * rows, (k + 1) * rows)
        put_partial(out.at[k], kv_heads, *zip(*[tuple(x[at] for x in p) for p in parts]))


def pack_kernel(n, cap, page_cap, slots, info, kv_text, incoming, out):
    tok = kv_text.shape[0]
    kvw = kv_text.shape[1] // 2
    blocks = tok // PAGE
    reach = min(tok, n * cap)
    hit = lax.broadcasted_iota(I32, (reach, n * cap), 0) == info[3:4, : n * cap]
    hot = jnp.where(hit, 1.0, 0.0)
    covered = jnp.sum(hot, axis=1, keepdims=True) > 0.0
    placed = dot(hot.astype(BF16), incoming[...])
    mixed = jnp.where(covered, placed, kv_text[:reach, :].astype(F32)).astype(BF16)
    out[...] = jnp.zeros(out.shape, BF16)
    for g in range(blocks):
        if (g + 1) * PAGE <= reach:
            rows = mixed[g * PAGE : (g + 1) * PAGE, :]
        else:
            rows = kv_text[g * PAGE : (g + 1) * PAGE, :]
        slot = slots[g]
        out[slot // page_cap, 0, slot % page_cap] = rows[:, :kvw]
        out[slot // page_cap, 1, slot % page_cap] = rows[:, kvw:]


def store_kernel(pages, keys, values, sems):
    copies = [pltpu.make_async_copy(pages.at[:, i], out, sems.at[i]) for i, out in enumerate((keys, values))]
    for c in copies:
        c.start()
    for c in copies:
        c.wait()


def join_kernel(steps, shares, fresh, attended):
    rows = fresh.shape[0] - STAT
    pieces = [shares.at[k] for k in range(shares.shape[0])] + [fresh]
    stats = [row_to_column(p[rows : rows + 1, :]) for p in pieces]
    tops = [s[:rows] for s in stats]
    highest = tops[0]
    for t in tops[1:]:
        highest = jnp.maximum(highest, t)
    numerator = jnp.zeros((rows, HD), F32)
    total = jnp.zeros((rows, 1), F32)
    for piece, s, t in zip(pieces, stats, tops):
        scale = jnp.exp(t - highest)
        numerator = numerator + piece[:rows, :] * scale
        total = total + s[rows:] * scale
    result = (numerator / total).astype(BF16)
    for h in range(rows // steps):
        attended[0, :, h * HD : (h + 1) * HD] = result[h * steps : (h + 1) * steps, :]


def body(
    text_rows,
    vis_rows,
    img_route,
    norm_gain,
    w_key,
    w_value,
    page_count,
    tail_len,
    page_dest,
    dec_req,
    dec_query,
    dec_key,
    dec_value,
):
    n = lax.axis_size("section")
    tok, half = text_rows.shape
    img = vis_rows.shape[0]
    kvw = w_key.shape[1]
    kv_heads = kvw // HD
    _, steps, q_width = dec_query.shape
    heads = q_width // HD
    q_rows = heads * steps
    blocks = tok // PAGE
    cap = max(2, (2 * img + n - 1) // n)
    page_cap = max(1, (blocks + n - 1) // n)

    def across(array):
        return lax.ppermute(array, "tensor", [(0, 1), (1, 0)])

    def exchange(array):
        return lax.all_to_all(array, "section", split_axis=0, concat_axis=0, tiled=True)

    def remote(array):
        return pltpu.with_memory_space_constraint(array, pltpu.HBM)

    def local(array):
        return pltpu.with_memory_space_constraint(array, pltpu.VMEM)

    vis_far = across(vis_rows)
    text_far = across(text_rows)
    query = dec_query.reshape(steps, heads, HD).transpose(1, 0, 2).reshape(1, q_rows, HD)
    queries = exchange(jnp.broadcast_to(query, (n, q_rows, HD)))

    width = max(tok, n * cap)
    arguments = (
        img_route.T,
        page_dest.T,
        page_count,
        tail_len,
        dec_req,
        query[0],
        dec_key[0],
        dec_value[0],
        text_rows,
        vis_rows,
        w_key,
        w_value,
    )
    info, slots, fresh, square, *near = call(
        lambda *refs: prepare_kernel((n, img, tok, blocks, cap, page_cap, kv_heads, steps), *refs),
        (
            jax.ShapeDtypeStruct((8, width), I32),
            jax.ShapeDtypeStruct((blocks,), I32),
            jax.ShapeDtypeStruct((q_rows + STAT, HD), F32),
            jax.ShapeDtypeStruct((tok + img, HD), F32),
            *[pltpu.VMEM(a.shape, a.dtype) for a in arguments[8:]],
        ),
        [ANY] * len(arguments),
        (VM, SM, VM, VM) + (VM,) * 4,
        [
            *[(pltpu.SMEM if 1 <= i <= 4 else pltpu.VMEM)(a.shape, a.dtype) for i, a in enumerate(arguments[:8])],
            pltpu.SMEM((n,), I32),
            pltpu.SemaphoreType.DMA((len(arguments),)),
        ],
        flops=1 << 20,
        traffic=2 * 2 * half * 2 * kvw * 2,
    )(*[remote(a) for a in arguments])
    text_near, vis_near, key_near, value_near = near

    kv_text, kv_vis, packed = call(
        lambda *refs: project_kernel((n, cap, min(1024, half)), *refs),
        (
            jax.ShapeDtypeStruct((tok, 2 * kvw), BF16),
            jax.ShapeDtypeStruct((img, 2 * kvw), BF16),
            jax.ShapeDtypeStruct((n * cap, 2 * kvw), BF16),
        ),
        [VM] * 9,
        (VM,) * 3,
        [pltpu.VMEM((tok + img, 2 * kvw), F32)],
        flops=2 * (tok + img) * 2 * half * 2 * kvw,
        traffic=2 * (tok + img) * 2 * half + 8 * half * kvw,
    )(
        local(text_near),
        text_far,
        local(vis_near),
        vis_far,
        remote(norm_gain.reshape(1, 2 * half)),
        local(key_near),
        local(value_near),
        square,
        info,
    )
    arrived = exchange(packed)

    partials = call(
        lambda *refs: attend_kernel(n, kv_heads, *refs),
        jax.ShapeDtypeStruct((n, q_rows + STAT, HD), F32),
        [VM] * 4,
        VM,
        flops=4 * n * q_rows * (tok + img) * HD,
        traffic=n * (q_rows + STAT) * HD * 4,
    )(queries, kv_text, kv_vis, info)
    shares = exchange(partials)

    sent = call(
        lambda *refs: pack_kernel(n, cap, page_cap, *refs),
        jax.ShapeDtypeStruct((n, 2, page_cap, PAGE, kvw), BF16),
        [SM, VM, VM, VM],
        VM,
        traffic=4 * tok * 2 * kvw,
    )(slots, info, kv_text, arrived)
    stored = exchange(sent)

    attended = call(
        lambda *refs: join_kernel(steps, *refs),
        jax.ShapeDtypeStruct(dec_query.shape, BF16),
        [VM] * 2,
        VM,
        traffic=(n + 1) * (q_rows + STAT) * HD * 4,
    )(shares, fresh)

    cache_key, cache_value = call(
        store_kernel,
        (jax.ShapeDtypeStruct((n, page_cap, PAGE, kvw), BF16),) * 2,
        [ANY],
        (ANY, ANY),
        [pltpu.SemaphoreType.DMA((2,))],
        traffic=4 * tok * 2 * kvw,
    )(stored)
    slots_here = n * page_cap
    return (
        attended,
        cache_key.reshape(slots_here, PAGE, kvw),
        cache_value.reshape(slots_here, PAGE, kvw),
    )


def solution(mesh):
    return jax.shard_map(
        body,
        mesh=mesh,
        in_specs=(
            P(("groups", "section"), "tensor"),
            P(("groups", "section"), "tensor"),
            P("groups", None),
            P(),
            P(None, "tensor"),
            P(None, "tensor"),
            P("groups"),
            P("groups"),
            P("groups", None),
            P("groups"),
            P(("groups", "section"), None, "tensor"),
            P(("groups", "section"), None, "tensor"),
            P(("groups", "section"), None, "tensor"),
        ),
        out_specs=(
            P(("groups", "section"), None, "tensor"),
            P(("groups", "section"), None, "tensor"),
            P(("groups", "section"), None, "tensor"),
        ),
        check_vma=False,
    )
```

```python
import jax
import jax.numpy as jnp
from jax import lax
from jax.experimental import pallas as pl
from jax.experimental.pallas import tpu as pltpu
from jax.sharding import PartitionSpec as P

HD = 128
PAGE = 16
LOWEST = -1e30
EPS = 1e-06
STAT = 8
F32 = jnp.float32
BF16 = jnp.bfloat16
I32 = jnp.int32

VM = pl.BlockSpec(memory_space=pltpu.VMEM)
SM = pl.BlockSpec(memory_space=pltpu.SMEM)
ANY = pl.BlockSpec(memory_space=pl.ANY)
MIB = 1 << 20


def call(kernel, out_shape, in_specs, out_specs, scratch=(), limit=16, flops=0, traffic=0):
    return pl.pallas_call(
        kernel,
        out_shape=out_shape,
        in_specs=in_specs,
        out_specs=out_specs,
        scratch_shapes=list(scratch),
        compiler_params=pltpu.CompilerParams(vmem_limit_bytes=limit * MIB),
        cost_estimate=pl.CostEstimate(flops=flops, bytes_accessed=traffic, transcendentals=0),
    )


def dot(a, b):
    return jnp.dot(a, b, preferred_element_type=F32)


def dot_t(a, b):
    return lax.dot_general(a, b, (((1,), (1,)), ((), ())), preferred_element_type=F32)


def diagonal(shape):
    return lax.broadcasted_iota(I32, shape, 0) == lax.broadcasted_iota(I32, shape, 1)


def column_to_row(column):
    rows = column.shape[0]
    return jnp.sum(jnp.where(diagonal((rows, rows)), column, 0.0), axis=0, keepdims=True)


def row_to_column(row):
    lanes = row.shape[1]
    return jnp.sum(jnp.where(diagonal((lanes, lanes)), row, 0.0), axis=1, keepdims=True)


def squares_of(rows):
    total = jnp.zeros((rows.shape[0], HD), F32)
    for c in range(0, rows.shape[1], HD):
        wide = rows[:, c : c + HD].astype(F32)
        total = total + wide * wide
    return total


def split_three(values):
    high = values.astype(BF16).astype(F32)
    rest = values - high
    middle = rest.astype(BF16).astype(F32)
    return high, middle, rest - middle


def softmax_parts(query, key, value, usable):
    scores = jnp.where(usable, dot_t(query, key) * HD**-0.5, LOWEST)
    top = jnp.max(scores, axis=1, keepdims=True)
    weights = jnp.where(usable, jnp.exp(scores - top), 0.0)
    return dot(weights.astype(BF16), value), top, jnp.sum(weights, axis=1, keepdims=True)


def prepare_kernel(sizes, *refs):
    n, img, tok, blocks, cap, lot, page_cap, kv_heads, steps = sizes
    far, (info, slots, fresh), near, small, (starts, sems) = (
        refs[:12],
        refs[12:15],
        refs[15:19],
        refs[19:27],
        refs[27:],
    )
    copies = [pltpu.make_async_copy(a, b, sems.at[i]) for i, (a, b) in enumerate(zip(far, small + near))]
    for c in copies:
        c.start()
    route, pages, count, tail, req, query, key, value = small
    for c in copies[: len(small)]:
        c.wait()
    pos = lax.axis_index("section")
    table = [route[:, e * img : (e + 1) * img] for e in range(n)]
    own = jnp.zeros((1, img), I32)
    for e in range(n):
        own = jnp.where(pos == e, table[e], own)
    marks = own == lax.broadcasted_iota(I32, (n, img), 0)
    ones = jnp.where(marks, 1.0, 0.0).astype(BF16)
    earlier = lax.broadcasted_iota(I32, (img, img), 0) < lax.broadcasted_iota(I32, (img, img), 1)
    prefix = dot(ones, jnp.where(earlier, 1.0, 0.0).astype(BF16))
    local = jnp.sum(jnp.where(marks, prefix, 0.0), axis=0, keepdims=True).astype(I32)
    info[0:1, :img] = own * lot + local
    lanes = lax.broadcasted_iota(I32, (1, n * lot), 1)
    source, inner = lanes // lot, lanes % lot
    fits = jnp.zeros((1, n * lot), I32)
    offset = jnp.zeros((1, n * lot), I32)
    for e in range(n):
        arriving = jnp.sum((table[e] == pos).astype(I32), axis=1, keepdims=True)
        fits = fits + jnp.where(source == e, arriving, 0)
        offset = offset + jnp.where(source > e, arriving, 0)
    info[2:3, : n * lot] = jnp.where(inner < fits, offset + inner, -1)
    total = jnp.int32(0)
    for r in range(n):
        starts[r] = total
        total = total + count[r]
    token = lax.broadcasted_iota(I32, (1, tok), 1) + pos * tok
    token_slot = jnp.full((1, tok), -1, I32)
    for b in range(n):
        r = req[b]
        first = starts[r] * PAGE
        last = first + (count[r] - 1) * PAGE + tail[r]
        token_slot = jnp.where((token >= first) & (token < last), b, token_slot)
    info[1:2, :tok] = token_slot
    for g in range(blocks):
        holder = pages[0, pos * blocks + g]
        slot = holder * page_cap
        for e in range(g):
            slot = slot + (pages[0, pos * blocks + e] == holder).astype(I32)
        slots[g] = slot
    rows = query.shape[0] // kv_heads
    row = lax.broadcasted_iota(I32, (rows, steps), 0)
    causal = lax.broadcasted_iota(I32, (rows, steps), 1) <= row % steps
    tops, totals = [], []
    for g in range(kv_heads):
        cols = slice(g * HD, (g + 1) * HD)
        own_query = query[g * rows : (g + 1) * rows, :]
        numerator, top, weight = softmax_parts(own_query, key[:, cols], value[:, cols], causal)
        fresh[g * rows : (g + 1) * rows, :] = numerator
        tops.append(top)
        totals.append(weight)
    stats = column_to_row(jnp.concatenate(tops + totals, axis=0))
    fresh[kv_heads * rows :, :] = jnp.broadcast_to(stats, (STAT, stats.shape[1]))
    for c in copies[len(small) :]:
        c.wait()


def project(near, far, gain, w_key, w_value, total, step):
    half = near.shape[1]
    kvw = w_key.shape[1]
    me = lax.axis_index("tensor")
    sums = jnp.sum(squares_of(near) + squares_of(far), axis=1, keepdims=True)
    scale = lax.rsqrt(sums / (2.0 * half) + EPS)
    for rows, side in ((near, me), (far, 1 - me)):
        for c in range(0, half, step):
            columns = pl.ds(pl.multiple_of(side * half + c, step), step)
            normed = (rows[:, c : c + step].astype(F32) * scale * gain[:, columns]).astype(BF16)
            for w, at in ((w_key, 0), (w_value, kvw)):
                part = dot(normed, w[columns, :])
                if rows is near and c == 0:
                    total[:, at : at + kvw] = part
                else:
                    total[:, at : at + kvw] += part


def vis_kernel(n, lot, step, near, far, gain, w_key, w_value, info, query, out, total):
    project(near, far, gain, w_key, w_value, total, step)
    img = near.shape[0]
    slot = lax.broadcasted_iota(I32, (n * lot, img), 0)
    chosen = jnp.where(slot == info[0:1, :img], 1.0, 0.0).astype(BF16)
    packed = dot(chosen, total[...].astype(BF16)).astype(BF16)
    q_lots = out.shape[1] - lot
    for k in range(n):
        for j in range(query.shape[0] // q_lots):
            out[k, :q_lots, j * HD : (j + 1) * HD] = query[j * q_lots : (j + 1) * q_lots, :]
        out[k, q_lots:, :] = packed[k * lot : (k + 1) * lot, :]


def text_kernel(step, near, far, gain, w_key, w_value, out, total):
    project(near, far, gain, w_key, w_value, total, step)
    out[...] = total[...].astype(BF16)


def attend_kernel(n, cap, lot, page_cap, kv_heads, slots, info, kv_text, arrived, out, kv):
    tok = kv_text.shape[0]
    kvw = kv_heads * HD
    q_lots = arrived.shape[1] - lot
    reach = min(tok, n * cap)
    hit = lax.broadcasted_iota(I32, (reach, n * lot), 0) == info[2:3, : n * lot]
    hot = jnp.where(hit, 1.0, 0.0)
    covered = jnp.sum(hot, axis=1, keepdims=True) > 0.0
    incoming = jnp.concatenate([arrived[k, q_lots:, :] for k in range(n)], axis=0)
    placed = dot(hot.astype(BF16), incoming)
    kv[:reach, :] = jnp.where(covered, placed, kv_text[:reach, :].astype(F32)).astype(BF16)
    if reach < tok:
        kv[reach:, :] = kv_text[reach:, :]
    chunk = page_cap * PAGE
    halves = 2 * kv_heads
    pages = halves * chunk
    out[:, :pages, :] = jnp.zeros((n, pages, HD), BF16)
    for g in range(tok // PAGE):
        slot = slots[g]
        for h in range(halves):
            at = pl.ds(pl.multiple_of((slot % page_cap) * PAGE + h * chunk, PAGE), PAGE)
            out[slot // page_cap, at, :] = kv[g * PAGE : (g + 1) * PAGE, h * HD : (h + 1) * HD]
    groups = arrived.shape[2] // HD // kv_heads
    rows = groups * q_lots
    slot = lax.broadcasted_iota(I32, (n * rows, 1), 0) // rows
    usable = slot == info[1:2, :tok]
    tops, totals = [], []
    for g in range(kv_heads):
        query = jnp.concatenate(
            [
                arrived[k, :q_lots, (g * groups + j) * HD : (g * groups + j + 1) * HD]
                for k in range(n)
                for j in range(groups)
            ],
            axis=0,
        )
        key = kv[:, g * HD : (g + 1) * HD]
        value = kv[:, kvw + g * HD : kvw + (g + 1) * HD]
        numerator, top, weight = softmax_parts(query, key, value, usable)
        numerator = numerator.astype(BF16)
        for k in range(n):
            out[k, pages + g * rows : pages + (g + 1) * rows, :] = numerator[k * rows : (k + 1) * rows, :]
        tops.append(top)
        totals.append(weight)
    line = lax.broadcasted_iota(I32, (PAGE, HD), 0)
    for k in range(n):
        at = slice(k * rows, (k + 1) * rows)
        stats = column_to_row(jnp.concatenate([x[at] for x in tops + totals], axis=0))
        high, middle, low = split_three(stats)
        lines = jnp.where(line == 0, high, jnp.where(line == 1, middle, jnp.where(line == 2, low, 0.0)))
        out[k, pages + kv_heads * rows :, :] = lines.astype(BF16)


def finish_kernel(steps, page_cap, shares, fresh, attended, keys, values, sems):
    n = shares.shape[0]
    rows = fresh.shape[0] - STAT
    chunk = page_cap * PAGE
    copies = []
    for i, out in enumerate((keys, values)):
        for h in range(out.shape[2] // HD):
            at = len(copies)
            copies.append(
                pltpu.make_async_copy(
                    shares.at[:, at * chunk : (at + 1) * chunk, :],
                    out.at[:, :, h * HD : (h + 1) * HD],
                    sems.at[at],
                )
            )
    for c in copies:
        c.start()
    pages = len(copies) * chunk
    stats = [row_to_column(fresh[rows : rows + 1, :])]
    for k in range(n):
        lines = shares[k, pages + rows :, :].astype(F32)
        stats.append(row_to_column(lines[0:1] + lines[1:2] + lines[2:3]))
    highest = stats[0][:rows]
    for s in stats[1:]:
        highest = jnp.maximum(highest, s[:rows])
    scale = jnp.exp(stats[0][:rows] - highest)
    numerator = fresh[:rows, :] * scale
    total = stats[0][rows:] * scale
    for k in range(n):
        scale = jnp.exp(stats[k + 1][:rows] - highest)
        numerator = numerator + shares[k, pages : pages + rows, :].astype(F32) * scale
        total = total + stats[k + 1][rows:] * scale
    result = (numerator / total).astype(BF16)
    for h in range(rows // steps):
        attended[0, :, h * HD : (h + 1) * HD] = result[h * steps : (h + 1) * steps, :]
    for c in copies:
        c.wait()


def body(
    text_rows,
    vis_rows,
    img_route,
    norm_gain,
    w_key,
    w_value,
    page_count,
    tail_len,
    page_dest,
    dec_req,
    dec_query,
    dec_key,
    dec_value,
):
    n = lax.axis_size("section")
    tok, half = text_rows.shape
    img = vis_rows.shape[0]
    kvw = w_key.shape[1]
    kv_heads = kvw // HD
    _, steps, q_width = dec_query.shape
    heads = q_width // HD
    q_rows = heads * steps
    blocks = tok // PAGE
    cap = max(2, (2 * img + n - 1) // n)
    page_cap = max(1, (blocks + n - 1) // n)

    def across(array):
        return lax.ppermute(array, "tensor", [(0, 1), (1, 0)])

    def exchange(array):
        return lax.all_to_all(array, "section", split_axis=0, concat_axis=0, tiled=True)

    def remote(array):
        return pltpu.with_memory_space_constraint(array, pltpu.HBM)

    def local(array):
        return pltpu.with_memory_space_constraint(array, pltpu.VMEM)

    vis_far = across(vis_rows)
    text_far = across(text_rows)
    query = dec_query.reshape(steps, heads, HD).transpose(1, 0, 2).reshape(q_rows, HD)

    lot = -(-cap // PAGE) * PAGE
    q_lots = q_rows * HD // (2 * kvw)
    width = max(tok, n * lot)
    arguments = (
        img_route.T,
        page_dest.T,
        page_count,
        tail_len,
        dec_req,
        query,
        dec_key[0],
        dec_value[0],
        w_key,
        w_value,
        vis_rows,
        text_rows,
    )
    info, slots, fresh, key_near, value_near, vis_near, text_near = call(
        lambda *refs: prepare_kernel((n, img, tok, blocks, cap, lot, page_cap, kv_heads, steps), *refs),
        (
            jax.ShapeDtypeStruct((8, width), I32),
            jax.ShapeDtypeStruct((blocks,), I32),
            jax.ShapeDtypeStruct((q_rows + STAT, HD), F32),
            *[pltpu.VMEM(a.shape, a.dtype) for a in arguments[8:]],
        ),
        [ANY] * len(arguments),
        (VM, SM, VM) + (VM,) * 4,
        [
            *[(pltpu.SMEM if 1 <= i <= 4 else pltpu.VMEM)(a.shape, a.dtype) for i, a in enumerate(arguments[:8])],
            pltpu.SMEM((n,), I32),
            pltpu.SemaphoreType.DMA((len(arguments),)),
        ],
        flops=1 << 20,
        traffic=2 * 2 * half * 2 * kvw * 2,
    )(*[remote(a) for a in arguments])
    gain = remote(norm_gain.reshape(1, 2 * half))
    weights = (gain, local(key_near), local(value_near))

    step = min(1024, half)
    packed = call(
        lambda *refs: vis_kernel(n, lot, step, *refs),
        jax.ShapeDtypeStruct((n, q_lots + lot, 2 * kvw), BF16),
        [VM] * 7,
        VM,
        [pltpu.VMEM((img, 2 * kvw), F32)],
        flops=2 * img * 2 * half * 2 * kvw,
        traffic=2 * img * 2 * half + 8 * half * kvw,
    )(local(vis_near), vis_far, *weights, info, remote(query))
    arrived = exchange(packed)

    kv_text = call(
        lambda *refs: text_kernel(step, *refs),
        jax.ShapeDtypeStruct((tok, 2 * kvw), BF16),
        [VM] * 5,
        VM,
        [pltpu.VMEM((tok, 2 * kvw), F32)],
        flops=2 * tok * 2 * half * 2 * kvw,
        traffic=2 * tok * 2 * half + 8 * half * kvw,
    )(local(text_near), text_far, *weights)

    sent = call(
        lambda *refs: attend_kernel(n, cap, lot, page_cap, kv_heads, *refs),
        jax.ShapeDtypeStruct((n, page_cap * PAGE * 2 * kv_heads + q_rows + PAGE, HD), BF16),
        [SM, VM, VM, VM],
        VM,
        [pltpu.VMEM((tok, 2 * kvw), BF16)],
        flops=4 * n * q_rows * tok * HD,
        traffic=n * (q_rows + STAT) * HD * 4,
    )(slots, info, kv_text, arrived)
    shares = exchange(sent)

    slots_here = n * page_cap
    attended, cache_key, cache_value = call(
        lambda *refs: finish_kernel(steps, page_cap, *refs),
        (
            jax.ShapeDtypeStruct(dec_query.shape, BF16),
            jax.ShapeDtypeStruct((n, page_cap * PAGE, kvw), BF16),
            jax.ShapeDtypeStruct((n, page_cap * PAGE, kvw), BF16),
        ),
        [VM, VM],
        (VM, ANY, ANY),
        [pltpu.SemaphoreType.DMA((2 * kv_heads,))],
        traffic=4 * tok * 2 * kvw,
    )(shares, fresh)
    return (
        attended,
        cache_key.reshape(slots_here, PAGE, kvw),
        cache_value.reshape(slots_here, PAGE, kvw),
    )


def solution(mesh):
    return jax.shard_map(
        body,
        mesh=mesh,
        in_specs=(
            P(("groups", "section"), "tensor"),
            P(("groups", "section"), "tensor"),
            P("groups", None),
            P(),
            P(None, "tensor"),
            P(None, "tensor"),
            P("groups"),
            P("groups"),
            P("groups", None),
            P("groups"),
            P(("groups", "section"), None, "tensor"),
            P(("groups", "section"), None, "tensor"),
            P(("groups", "section"), None, "tensor"),
        ),
        out_specs=(
            P(("groups", "section"), None, "tensor"),
            P(("groups", "section"), None, "tensor"),
            P(("groups", "section"), None, "tensor"),
        ),
        check_vma=False,
    )
```

```python
import jax
import jax.numpy as jnp
from jax import lax
from jax.experimental import pallas as pl
from jax.experimental.pallas import tpu as pltpu
from jax.sharding import PartitionSpec as P

HD = 128
PAGE = 16
LOWEST = -1e30
EPS = 1e-06
STAT = 8
F32 = jnp.float32
BF16 = jnp.bfloat16
I32 = jnp.int32

VM = pl.BlockSpec(memory_space=pltpu.VMEM)
SM = pl.BlockSpec(memory_space=pltpu.SMEM)
ANY = pl.BlockSpec(memory_space=pl.ANY)
MIB = 1 << 20


def call(kernel, out_shape, in_specs, out_specs, scratch=(), limit=16, flops=0, traffic=0):
    return pl.pallas_call(
        kernel,
        out_shape=out_shape,
        in_specs=in_specs,
        out_specs=out_specs,
        scratch_shapes=list(scratch),
        compiler_params=pltpu.CompilerParams(vmem_limit_bytes=limit * MIB),
        cost_estimate=pl.CostEstimate(flops=flops, bytes_accessed=traffic, transcendentals=0),
    )


def dot(a, b):
    return jnp.dot(a, b, preferred_element_type=F32)


def dot_t(a, b):
    return lax.dot_general(a, b, (((1,), (1,)), ((), ())), preferred_element_type=F32)


def diagonal(shape):
    return lax.broadcasted_iota(I32, shape, 0) == lax.broadcasted_iota(I32, shape, 1)


def column_to_row(column):
    rows = column.shape[0]
    return jnp.sum(jnp.where(diagonal((rows, rows)), column, 0.0), axis=0, keepdims=True)


def row_to_column(row):
    lanes = row.shape[1]
    return jnp.sum(jnp.where(diagonal((lanes, lanes)), row, 0.0), axis=1, keepdims=True)


def squares_of(rows):
    total = jnp.zeros((rows.shape[0], HD), F32)
    for c in range(0, rows.shape[1], HD):
        wide = rows[:, c : c + HD].astype(F32)
        total = total + wide * wide
    return total


def split_three(values):
    high = values.astype(BF16).astype(F32)
    rest = values - high
    middle = rest.astype(BF16).astype(F32)
    return high, middle, rest - middle


def softmax_parts(query, key, value, usable):
    scores = jnp.where(usable, dot_t(query, key) * HD**-0.5, LOWEST)
    top = jnp.max(scores, axis=1, keepdims=True)
    weights = jnp.where(usable, jnp.exp(scores - top), 0.0)
    return dot(weights.astype(BF16), value), top, jnp.sum(weights, axis=1, keepdims=True)


def prepare_kernel(sizes, *refs):
    n, img, tok, blocks, cap, lot, page_cap, kv_heads, steps = sizes
    far, (info, slots, fresh), small, (starts, sems) = refs[:8], refs[8:11], refs[11:19], refs[19:]
    copies = [pltpu.make_async_copy(a, b, sems.at[i]) for i, (a, b) in enumerate(zip(far, small))]
    for c in copies:
        c.start()
    route, pages, count, tail, req, query, key, value = small
    for c in copies:
        c.wait()
    pos = lax.axis_index("section")
    table = [route[:, e * img : (e + 1) * img] for e in range(n)]
    own = jnp.zeros((1, img), I32)
    for e in range(n):
        own = jnp.where(pos == e, table[e], own)
    marks = own == lax.broadcasted_iota(I32, (n, img), 0)
    ones = jnp.where(marks, 1.0, 0.0).astype(BF16)
    earlier = lax.broadcasted_iota(I32, (img, img), 0) < lax.broadcasted_iota(I32, (img, img), 1)
    prefix = dot(ones, jnp.where(earlier, 1.0, 0.0).astype(BF16))
    local = jnp.sum(jnp.where(marks, prefix, 0.0), axis=0, keepdims=True).astype(I32)
    info[0:1, :img] = own * lot + local
    lanes = lax.broadcasted_iota(I32, (1, n * lot), 1)
    source, inner = lanes // lot, lanes % lot
    fits = jnp.zeros((1, n * lot), I32)
    offset = jnp.zeros((1, n * lot), I32)
    for e in range(n):
        arriving = jnp.sum((table[e] == pos).astype(I32), axis=1, keepdims=True)
        fits = fits + jnp.where(source == e, arriving, 0)
        offset = offset + jnp.where(source > e, arriving, 0)
    info[2:3, : n * lot] = jnp.where(inner < fits, offset + inner, -1)
    total = jnp.int32(0)
    for r in range(n):
        starts[r] = total
        total = total + count[r]
    token = lax.broadcasted_iota(I32, (1, tok), 1) + pos * tok
    token_slot = jnp.full((1, tok), -1, I32)
    for b in range(n):
        r = req[b]
        first = starts[r] * PAGE
        last = first + (count[r] - 1) * PAGE + tail[r]
        token_slot = jnp.where((token >= first) & (token < last), b, token_slot)
    info[1:2, :tok] = token_slot
    for g in range(blocks):
        holder = pages[0, pos * blocks + g]
        slot = holder * page_cap
        for e in range(g):
            slot = slot + (pages[0, pos * blocks + e] == holder).astype(I32)
        slots[g] = slot
    rows = query.shape[0] // kv_heads
    row = lax.broadcasted_iota(I32, (rows, steps), 0)
    causal = lax.broadcasted_iota(I32, (rows, steps), 1) <= row % steps
    tops, totals = [], []
    for g in range(kv_heads):
        cols = slice(g * HD, (g + 1) * HD)
        own_query = query[g * rows : (g + 1) * rows, :]
        numerator, top, weight = softmax_parts(own_query, key[:, cols], value[:, cols], causal)
        fresh[g * rows : (g + 1) * rows, :] = numerator
        tops.append(top)
        totals.append(weight)
    stats = column_to_row(jnp.concatenate(tops + totals, axis=0))
    fresh[kv_heads * rows :, :] = jnp.broadcast_to(stats, (STAT, stats.shape[1]))


def project(near_far, far, gain, w_key_far, w_value_far, near, w_key, w_value, total, sems, step):
    half = near.shape[1]
    kvw = w_key.shape[1]
    me = lax.axis_index("tensor")
    first = pltpu.make_async_copy(near_far, near, sems.at[0])
    first.start()
    loads = []
    for side in (me, 1 - me):
        for c in range(0, half, step):
            at = len(loads) * step
            columns = pl.ds(pl.multiple_of(side * half + c, step), step)
            pair = [
                pltpu.make_async_copy(w.at[columns], held.at[at : at + step], sems.at[2 * len(loads) + i])
                for i, (w, held) in enumerate(((w_key_far, w_key), (w_value_far, w_value)), 1)
            ]
            for copy in pair:
                copy.start()
            loads.append((columns, pair))
    sums = squares_of(far)
    first.wait()
    sums = jnp.sum(squares_of(near) + sums, axis=1, keepdims=True)
    scale = lax.rsqrt(sums / (2.0 * half) + EPS)
    for i, (columns, pair) in enumerate(loads):
        rows = near if i * step < half else far
        c = i * step % half
        normed = (rows[:, c : c + step].astype(F32) * scale * gain[:, columns]).astype(BF16)
        for copy, w, at in zip(pair, (w_key, w_value), (0, kvw)):
            copy.wait()
            part = dot(normed, w[i * step : (i + 1) * step, :])
            if i == 0:
                total[:, at : at + kvw] = part
            else:
                total[:, at : at + kvw] += part


def vis_kernel(n, lot, step, near, far, gain, w_key, w_value, info, query, out, *scratch):
    project(near, far, gain, w_key, w_value, *scratch, step)
    total = scratch[3]
    img = near.shape[0]
    slot = lax.broadcasted_iota(I32, (n * lot, img), 0)
    chosen = jnp.where(slot == info[0:1, :img], 1.0, 0.0).astype(BF16)
    packed = dot(chosen, total[...].astype(BF16)).astype(BF16)
    q_lots = out.shape[1] - lot
    for k in range(n):
        for j in range(query.shape[0] // q_lots):
            out[k, :q_lots, j * HD : (j + 1) * HD] = query[j * q_lots : (j + 1) * q_lots, :]
        out[k, q_lots:, :] = packed[k * lot : (k + 1) * lot, :]


def text_kernel(step, near, far, gain, w_key, w_value, out, *scratch):
    project(near, far, gain, w_key, w_value, *scratch, step)
    out[...] = scratch[3][...].astype(BF16)


def attend_kernel(n, cap, lot, page_cap, kv_heads, slots, info, kv_text, arrived, out, kv):
    tok = kv_text.shape[0]
    kvw = kv_heads * HD
    q_lots = arrived.shape[1] - lot
    reach = min(tok, n * cap)
    hit = lax.broadcasted_iota(I32, (reach, n * lot), 0) == info[2:3, : n * lot]
    hot = jnp.where(hit, 1.0, 0.0)
    covered = jnp.sum(hot, axis=1, keepdims=True) > 0.0
    incoming = jnp.concatenate([arrived[k, q_lots:, :] for k in range(n)], axis=0)
    placed = dot(hot.astype(BF16), incoming)
    kv[:reach, :] = jnp.where(covered, placed, kv_text[:reach, :].astype(F32)).astype(BF16)
    if reach < tok:
        kv[reach:, :] = kv_text[reach:, :]
    chunk = page_cap * PAGE
    halves = 2 * kv_heads
    pages = halves * chunk
    out[:, :pages, :] = jnp.zeros((n, pages, HD), BF16)
    for g in range(tok // PAGE):
        slot = slots[g]
        for h in range(halves):
            at = pl.ds(pl.multiple_of((slot % page_cap) * PAGE + h * chunk, PAGE), PAGE)
            out[slot // page_cap, at, :] = kv[g * PAGE : (g + 1) * PAGE, h * HD : (h + 1) * HD]
    groups = arrived.shape[2] // HD // kv_heads
    rows = groups * q_lots
    slot = lax.broadcasted_iota(I32, (n * rows, 1), 0) // rows
    usable = slot == info[1:2, :tok]
    tops, totals = [], []
    for g in range(kv_heads):
        query = jnp.concatenate(
            [
                arrived[k, :q_lots, (g * groups + j) * HD : (g * groups + j + 1) * HD]
                for k in range(n)
                for j in range(groups)
            ],
            axis=0,
        )
        key = kv[:, g * HD : (g + 1) * HD]
        value = kv[:, kvw + g * HD : kvw + (g + 1) * HD]
        numerator, top, weight = softmax_parts(query, key, value, usable)
        numerator = numerator.astype(BF16)
        for k in range(n):
            out[k, pages + g * rows : pages + (g + 1) * rows, :] = numerator[k * rows : (k + 1) * rows, :]
        tops.append(top)
        totals.append(weight)
    line = lax.broadcasted_iota(I32, (PAGE, HD), 0)
    for k in range(n):
        at = slice(k * rows, (k + 1) * rows)
        stats = column_to_row(jnp.concatenate([x[at] for x in tops + totals], axis=0))
        high, middle, low = split_three(stats)
        lines = jnp.where(line == 0, high, jnp.where(line == 1, middle, jnp.where(line == 2, low, 0.0)))
        out[k, pages + kv_heads * rows :, :] = lines.astype(BF16)


def finish_kernel(steps, page_cap, shares, fresh, attended, keys, values, sems):
    n = shares.shape[0]
    rows = fresh.shape[0] - STAT
    chunk = page_cap * PAGE
    copies = []
    for i, out in enumerate((keys, values)):
        for h in range(out.shape[2] // HD):
            at = len(copies)
            copies.append(
                pltpu.make_async_copy(
                    shares.at[:, at * chunk : (at + 1) * chunk, :],
                    out.at[:, :, h * HD : (h + 1) * HD],
                    sems.at[at],
                )
            )
    for c in copies:
        c.start()
    pages = len(copies) * chunk
    stats = [row_to_column(fresh[rows : rows + 1, :])]
    for k in range(n):
        lines = shares[k, pages + rows :, :].astype(F32)
        stats.append(row_to_column(lines[0:1] + lines[1:2] + lines[2:3]))
    highest = stats[0][:rows]
    for s in stats[1:]:
        highest = jnp.maximum(highest, s[:rows])
    scale = jnp.exp(stats[0][:rows] - highest)
    numerator = fresh[:rows, :] * scale
    total = stats[0][rows:] * scale
    for k in range(n):
        scale = jnp.exp(stats[k + 1][:rows] - highest)
        numerator = numerator + shares[k, pages : pages + rows, :].astype(F32) * scale
        total = total + stats[k + 1][rows:] * scale
    result = (numerator / total).astype(BF16)
    for h in range(rows // steps):
        attended[0, :, h * HD : (h + 1) * HD] = result[h * steps : (h + 1) * steps, :]
    for c in copies:
        c.wait()


def body(
    text_rows,
    vis_rows,
    img_route,
    norm_gain,
    w_key,
    w_value,
    page_count,
    tail_len,
    page_dest,
    dec_req,
    dec_query,
    dec_key,
    dec_value,
):
    n = lax.axis_size("section")
    tok, half = text_rows.shape
    img = vis_rows.shape[0]
    kvw = w_key.shape[1]
    kv_heads = kvw // HD
    _, steps, q_width = dec_query.shape
    heads = q_width // HD
    q_rows = heads * steps
    blocks = tok // PAGE
    cap = max(2, (2 * img + n - 1) // n)
    page_cap = max(1, (blocks + n - 1) // n)

    def across(array):
        return lax.ppermute(array, "tensor", [(0, 1), (1, 0)])

    def exchange(array):
        return lax.all_to_all(array, "section", split_axis=0, concat_axis=0, tiled=True)

    def remote(array):
        return pltpu.with_memory_space_constraint(array, pltpu.HBM)

    vis_far = across(vis_rows)
    text_far = across(text_rows)
    query = dec_query.reshape(steps, heads, HD).transpose(1, 0, 2).reshape(q_rows, HD)

    lot = -(-cap // PAGE) * PAGE
    q_lots = q_rows * HD // (2 * kvw)
    width = max(tok, n * lot)
    arguments = (
        img_route.T,
        page_dest.T,
        page_count,
        tail_len,
        dec_req,
        query,
        dec_key[0],
        dec_value[0],
    )
    info, slots, fresh = call(
        lambda *refs: prepare_kernel((n, img, tok, blocks, cap, lot, page_cap, kv_heads, steps), *refs),
        (
            jax.ShapeDtypeStruct((8, width), I32),
            jax.ShapeDtypeStruct((blocks,), I32),
            jax.ShapeDtypeStruct((q_rows + STAT, HD), F32),
        ),
        [ANY] * len(arguments),
        (VM, SM, VM),
        [
            *[(pltpu.SMEM if 1 <= i <= 4 else pltpu.VMEM)(a.shape, a.dtype) for i, a in enumerate(arguments)],
            pltpu.SMEM((n,), I32),
            pltpu.SemaphoreType.DMA((len(arguments),)),
        ],
        flops=1 << 20,
        traffic=1 << 22,
    )(*[remote(a) for a in arguments])

    step = min(1024, half)
    weights = (remote(norm_gain.reshape(1, 2 * half)), remote(w_key), remote(w_value))

    def projection(kernel, out_shape, rows, others):
        return call(
            kernel,
            out_shape,
            [ANY, VM, VM, ANY, ANY] + [VM] * others,
            VM,
            [
                pltpu.VMEM((rows, half), BF16),
                pltpu.VMEM(w_key.shape, BF16),
                pltpu.VMEM(w_value.shape, BF16),
                pltpu.VMEM((rows, 2 * kvw), F32),
                pltpu.SemaphoreType.DMA((1 + 4 * half // step,)),
            ],
            limit=24,
            flops=2 * rows * 2 * half * 2 * kvw,
            traffic=2 * rows * 2 * half + 8 * half * kvw,
        )

    packed = projection(
        lambda *refs: vis_kernel(n, lot, step, *refs),
        jax.ShapeDtypeStruct((n, q_lots + lot, 2 * kvw), BF16),
        img,
        2,
    )(remote(vis_rows), vis_far, *weights, info, remote(query))
    arrived = exchange(packed)

    kv_text = projection(
        lambda *refs: text_kernel(step, *refs), jax.ShapeDtypeStruct((tok, 2 * kvw), BF16), tok, 0
    )(remote(text_rows), text_far, *weights)

    sent = call(
        lambda *refs: attend_kernel(n, cap, lot, page_cap, kv_heads, *refs),
        jax.ShapeDtypeStruct((n, page_cap * PAGE * 2 * kv_heads + q_rows + PAGE, HD), BF16),
        [SM, VM, VM, VM],
        VM,
        [pltpu.VMEM((tok, 2 * kvw), BF16)],
        flops=4 * n * q_rows * tok * HD,
        traffic=n * (q_rows + STAT) * HD * 4,
    )(slots, info, kv_text, arrived)
    shares = exchange(sent)

    slots_here = n * page_cap
    attended, cache_key, cache_value = call(
        lambda *refs: finish_kernel(steps, page_cap, *refs),
        (
            jax.ShapeDtypeStruct(dec_query.shape, BF16),
            jax.ShapeDtypeStruct((n, page_cap * PAGE, kvw), BF16),
            jax.ShapeDtypeStruct((n, page_cap * PAGE, kvw), BF16),
        ),
        [VM, VM],
        (VM, ANY, ANY),
        [pltpu.SemaphoreType.DMA((2 * kv_heads,))],
        traffic=4 * tok * 2 * kvw,
    )(shares, fresh)
    return (
        attended,
        cache_key.reshape(slots_here, PAGE, kvw),
        cache_value.reshape(slots_here, PAGE, kvw),
    )


def solution(mesh):
    return jax.shard_map(
        body,
        mesh=mesh,
        in_specs=(
            P(("groups", "section"), "tensor"),
            P(("groups", "section"), "tensor"),
            P("groups", None),
            P(),
            P(None, "tensor"),
            P(None, "tensor"),
            P("groups"),
            P("groups"),
            P("groups", None),
            P("groups"),
            P(("groups", "section"), None, "tensor"),
            P(("groups", "section"), None, "tensor"),
            P(("groups", "section"), None, "tensor"),
        ),
        out_specs=(
            P(("groups", "section"), None, "tensor"),
            P(("groups", "section"), None, "tensor"),
            P(("groups", "section"), None, "tensor"),
        ),
        check_vma=False,
    )
```

```python
import jax
import jax.numpy as jnp
from jax import lax
from jax.experimental import pallas as pl
from jax.experimental.pallas import tpu as pltpu
from jax.sharding import PartitionSpec as P

HD = 128
PAGE = 16
LOWEST = -1e30
EPS = 1e-06
STAT = 8
F32 = jnp.float32
BF16 = jnp.bfloat16
I32 = jnp.int32

VM = pl.BlockSpec(memory_space=pltpu.VMEM)
SM = pl.BlockSpec(memory_space=pltpu.SMEM)
ANY = pl.BlockSpec(memory_space=pl.ANY)
MIB = 1 << 20


def call(kernel, out_shape, in_specs, out_specs, scratch=(), limit=16, flops=0, traffic=0):
    return pl.pallas_call(
        kernel,
        out_shape=out_shape,
        in_specs=in_specs,
        out_specs=out_specs,
        scratch_shapes=list(scratch),
        compiler_params=pltpu.CompilerParams(vmem_limit_bytes=limit * MIB),
        cost_estimate=pl.CostEstimate(flops=flops, bytes_accessed=traffic, transcendentals=0),
    )


def dot(a, b):
    return jnp.dot(a, b, preferred_element_type=F32)


def dot_t(a, b):
    return lax.dot_general(a, b, (((1,), (1,)), ((), ())), preferred_element_type=F32)


def diagonal(shape):
    return lax.broadcasted_iota(I32, shape, 0) == lax.broadcasted_iota(I32, shape, 1)


def column_to_row(column):
    rows = column.shape[0]
    return jnp.sum(jnp.where(diagonal((rows, rows)), column, 0.0), axis=0, keepdims=True)


def row_to_column(row):
    lanes = row.shape[1]
    return jnp.sum(jnp.where(diagonal((lanes, lanes)), row, 0.0), axis=1, keepdims=True)


def squares_of(rows):
    total = jnp.zeros((rows.shape[0], HD), F32)
    for c in range(0, rows.shape[1], HD):
        wide = rows[:, c : c + HD].astype(F32)
        total = total + wide * wide
    return total


def split_three(values):
    high = values.astype(BF16).astype(F32)
    rest = values - high
    middle = rest.astype(BF16).astype(F32)
    return high, middle, rest - middle


def softmax_parts(query, key, value, usable):
    scores = jnp.where(usable, dot_t(query, key) * HD**-0.5, LOWEST)
    top = jnp.max(scores, axis=1, keepdims=True)
    weights = jnp.where(usable, jnp.exp(scores - top), 0.0)
    return dot(weights.astype(BF16), value), top, jnp.sum(weights, axis=1, keepdims=True)


def prepare_kernel(sizes, *refs):
    n, img, tok, blocks, lot, page_cap = sizes
    far, (info, slots), near, small, (starts, sems) = refs[:8], refs[8:10], refs[10:13], refs[13:18], refs[18:]
    copies = [pltpu.make_async_copy(a, b, sems.at[i]) for i, (a, b) in enumerate(zip(far, small + near))]
    for c in copies:
        c.start()
    route, pages, count, tail, req = small
    for c in copies[: len(small)]:
        c.wait()
    pos = lax.axis_index("section")
    table = [route[:, e * img : (e + 1) * img] for e in range(n)]
    own = jnp.zeros((1, img), I32)
    for e in range(n):
        own = jnp.where(pos == e, table[e], own)
    marks = own == lax.broadcasted_iota(I32, (n, img), 0)
    ones = jnp.where(marks, 1.0, 0.0).astype(BF16)
    earlier = lax.broadcasted_iota(I32, (img, img), 0) < lax.broadcasted_iota(I32, (img, img), 1)
    prefix = dot(ones, jnp.where(earlier, 1.0, 0.0).astype(BF16))
    local = jnp.sum(jnp.where(marks, prefix, 0.0), axis=0, keepdims=True).astype(I32)
    info[0:1, :img] = own * lot + local
    lanes = lax.broadcasted_iota(I32, (1, n * lot), 1)
    source, inner = lanes // lot, lanes % lot
    fits = jnp.zeros((1, n * lot), I32)
    offset = jnp.zeros((1, n * lot), I32)
    for e in range(n):
        arriving = jnp.sum((table[e] == pos).astype(I32), axis=1, keepdims=True)
        fits = fits + jnp.where(source == e, arriving, 0)
        offset = offset + jnp.where(source > e, arriving, 0)
    info[2:3, : n * lot] = jnp.where(inner < fits, offset + inner, -1)
    total = jnp.int32(0)
    for r in range(n):
        starts[r] = total
        total = total + count[r]
    token = lax.broadcasted_iota(I32, (1, tok), 1) + pos * tok
    token_slot = jnp.full((1, tok), -1, I32)
    for b in range(n):
        r = req[b]
        first = starts[r] * PAGE
        last = first + (count[r] - 1) * PAGE + tail[r]
        token_slot = jnp.where((token >= first) & (token < last), b, token_slot)
    info[1:2, :tok] = token_slot
    for g in range(blocks):
        holder = pages[0, pos * blocks + g]
        slot = holder * page_cap
        for e in range(g):
            slot = slot + (pages[0, pos * blocks + e] == holder).astype(I32)
        slots[g] = slot
    for c in copies[len(small) :]:
        c.wait()


def scale_of(near, far):
    sums = jnp.sum(squares_of(near) + squares_of(far), axis=1, keepdims=True)
    return lax.rsqrt(sums / (2.0 * near.shape[1]) + EPS)


def normed_rows(rows, c, step, scale, gain):
    return (rows[:, c : c + step].astype(F32) * scale * gain).astype(BF16)


def add_part(total, at, normed, w, begin):
    part = dot(normed, w)
    columns = slice(at, at + part.shape[1])
    if begin:
        total[:, columns] = part
    else:
        total[:, columns] += part


def vis_kernel(n, lot, step, near, far, gain, w_key, w_value, info, query, out, total):
    img, half = near.shape
    kvw = w_key.shape[1]
    me = lax.axis_index("tensor")
    scale = scale_of(near, far)
    for rows, side in ((near, me), (far, 1 - me)):
        for c in range(0, half, step):
            columns = pl.ds(pl.multiple_of(side * half + c, step), step)
            normed = normed_rows(rows, c, step, scale, gain[:, columns])
            for w, at in ((w_key, 0), (w_value, kvw)):
                add_part(total, at, normed, w[columns, :], rows is near and c == 0)
    slot = lax.broadcasted_iota(I32, (n * lot, img), 0)
    chosen = jnp.where(slot == info[0:1, :img], 1.0, 0.0).astype(BF16)
    packed = dot(chosen, total[...].astype(BF16)).astype(BF16)
    q_lots = out.shape[1] - lot
    for k in range(n):
        for j in range(query.shape[0] // q_lots):
            out[k, :q_lots, j * HD : (j + 1) * HD] = query[j * q_lots : (j + 1) * q_lots, :]
        out[k, q_lots:, :] = packed[k * lot : (k + 1) * lot, :]


def text_kernel(load, step, near_far, far, gain, w_key_far, w_value_far, out, near, w_key, w_value, total, sems):
    half = near.shape[1]
    kvw = w_key.shape[1]
    me = lax.axis_index("tensor")
    first = pltpu.make_async_copy(near_far, near, sems.at[0])
    first.start()
    loads = []
    for side in (me, 1 - me):
        for c in range(0, half, load):
            at = len(loads) * load
            columns = pl.ds(pl.multiple_of(side * half + c, load), load)
            pair = [
                pltpu.make_async_copy(w.at[columns], held.at[at : at + load], sems.at[2 * len(loads) + i])
                for i, (w, held) in enumerate(((w_key_far, w_key), (w_value_far, w_value)), 1)
            ]
            for copy in pair:
                copy.start()
            loads.append(pair)
    sums = squares_of(far)
    first.wait()
    sums = jnp.sum(squares_of(near) + sums, axis=1, keepdims=True)
    scale = lax.rsqrt(sums / (2.0 * half) + EPS)
    for i, pair in enumerate(loads):
        for copy in pair:
            copy.wait()
        for at in range(i * load, (i + 1) * load, step):
            rows, side = (near, me) if at < half else (far, 1 - me)
            c = at % half
            columns = pl.ds(pl.multiple_of(side * half + c, step), step)
            normed = normed_rows(rows, c, step, scale, gain[:, columns])
            for w, col in ((w_key, 0), (w_value, kvw)):
                add_part(total, col, normed, w[at : at + step, :], at == 0)
    out[...] = total[...].astype(BF16)


def attend_kernel(n, cap, lot, page_cap, kv_heads, slots, info, kv_text, arrived, out, own, kv, held):
    pos = lax.axis_index("section")
    tok = kv_text.shape[0]
    kvw = kv_heads * HD
    q_lots = arrived.shape[1] - lot
    reach = min(tok, n * cap)
    hit = lax.broadcasted_iota(I32, (reach, n * lot), 0) == info[2:3, : n * lot]
    hot = jnp.where(hit, 1.0, 0.0)
    covered = jnp.sum(hot, axis=1, keepdims=True) > 0.0
    incoming = jnp.concatenate([arrived[k, q_lots:, :] for k in range(n)], axis=0)
    placed = dot(hot.astype(BF16), incoming)
    kv[:reach, :] = jnp.where(covered, placed, kv_text[:reach, :].astype(F32)).astype(BF16)
    if reach < tok:
        kv[reach:, :] = kv_text[reach:, :]
    chunk = page_cap * PAGE
    halves = 2 * kv_heads
    pages = halves * chunk
    out[:, :pages, :] = jnp.zeros((n, pages, HD), BF16)
    for g in range(tok // PAGE):
        slot = slots[g]
        for h in range(halves):
            at = pl.ds(pl.multiple_of((slot % page_cap) * PAGE + h * chunk, PAGE), PAGE)
            out[slot // page_cap, at, :] = kv[g * PAGE : (g + 1) * PAGE, h * HD : (h + 1) * HD]
    groups = arrived.shape[2] // HD // kv_heads
    rows = groups * q_lots
    slot = lax.broadcasted_iota(I32, (n * rows, 1), 0) // rows
    usable = slot == info[1:2, :tok]
    tops, totals = [], []
    for g in range(kv_heads):
        query = jnp.concatenate(
            [
                arrived[k, :q_lots, (g * groups + j) * HD : (g * groups + j + 1) * HD]
                for k in range(n)
                for j in range(groups)
            ],
            axis=0,
        )
        key = kv[:, g * HD : (g + 1) * HD]
        value = kv[:, kvw + g * HD : kvw + (g + 1) * HD]
        numerator, top, weight = softmax_parts(query, key, value, usable)
        held[g * n * rows : (g + 1) * n * rows, :] = numerator
        own[g * rows : (g + 1) * rows, :] = held[pl.ds(pl.multiple_of((g * n + pos) * rows, rows), rows), :]
        numerator = numerator.astype(BF16)
        for k in range(n):
            out[k, pages + g * rows : pages + (g + 1) * rows, :] = numerator[k * rows : (k + 1) * rows, :]
        tops.append(top)
        totals.append(weight)
    line = lax.broadcasted_iota(I32, (PAGE, HD), 0)
    for k in range(n):
        at = slice(k * rows, (k + 1) * rows)
        stats = column_to_row(jnp.concatenate([x[at] for x in tops + totals], axis=0))

        @pl.when(pos == k)
        def _():
            own[kv_heads * rows :, :] = jnp.broadcast_to(stats, (STAT, stats.shape[1]))

        high, middle, low = split_three(stats)
        lines = jnp.where(line == 0, high, jnp.where(line == 1, middle, jnp.where(line == 2, low, 0.0)))
        out[k, pages + kv_heads * rows :, :] = lines.astype(BF16)


def combine(pieces, highest):
    numerator, total = 0.0, 0.0
    for rows, top, weight in pieces:
        scale = jnp.exp(top - highest)
        numerator = numerator + rows * scale
        total = total + weight * scale
    return numerator, total


def fresh_kernel(kv_heads, steps, query, key, value, own, mine):
    rows = query.shape[0] // kv_heads
    every = kv_heads * rows
    row = lax.broadcasted_iota(I32, (rows, steps), 0)
    causal = lax.broadcasted_iota(I32, (rows, steps), 1) <= row % steps
    stats = row_to_column(own[every : every + 1, :])
    tops, totals = [], []
    for g in range(kv_heads):
        cols = slice(g * HD, (g + 1) * HD)
        at = slice(g * rows, (g + 1) * rows)
        fresh = softmax_parts(query[at, :], key[:, cols], value[:, cols], causal)
        share = (own[at, :], stats[at], stats[every + g * rows : every + (g + 1) * rows])
        highest = jnp.maximum(fresh[1], share[1])
        numerator, total = combine((fresh, share), highest)
        mine[at, :] = numerator
        tops.append(highest)
        totals.append(total)
    line = column_to_row(jnp.concatenate(tops + totals, axis=0))
    mine[every:, :] = jnp.broadcast_to(line, (STAT, line.shape[1]))


def finish_kernel(steps, page_cap, shares, mine, attended, keys, values, sems):
    n = shares.shape[0]
    pos = lax.axis_index("section")
    rows = mine.shape[0] - STAT
    chunk = page_cap * PAGE
    copies = []
    for i, out in enumerate((keys, values)):
        for h in range(out.shape[2] // HD):
            at = len(copies)
            copies.append(
                pltpu.make_async_copy(
                    shares.at[:, at * chunk : (at + 1) * chunk, :],
                    out.at[:, :, h * HD : (h + 1) * HD],
                    sems.at[at],
                )
            )
    for c in copies:
        c.start()
    pages = len(copies) * chunk
    stats = row_to_column(mine[rows : rows + 1, :])
    pieces = [(mine[:rows, :], stats[:rows], stats[rows:])]
    for k in range(n):
        lines = shares[k, pages + rows :, :].astype(F32)
        stats = row_to_column(lines[0:1] + lines[1:2] + lines[2:3])
        away = pos != k
        top = jnp.where(away, stats[:rows], LOWEST)
        weight = jnp.where(away, stats[rows:], 0.0)
        pieces.append((jnp.where(away, shares[k, pages : pages + rows, :].astype(F32), 0.0), top, weight))
    highest = pieces[0][1]
    for p in pieces[1:]:
        highest = jnp.maximum(highest, p[1])
    numerator, total = combine(pieces, highest)
    result = (numerator / total).astype(BF16)
    for h in range(rows // steps):
        attended[0, :, h * HD : (h + 1) * HD] = result[h * steps : (h + 1) * steps, :]
    for c in copies:
        c.wait()


def body(
    text_rows,
    vis_rows,
    img_route,
    norm_gain,
    w_key,
    w_value,
    page_count,
    tail_len,
    page_dest,
    dec_req,
    dec_query,
    dec_key,
    dec_value,
):
    n = lax.axis_size("section")
    tok, half = text_rows.shape
    img = vis_rows.shape[0]
    kvw = w_key.shape[1]
    kv_heads = kvw // HD
    _, steps, q_width = dec_query.shape
    heads = q_width // HD
    q_rows = heads * steps
    blocks = tok // PAGE
    cap = max(2, (2 * img + n - 1) // n)
    page_cap = max(1, (blocks + n - 1) // n)

    def across(array):
        return lax.ppermute(array, "tensor", [(0, 1), (1, 0)])

    def exchange(array):
        return lax.all_to_all(array, "section", split_axis=0, concat_axis=0, tiled=True)

    def remote(array):
        return pltpu.with_memory_space_constraint(array, pltpu.HBM)

    def local(array):
        return pltpu.with_memory_space_constraint(array, pltpu.VMEM)

    vis_far = across(vis_rows)
    text_far = across(text_rows)
    query = dec_query.reshape(steps, heads, HD).transpose(1, 0, 2).reshape(q_rows, HD)

    lot = -(-cap // PAGE) * PAGE
    q_lots = q_rows * HD // (2 * kvw)
    width = max(tok, n * lot)
    arguments = (img_route.T, page_dest.T, page_count, tail_len, dec_req, w_key, w_value, vis_rows)
    info, slots, key_near, value_near, vis_near = call(
        lambda *refs: prepare_kernel((n, img, tok, blocks, lot, page_cap), *refs),
        (
            jax.ShapeDtypeStruct((8, width), I32),
            jax.ShapeDtypeStruct((blocks,), I32),
            *[pltpu.VMEM(a.shape, a.dtype) for a in arguments[5:]],
        ),
        [ANY] * len(arguments),
        (VM, SM) + (VM,) * 3,
        [
            *[(pltpu.VMEM if i == 0 else pltpu.SMEM)(a.shape, a.dtype) for i, a in enumerate(arguments[:5])],
            pltpu.SMEM((n,), I32),
            pltpu.SemaphoreType.DMA((len(arguments),)),
        ],
        flops=1 << 20,
        traffic=2 * 2 * half * 2 * kvw * 2,
    )(*[remote(a) for a in arguments])

    step = min(1024, half)
    load = min(2048, half)
    gain = remote(norm_gain.reshape(1, 2 * half))

    packed = call(
        lambda *refs: vis_kernel(n, lot, step, *refs),
        jax.ShapeDtypeStruct((n, q_lots + lot, 2 * kvw), BF16),
        [VM] * 7,
        VM,
        [pltpu.VMEM((img, 2 * kvw), F32)],
        flops=2 * img * 2 * half * 2 * kvw,
        traffic=2 * img * 2 * half + 8 * half * kvw,
    )(local(vis_near), vis_far, gain, local(key_near), local(value_near), info, remote(query))
    arrived = exchange(packed)

    kv_text = call(
        lambda *refs: text_kernel(load, step, *refs),
        jax.ShapeDtypeStruct((tok, 2 * kvw), BF16),
        [ANY, VM, VM, ANY, ANY],
        VM,
        [
            pltpu.VMEM((tok, half), BF16),
            pltpu.VMEM(w_key.shape, BF16),
            pltpu.VMEM(w_value.shape, BF16),
            pltpu.VMEM((tok, 2 * kvw), F32),
            pltpu.SemaphoreType.DMA((1 + 4 * half // load,)),
        ],
        limit=24,
        flops=2 * tok * 2 * half * 2 * kvw,
        traffic=2 * tok * 2 * half + 8 * half * kvw,
    )(remote(text_rows), text_far, gain, remote(w_key), remote(w_value))

    sent, own = call(
        lambda *refs: attend_kernel(n, cap, lot, page_cap, kv_heads, *refs),
        (
            jax.ShapeDtypeStruct((n, page_cap * PAGE * 2 * kv_heads + q_rows + PAGE, HD), BF16),
            jax.ShapeDtypeStruct((q_rows + STAT, HD), F32),
        ),
        [SM, VM, VM, VM],
        (VM, VM),
        [pltpu.VMEM((tok, 2 * kvw), BF16), pltpu.VMEM((n * q_rows, HD), F32)],
        flops=4 * n * q_rows * tok * HD,
        traffic=n * (q_rows + STAT) * HD * 4,
    )(slots, info, kv_text, arrived)
    shares = exchange(sent)

    mine = call(
        lambda *refs: fresh_kernel(kv_heads, steps, *refs),
        jax.ShapeDtypeStruct((q_rows + STAT, HD), F32),
        [VM] * 4,
        VM,
        flops=1 << 20,
        traffic=1 << 18,
    )(remote(query), remote(dec_key[0]), remote(dec_value[0]), own)

    slots_here = n * page_cap
    attended, cache_key, cache_value = call(
        lambda *refs: finish_kernel(steps, page_cap, *refs),
        (
            jax.ShapeDtypeStruct(dec_query.shape, BF16),
            jax.ShapeDtypeStruct((n, page_cap * PAGE, kvw), BF16),
            jax.ShapeDtypeStruct((n, page_cap * PAGE, kvw), BF16),
        ),
        [VM, VM],
        (VM, ANY, ANY),
        [pltpu.SemaphoreType.DMA((2 * kv_heads,))],
        traffic=4 * tok * 2 * kvw,
    )(shares, mine)
    return (
        attended,
        cache_key.reshape(slots_here, PAGE, kvw),
        cache_value.reshape(slots_here, PAGE, kvw),
    )


def solution(mesh):
    return jax.shard_map(
        body,
        mesh=mesh,
        in_specs=(
            P(("groups", "section"), "tensor"),
            P(("groups", "section"), "tensor"),
            P("groups", None),
            P(),
            P(None, "tensor"),
            P(None, "tensor"),
            P("groups"),
            P("groups"),
            P("groups", None),
            P("groups"),
            P(("groups", "section"), None, "tensor"),
            P(("groups", "section"), None, "tensor"),
            P(("groups", "section"), None, "tensor"),
        ),
        out_specs=(
            P(("groups", "section"), None, "tensor"),
            P(("groups", "section"), None, "tensor"),
            P(("groups", "section"), None, "tensor"),
        ),
        check_vma=False,
    )
```

```python
import jax
import jax.numpy as jnp
from jax import lax
from jax.experimental import pallas as pl
from jax.experimental.pallas import tpu as pltpu
from jax.sharding import PartitionSpec as P

HD = 128
PAGE = 16
LOWEST = -1e30
EPS = 1e-06
STAT = 8
F32 = jnp.float32
BF16 = jnp.bfloat16
I32 = jnp.int32

VM = pl.BlockSpec(memory_space=pltpu.VMEM)
SM = pl.BlockSpec(memory_space=pltpu.SMEM)
ANY = pl.BlockSpec(memory_space=pl.ANY)
MIB = 1 << 20


def call(kernel, out_shape, in_specs, out_specs, scratch=(), limit=16, flops=0, traffic=0):
    return pl.pallas_call(
        kernel,
        out_shape=out_shape,
        in_specs=in_specs,
        out_specs=out_specs,
        scratch_shapes=list(scratch),
        compiler_params=pltpu.CompilerParams(vmem_limit_bytes=limit * MIB),
        cost_estimate=pl.CostEstimate(flops=flops, bytes_accessed=traffic, transcendentals=0),
    )


def dot(a, b):
    return jnp.dot(a, b, preferred_element_type=F32)


def dot_t(a, b):
    return lax.dot_general(a, b, (((1,), (1,)), ((), ())), preferred_element_type=F32)


def diagonal(shape):
    return lax.broadcasted_iota(I32, shape, 0) == lax.broadcasted_iota(I32, shape, 1)


def column_to_row(column):
    rows = column.shape[0]
    return jnp.sum(jnp.where(diagonal((rows, rows)), column, 0.0), axis=0, keepdims=True)


def row_to_column(row):
    lanes = row.shape[1]
    return jnp.sum(jnp.where(diagonal((lanes, lanes)), row, 0.0), axis=1, keepdims=True)


def squares_of(rows):
    total = jnp.zeros((rows.shape[0], HD), F32)
    for c in range(0, rows.shape[1], HD):
        wide = rows[:, c : c + HD].astype(F32)
        total = total + wide * wide
    return total


def split_three(values):
    high = values.astype(BF16).astype(F32)
    rest = values - high
    middle = rest.astype(BF16).astype(F32)
    return high, middle, rest - middle


def softmax_parts(query, key, value, usable):
    scores = jnp.where(usable, dot_t(query, key) * HD**-0.5, LOWEST)
    top = jnp.max(scores, axis=1, keepdims=True)
    weights = jnp.where(usable, jnp.exp(scores - top), 0.0)
    return dot(weights.astype(BF16), value), top, jnp.sum(weights, axis=1, keepdims=True)


def prepare_kernel(sizes, *refs):
    n, img, tok, blocks, page_cap = sizes
    far, (info, places, slots, square, near), near_weights, rest = refs[:9], refs[9:14], refs[14:16], refs[16:]
    small, (starts, sems) = rest[:5], rest[5:]
    targets = (*small, near.at[:tok], near.at[tok:], *near_weights)
    copies = [pltpu.make_async_copy(a, b, sems.at[i]) for i, (a, b) in enumerate(zip(far, targets))]
    for c in copies:
        c.start()
    route, pages, count, tail, req = small
    for c in copies[: len(small)]:
        c.wait()
    pos = lax.axis_index("section")
    stations = lax.broadcasted_iota(I32, (n, img), 0)
    earlier = lax.broadcasted_iota(I32, (img, img), 0) < lax.broadcasted_iota(I32, (img, img), 1)
    earlier = jnp.where(earlier, 1.0, 0.0).astype(BF16)
    before = jnp.zeros((n, 1), F32)
    place = jnp.zeros((1, img), I32)
    for e in range(n):
        target = route[:, e * img : (e + 1) * img]
        marks = jnp.where(target == stations, 1.0, 0.0)
        prefix = dot(marks.astype(BF16), earlier) + before
        rank = jnp.sum(marks * prefix, axis=0, keepdims=True).astype(I32)
        here = target * tok + rank
        places[:, e * img : (e + 1) * img] = here
        place = jnp.where(pos == e, here, place)
        before = before + jnp.sum(marks, axis=1, keepdims=True)
    mine = lax.broadcasted_iota(I32, (n, 1), 0) == pos
    replaced = jnp.sum(jnp.where(mine, before, 0.0), axis=0, keepdims=True).astype(I32)
    total = jnp.int32(0)
    for r in range(n):
        starts[r] = total
        total = total + count[r]
    inside = lax.broadcasted_iota(I32, (1, tok), 1)
    token = inside + pos * tok
    text_slot = jnp.full((1, tok), -1, I32)
    vis_slot = jnp.full((1, img), -1, I32)
    for b in range(n):
        r = req[b]
        first = starts[r] * PAGE
        last = first + (count[r] - 1) * PAGE + tail[r]
        text_slot = jnp.where((token >= first) & (token < last), b, text_slot)
        vis_slot = jnp.where((place >= first) & (place < last), b, vis_slot)
    info[0:1, :tok] = jnp.where(inside < replaced, -1, text_slot)
    info[1:2, :img] = vis_slot
    for g in range(blocks):
        holder = pages[0, pos * blocks + g]
        slot = holder * page_cap
        for e in range(g):
            slot = slot + (pages[0, pos * blocks + e] == holder).astype(I32)
        slots[g] = slot
    for c in copies[len(small) : len(small) + 2]:
        c.wait()
    square[...] = squares_of(near)
    for c in copies[len(small) + 2 :]:
        c.wait()


def project_kernel(step, near, text_far, vis_far, gain, w_key, w_value, square, kv_text, kv_vis, total):
    tok, half = text_far.shape
    kvw = w_key.shape[1]
    me = lax.axis_index("tensor")
    far = (text_far, vis_far)
    sums = [jnp.sum(square[:tok, :] + squares_of(text_far), axis=1, keepdims=True)]
    sums.append(jnp.sum(square[tok:, :] + squares_of(vis_far), axis=1, keepdims=True))
    scales = [lax.rsqrt(x / (2.0 * half) + EPS) for x in sums]
    for nearby, side in ((True, me), (False, 1 - me)):
        rows = (near.at[:tok], near.at[tok:]) if nearby else far
        for c in range(0, half, step):
            columns = pl.ds(pl.multiple_of(side * half + c, step), step)
            scaled = gain[:, columns]
            normed = jnp.concatenate(
                [(x[:, c : c + step].astype(F32) * s * scaled).astype(BF16) for x, s in zip(rows, scales)], axis=0
            )
            for w, at in ((w_key, 0), (w_value, kvw)):
                part = dot(normed, w[columns, :])
                if nearby and c == 0:
                    total[:, at : at + kvw] = part
                else:
                    total[:, at : at + kvw] += part
    kv_text[...] = total[:tok, :].astype(BF16)
    kv_vis[...] = total[tok:, :].astype(BF16)


def attend_kernel(n, page_cap, kv_heads, slots, info, kv_text, kv_vis, queries, out, own, held):
    pos = lax.axis_index("section")
    tok, img = kv_text.shape[0], kv_vis.shape[0]
    kvw = kv_heads * HD
    chunk = page_cap * PAGE
    halves = 2 * kv_heads
    pages = halves * chunk
    out[:, :pages, :] = jnp.zeros((n, pages, HD), BF16)
    for g in range(tok // PAGE):
        slot = slots[g]
        for h in range(halves):
            at = pl.ds(pl.multiple_of((slot % page_cap) * PAGE + h * chunk, PAGE), PAGE)
            out[slot // page_cap, at, :] = kv_text[g * PAGE : (g + 1) * PAGE, h * HD : (h + 1) * HD]
    rows = queries.shape[0] // n // kv_heads
    slot = lax.broadcasted_iota(I32, (n * rows, 1), 0) // rows
    text_ok = slot == info[0:1, :tok]
    vis_ok = slot == info[1:2, :img]
    tops, totals = [], []
    for g in range(kv_heads):
        at = [(k * kv_heads + g) * rows for k in range(n)]
        query = jnp.concatenate([queries[x : x + rows, :HD] for x in at], axis=0)
        cols = slice(g * HD, (g + 1) * HD)
        vcols = slice(kvw + g * HD, kvw + (g + 1) * HD)
        s_text = jnp.where(text_ok, dot_t(query, kv_text[:, cols]) * HD**-0.5, LOWEST)
        s_vis = jnp.where(vis_ok, dot_t(query, kv_vis[:, cols]) * HD**-0.5, LOWEST)
        top = jnp.maximum(jnp.max(s_text, axis=1, keepdims=True), jnp.max(s_vis, axis=1, keepdims=True))
        w_text = jnp.where(text_ok, jnp.exp(s_text - top), 0.0)
        w_vis = jnp.where(vis_ok, jnp.exp(s_vis - top), 0.0)
        weight = jnp.sum(w_text, axis=1, keepdims=True) + jnp.sum(w_vis, axis=1, keepdims=True)
        numerator = dot(w_text.astype(BF16), kv_text[:, vcols]) + dot(w_vis.astype(BF16), kv_vis[:, vcols])
        held[g * n * rows : (g + 1) * n * rows, :] = numerator
        own[g * rows : (g + 1) * rows, :] = held[pl.ds(pl.multiple_of((g * n + pos) * rows, rows), rows), :]
        numerator = numerator.astype(BF16)
        for k in range(n):
            out[k, pages + g * rows : pages + (g + 1) * rows, :] = numerator[k * rows : (k + 1) * rows, :]
        tops.append(top)
        totals.append(weight)
    line = lax.broadcasted_iota(I32, (PAGE, HD), 0)
    for k in range(n):
        at = slice(k * rows, (k + 1) * rows)
        stats = column_to_row(jnp.concatenate([x[at] for x in tops + totals], axis=0))

        @pl.when(pos == k)
        def _():
            own[kv_heads * rows :, :] = jnp.broadcast_to(stats, (STAT, stats.shape[1]))

        high, middle, low = split_three(stats)
        lines = jnp.where(line == 0, high, jnp.where(line == 1, middle, jnp.where(line == 2, low, 0.0)))
        out[k, pages + kv_heads * rows :, :] = lines.astype(BF16)


def place_kernel(n, blocks, page_cap, pages, places, vis, token, placed):
    pos = lax.axis_index("section")
    lanes = n * blocks
    here = pages[...] == pos
    ones = jnp.where(here, 1.0, 0.0)
    first = lax.broadcasted_iota(I32, (lanes, lanes), 0)
    second = lax.broadcasted_iota(I32, (lanes, lanes), 1)
    earlier = (first < second) & (first // blocks == second // blocks)
    rank = dot(jnp.broadcast_to(ones, (STAT, lanes)).astype(BF16), jnp.where(earlier, 1.0, 0.0).astype(BF16))
    page = lax.broadcasted_iota(I32, (1, lanes), 1)
    slot = jnp.where(here, page // blocks * page_cap + rank[0:1].astype(I32), -1)
    rows = n * page_cap * PAGE
    row = lax.broadcasted_iota(I32, (rows, 1), 0)
    found = jnp.max(jnp.where(row // PAGE == slot, page, -1), axis=1, keepdims=True)
    at = jnp.where(found < 0, -1, found * PAGE + row % PAGE)
    hot = jnp.where(at == places[...], 1.0, 0.0)
    covered = jnp.sum(hot, axis=1, keepdims=True)
    token[...] = jnp.broadcast_to(covered, token.shape)
    placed[...] = dot(hot.astype(BF16), vis[...]).astype(BF16)


def combine(pieces, highest):
    numerator, total = 0.0, 0.0
    for rows, top, weight in pieces:
        scale = jnp.exp(top - highest)
        numerator = numerator + rows * scale
        total = total + weight * scale
    return numerator, total


def fresh_kernel(kv_heads, steps, query, key, value, own, mine):
    rows = query.shape[0] // kv_heads
    every = kv_heads * rows
    row = lax.broadcasted_iota(I32, (rows, steps), 0)
    causal = lax.broadcasted_iota(I32, (rows, steps), 1) <= row % steps
    stats = row_to_column(own[every : every + 1, :])
    tops, totals = [], []
    for g in range(kv_heads):
        cols = slice(g * HD, (g + 1) * HD)
        at = slice(g * rows, (g + 1) * rows)
        fresh = softmax_parts(query[at, :], key[:, cols], value[:, cols], causal)
        share = (own[at, :], stats[at], stats[every + g * rows : every + (g + 1) * rows])
        highest = jnp.maximum(fresh[1], share[1])
        numerator, total = combine((fresh, share), highest)
        mine[at, :] = numerator
        tops.append(highest)
        totals.append(total)
    line = column_to_row(jnp.concatenate(tops + totals, axis=0))
    mine[every:, :] = jnp.broadcast_to(line, (STAT, line.shape[1]))


def finish_kernel(steps, page_cap, shares, mine, covered, placed, attended, keys, values):
    n = shares.shape[0]
    pos = lax.axis_index("section")
    rows = mine.shape[0] - STAT
    chunk = page_cap * PAGE
    halves = keys.shape[2] // HD
    for k in range(n):
        at = slice(k * chunk, (k + 1) * chunk)
        inserted = covered[at, :] > 0.0
        for i, out in enumerate((keys, values)):
            for h in range(halves):
                part = i * halves + h
                text = shares[k, part * chunk : (part + 1) * chunk, :].astype(F32)
                image = placed[at, part * HD : (part + 1) * HD].astype(F32)
                out[k, :, h * HD : (h + 1) * HD] = jnp.where(inserted, image, text).astype(BF16)
    pages = 2 * halves * chunk
    stats = row_to_column(mine[rows : rows + 1, :])
    pieces = [(mine[:rows, :], stats[:rows], stats[rows:])]
    for k in range(n):
        lines = shares[k, pages + rows :, :].astype(F32)
        stats = row_to_column(lines[0:1] + lines[1:2] + lines[2:3])
        away = pos != k
        top = jnp.where(away, stats[:rows], LOWEST)
        weight = jnp.where(away, stats[rows:], 0.0)
        pieces.append((jnp.where(away, shares[k, pages : pages + rows, :].astype(F32), 0.0), top, weight))
    highest = pieces[0][1]
    for p in pieces[1:]:
        highest = jnp.maximum(highest, p[1])
    numerator, total = combine(pieces, highest)
    result = (numerator / total).astype(BF16)
    for h in range(rows // steps):
        attended[0, :, h * HD : (h + 1) * HD] = result[h * steps : (h + 1) * steps, :]


def body(
    text_rows,
    vis_rows,
    img_route,
    norm_gain,
    w_key,
    w_value,
    page_count,
    tail_len,
    page_dest,
    dec_req,
    dec_query,
    dec_key,
    dec_value,
):
    n = lax.axis_size("section")
    tok, half = text_rows.shape
    img = vis_rows.shape[0]
    kvw = w_key.shape[1]
    kv_heads = kvw // HD
    _, steps, q_width = dec_query.shape
    heads = q_width // HD
    q_rows = heads * steps
    blocks = tok // PAGE
    cap = max(2, (2 * img + n - 1) // n)
    page_cap = max(1, (blocks + n - 1) // n)

    def across(array):
        return lax.ppermute(array, "tensor", [(0, 1), (1, 0)])

    def exchange(array):
        return lax.all_to_all(array, "section", split_axis=0, concat_axis=0, tiled=True)

    def remote(array):
        return pltpu.with_memory_space_constraint(array, pltpu.HBM)

    def local(array):
        return pltpu.with_memory_space_constraint(array, pltpu.VMEM)

    vis_far = across(vis_rows)
    text_far = across(text_rows)
    query = dec_query.reshape(steps, heads, HD).transpose(1, 0, 2).reshape(q_rows, HD)

    def gathered(array):
        return lax.all_gather(array, "section", axis=0, tiled=True)

    queries = gathered(jnp.pad(query, ((0, 0), (0, 2 * kvw - HD))))
    routes, page_row = img_route.T, page_dest.T
    arguments = (routes, page_row, page_count, tail_len, dec_req, text_rows, vis_rows, w_key, w_value)
    info, places, slots, square, near, key_near, value_near = call(
        lambda *refs: prepare_kernel((n, img, tok, blocks, page_cap), *refs),
        (
            jax.ShapeDtypeStruct((8, max(tok, img)), I32),
            jax.ShapeDtypeStruct((1, n * img), I32),
            jax.ShapeDtypeStruct((blocks,), I32),
            jax.ShapeDtypeStruct((tok + img, HD), F32),
            pltpu.VMEM((tok + img, half), BF16),
            pltpu.VMEM(w_key.shape, BF16),
            pltpu.VMEM(w_value.shape, BF16),
        ),
        [ANY] * len(arguments),
        (VM, VM, SM) + (VM,) * 4,
        [
            *[(pltpu.VMEM if i == 0 else pltpu.SMEM)(a.shape, a.dtype) for i, a in enumerate(arguments[:5])],
            pltpu.SMEM((n,), I32),
            pltpu.SemaphoreType.DMA((len(arguments),)),
        ],
        flops=1 << 20,
        traffic=2 * 2 * half * 2 * kvw * 2,
    )(*[remote(a) for a in arguments])

    kv_text, kv_vis = call(
        lambda *refs: project_kernel(min(1024, half), *refs),
        (
            jax.ShapeDtypeStruct((tok, 2 * kvw), BF16),
            jax.ShapeDtypeStruct((img, 2 * kvw), BF16),
        ),
        [VM] * 7,
        (VM, VM),
        [pltpu.VMEM((tok + img, 2 * kvw), F32)],
        flops=2 * (tok + img) * 2 * half * 2 * kvw,
        traffic=2 * (tok + img) * 2 * half + 8 * half * kvw,
    )(
        local(near),
        text_far,
        vis_far,
        remote(norm_gain.reshape(1, 2 * half)),
        local(key_near),
        local(value_near),
        square,
    )
    vis_all = gathered(kv_vis)

    sent, own = call(
        lambda *refs: attend_kernel(n, page_cap, kv_heads, *refs),
        (
            jax.ShapeDtypeStruct((n, page_cap * PAGE * 2 * kv_heads + q_rows + PAGE, HD), BF16),
            jax.ShapeDtypeStruct((q_rows + STAT, HD), F32),
        ),
        [SM] + [VM] * 4,
        (VM, VM),
        [pltpu.VMEM((n * q_rows, HD), F32)],
        limit=24,
        flops=4 * n * q_rows * tok * HD,
        traffic=n * (q_rows + STAT) * HD * 4,
    )(slots, info, kv_text, kv_vis, queries)
    shares = exchange(sent)

    mine = call(
        lambda *refs: fresh_kernel(kv_heads, steps, *refs),
        jax.ShapeDtypeStruct((q_rows + STAT, HD), F32),
        [VM] * 4,
        VM,
        flops=1 << 20,
        traffic=1 << 18,
    )(remote(query), remote(dec_key[0]), remote(dec_value[0]), own)

    rows = n * page_cap * PAGE
    covered, placed = call(
        lambda *refs: place_kernel(n, blocks, page_cap, *refs),
        (jax.ShapeDtypeStruct((rows, HD), F32), jax.ShapeDtypeStruct((rows, 2 * kvw), BF16)),
        [VM] * 3,
        (VM, VM),
        limit=32,
        flops=2 * rows * n * img * 2 * kvw,
        traffic=2 * n * img * 2 * kvw,
    )(remote(page_row), places, vis_all)

    attended, cache_key, cache_value = call(
        lambda *refs: finish_kernel(steps, page_cap, *refs),
        (
            jax.ShapeDtypeStruct(dec_query.shape, BF16),
            jax.ShapeDtypeStruct((n, page_cap * PAGE, kvw), BF16),
            jax.ShapeDtypeStruct((n, page_cap * PAGE, kvw), BF16),
        ),
        [VM] * 4,
        (VM, VM, VM),
        traffic=4 * tok * 2 * kvw,
    )(shares, mine, covered, placed)
    slots_here = n * page_cap
    return (
        attended,
        cache_key.reshape(slots_here, PAGE, kvw),
        cache_value.reshape(slots_here, PAGE, kvw),
    )


def solution(mesh):
    return jax.shard_map(
        body,
        mesh=mesh,
        in_specs=(
            P(("groups", "section"), "tensor"),
            P(("groups", "section"), "tensor"),
            P("groups", None),
            P(),
            P(None, "tensor"),
            P(None, "tensor"),
            P("groups"),
            P("groups"),
            P("groups", None),
            P("groups"),
            P(("groups", "section"), None, "tensor"),
            P(("groups", "section"), None, "tensor"),
            P(("groups", "section"), None, "tensor"),
        ),
        out_specs=(
            P(("groups", "section"), None, "tensor"),
            P(("groups", "section"), None, "tensor"),
            P(("groups", "section"), None, "tensor"),
        ),
        check_vma=False,
    )
```

```python
import jax
import jax.numpy as jnp
from jax import lax
from jax.experimental import pallas as pl
from jax.experimental.pallas import tpu as pltpu
from jax.sharding import PartitionSpec as P

HD = 128
PAGE = 16
LOWEST = -1e30
EPS = 1e-06
STAT = 8
F32 = jnp.float32
BF16 = jnp.bfloat16
I32 = jnp.int32

VM = pl.BlockSpec(memory_space=pltpu.VMEM)
SM = pl.BlockSpec(memory_space=pltpu.SMEM)
ANY = pl.BlockSpec(memory_space=pl.ANY)
MIB = 1 << 20


def call(kernel, out_shape, in_specs, out_specs, scratch=(), limit=16, flops=0, traffic=0):
    return pl.pallas_call(
        kernel,
        out_shape=out_shape,
        in_specs=in_specs,
        out_specs=out_specs,
        scratch_shapes=list(scratch),
        compiler_params=pltpu.CompilerParams(vmem_limit_bytes=limit * MIB),
        cost_estimate=pl.CostEstimate(flops=flops, bytes_accessed=traffic, transcendentals=0),
    )


def dot(a, b):
    return jnp.dot(a, b, preferred_element_type=F32)


def dot_t(a, b):
    return lax.dot_general(a, b, (((1,), (1,)), ((), ())), preferred_element_type=F32)


def diagonal(shape):
    return lax.broadcasted_iota(I32, shape, 0) == lax.broadcasted_iota(I32, shape, 1)


def column_to_row(column):
    rows = column.shape[0]
    return jnp.sum(jnp.where(diagonal((rows, rows)), column, 0.0), axis=0, keepdims=True)


def row_to_column(row):
    lanes = row.shape[1]
    return jnp.sum(jnp.where(diagonal((lanes, lanes)), row, 0.0), axis=1, keepdims=True)


def squares_of(rows):
    total = jnp.zeros((rows.shape[0], HD), F32)
    for c in range(0, rows.shape[1], HD):
        wide = rows[:, c : c + HD].astype(F32)
        total = total + wide * wide
    return total


def split_three(values):
    high = values.astype(BF16).astype(F32)
    rest = values - high
    middle = rest.astype(BF16).astype(F32)
    return high, middle, rest - middle


def softmax_parts(query, key, value, usable):
    scores = jnp.where(usable, dot_t(query, key) * HD**-0.5, LOWEST)
    top = jnp.max(scores, axis=1, keepdims=True)
    weights = jnp.where(usable, jnp.exp(scores - top), 0.0)
    return dot(weights.astype(BF16), value), top, jnp.sum(weights, axis=1, keepdims=True)


def prepare_kernel(sizes, *refs):
    n, img, tok, blocks, lot, page_cap = sizes
    far, (info, slots), near, small, (starts, sems) = refs[:8], refs[8:10], refs[10:13], refs[13:18], refs[18:]
    half = near[0].shape[0]
    mine = pl.ds(pl.multiple_of(lax.axis_index("tensor") * half, half), half)
    sources = (*far[:5], far[5].at[mine], far[6].at[mine], far[7])
    copies = [pltpu.make_async_copy(a, b, sems.at[i]) for i, (a, b) in enumerate(zip(sources, small + near))]
    for c in copies:
        c.start()
    route, pages, count, tail, req = small
    for c in copies[: len(small)]:
        c.wait()
    pos = lax.axis_index("section")
    table = [route[:, e * img : (e + 1) * img] for e in range(n)]
    own = jnp.zeros((1, img), I32)
    for e in range(n):
        own = jnp.where(pos == e, table[e], own)
    marks = own == lax.broadcasted_iota(I32, (n, img), 0)
    ones = jnp.where(marks, 1.0, 0.0).astype(BF16)
    earlier = lax.broadcasted_iota(I32, (img, img), 0) < lax.broadcasted_iota(I32, (img, img), 1)
    prefix = dot(ones, jnp.where(earlier, 1.0, 0.0).astype(BF16))
    local = jnp.sum(jnp.where(marks, prefix, 0.0), axis=0, keepdims=True).astype(I32)
    info[0:1, :img] = own * lot + local
    lanes = lax.broadcasted_iota(I32, (1, n * lot), 1)
    source, inner = lanes // lot, lanes % lot
    fits = jnp.zeros((1, n * lot), I32)
    offset = jnp.zeros((1, n * lot), I32)
    for e in range(n):
        arriving = jnp.sum((table[e] == pos).astype(I32), axis=1, keepdims=True)
        fits = fits + jnp.where(source == e, arriving, 0)
        offset = offset + jnp.where(source > e, arriving, 0)
    info[2:3, : n * lot] = jnp.where(inner < fits, offset + inner, -1)
    total = jnp.int32(0)
    for r in range(n):
        starts[r] = total
        total = total + count[r]
    token = lax.broadcasted_iota(I32, (1, tok), 1) + pos * tok
    token_slot = jnp.full((1, tok), -1, I32)
    for b in range(n):
        r = req[b]
        first = starts[r] * PAGE
        last = first + (count[r] - 1) * PAGE + tail[r]
        token_slot = jnp.where((token >= first) & (token < last), b, token_slot)
    info[1:2, :tok] = token_slot
    for g in range(blocks):
        holder = pages[0, pos * blocks + g]
        slot = holder * page_cap
        for e in range(g):
            slot = slot + (pages[0, pos * blocks + e] == holder).astype(I32)
        slots[g] = slot
    for c in copies[len(small) :]:
        c.wait()


def scale_of(near, far):
    sums = jnp.sum(squares_of(near) + squares_of(far), axis=1, keepdims=True)
    return lax.rsqrt(sums / (2.0 * near.shape[1]) + EPS)


def normed_rows(rows, c, step, scale, gain):
    return (rows[:, c : c + step].astype(F32) * scale * gain).astype(BF16)


def add_part(total, at, normed, w, begin):
    part = dot(normed, w)
    columns = slice(at, at + part.shape[1])
    if begin:
        total[:, columns] = part
    else:
        total[:, columns] += part


def vis_kernel(n, lot, step, *refs):
    near, far, gain, key_near, value_near, w_key, w_value, info, query, out, key_far, value_far, total, sems = refs
    img, half = near.shape
    kvw = w_key.shape[1]
    me = lax.axis_index("tensor")
    other = pl.ds(pl.multiple_of((1 - me) * half, half), half)
    pairs = ((w_key, key_far), (w_value, value_far))
    copies = [pltpu.make_async_copy(w.at[other], held, sems.at[i]) for i, (w, held) in enumerate(pairs)]
    for c in copies:
        c.start()
    scale = scale_of(near, far)
    for rows, side, weights in ((near, me, (key_near, value_near)), (far, 1 - me, (key_far, value_far))):
        if rows is far:
            for c in copies:
                c.wait()
        for c in range(0, half, step):
            columns = pl.ds(pl.multiple_of(side * half + c, step), step)
            normed = normed_rows(rows, c, step, scale, gain[:, columns])
            for w, at in zip(weights, (0, kvw)):
                add_part(total, at, normed, w[c : c + step, :], rows is near and c == 0)
    slot = lax.broadcasted_iota(I32, (n * lot, img), 0)
    chosen = jnp.where(slot == info[0:1, :img], 1.0, 0.0).astype(BF16)
    packed = dot(chosen, total[...].astype(BF16)).astype(BF16)
    q_lots = out.shape[1] - lot
    for k in range(n):
        for j in range(query.shape[0] // q_lots):
            out[k, :q_lots, j * HD : (j + 1) * HD] = query[j * q_lots : (j + 1) * q_lots, :]
        out[k, q_lots:, :] = packed[k * lot : (k + 1) * lot, :]


def put_page(out, page_cap, slot, rows):
    chunk = page_cap * PAGE
    for h in range(rows.shape[1] // HD):
        at = pl.ds(pl.multiple_of((slot % page_cap) * PAGE + h * chunk, PAGE), PAGE)
        out[slot // page_cap, at, :] = rows[:, h * HD : (h + 1) * HD]


def text_kernel(load, step, page_cap, q_rows, *refs):
    near_far, far, gain, w_key_far, w_value_far, info, slots, out, bias, base, near, w_key, w_value, total, sems = refs
    half = near.shape[1]
    kvw = w_key.shape[1]
    me = lax.axis_index("tensor")
    first = pltpu.make_async_copy(near_far, near, sems.at[0])
    first.start()
    loads = []
    for side in (me, 1 - me):
        for c in range(0, half, load):
            at = len(loads) * load
            columns = pl.ds(pl.multiple_of(side * half + c, load), load)
            pair = [
                pltpu.make_async_copy(w.at[columns], held.at[at : at + load], sems.at[2 * len(loads) + i])
                for i, (w, held) in enumerate(((w_key_far, w_key), (w_value_far, w_value)), 1)
            ]
            for copy in pair:
                copy.start()
            loads.append(pair)
    sums = squares_of(far)
    first.wait()
    sums = jnp.sum(squares_of(near) + sums, axis=1, keepdims=True)
    scale = lax.rsqrt(sums / (2.0 * half) + EPS)
    for i, pair in enumerate(loads):
        for copy in pair:
            copy.wait()
        for at in range(i * load, (i + 1) * load, step):
            rows, side = (near, me) if at < half else (far, 1 - me)
            c = at % half
            columns = pl.ds(pl.multiple_of(side * half + c, step), step)
            normed = normed_rows(rows, c, step, scale, gain[:, columns])
            for w, col in ((w_key, 0), (w_value, kvw)):
                add_part(total, col, normed, w[at : at + step, :], at == 0)
    out[...] = total[...].astype(BF16)
    base[...] = jnp.zeros(base.shape, BF16)
    tok = near.shape[0]
    for g in range(tok // PAGE):
        put_page(base, page_cap, slots[g], out[g * PAGE : (g + 1) * PAGE, :])
    token_slot = row_to_column(info[1:2, :tok].astype(F32))
    lanes = lax.broadcasted_iota(I32, bias.shape, 1) // q_rows
    bias[...] = jnp.where(token_slot == lanes.astype(F32), 0.0, LOWEST)


def attend_kernel(n, cap, lot, page_cap, kv_heads, slots, info, kv_text, arrived, bias, base, out, own, mixed, held, rows_held):
    pos = lax.axis_index("section")
    tok = kv_text.shape[0]
    kvw = kv_heads * HD
    q_lots = arrived.shape[1] - lot
    reach = min(tok, n * cap)
    hit = lax.broadcasted_iota(I32, (reach, n * lot), 0) == info[2:3, : n * lot]
    hot = jnp.where(hit, 1.0, 0.0)
    covered = jnp.sum(hot, axis=1, keepdims=True) > 0.0
    incoming = jnp.concatenate([arrived[k, q_lots:, :] for k in range(n)], axis=0)
    placed = dot(hot.astype(BF16), incoming)
    mixed[...] = jnp.where(covered, placed, kv_text[:reach, :].astype(F32)).astype(BF16)
    groups = arrived.shape[2] // HD // kv_heads
    rows = groups * q_lots
    pages = base.shape[1]
    out[:, :pages, :] = base[...]
    for g in range(reach // PAGE):
        put_page(out, page_cap, slots[g], mixed[g * PAGE : (g + 1) * PAGE, :])
    for g in range(kv_heads):
        query = jnp.concatenate(
            [
                arrived[k, :q_lots, (g * groups + j) * HD : (g * groups + j + 1) * HD]
                for k in range(n)
                for j in range(groups)
            ],
            axis=0,
        )
        cols = slice(g * HD, (g + 1) * HD)
        vcols = slice(kvw + g * HD, kvw + (g + 1) * HD)
        key = jnp.concatenate([mixed[:, cols], kv_text[reach:, cols]], axis=0)
        value = jnp.concatenate([mixed[:, vcols], kv_text[reach:, vcols]], axis=0)
        scores = dot_t(key, query) * HD**-0.5 + bias[...]
        top = jnp.max(scores, axis=0, keepdims=True)
        weights = jnp.exp(scores - top)
        rows_held[g : g + 1, :] = top
        rows_held[kv_heads + g : kv_heads + g + 1, :] = jnp.sum(weights, axis=0, keepdims=True)
        numerator = lax.dot_general(
            weights.astype(BF16), value, (((0,), (0,)), ((), ())), preferred_element_type=F32
        )
        held[g * n * rows : (g + 1) * n * rows, :] = numerator
        own[g * rows : (g + 1) * rows, :] = held[pl.ds(pl.multiple_of((g * n + pos) * rows, rows), rows), :]
        numerator = numerator.astype(BF16)
        for k in range(n):
            out[k, pages + g * rows : pages + (g + 1) * rows, :] = numerator[k * rows : (k + 1) * rows, :]
    stat_rows = 2 * kv_heads
    share = HD // rows
    window = pl.ds(pl.multiple_of(pos // share * HD, HD), HD)
    own[kv_heads * rows : kv_heads * rows + stat_rows, :] = rows_held[:stat_rows, window]
    blank = jnp.zeros((PAGE - 3 * stat_rows, HD), F32)
    for w in range(-(-n // share)):
        stats = rows_held[:stat_rows, w * HD : (w + 1) * HD]
        lines = jnp.concatenate([*split_three(stats), blank], axis=0).astype(BF16)
        for k in range(w * share, min(n, (w + 1) * share)):
            out[k, pages + kv_heads * rows :, :] = lines


def pick_column(row, rows, start):
    shape = (rows, HD)
    chosen = lax.broadcasted_iota(I32, shape, 1) == lax.broadcasted_iota(I32, shape, 0) + start
    return jnp.sum(jnp.where(chosen, row, 0.0), axis=1, keepdims=True)


def combine(pieces, highest):
    numerator, total = 0.0, 0.0
    for rows, top, weight in pieces:
        scale = jnp.exp(top - highest)
        numerator = numerator + rows * scale
        total = total + weight * scale
    return numerator, total


def fresh_kernel(kv_heads, steps, query, key, value, own, mine):
    rows = query.shape[0] // kv_heads
    every = kv_heads * rows
    start = lax.axis_index("section") % (HD // rows) * rows
    row = lax.broadcasted_iota(I32, (rows, steps), 0)
    causal = lax.broadcasted_iota(I32, (rows, steps), 1) <= row % steps
    tops, totals = [], []
    for g in range(kv_heads):
        cols = slice(g * HD, (g + 1) * HD)
        at = slice(g * rows, (g + 1) * rows)
        fresh = softmax_parts(query[at, :], key[:, cols], value[:, cols], causal)
        share = (
            own[at, :],
            pick_column(own[every + g : every + g + 1, :], rows, start),
            pick_column(own[every + kv_heads + g : every + kv_heads + g + 1, :], rows, start),
        )
        highest = jnp.maximum(fresh[1], share[1])
        numerator, total = combine((fresh, share), highest)
        mine[at, :] = numerator
        tops.append(highest)
        totals.append(total)
    line = column_to_row(jnp.concatenate(tops + totals, axis=0))
    mine[every:, :] = jnp.broadcast_to(line, (STAT, line.shape[1]))


def finish_kernel(kv_heads, steps, page_cap, shares, mine, attended, keys, values):
    n = shares.shape[0]
    pos = lax.axis_index("section")
    every = mine.shape[0] - STAT
    rows = every // kv_heads
    start = pos % (HD // rows) * rows
    chunk = page_cap * PAGE
    halves = keys.shape[2] // HD
    for k in range(n):
        for i, out in enumerate((keys, values)):
            for h in range(halves):
                part = i * halves + h
                out[k, :, h * HD : (h + 1) * HD] = shares[k, part * chunk : (part + 1) * chunk, :]
    pages = 2 * halves * chunk
    stats = row_to_column(mine[every : every + 1, :])
    lines = []
    for k in range(n):
        three = shares[k, pages + every :, :].astype(F32)
        size = 2 * kv_heads
        lines.append(three[:size] + three[size : 2 * size] + three[2 * size : 3 * size])
    for g in range(kv_heads):
        at = slice(g * rows, (g + 1) * rows)
        pieces = [(mine[at, :], stats[at], stats[every + g * rows : every + (g + 1) * rows])]
        for k in range(n):
            away = pos != k
            top = jnp.where(away, pick_column(lines[k][g : g + 1], rows, start), LOWEST)
            weight = jnp.where(away, pick_column(lines[k][kv_heads + g : kv_heads + g + 1], rows, start), 0.0)
            share = shares[k, pages + g * rows : pages + (g + 1) * rows, :].astype(F32)
            pieces.append((share, top, weight))
        highest = pieces[0][1]
        for p in pieces[1:]:
            highest = jnp.maximum(highest, p[1])
        numerator, total = combine(pieces, highest)
        result = (numerator / total).astype(BF16)
        for h in range(rows // steps):
            to = (g * rows // steps + h) * HD
            attended[0, :, to : to + HD] = result[h * steps : (h + 1) * steps, :]


def body(
    text_rows,
    vis_rows,
    img_route,
    norm_gain,
    w_key,
    w_value,
    page_count,
    tail_len,
    page_dest,
    dec_req,
    dec_query,
    dec_key,
    dec_value,
):
    n = lax.axis_size("section")
    tok, half = text_rows.shape
    img = vis_rows.shape[0]
    kvw = w_key.shape[1]
    kv_heads = kvw // HD
    _, steps, q_width = dec_query.shape
    heads = q_width // HD
    q_rows = heads * steps
    blocks = tok // PAGE
    cap = max(2, (2 * img + n - 1) // n)
    page_cap = max(1, (blocks + n - 1) // n)

    def across(array):
        return lax.ppermute(array, "tensor", [(0, 1), (1, 0)])

    def exchange(array):
        return lax.all_to_all(array, "section", split_axis=0, concat_axis=0, tiled=True)

    def remote(array):
        return pltpu.with_memory_space_constraint(array, pltpu.HBM)

    def local(array):
        return pltpu.with_memory_space_constraint(array, pltpu.VMEM)

    vis_far = across(vis_rows)
    text_far = across(text_rows)
    query = dec_query.reshape(steps, heads, HD).transpose(1, 0, 2).reshape(q_rows, HD)

    lot = -(-cap // PAGE) * PAGE
    q_lots = q_rows * HD // (2 * kvw)
    width = max(tok, n * lot)
    arguments = (img_route.T, page_dest.T, page_count, tail_len, dec_req, w_key, w_value, vis_rows)
    info, slots, key_near, value_near, vis_near = call(
        lambda *refs: prepare_kernel((n, img, tok, blocks, lot, page_cap), *refs),
        (
            jax.ShapeDtypeStruct((8, width), I32),
            jax.ShapeDtypeStruct((blocks,), I32),
            pltpu.VMEM((half, kvw), BF16),
            pltpu.VMEM((half, kvw), BF16),
            pltpu.VMEM(vis_rows.shape, BF16),
        ),
        [ANY] * len(arguments),
        (VM, SM) + (VM,) * 3,
        [
            *[(pltpu.VMEM if i == 0 else pltpu.SMEM)(a.shape, a.dtype) for i, a in enumerate(arguments[:5])],
            pltpu.SMEM((n,), I32),
            pltpu.SemaphoreType.DMA((len(arguments),)),
        ],
        flops=1 << 20,
        traffic=2 * 2 * half * 2 * kvw * 2,
    )(*[remote(a) for a in arguments])

    step = min(1024, half)
    load = min(2048, half)
    gain = remote(norm_gain.reshape(1, 2 * half))

    packed = call(
        lambda *refs: vis_kernel(n, lot, step, *refs),
        jax.ShapeDtypeStruct((n, q_lots + lot, 2 * kvw), BF16),
        [VM] * 5 + [ANY] * 2 + [VM] * 2,
        VM,
        [
            pltpu.VMEM((half, kvw), BF16),
            pltpu.VMEM((half, kvw), BF16),
            pltpu.VMEM((img, 2 * kvw), F32),
            pltpu.SemaphoreType.DMA((2,)),
        ],
        flops=64 * img * 2 * half * 2 * kvw,
        traffic=2 * img * 2 * half + 8 * half * kvw,
    )(
        local(vis_near),
        vis_far,
        gain,
        local(key_near),
        local(value_near),
        remote(w_key),
        remote(w_value),
        info,
        remote(query),
    )
    arrived = exchange(packed)

    block = page_cap * PAGE * 2 * kv_heads + q_rows + PAGE
    kv_text, bias, base = call(
        lambda *refs: text_kernel(load, step, page_cap, q_rows // kv_heads, *refs),
        (
            jax.ShapeDtypeStruct((tok, 2 * kvw), BF16),
            jax.ShapeDtypeStruct((tok, n * q_rows // kv_heads), F32),
            jax.ShapeDtypeStruct((n, block - q_rows - PAGE, HD), BF16),
        ),
        [ANY, VM, VM, ANY, ANY, VM, SM],
        (VM, VM, VM),
        [
            pltpu.VMEM((tok, half), BF16),
            pltpu.VMEM(w_key.shape, BF16),
            pltpu.VMEM(w_value.shape, BF16),
            pltpu.VMEM((tok, 2 * kvw), F32),
            pltpu.SemaphoreType.DMA((1 + 4 * half // load,)),
        ],
        limit=24,
        flops=2 * tok * 2 * half * 2 * kvw,
        traffic=2 * tok * 2 * half + 8 * half * kvw,
    )(remote(text_rows), text_far, gain, remote(w_key), remote(w_value), info, slots)

    sent, own = call(
        lambda *refs: attend_kernel(n, cap, lot, page_cap, kv_heads, *refs),
        (
            jax.ShapeDtypeStruct((n, block, HD), BF16),
            jax.ShapeDtypeStruct((q_rows + STAT, HD), F32),
        ),
        [SM] + [VM] * 5,
        (VM, VM),
        [
            pltpu.VMEM((min(tok, n * cap), 2 * kvw), BF16),
            pltpu.VMEM((n * q_rows, HD), F32),
            pltpu.VMEM((STAT, n * q_rows // kv_heads), F32),
        ],
        flops=4 * n * q_rows * tok * HD,
        traffic=n * (q_rows + STAT) * HD * 4,
    )(slots, info, kv_text, arrived, bias, base)
    shares = exchange(sent)

    mine = call(
        lambda *refs: fresh_kernel(kv_heads, steps, *refs),
        jax.ShapeDtypeStruct((q_rows + STAT, HD), F32),
        [VM] * 4,
        VM,
        flops=1 << 20,
        traffic=1 << 18,
    )(remote(query), remote(dec_key[0]), remote(dec_value[0]), own)

    slots_here = n * page_cap
    attended, cache_key, cache_value = call(
        lambda *refs: finish_kernel(kv_heads, steps, page_cap, *refs),
        (
            jax.ShapeDtypeStruct(dec_query.shape, BF16),
            jax.ShapeDtypeStruct((n, page_cap * PAGE, kvw), BF16),
            jax.ShapeDtypeStruct((n, page_cap * PAGE, kvw), BF16),
        ),
        [VM, VM],
        (VM, VM, VM),
        traffic=4 * tok * 2 * kvw,
    )(shares, mine)
    return (
        attended,
        cache_key.reshape(slots_here, PAGE, kvw),
        cache_value.reshape(slots_here, PAGE, kvw),
    )


def solution(mesh):
    return jax.shard_map(
        body,
        mesh=mesh,
        in_specs=(
            P(("groups", "section"), "tensor"),
            P(("groups", "section"), "tensor"),
            P("groups", None),
            P(),
            P(None, "tensor"),
            P(None, "tensor"),
            P("groups"),
            P("groups"),
            P("groups", None),
            P("groups"),
            P(("groups", "section"), None, "tensor"),
            P(("groups", "section"), None, "tensor"),
            P(("groups", "section"), None, "tensor"),
        ),
        out_specs=(
            P(("groups", "section"), None, "tensor"),
            P(("groups", "section"), None, "tensor"),
            P(("groups", "section"), None, "tensor"),
        ),
        check_vma=False,
    )
```

```python
import jax
import jax.numpy as jnp
from jax import lax
from jax.experimental import pallas as pl
from jax.experimental.pallas import tpu as pltpu
from jax.sharding import PartitionSpec as P

HD = 128
PAGE = 16
LOWEST = -1e30
EPS = 1e-06
STAT = 8
F32 = jnp.float32
BF16 = jnp.bfloat16
I32 = jnp.int32

VM = pl.BlockSpec(memory_space=pltpu.VMEM)
SM = pl.BlockSpec(memory_space=pltpu.SMEM)
ANY = pl.BlockSpec(memory_space=pl.ANY)
MIB = 1 << 20


def call(kernel, out_shape, in_specs, out_specs, scratch=(), limit=16, flops=0, traffic=0):
    return pl.pallas_call(
        kernel,
        out_shape=out_shape,
        in_specs=in_specs,
        out_specs=out_specs,
        scratch_shapes=list(scratch),
        compiler_params=pltpu.CompilerParams(vmem_limit_bytes=limit * MIB),
        cost_estimate=pl.CostEstimate(flops=flops, bytes_accessed=traffic, transcendentals=0),
    )


def dot(a, b):
    return jnp.dot(a, b, preferred_element_type=F32)


def dot_t(a, b):
    return lax.dot_general(a, b, (((1,), (1,)), ((), ())), preferred_element_type=F32)


def diagonal(shape):
    return lax.broadcasted_iota(I32, shape, 0) == lax.broadcasted_iota(I32, shape, 1)


def column_to_row(column):
    rows = column.shape[0]
    return jnp.sum(jnp.where(diagonal((rows, rows)), column, 0.0), axis=0, keepdims=True)


def row_to_column(row):
    lanes = row.shape[1]
    return jnp.sum(jnp.where(diagonal((lanes, lanes)), row, 0.0), axis=1, keepdims=True)


def squares_of(rows):
    total = jnp.zeros((rows.shape[0], HD), F32)
    for c in range(0, rows.shape[1], HD):
        wide = rows[:, c : c + HD].astype(F32)
        total = total + wide * wide
    return total


def split_three(values):
    high = values.astype(BF16).astype(F32)
    rest = values - high
    middle = rest.astype(BF16).astype(F32)
    return high, middle, rest - middle


def softmax_parts(query, key, value, usable):
    scores = jnp.where(usable, dot_t(query, key) * HD**-0.5, LOWEST)
    top = jnp.max(scores, axis=1, keepdims=True)
    weights = jnp.where(usable, jnp.exp(scores - top), 0.0)
    return dot(weights.astype(BF16), value), top, jnp.sum(weights, axis=1, keepdims=True)


def prepare_kernel(sizes, *refs):
    n, img, tok, blocks, lot, page_cap, q_rows = sizes
    far, (info, slots, bias, square, near), more, rest = refs[:11], refs[11:16], refs[16:20], refs[20:]
    small, (starts, sems) = rest[:5], rest[5:]
    targets = (*small, near.at[:tok], near.at[tok:], *more)
    copies = [pltpu.make_async_copy(a, b, sems.at[i]) for i, (a, b) in enumerate(zip(far, targets))]
    for c in copies:
        c.start()
    route, pages, count, tail, req = small
    for c in copies[: len(small)]:
        c.wait()
    pos = lax.axis_index("section")
    table = [route[:, e * img : (e + 1) * img] for e in range(n)]
    own = jnp.zeros((1, img), I32)
    for e in range(n):
        own = jnp.where(pos == e, table[e], own)
    marks = own == lax.broadcasted_iota(I32, (n, img), 0)
    ones = jnp.where(marks, 1.0, 0.0).astype(BF16)
    earlier = lax.broadcasted_iota(I32, (img, img), 0) < lax.broadcasted_iota(I32, (img, img), 1)
    prefix = dot(ones, jnp.where(earlier, 1.0, 0.0).astype(BF16))
    local = jnp.sum(jnp.where(marks, prefix, 0.0), axis=0, keepdims=True).astype(I32)
    info[0:1, :img] = jnp.bitwise_xor(own, pos) * lot + local
    lanes = lax.broadcasted_iota(I32, (1, n * lot), 1)
    source, inner = jnp.bitwise_xor(lanes // lot, pos), lanes % lot
    fits = jnp.zeros((1, n * lot), I32)
    offset = jnp.zeros((1, n * lot), I32)
    for e in range(n):
        arriving = jnp.sum((table[e] == pos).astype(I32), axis=1, keepdims=True)
        fits = fits + jnp.where(source == e, arriving, 0)
        offset = offset + jnp.where(source > e, arriving, 0)
    info[1:2, : n * lot] = jnp.where(inner < fits, offset + inner, -1)
    total = jnp.int32(0)
    for r in range(n):
        starts[r] = total
        total = total + count[r]
    token = lax.broadcasted_iota(I32, (1, tok), 1) + pos * tok
    token_slot = jnp.full((1, tok), -1, I32)
    for b in range(n):
        r = req[b]
        first = starts[r] * PAGE
        last = first + (count[r] - 1) * PAGE + tail[r]
        token_slot = jnp.where((token >= first) & (token < last), b, token_slot)
    column = row_to_column(token_slot.astype(F32))
    member = jnp.bitwise_xor(lax.broadcasted_iota(I32, (1, bias.shape[1]), 1) // q_rows, pos)
    bias[...] = jnp.where(column == member.astype(F32), 0.0, LOWEST)
    for g in range(blocks):
        holder = pages[0, pos * blocks + g]
        slot = holder * page_cap
        for e in range(g):
            slot = slot + (pages[0, pos * blocks + e] == holder).astype(I32)
        slots[g] = slot
    for c in copies[len(small) : len(small) + 2]:
        c.wait()
    square[...] = squares_of(near)
    for c in copies[len(small) + 2 :]:
        c.wait()


def project_kernel(n, lot, step, near, text_far, vis_far, w_key, w_value, gain, query, square, info, kv_text, *rest):
    packed, total = rest[:-1], rest[-1]
    tok, half = text_far.shape
    img = vis_far.shape[0]
    kvw = w_key.shape[1]
    me = lax.axis_index("tensor")
    far = (text_far, vis_far)
    sums = [jnp.sum(square[:tok, :] + squares_of(text_far), axis=1, keepdims=True)]
    sums.append(jnp.sum(square[tok:, :] + squares_of(vis_far), axis=1, keepdims=True))
    scales = [lax.rsqrt(x / (2.0 * half) + EPS) for x in sums]
    for nearby, side in ((True, me), (False, 1 - me)):
        rows = (near.at[:tok], near.at[tok:]) if nearby else far
        for c in range(0, half, step):
            columns = pl.ds(pl.multiple_of(side * half + c, step), step)
            scaled = gain[:, columns]
            normed = jnp.concatenate(
                [(x[:, c : c + step].astype(F32) * s * scaled).astype(BF16) for x, s in zip(rows, scales)], axis=0
            )
            for w, at in ((w_key, 0), (w_value, kvw)):
                part = dot(normed, w[columns, :])
                if nearby and c == 0:
                    total[:, at : at + kvw] = part
                else:
                    total[:, at : at + kvw] += part
    kv_text[...] = total[:tok, :].astype(BF16)
    slot = lax.broadcasted_iota(I32, (n * lot, img), 0)
    chosen = jnp.where(slot == info[0:1, :img], 1.0, 0.0).astype(BF16)
    images = dot(chosen, total[tok:, :].astype(BF16)).astype(BF16)
    q_lots = packed[0].shape[0] - lot
    for k in range(n):
        for j in range(query.shape[0] // q_lots):
            packed[k][:q_lots, j * HD : (j + 1) * HD] = query[j * q_lots : (j + 1) * q_lots, :]
        packed[k][q_lots:, :] = images[k * lot : (k + 1) * lot, :]


def put_page(out, page_cap, slot, rows):
    chunk = page_cap * PAGE
    for h in range(rows.shape[1] // HD):
        at = pl.ds(pl.multiple_of((slot % page_cap) * PAGE + h * chunk, PAGE), PAGE)
        out[slot // page_cap, at, :] = rows[:, h * HD : (h + 1) * HD]


def attend_kernel(n, cap, lot, page_cap, kv_heads, slots, info, kv_text, bias, *rest):
    arrived, (out, own, mixed, held) = rest[:n], rest[n:]
    pos = lax.axis_index("section")
    tok = kv_text.shape[0]
    kvw = kv_heads * HD
    q_lots = arrived[0].shape[0] - lot
    reach = min(tok, n * cap)
    hit = lax.broadcasted_iota(I32, (reach, n * lot), 0) == info[1:2, : n * lot]
    hot = jnp.where(hit, 1.0, 0.0)
    covered = jnp.sum(hot, axis=1, keepdims=True) > 0.0
    incoming = jnp.concatenate([x[q_lots:, :] for x in arrived], axis=0)
    placed = dot(hot.astype(BF16), incoming)
    mixed[...] = jnp.where(covered, placed, kv_text[:reach, :].astype(F32)).astype(BF16)
    groups = arrived[0].shape[1] // HD // kv_heads
    rows = groups * q_lots
    pages = page_cap * PAGE * 2 * kv_heads
    out[:, :pages, :] = jnp.zeros((n, pages, HD), BF16)
    for g in range(tok // PAGE):
        at = slice(g * PAGE, (g + 1) * PAGE)
        put_page(out, page_cap, slots[g], mixed[at, :] if (g + 1) * PAGE <= reach else kv_text[at, :])
    for g in range(kv_heads):
        query = jnp.concatenate(
            [x[:q_lots, (g * groups + j) * HD : (g * groups + j + 1) * HD] for x in arrived for j in range(groups)],
            axis=0,
        )
        cols = slice(g * HD, (g + 1) * HD)
        vcols = slice(kvw + g * HD, kvw + (g + 1) * HD)
        key = jnp.concatenate([mixed[:, cols], kv_text[reach:, cols]], axis=0)
        value = jnp.concatenate([mixed[:, vcols], kv_text[reach:, vcols]], axis=0)
        scores = dot_t(key, query) * HD**-0.5 + bias[...]
        top = jnp.max(scores, axis=0, keepdims=True)
        weights = jnp.exp(scores - top)
        held[g : g + 1, :] = top
        held[kv_heads + g : kv_heads + g + 1, :] = jnp.sum(weights, axis=0, keepdims=True)
        numerator = lax.dot_general(
            weights.astype(BF16), value, (((0,), (0,)), ((), ())), preferred_element_type=F32
        )
        own[g * rows : (g + 1) * rows, :] = numerator[:rows, :]
        numerator = numerator.astype(BF16)
        for k in range(n):
            to = jnp.bitwise_xor(pos, k)
            out[to, pages + g * rows : pages + (g + 1) * rows, :] = numerator[k * rows : (k + 1) * rows, :]
    stat_rows = 2 * kv_heads
    share = HD // rows
    own[kv_heads * rows : kv_heads * rows + stat_rows, :] = held[:stat_rows, :HD]
    blank = jnp.zeros((PAGE - 3 * stat_rows, HD), F32)
    for w in range(-(-n // share)):
        stats = held[:stat_rows, w * HD : (w + 1) * HD]
        lines = jnp.concatenate([*split_three(stats), blank], axis=0).astype(BF16)
        for k in range(w * share, min(n, (w + 1) * share)):
            out[jnp.bitwise_xor(pos, k), pages + kv_heads * rows :, :] = lines


def pick_column(row, rows, start):
    shape = (rows, HD)
    chosen = lax.broadcasted_iota(I32, shape, 1) == lax.broadcasted_iota(I32, shape, 0) + start
    return jnp.sum(jnp.where(chosen, row, 0.0), axis=1, keepdims=True)


def combine(pieces, highest):
    numerator, total = 0.0, 0.0
    for rows, top, weight in pieces:
        scale = jnp.exp(top - highest)
        numerator = numerator + rows * scale
        total = total + weight * scale
    return numerator, total


def fresh_kernel(kv_heads, steps, query, key, value, own, mine):
    rows = query.shape[0] // kv_heads
    every = kv_heads * rows
    row = lax.broadcasted_iota(I32, (rows, steps), 0)
    causal = lax.broadcasted_iota(I32, (rows, steps), 1) <= row % steps
    tops, totals = [], []
    for g in range(kv_heads):
        cols = slice(g * HD, (g + 1) * HD)
        at = slice(g * rows, (g + 1) * rows)
        fresh = softmax_parts(query[at, :], key[:, cols], value[:, cols], causal)
        share = (
            own[at, :],
            pick_column(own[every + g : every + g + 1, :], rows, 0),
            pick_column(own[every + kv_heads + g : every + kv_heads + g + 1, :], rows, 0),
        )
        highest = jnp.maximum(fresh[1], share[1])
        numerator, total = combine((fresh, share), highest)
        mine[at, :] = numerator
        tops.append(highest)
        totals.append(total)
    line = column_to_row(jnp.concatenate(tops + totals, axis=0))
    mine[every:, :] = jnp.broadcast_to(line, (STAT, line.shape[1]))


def finish_kernel(kv_heads, steps, page_cap, shares, mine, attended, keys, values):
    n = shares.shape[0]
    pos = lax.axis_index("section")
    every = mine.shape[0] - STAT
    rows = every // kv_heads
    chunk = page_cap * PAGE
    halves = keys.shape[2] // HD
    for k in range(n):
        for i, out in enumerate((keys, values)):
            for h in range(halves):
                part = i * halves + h
                out[k, :, h * HD : (h + 1) * HD] = shares[k, part * chunk : (part + 1) * chunk, :]
    pages = 2 * halves * chunk
    stats = row_to_column(mine[every : every + 1, :])
    lines = []
    for k in range(n):
        three = shares[k, pages + every :, :].astype(F32)
        size = 2 * kv_heads
        lines.append(three[:size] + three[size : 2 * size] + three[2 * size : 3 * size])
    for g in range(kv_heads):
        at = slice(g * rows, (g + 1) * rows)
        pieces = [(mine[at, :], stats[at], stats[every + g * rows : every + (g + 1) * rows])]
        for k in range(n):
            away = pos != k
            start = jnp.bitwise_xor(pos, k) % (HD // rows) * rows
            top = jnp.where(away, pick_column(lines[k][g : g + 1], rows, start), LOWEST)
            weight = jnp.where(away, pick_column(lines[k][kv_heads + g : kv_heads + g + 1], rows, start), 0.0)
            share = shares[k, pages + g * rows : pages + (g + 1) * rows, :].astype(F32)
            pieces.append((share, top, weight))
        highest = pieces[0][1]
        for p in pieces[1:]:
            highest = jnp.maximum(highest, p[1])
        numerator, total = combine(pieces, highest)
        result = (numerator / total).astype(BF16)
        for h in range(rows // steps):
            to = (g * rows // steps + h) * HD
            attended[0, :, to : to + HD] = result[h * steps : (h + 1) * steps, :]


def body(
    text_rows,
    vis_rows,
    img_route,
    norm_gain,
    w_key,
    w_value,
    page_count,
    tail_len,
    page_dest,
    dec_req,
    dec_query,
    dec_key,
    dec_value,
):
    n = lax.axis_size("section")
    tok, half = text_rows.shape
    img = vis_rows.shape[0]
    kvw = w_key.shape[1]
    kv_heads = kvw // HD
    _, steps, q_width = dec_query.shape
    heads = q_width // HD
    q_rows = heads * steps
    blocks = tok // PAGE
    cap = max(2, (2 * img + n - 1) // n)
    page_cap = max(1, (blocks + n - 1) // n)

    def across(array):
        return lax.ppermute(array, "tensor", [(0, 1), (1, 0)])

    def swap(array, k):
        return lax.ppermute(array, "section", [(i, i ^ k) for i in range(n)])

    def exchange(array):
        return lax.all_to_all(array, "section", split_axis=0, concat_axis=0, tiled=True)

    def remote(array):
        return pltpu.with_memory_space_constraint(array, pltpu.HBM)

    def local(array):
        return pltpu.with_memory_space_constraint(array, pltpu.VMEM)

    vis_far = across(vis_rows)
    text_far = across(text_rows)
    query = dec_query.reshape(steps, heads, HD).transpose(1, 0, 2).reshape(q_rows, HD)

    lot = -(-cap // PAGE) * PAGE
    q_lots = q_rows * HD // (2 * kvw)
    width = max(tok, n * lot)
    arguments = (
        img_route.T,
        page_dest.T,
        page_count,
        tail_len,
        dec_req,
        text_rows,
        vis_rows,
        w_key,
        w_value,
        norm_gain.reshape(1, 2 * half),
        query,
    )
    info, slots, bias, square, near, *more = call(
        lambda *refs: prepare_kernel((n, img, tok, blocks, lot, page_cap, q_rows // kv_heads), *refs),
        (
            jax.ShapeDtypeStruct((8, width), I32),
            jax.ShapeDtypeStruct((blocks,), I32),
            jax.ShapeDtypeStruct((tok, n * q_rows // kv_heads), F32),
            jax.ShapeDtypeStruct((tok + img, HD), F32),
            pltpu.VMEM((tok + img, half), BF16),
            *[pltpu.VMEM(a.shape, a.dtype) for a in arguments[7:]],
        ),
        [ANY] * len(arguments),
        (VM, SM) + (VM,) * 7,
        [
            *[(pltpu.VMEM if i == 0 else pltpu.SMEM)(a.shape, a.dtype) for i, a in enumerate(arguments[:5])],
            pltpu.SMEM((n,), I32),
            pltpu.SemaphoreType.DMA((len(arguments),)),
        ],
        flops=1 << 20,
        traffic=2 * 2 * half * 2 * kvw * 2,
    )(*[remote(a) for a in arguments])

    kv_text, *packed = call(
        lambda *refs: project_kernel(n, lot, min(1024, half), *refs),
        (
            jax.ShapeDtypeStruct((tok, 2 * kvw), BF16),
            *[jax.ShapeDtypeStruct((q_lots + lot, 2 * kvw), BF16)] * n,
        ),
        [VM] * 9,
        (VM,) * (1 + n),
        [pltpu.VMEM((tok + img, 2 * kvw), F32)],
        flops=2 * (tok + img) * 2 * half * 2 * kvw,
        traffic=2 * (tok + img) * 2 * half + 8 * half * kvw,
    )(local(near), text_far, vis_far, *[local(a) for a in more], square, info)
    arrived = [packed[0]] + [swap(packed[k], k) for k in range(1, n)]

    block = page_cap * PAGE * 2 * kv_heads + q_rows + PAGE
    sent, own = call(
        lambda *refs: attend_kernel(n, cap, lot, page_cap, kv_heads, *refs),
        (
            jax.ShapeDtypeStruct((n, block, HD), BF16),
            jax.ShapeDtypeStruct((q_rows + STAT, HD), F32),
        ),
        [SM] + [VM] * (3 + n),
        (VM, VM),
        [
            pltpu.VMEM((min(tok, n * cap), 2 * kvw), BF16),
            pltpu.VMEM((STAT, n * q_rows // kv_heads), F32),
        ],
        flops=4 * n * q_rows * tok * HD,
        traffic=n * (q_rows + STAT) * HD * 4,
    )(slots, info, kv_text, bias, *arrived)
    shares = exchange(sent)

    mine = call(
        lambda *refs: fresh_kernel(kv_heads, steps, *refs),
        jax.ShapeDtypeStruct((q_rows + STAT, HD), F32),
        [VM] * 4,
        VM,
        flops=1 << 20,
        traffic=1 << 18,
    )(remote(query), remote(dec_key[0]), remote(dec_value[0]), own)

    slots_here = n * page_cap
    attended, cache_key, cache_value = call(
        lambda *refs: finish_kernel(kv_heads, steps, page_cap, *refs),
        (
            jax.ShapeDtypeStruct(dec_query.shape, BF16),
            jax.ShapeDtypeStruct((n, page_cap * PAGE, kvw), BF16),
            jax.ShapeDtypeStruct((n, page_cap * PAGE, kvw), BF16),
        ),
        [VM, VM],
        (VM, VM, VM),
        traffic=4 * tok * 2 * kvw,
    )(shares, mine)
    return (
        attended,
        cache_key.reshape(slots_here, PAGE, kvw),
        cache_value.reshape(slots_here, PAGE, kvw),
    )


def solution(mesh):
    return jax.shard_map(
        body,
        mesh=mesh,
        in_specs=(
            P(("groups", "section"), "tensor"),
            P(("groups", "section"), "tensor"),
            P("groups", None),
            P(),
            P(None, "tensor"),
            P(None, "tensor"),
            P("groups"),
            P("groups"),
            P("groups", None),
            P("groups"),
            P(("groups", "section"), None, "tensor"),
            P(("groups", "section"), None, "tensor"),
            P(("groups", "section"), None, "tensor"),
        ),
        out_specs=(
            P(("groups", "section"), None, "tensor"),
            P(("groups", "section"), None, "tensor"),
            P(("groups", "section"), None, "tensor"),
        ),
        check_vma=False,
    )
```

```python
import jax
import jax.numpy as jnp
from jax import lax
from jax.experimental import pallas as pl
from jax.experimental.pallas import tpu as pltpu
from jax.sharding import PartitionSpec as P

HD = 128
PAGE = 16
LOWEST = -1e30
EPS = 1e-06
STAT = 8
F32 = jnp.float32
BF16 = jnp.bfloat16
I32 = jnp.int32

VM = pl.BlockSpec(memory_space=pltpu.VMEM)
SM = pl.BlockSpec(memory_space=pltpu.SMEM)
ANY = pl.BlockSpec(memory_space=pl.ANY)
MIB = 1 << 20


def call(kernel, out_shape, in_specs, out_specs, scratch=(), limit=16, flops=0, traffic=0):
    return pl.pallas_call(
        kernel,
        out_shape=out_shape,
        in_specs=in_specs,
        out_specs=out_specs,
        scratch_shapes=list(scratch),
        compiler_params=pltpu.CompilerParams(vmem_limit_bytes=limit * MIB),
        cost_estimate=pl.CostEstimate(flops=flops, bytes_accessed=traffic, transcendentals=0),
    )


def dot(a, b):
    return jnp.dot(a, b, preferred_element_type=F32)


def dot_t(a, b):
    return lax.dot_general(a, b, (((1,), (1,)), ((), ())), preferred_element_type=F32)


def diagonal(shape):
    return lax.broadcasted_iota(I32, shape, 0) == lax.broadcasted_iota(I32, shape, 1)


def column_to_row(column):
    rows = column.shape[0]
    return jnp.sum(jnp.where(diagonal((rows, rows)), column, 0.0), axis=0, keepdims=True)


def row_to_column(row):
    lanes = row.shape[1]
    return jnp.sum(jnp.where(diagonal((lanes, lanes)), row, 0.0), axis=1, keepdims=True)


def squares_of(rows):
    total = jnp.zeros((rows.shape[0], HD), F32)
    for c in range(0, rows.shape[1], HD):
        wide = rows[:, c : c + HD].astype(F32)
        total = total + wide * wide
    return total


def split_three(values):
    high = values.astype(BF16).astype(F32)
    rest = values - high
    middle = rest.astype(BF16).astype(F32)
    return high, middle, rest - middle


def softmax_parts(query, key, value, usable):
    scores = jnp.where(usable, dot_t(query, key) * HD**-0.5, LOWEST)
    top = jnp.max(scores, axis=1, keepdims=True)
    weights = jnp.where(usable, jnp.exp(scores - top), 0.0)
    return dot(weights.astype(BF16), value), top, jnp.sum(weights, axis=1, keepdims=True)


def prepare_kernel(sizes, *refs):
    n, img, tok, blocks, lot, page_cap = sizes
    far, (info, slots), near, small, (starts, sems) = refs[:10], refs[10:12], refs[12:17], refs[17:22], refs[22:]
    held = near[0].shape[0]
    half = near[2].shape[1]
    me = lax.axis_index("tensor")
    pairs = list(zip(far[:5], small)) + list(zip(far[7:], near[2:]))
    for w, kept in zip(far[5:7], near[:2]):
        for start, at, size in ((me * half, 0, half), ((1 - me) * half, half, held - half)):
            source = pl.ds(pl.multiple_of(start, held - half), size)
            pairs.append((w.at[source], kept.at[at : at + size]))
    copies = [pltpu.make_async_copy(a, b, sems.at[i]) for i, (a, b) in enumerate(pairs)]
    for c in copies:
        c.start()
    route, pages, count, tail, req = small
    for c in copies[: len(small)]:
        c.wait()
    pos = lax.axis_index("section")
    table = [route[:, e * img : (e + 1) * img] for e in range(n)]
    own = jnp.zeros((1, img), I32)
    for e in range(n):
        own = jnp.where(pos == e, table[e], own)
    marks = own == lax.broadcasted_iota(I32, (n, img), 0)
    ones = jnp.where(marks, 1.0, 0.0).astype(BF16)
    earlier = lax.broadcasted_iota(I32, (img, img), 0) < lax.broadcasted_iota(I32, (img, img), 1)
    prefix = dot(ones, jnp.where(earlier, 1.0, 0.0).astype(BF16))
    local = jnp.sum(jnp.where(marks, prefix, 0.0), axis=0, keepdims=True).astype(I32)
    info[0:1, :img] = own * lot + local
    lanes = lax.broadcasted_iota(I32, (1, n * lot), 1)
    source, inner = lanes // lot, lanes % lot
    fits = jnp.zeros((1, n * lot), I32)
    offset = jnp.zeros((1, n * lot), I32)
    for e in range(n):
        arriving = jnp.sum((table[e] == pos).astype(I32), axis=1, keepdims=True)
        fits = fits + jnp.where(source == e, arriving, 0)
        offset = offset + jnp.where(source > e, arriving, 0)
    info[2:3, : n * lot] = jnp.where(inner < fits, offset + inner, -1)
    total = jnp.int32(0)
    for r in range(n):
        starts[r] = total
        total = total + count[r]
    token = lax.broadcasted_iota(I32, (1, tok), 1) + pos * tok
    token_slot = jnp.full((1, tok), -1, I32)
    for b in range(n):
        r = req[b]
        first = starts[r] * PAGE
        last = first + (count[r] - 1) * PAGE + tail[r]
        token_slot = jnp.where((token >= first) & (token < last), b, token_slot)
    info[1:2, :tok] = token_slot
    for g in range(blocks):
        holder = pages[0, pos * blocks + g]
        slot = holder * page_cap
        for e in range(g):
            slot = slot + (pages[0, pos * blocks + e] == holder).astype(I32)
        slots[g] = slot
    for c in copies[len(small) :]:
        c.wait()


def scale_of(near, far):
    sums = jnp.sum(squares_of(near) + squares_of(far), axis=1, keepdims=True)
    return lax.rsqrt(sums / (2.0 * near.shape[1]) + EPS)


def normed_rows(rows, c, step, scale, gain):
    return (rows[:, c : c + step].astype(F32) * scale * gain).astype(BF16)


def add_part(total, at, normed, w, begin):
    part = dot(normed, w)
    columns = slice(at, at + part.shape[1])
    if begin:
        total[:, columns] = part
    else:
        total[:, columns] += part


def vis_kernel(n, lot, step, *refs):
    near, far, gain, query, key_held, value_held, w_key, w_value, info, out, key_rest, value_rest, total, sems = refs
    img, half = near.shape
    kvw = w_key.shape[1]
    me = lax.axis_index("tensor")
    held, size = key_held.shape[0], key_rest.shape[0]
    last = pl.ds(pl.multiple_of((1 - me) * half + held - half, size), size)
    pairs = ((w_key, key_rest), (w_value, value_rest))
    copies = [pltpu.make_async_copy(w.at[last], kept, sems.at[i]) for i, (w, kept) in enumerate(pairs)]
    for c in copies:
        c.start()
    scale = scale_of(near, far)
    for at in range(0, 2 * half, step):
        if at == held:
            for c in copies:
                c.wait()
        rows, side = (near, me) if at < half else (far, 1 - me)
        weights, w_at = ((key_held, value_held), at) if at < held else ((key_rest, value_rest), at - held)
        c = at % half
        columns = pl.ds(pl.multiple_of(side * half + c, step), step)
        normed = normed_rows(rows, c, step, scale, gain[:, columns])
        for w, col in zip(weights, (0, kvw)):
            add_part(total, col, normed, w[w_at : w_at + step, :], at == 0)
    slot = lax.broadcasted_iota(I32, (n * lot, img), 0)
    chosen = jnp.where(slot == info[0:1, :img], 1.0, 0.0).astype(BF16)
    packed = dot(chosen, total[...].astype(BF16)).astype(BF16)
    q_lots = out.shape[1] - lot
    for k in range(n):
        for j in range(query.shape[0] // q_lots):
            out[k, :q_lots, j * HD : (j + 1) * HD] = query[j * q_lots : (j + 1) * q_lots, :]
        out[k, q_lots:, :] = packed[k * lot : (k + 1) * lot, :]


def put_page(out, page_cap, slot, rows):
    chunk = page_cap * PAGE
    for h in range(rows.shape[1] // HD):
        at = pl.ds(pl.multiple_of((slot % page_cap) * PAGE + h * chunk, PAGE), PAGE)
        out[slot // page_cap, at, :] = rows[:, h * HD : (h + 1) * HD]


def text_kernel(load, step, page_cap, q_rows, *refs):
    near_far, far, gain, w_key_far, w_value_far, info, slots, out, bias, base, near, w_key, w_value, total, sems = refs
    half = near.shape[1]
    kvw = w_key.shape[1]
    me = lax.axis_index("tensor")
    first = pltpu.make_async_copy(near_far, near, sems.at[0])
    first.start()
    loads = []
    for side in (me, 1 - me):
        for c in range(0, half, load):
            at = len(loads) * load
            columns = pl.ds(pl.multiple_of(side * half + c, load), load)
            pair = [
                pltpu.make_async_copy(w.at[columns], held.at[at : at + load], sems.at[2 * len(loads) + i])
                for i, (w, held) in enumerate(((w_key_far, w_key), (w_value_far, w_value)), 1)
            ]
            for copy in pair:
                copy.start()
            loads.append(pair)
    sums = squares_of(far)
    first.wait()
    sums = jnp.sum(squares_of(near) + sums, axis=1, keepdims=True)
    scale = lax.rsqrt(sums / (2.0 * half) + EPS)
    for i, pair in enumerate(loads):
        for copy in pair:
            copy.wait()
        for at in range(i * load, (i + 1) * load, step):
            rows, side = (near, me) if at < half else (far, 1 - me)
            c = at % half
            columns = pl.ds(pl.multiple_of(side * half + c, step), step)
            normed = normed_rows(rows, c, step, scale, gain[:, columns])
            for w, col in ((w_key, 0), (w_value, kvw)):
                add_part(total, col, normed, w[at : at + step, :], at == 0)
    out[...] = total[...].astype(BF16)
    base[...] = jnp.zeros(base.shape, BF16)
    tok = near.shape[0]
    for g in range(tok // PAGE):
        put_page(base, page_cap, slots[g], out[g * PAGE : (g + 1) * PAGE, :])
    token_slot = row_to_column(info[1:2, :tok].astype(F32))
    lanes = lax.broadcasted_iota(I32, bias.shape, 1) // q_rows
    bias[...] = jnp.where(token_slot == lanes.astype(F32), 0.0, LOWEST)


def attend_kernel(n, cap, lot, page_cap, kv_heads, slots, info, kv_text, arrived, bias, base, out, own, mixed, held, rows_held):
    pos = lax.axis_index("section")
    tok = kv_text.shape[0]
    kvw = kv_heads * HD
    q_lots = arrived.shape[1] - lot
    reach = min(tok, n * cap)
    hit = lax.broadcasted_iota(I32, (reach, n * lot), 0) == info[2:3, : n * lot]
    hot = jnp.where(hit, 1.0, 0.0)
    covered = jnp.sum(hot, axis=1, keepdims=True) > 0.0
    incoming = jnp.concatenate([arrived[k, q_lots:, :] for k in range(n)], axis=0)
    placed = dot(hot.astype(BF16), incoming)
    mixed[...] = jnp.where(covered, placed, kv_text[:reach, :].astype(F32)).astype(BF16)
    groups = arrived.shape[2] // HD // kv_heads
    rows = groups * q_lots
    pages = base.shape[1]
    out[:, :pages, :] = base[...]
    for g in range(reach // PAGE):
        put_page(out, page_cap, slots[g], mixed[g * PAGE : (g + 1) * PAGE, :])
    for g in range(kv_heads):
        query = jnp.concatenate(
            [
                arrived[k, :q_lots, (g * groups + j) * HD : (g * groups + j + 1) * HD]
                for k in range(n)
                for j in range(groups)
            ],
            axis=0,
        )
        cols = slice(g * HD, (g + 1) * HD)
        vcols = slice(kvw + g * HD, kvw + (g + 1) * HD)
        key = jnp.concatenate([mixed[:, cols], kv_text[reach:, cols]], axis=0)
        value = jnp.concatenate([mixed[:, vcols], kv_text[reach:, vcols]], axis=0)
        scores = dot_t(key, query) * HD**-0.5 + bias[...]
        top = jnp.max(scores, axis=0, keepdims=True)
        weights = jnp.exp(scores - top)
        rows_held[g : g + 1, :] = top
        rows_held[kv_heads + g : kv_heads + g + 1, :] = jnp.sum(weights, axis=0, keepdims=True)
        numerator = lax.dot_general(
            weights.astype(BF16), value, (((0,), (0,)), ((), ())), preferred_element_type=F32
        )
        held[g * n * rows : (g + 1) * n * rows, :] = numerator
        own[g * rows : (g + 1) * rows, :] = held[pl.ds(pl.multiple_of((g * n + pos) * rows, rows), rows), :]
        numerator = numerator.astype(BF16)
        for k in range(n):
            out[k, pages + g * rows : pages + (g + 1) * rows, :] = numerator[k * rows : (k + 1) * rows, :]
    stat_rows = 2 * kv_heads
    share = HD // rows
    window = pl.ds(pl.multiple_of(pos // share * HD, HD), HD)
    own[kv_heads * rows : kv_heads * rows + stat_rows, :] = rows_held[:stat_rows, window]
    blank = jnp.zeros((PAGE - 3 * stat_rows, HD), F32)
    for w in range(-(-n // share)):
        stats = rows_held[:stat_rows, w * HD : (w + 1) * HD]
        lines = jnp.concatenate([*split_three(stats), blank], axis=0).astype(BF16)
        for k in range(w * share, min(n, (w + 1) * share)):
            out[k, pages + kv_heads * rows :, :] = lines


def pick_column(row, rows, start):
    shape = (rows, HD)
    chosen = lax.broadcasted_iota(I32, shape, 1) == lax.broadcasted_iota(I32, shape, 0) + start
    return jnp.sum(jnp.where(chosen, row, 0.0), axis=1, keepdims=True)


def combine(pieces, highest):
    numerator, total = 0.0, 0.0
    for rows, top, weight in pieces:
        scale = jnp.exp(top - highest)
        numerator = numerator + rows * scale
        total = total + weight * scale
    return numerator, total


def fresh_kernel(kv_heads, steps, query, key, value, own, mine):
    rows = query.shape[0] // kv_heads
    every = kv_heads * rows
    start = lax.axis_index("section") % (HD // rows) * rows
    row = lax.broadcasted_iota(I32, (rows, steps), 0)
    causal = lax.broadcasted_iota(I32, (rows, steps), 1) <= row % steps
    tops, totals = [], []
    for g in range(kv_heads):
        cols = slice(g * HD, (g + 1) * HD)
        at = slice(g * rows, (g + 1) * rows)
        fresh = softmax_parts(query[at, :], key[:, cols], value[:, cols], causal)
        share = (
            own[at, :],
            pick_column(own[every + g : every + g + 1, :], rows, start),
            pick_column(own[every + kv_heads + g : every + kv_heads + g + 1, :], rows, start),
        )
        highest = jnp.maximum(fresh[1], share[1])
        numerator, total = combine((fresh, share), highest)
        mine[at, :] = numerator
        tops.append(highest)
        totals.append(total)
    line = column_to_row(jnp.concatenate(tops + totals, axis=0))
    mine[every:, :] = jnp.broadcast_to(line, (STAT, line.shape[1]))


def finish_kernel(kv_heads, steps, page_cap, shares, mine, attended, keys, values):
    n = shares.shape[0]
    pos = lax.axis_index("section")
    every = mine.shape[0] - STAT
    rows = every // kv_heads
    start = pos % (HD // rows) * rows
    chunk = page_cap * PAGE
    halves = keys.shape[2] // HD
    for k in range(n):
        for i, out in enumerate((keys, values)):
            for h in range(halves):
                part = i * halves + h
                out[k, :, h * HD : (h + 1) * HD] = shares[k, part * chunk : (part + 1) * chunk, :]
    pages = 2 * halves * chunk
    stats = row_to_column(mine[every : every + 1, :])
    lines = []
    for k in range(n):
        three = shares[k, pages + every :, :].astype(F32)
        size = 2 * kv_heads
        lines.append(three[:size] + three[size : 2 * size] + three[2 * size : 3 * size])
    for g in range(kv_heads):
        at = slice(g * rows, (g + 1) * rows)
        pieces = [(mine[at, :], stats[at], stats[every + g * rows : every + (g + 1) * rows])]
        for k in range(n):
            away = pos != k
            top = jnp.where(away, pick_column(lines[k][g : g + 1], rows, start), LOWEST)
            weight = jnp.where(away, pick_column(lines[k][kv_heads + g : kv_heads + g + 1], rows, start), 0.0)
            share = shares[k, pages + g * rows : pages + (g + 1) * rows, :].astype(F32)
            pieces.append((share, top, weight))
        highest = pieces[0][1]
        for p in pieces[1:]:
            highest = jnp.maximum(highest, p[1])
        numerator, total = combine(pieces, highest)
        result = (numerator / total).astype(BF16)
        for h in range(rows // steps):
            to = (g * rows // steps + h) * HD
            attended[0, :, to : to + HD] = result[h * steps : (h + 1) * steps, :]


def body(
    text_rows,
    vis_rows,
    img_route,
    norm_gain,
    w_key,
    w_value,
    page_count,
    tail_len,
    page_dest,
    dec_req,
    dec_query,
    dec_key,
    dec_value,
):
    n = lax.axis_size("section")
    tok, half = text_rows.shape
    img = vis_rows.shape[0]
    kvw = w_key.shape[1]
    kv_heads = kvw // HD
    _, steps, q_width = dec_query.shape
    heads = q_width // HD
    q_rows = heads * steps
    blocks = tok // PAGE
    cap = max(2, (2 * img + n - 1) // n)
    page_cap = max(1, (blocks + n - 1) // n)

    def across(array):
        return lax.ppermute(array, "tensor", [(0, 1), (1, 0)])

    def exchange(array):
        return lax.all_to_all(array, "section", split_axis=0, concat_axis=0, tiled=True)

    def remote(array):
        return pltpu.with_memory_space_constraint(array, pltpu.HBM)

    def local(array):
        return pltpu.with_memory_space_constraint(array, pltpu.VMEM)

    vis_far = across(vis_rows)
    text_far = across(text_rows)
    query = dec_query.reshape(steps, heads, HD).transpose(1, 0, 2).reshape(q_rows, HD)

    lot = -(-cap // PAGE) * PAGE
    q_lots = q_rows * HD // (2 * kvw)
    width = max(tok, n * lot)
    gain = norm_gain.reshape(1, 2 * half)
    held = half + half // 2
    arguments = (
        img_route.T,
        page_dest.T,
        page_count,
        tail_len,
        dec_req,
        w_key,
        w_value,
        vis_rows,
        gain,
        query,
    )
    info, slots, key_held, value_held, vis_near, gain_near, query_near = call(
        lambda *refs: prepare_kernel((n, img, tok, blocks, lot, page_cap), *refs),
        (
            jax.ShapeDtypeStruct((8, width), I32),
            jax.ShapeDtypeStruct((blocks,), I32),
            pltpu.VMEM((held, kvw), BF16),
            pltpu.VMEM((held, kvw), BF16),
            *[pltpu.VMEM(a.shape, a.dtype) for a in arguments[7:]],
        ),
        [ANY] * len(arguments),
        (VM, SM) + (VM,) * 5,
        [
            *[(pltpu.VMEM if i == 0 else pltpu.SMEM)(a.shape, a.dtype) for i, a in enumerate(arguments[:5])],
            pltpu.SMEM((n,), I32),
            pltpu.SemaphoreType.DMA((len(arguments) + 2,)),
        ],
        flops=1 << 20,
        traffic=2 * 2 * half * 2 * kvw * 2,
    )(*[remote(a) for a in arguments])

    step = min(1024, half)
    load = min(2048, half)

    packed = call(
        lambda *refs: vis_kernel(n, lot, step, *refs),
        pltpu.VMEM((n, q_lots + lot, 2 * kvw), BF16),
        [VM] * 6 + [ANY] * 2 + [VM],
        VM,
        [
            pltpu.VMEM((2 * half - held, kvw), BF16),
            pltpu.VMEM((2 * half - held, kvw), BF16),
            pltpu.VMEM((img, 2 * kvw), F32),
            pltpu.SemaphoreType.DMA((2,)),
        ],
        flops=64 * img * 2 * half * 2 * kvw,
        traffic=2 * img * 2 * half + 8 * half * kvw,
    )(
        local(vis_near),
        vis_far,
        local(gain_near),
        local(query_near),
        local(key_held),
        local(value_held),
        remote(w_key),
        remote(w_value),
        info,
    )
    arrived = exchange(packed)

    block = page_cap * PAGE * 2 * kv_heads + q_rows + PAGE
    kv_text, bias, base = call(
        lambda *refs: text_kernel(load, step, page_cap, q_rows // kv_heads, *refs),
        (
            jax.ShapeDtypeStruct((tok, 2 * kvw), BF16),
            jax.ShapeDtypeStruct((tok, n * q_rows // kv_heads), F32),
            jax.ShapeDtypeStruct((n, block - q_rows - PAGE, HD), BF16),
        ),
        [ANY, VM, VM, ANY, ANY, VM, SM],
        (VM, VM, VM),
        [
            pltpu.VMEM((tok, half), BF16),
            pltpu.VMEM(w_key.shape, BF16),
            pltpu.VMEM(w_value.shape, BF16),
            pltpu.VMEM((tok, 2 * kvw), F32),
            pltpu.SemaphoreType.DMA((1 + 4 * half // load,)),
        ],
        limit=24,
        flops=2 * tok * 2 * half * 2 * kvw,
        traffic=2 * tok * 2 * half + 8 * half * kvw,
    )(remote(text_rows), text_far, remote(gain), remote(w_key), remote(w_value), info, slots)

    sent, own = call(
        lambda *refs: attend_kernel(n, cap, lot, page_cap, kv_heads, *refs),
        (
            pltpu.VMEM((n, block, HD), BF16),
            jax.ShapeDtypeStruct((q_rows + STAT, HD), F32),
        ),
        [SM] + [VM] * 5,
        (VM, VM),
        [
            pltpu.VMEM((min(tok, n * cap), 2 * kvw), BF16),
            pltpu.VMEM((n * q_rows, HD), F32),
            pltpu.VMEM((STAT, n * q_rows // kv_heads), F32),
        ],
        flops=4 * n * q_rows * tok * HD,
        traffic=n * (q_rows + STAT) * HD * 4,
    )(slots, info, kv_text, arrived, bias, base)
    shares = exchange(sent)

    mine = call(
        lambda *refs: fresh_kernel(kv_heads, steps, *refs),
        jax.ShapeDtypeStruct((q_rows + STAT, HD), F32),
        [VM] * 4,
        VM,
        flops=1 << 20,
        traffic=1 << 18,
    )(remote(query), remote(dec_key[0]), remote(dec_value[0]), own)

    slots_here = n * page_cap
    attended, cache_key, cache_value = call(
        lambda *refs: finish_kernel(kv_heads, steps, page_cap, *refs),
        (
            jax.ShapeDtypeStruct(dec_query.shape, BF16),
            jax.ShapeDtypeStruct((n, page_cap * PAGE, kvw), BF16),
            jax.ShapeDtypeStruct((n, page_cap * PAGE, kvw), BF16),
        ),
        [VM, VM],
        (VM, VM, VM),
        traffic=4 * tok * 2 * kvw,
    )(shares, mine)
    return (
        attended,
        cache_key.reshape(slots_here, PAGE, kvw),
        cache_value.reshape(slots_here, PAGE, kvw),
    )


def solution(mesh):
    return jax.shard_map(
        body,
        mesh=mesh,
        in_specs=(
            P(("groups", "section"), "tensor"),
            P(("groups", "section"), "tensor"),
            P("groups", None),
            P(),
            P(None, "tensor"),
            P(None, "tensor"),
            P("groups"),
            P("groups"),
            P("groups", None),
            P("groups"),
            P(("groups", "section"), None, "tensor"),
            P(("groups", "section"), None, "tensor"),
            P(("groups", "section"), None, "tensor"),
        ),
        out_specs=(
            P(("groups", "section"), None, "tensor"),
            P(("groups", "section"), None, "tensor"),
            P(("groups", "section"), None, "tensor"),
        ),
        check_vma=False,
    )
```

```python
import jax
import jax.numpy as jnp
from jax import lax
from jax.experimental import pallas as pl
from jax.experimental.pallas import tpu as pltpu
from jax.sharding import PartitionSpec as P

HD = 128
PAGE = 16
LOWEST = -1e30
EPS = 1e-06
STAT = 8
F32 = jnp.float32
BF16 = jnp.bfloat16
I32 = jnp.int32

VM = pl.BlockSpec(memory_space=pltpu.VMEM)
SM = pl.BlockSpec(memory_space=pltpu.SMEM)
ANY = pl.BlockSpec(memory_space=pl.ANY)
MIB = 1 << 20


def call(kernel, out_shape, in_specs, out_specs, scratch=(), limit=16, flops=0, traffic=0):
    return pl.pallas_call(
        kernel,
        out_shape=out_shape,
        in_specs=in_specs,
        out_specs=out_specs,
        scratch_shapes=list(scratch),
        compiler_params=pltpu.CompilerParams(vmem_limit_bytes=limit * MIB),
        cost_estimate=pl.CostEstimate(flops=flops, bytes_accessed=traffic, transcendentals=0),
    )


def rank_of(section, n):
    return jnp.where(section < n // 2, n - 2 - 2 * section, 2 * section - n + 1)


def section_of(rank, n):
    return n // 2 - 1 - rank // 2 + rank % 2 * (rank // 2 * 2 + 1)


def dot(a, b):
    return jnp.dot(a, b, preferred_element_type=F32)


def dot_t(a, b):
    return lax.dot_general(a, b, (((1,), (1,)), ((), ())), preferred_element_type=F32)


def diagonal(shape):
    return lax.broadcasted_iota(I32, shape, 0) == lax.broadcasted_iota(I32, shape, 1)


def column_to_row(column):
    rows = column.shape[0]
    return jnp.sum(jnp.where(diagonal((rows, rows)), column, 0.0), axis=0, keepdims=True)


def row_to_column(row):
    lanes = row.shape[1]
    return jnp.sum(jnp.where(diagonal((lanes, lanes)), row, 0.0), axis=1, keepdims=True)


def squares_of(rows):
    total = jnp.zeros((rows.shape[0], HD), F32)
    for c in range(0, rows.shape[1], HD):
        wide = rows[:, c : c + HD].astype(F32)
        total = total + wide * wide
    return total


def split_three(values):
    high = values.astype(BF16).astype(F32)
    rest = values - high
    middle = rest.astype(BF16).astype(F32)
    return high, middle, rest - middle


def softmax_parts(query, key, value, usable):
    scores = jnp.where(usable, dot_t(query, key) * HD**-0.5, LOWEST)
    top = jnp.max(scores, axis=1, keepdims=True)
    weights = jnp.where(usable, jnp.exp(scores - top), 0.0)
    return dot(weights.astype(BF16), value), top, jnp.sum(weights, axis=1, keepdims=True)


def prepare_kernel(sizes, *refs):
    n, img, tok, blocks, lot, page_cap = sizes
    far, (info, slots), near, small, (starts, sems) = refs[:10], refs[10:12], refs[12:17], refs[17:22], refs[22:]
    held = near[0].shape[0]
    half = near[2].shape[1]
    me = lax.axis_index("tensor")
    pairs = list(zip(far[:5], small)) + list(zip(far[7:], near[2:]))
    for w, kept in zip(far[5:7], near[:2]):
        for start, at, size in ((me * half, 0, half), ((1 - me) * half, half, held - half)):
            source = pl.ds(pl.multiple_of(start, held - half), size)
            pairs.append((w.at[source], kept.at[at : at + size]))
    copies = [pltpu.make_async_copy(a, b, sems.at[i]) for i, (a, b) in enumerate(pairs)]
    for c in copies:
        c.start()
    route, pages, count, tail, req = small
    for c in copies[: len(small)]:
        c.wait()
    pos = lax.axis_index("section")
    table = [route[:, e * img : (e + 1) * img] for e in range(n)]
    own = jnp.zeros((1, img), I32)
    for e in range(n):
        own = jnp.where(pos == e, table[e], own)
    marks = own == lax.broadcasted_iota(I32, (n, img), 0)
    ones = jnp.where(marks, 1.0, 0.0).astype(BF16)
    earlier = lax.broadcasted_iota(I32, (img, img), 0) < lax.broadcasted_iota(I32, (img, img), 1)
    prefix = dot(ones, jnp.where(earlier, 1.0, 0.0).astype(BF16))
    local = jnp.sum(jnp.where(marks, prefix, 0.0), axis=0, keepdims=True).astype(I32)
    info[0:1, :img] = rank_of(own, n) * lot + local
    lanes = lax.broadcasted_iota(I32, (1, n * lot), 1)
    source, inner = section_of(lanes // lot, n), lanes % lot
    fits = jnp.zeros((1, n * lot), I32)
    offset = jnp.zeros((1, n * lot), I32)
    for e in range(n):
        arriving = jnp.sum((table[e] == pos).astype(I32), axis=1, keepdims=True)
        fits = fits + jnp.where(source == e, arriving, 0)
        offset = offset + jnp.where(source > e, arriving, 0)
    info[2:3, : n * lot] = jnp.where(inner < fits, offset + inner, -1)
    total = jnp.int32(0)
    for r in range(n):
        starts[r] = total
        total = total + count[r]
    token = lax.broadcasted_iota(I32, (1, tok), 1) + pos * tok
    token_slot = jnp.full((1, tok), -1, I32)
    for b in range(n):
        r = req[b]
        first = starts[r] * PAGE
        last = first + (count[r] - 1) * PAGE + tail[r]
        token_slot = jnp.where((token >= first) & (token < last), b, token_slot)
    info[1:2, :tok] = token_slot
    for g in range(blocks):
        holder = pages[0, pos * blocks + g]
        slot = rank_of(holder, n) * page_cap
        for e in range(g):
            slot = slot + (pages[0, pos * blocks + e] == holder).astype(I32)
        slots[g] = slot
    for c in copies[len(small) :]:
        c.wait()


def scale_of(near, far):
    sums = jnp.sum(squares_of(near) + squares_of(far), axis=1, keepdims=True)
    return lax.rsqrt(sums / (2.0 * near.shape[1]) + EPS)


def normed_rows(rows, c, step, scale, gain):
    return (rows[:, c : c + step].astype(F32) * scale * gain).astype(BF16)


def add_part(total, at, normed, w, begin):
    part = dot(normed, w)
    columns = slice(at, at + part.shape[1])
    if begin:
        total[:, columns] = part
    else:
        total[:, columns] += part


def vis_kernel(n, lot, step, *refs):
    near, far, gain, query, key_held, value_held, w_key, w_value, info, out, key_rest, value_rest, total, sems = refs
    img, half = near.shape
    kvw = w_key.shape[1]
    me = lax.axis_index("tensor")
    held, size = key_held.shape[0], key_rest.shape[0]
    last = pl.ds(pl.multiple_of((1 - me) * half + held - half, size), size)
    pairs = ((w_key, key_rest), (w_value, value_rest))
    copies = [pltpu.make_async_copy(w.at[last], kept, sems.at[i]) for i, (w, kept) in enumerate(pairs)]
    for c in copies:
        c.start()
    scale = scale_of(near, far)
    for at in range(0, 2 * half, step):
        if at == held:
            for c in copies:
                c.wait()
        rows, side = (near, me) if at < half else (far, 1 - me)
        weights, w_at = ((key_held, value_held), at) if at < held else ((key_rest, value_rest), at - held)
        c = at % half
        columns = pl.ds(pl.multiple_of(side * half + c, step), step)
        normed = normed_rows(rows, c, step, scale, gain[:, columns])
        for w, col in zip(weights, (0, kvw)):
            add_part(total, col, normed, w[w_at : w_at + step, :], at == 0)
    slot = lax.broadcasted_iota(I32, (n * lot, img), 0)
    chosen = jnp.where(slot == info[0:1, :img], 1.0, 0.0).astype(BF16)
    packed = dot(chosen, total[...].astype(BF16)).astype(BF16)
    q_lots = out.shape[1] - lot
    for k in range(n):
        for j in range(query.shape[0] // q_lots):
            out[k, :q_lots, j * HD : (j + 1) * HD] = query[j * q_lots : (j + 1) * q_lots, :]
        out[k, q_lots:, :] = packed[k * lot : (k + 1) * lot, :]


def put_page(out, page_cap, slot, rows):
    chunk = page_cap * PAGE
    for h in range(rows.shape[1] // HD):
        at = pl.ds(pl.multiple_of((slot % page_cap) * PAGE + h * chunk, PAGE), PAGE)
        out[slot // page_cap, at, :] = rows[:, h * HD : (h + 1) * HD]


def text_kernel(load, step, page_cap, q_rows, *refs):
    near_far, far, gain, w_key_far, w_value_far, info, slots, out, bias, base, near, w_key, w_value, total, sems = refs
    half = near.shape[1]
    kvw = w_key.shape[1]
    me = lax.axis_index("tensor")
    first = pltpu.make_async_copy(near_far, near, sems.at[0])
    first.start()
    loads = []
    for side in (me, 1 - me):
        for c in range(0, half, load):
            at = len(loads) * load
            columns = pl.ds(pl.multiple_of(side * half + c, load), load)
            pair = [
                pltpu.make_async_copy(w.at[columns], held.at[at : at + load], sems.at[2 * len(loads) + i])
                for i, (w, held) in enumerate(((w_key_far, w_key), (w_value_far, w_value)), 1)
            ]
            for copy in pair:
                copy.start()
            loads.append(pair)
    sums = squares_of(far)
    first.wait()
    sums = jnp.sum(squares_of(near) + sums, axis=1, keepdims=True)
    scale = lax.rsqrt(sums / (2.0 * half) + EPS)
    for i, pair in enumerate(loads):
        for copy in pair:
            copy.wait()
        for at in range(i * load, (i + 1) * load, step):
            rows, side = (near, me) if at < half else (far, 1 - me)
            c = at % half
            columns = pl.ds(pl.multiple_of(side * half + c, step), step)
            normed = normed_rows(rows, c, step, scale, gain[:, columns])
            for w, col in ((w_key, 0), (w_value, kvw)):
                add_part(total, col, normed, w[at : at + step, :], at == 0)
    out[...] = total[...].astype(BF16)
    base[...] = jnp.zeros(base.shape, BF16)
    tok = near.shape[0]
    for g in range(tok // PAGE):
        put_page(base, page_cap, slots[g], out[g * PAGE : (g + 1) * PAGE, :])
    token_slot = row_to_column(info[1:2, :tok].astype(F32))
    lanes = section_of(lax.broadcasted_iota(I32, bias.shape, 1) // q_rows, bias.shape[1] // q_rows)
    bias[...] = jnp.where(token_slot == lanes.astype(F32), 0.0, LOWEST)


def attend_kernel(n, cap, lot, page_cap, kv_heads, slots, info, kv_text, arrived, bias, base, out, own, mixed, held, rows_held):
    rank = rank_of(lax.axis_index("section"), n)
    tok = kv_text.shape[0]
    kvw = kv_heads * HD
    q_lots = arrived.shape[1] - lot
    reach = min(tok, n * cap)
    hit = lax.broadcasted_iota(I32, (reach, n * lot), 0) == info[2:3, : n * lot]
    hot = jnp.where(hit, 1.0, 0.0)
    covered = jnp.sum(hot, axis=1, keepdims=True) > 0.0
    incoming = jnp.concatenate([arrived[k, q_lots:, :] for k in range(n)], axis=0)
    placed = dot(hot.astype(BF16), incoming)
    mixed[...] = jnp.where(covered, placed, kv_text[:reach, :].astype(F32)).astype(BF16)
    groups = arrived.shape[2] // HD // kv_heads
    rows = groups * q_lots
    pages = base.shape[1]
    out[:, :pages, :] = base[...]
    for g in range(reach // PAGE):
        put_page(out, page_cap, slots[g], mixed[g * PAGE : (g + 1) * PAGE, :])
    for g in range(kv_heads):
        query = jnp.concatenate(
            [
                arrived[k, :q_lots, (g * groups + j) * HD : (g * groups + j + 1) * HD]
                for k in range(n)
                for j in range(groups)
            ],
            axis=0,
        )
        cols = slice(g * HD, (g + 1) * HD)
        vcols = slice(kvw + g * HD, kvw + (g + 1) * HD)
        key = jnp.concatenate([mixed[:, cols], kv_text[reach:, cols]], axis=0)
        value = jnp.concatenate([mixed[:, vcols], kv_text[reach:, vcols]], axis=0)
        scores = dot_t(key, query) * HD**-0.5 + bias[...]
        top = jnp.max(scores, axis=0, keepdims=True)
        weights = jnp.exp(scores - top)
        rows_held[g : g + 1, :] = top
        rows_held[kv_heads + g : kv_heads + g + 1, :] = jnp.sum(weights, axis=0, keepdims=True)
        numerator = lax.dot_general(
            weights.astype(BF16), value, (((0,), (0,)), ((), ())), preferred_element_type=F32
        )
        held[g * n * rows : (g + 1) * n * rows, :] = numerator
        own[g * rows : (g + 1) * rows, :] = held[pl.ds(pl.multiple_of((g * n + rank) * rows, rows), rows), :]
        numerator = numerator.astype(BF16)
        for k in range(n):
            out[k, pages + g * rows : pages + (g + 1) * rows, :] = numerator[k * rows : (k + 1) * rows, :]
    stat_rows = 2 * kv_heads
    share = HD // rows
    window = pl.ds(pl.multiple_of(rank // share * HD, HD), HD)
    own[kv_heads * rows : kv_heads * rows + stat_rows, :] = rows_held[:stat_rows, window]
    blank = jnp.zeros((PAGE - 3 * stat_rows, HD), F32)
    for w in range(-(-n // share)):
        stats = rows_held[:stat_rows, w * HD : (w + 1) * HD]
        lines = jnp.concatenate([*split_three(stats), blank], axis=0).astype(BF16)
        for k in range(w * share, min(n, (w + 1) * share)):
            out[k, pages + kv_heads * rows :, :] = lines


def pick_column(row, rows, start):
    shape = (rows, HD)
    chosen = lax.broadcasted_iota(I32, shape, 1) == lax.broadcasted_iota(I32, shape, 0) + start
    return jnp.sum(jnp.where(chosen, row, 0.0), axis=1, keepdims=True)


def combine(pieces, highest):
    numerator, total = 0.0, 0.0
    for rows, top, weight in pieces:
        scale = jnp.exp(top - highest)
        numerator = numerator + rows * scale
        total = total + weight * scale
    return numerator, total


def fresh_kernel(n, kv_heads, steps, query, key, value, own, mine):
    rows = query.shape[0] // kv_heads
    every = kv_heads * rows
    start = rank_of(lax.axis_index("section"), n) % (HD // rows) * rows
    row = lax.broadcasted_iota(I32, (rows, steps), 0)
    causal = lax.broadcasted_iota(I32, (rows, steps), 1) <= row % steps
    tops, totals = [], []
    for g in range(kv_heads):
        cols = slice(g * HD, (g + 1) * HD)
        at = slice(g * rows, (g + 1) * rows)
        fresh = softmax_parts(query[at, :], key[:, cols], value[:, cols], causal)
        share = (
            own[at, :],
            pick_column(own[every + g : every + g + 1, :], rows, start),
            pick_column(own[every + kv_heads + g : every + kv_heads + g + 1, :], rows, start),
        )
        highest = jnp.maximum(fresh[1], share[1])
        numerator, total = combine((fresh, share), highest)
        mine[at, :] = numerator
        tops.append(highest)
        totals.append(total)
    line = column_to_row(jnp.concatenate(tops + totals, axis=0))
    mine[every:, :] = jnp.broadcast_to(line, (STAT, line.shape[1]))


def finish_kernel(kv_heads, steps, page_cap, shares, mine, attended, keys, values):
    n = shares.shape[0]
    pos = lax.axis_index("section")
    every = mine.shape[0] - STAT
    rows = every // kv_heads
    start = rank_of(pos, n) % (HD // rows) * rows
    chunk = page_cap * PAGE
    halves = keys.shape[2] // HD
    for k in range(n):
        for i, out in enumerate((keys, values)):
            for h in range(halves):
                part = i * halves + h
                out[section_of(k, n), :, h * HD : (h + 1) * HD] = shares[k, part * chunk : (part + 1) * chunk, :]
    pages = 2 * halves * chunk
    stats = row_to_column(mine[every : every + 1, :])
    lines = []
    for k in range(n):
        three = shares[k, pages + every :, :].astype(F32)
        size = 2 * kv_heads
        lines.append(three[:size] + three[size : 2 * size] + three[2 * size : 3 * size])
    for g in range(kv_heads):
        at = slice(g * rows, (g + 1) * rows)
        pieces = [(mine[at, :], stats[at], stats[every + g * rows : every + (g + 1) * rows])]
        for k in range(n):
            away = pos != section_of(k, n)
            top = jnp.where(away, pick_column(lines[k][g : g + 1], rows, start), LOWEST)
            weight = jnp.where(away, pick_column(lines[k][kv_heads + g : kv_heads + g + 1], rows, start), 0.0)
            share = shares[k, pages + g * rows : pages + (g + 1) * rows, :].astype(F32)
            pieces.append((share, top, weight))
        highest = pieces[0][1]
        for p in pieces[1:]:
            highest = jnp.maximum(highest, p[1])
        numerator, total = combine(pieces, highest)
        result = (numerator / total).astype(BF16)
        for h in range(rows // steps):
            to = (g * rows // steps + h) * HD
            attended[0, :, to : to + HD] = result[h * steps : (h + 1) * steps, :]


def body(
    text_rows,
    vis_rows,
    img_route,
    norm_gain,
    w_key,
    w_value,
    page_count,
    tail_len,
    page_dest,
    dec_req,
    dec_query,
    dec_key,
    dec_value,
):
    n = lax.axis_size("section")
    tok, half = text_rows.shape
    img = vis_rows.shape[0]
    kvw = w_key.shape[1]
    kv_heads = kvw // HD
    _, steps, q_width = dec_query.shape
    heads = q_width // HD
    q_rows = heads * steps
    blocks = tok // PAGE
    cap = max(2, (2 * img + n - 1) // n)
    page_cap = max(1, (blocks + n - 1) // n)

    def across(array):
        return lax.ppermute(array, "tensor", [(0, 1), (1, 0)])

    def exchange(array):
        order = [[section_of(rank, n) for rank in range(n)]]
        return lax.all_to_all(array, "section", split_axis=0, concat_axis=0, tiled=True, axis_index_groups=order)

    def remote(array):
        return pltpu.with_memory_space_constraint(array, pltpu.HBM)

    def local(array):
        return pltpu.with_memory_space_constraint(array, pltpu.VMEM)

    vis_far = across(vis_rows)
    text_far = across(text_rows)
    query = dec_query.reshape(steps, heads, HD).transpose(1, 0, 2).reshape(q_rows, HD)

    lot = -(-cap // PAGE) * PAGE
    q_lots = q_rows * HD // (2 * kvw)
    width = max(tok, n * lot)
    gain = norm_gain.reshape(1, 2 * half)
    held = half + half // 2
    arguments = (
        img_route.T,
        page_dest.T,
        page_count,
        tail_len,
        dec_req,
        w_key,
        w_value,
        vis_rows,
        gain,
        query,
    )
    info, slots, key_held, value_held, vis_near, gain_near, query_near = call(
        lambda *refs: prepare_kernel((n, img, tok, blocks, lot, page_cap), *refs),
        (
            jax.ShapeDtypeStruct((8, width), I32),
            jax.ShapeDtypeStruct((blocks,), I32),
            pltpu.VMEM((held, kvw), BF16),
            pltpu.VMEM((held, kvw), BF16),
            *[pltpu.VMEM(a.shape, a.dtype) for a in arguments[7:]],
        ),
        [ANY] * len(arguments),
        (VM, SM) + (VM,) * 5,
        [
            *[(pltpu.VMEM if i == 0 else pltpu.SMEM)(a.shape, a.dtype) for i, a in enumerate(arguments[:5])],
            pltpu.SMEM((n,), I32),
            pltpu.SemaphoreType.DMA((len(arguments) + 2,)),
        ],
        flops=1 << 20,
        traffic=2 * 2 * half * 2 * kvw * 2,
    )(*[remote(a) for a in arguments])

    step = min(1024, half)
    load = min(2048, half)

    packed = call(
        lambda *refs: vis_kernel(n, lot, step, *refs),
        pltpu.VMEM((n, q_lots + lot, 2 * kvw), BF16),
        [VM] * 6 + [ANY] * 2 + [VM],
        VM,
        [
            pltpu.VMEM((2 * half - held, kvw), BF16),
            pltpu.VMEM((2 * half - held, kvw), BF16),
            pltpu.VMEM((img, 2 * kvw), F32),
            pltpu.SemaphoreType.DMA((2,)),
        ],
        flops=64 * img * 2 * half * 2 * kvw,
        traffic=2 * img * 2 * half + 8 * half * kvw,
    )(
        local(vis_near),
        vis_far,
        local(gain_near),
        local(query_near),
        local(key_held),
        local(value_held),
        remote(w_key),
        remote(w_value),
        info,
    )
    arrived = exchange(packed)

    block = page_cap * PAGE * 2 * kv_heads + q_rows + PAGE
    kv_text, bias, base = call(
        lambda *refs: text_kernel(load, step, page_cap, q_rows // kv_heads, *refs),
        (
            jax.ShapeDtypeStruct((tok, 2 * kvw), BF16),
            jax.ShapeDtypeStruct((tok, n * q_rows // kv_heads), F32),
            jax.ShapeDtypeStruct((n, block - q_rows - PAGE, HD), BF16),
        ),
        [ANY, VM, VM, ANY, ANY, VM, SM],
        (VM, VM, VM),
        [
            pltpu.VMEM((tok, half), BF16),
            pltpu.VMEM(w_key.shape, BF16),
            pltpu.VMEM(w_value.shape, BF16),
            pltpu.VMEM((tok, 2 * kvw), F32),
            pltpu.SemaphoreType.DMA((1 + 4 * half // load,)),
        ],
        limit=24,
        flops=2 * tok * 2 * half * 2 * kvw,
        traffic=2 * tok * 2 * half + 8 * half * kvw,
    )(remote(text_rows), text_far, remote(gain), remote(w_key), remote(w_value), info, slots)

    sent, own = call(
        lambda *refs: attend_kernel(n, cap, lot, page_cap, kv_heads, *refs),
        (
            pltpu.VMEM((n, block, HD), BF16),
            jax.ShapeDtypeStruct((q_rows + STAT, HD), F32),
        ),
        [SM] + [VM] * 5,
        (VM, VM),
        [
            pltpu.VMEM((min(tok, n * cap), 2 * kvw), BF16),
            pltpu.VMEM((n * q_rows, HD), F32),
            pltpu.VMEM((STAT, n * q_rows // kv_heads), F32),
        ],
        flops=4 * n * q_rows * tok * HD,
        traffic=n * (q_rows + STAT) * HD * 4,
    )(slots, info, kv_text, arrived, bias, base)
    shares = exchange(sent)

    mine = call(
        lambda *refs: fresh_kernel(n, kv_heads, steps, *refs),
        jax.ShapeDtypeStruct((q_rows + STAT, HD), F32),
        [VM] * 4,
        VM,
        flops=1 << 20,
        traffic=1 << 18,
    )(remote(query), remote(dec_key[0]), remote(dec_value[0]), own)

    slots_here = n * page_cap
    attended, cache_key, cache_value = call(
        lambda *refs: finish_kernel(kv_heads, steps, page_cap, *refs),
        (
            jax.ShapeDtypeStruct(dec_query.shape, BF16),
            jax.ShapeDtypeStruct((n, page_cap * PAGE, kvw), BF16),
            jax.ShapeDtypeStruct((n, page_cap * PAGE, kvw), BF16),
        ),
        [VM, VM],
        (VM, VM, VM),
        traffic=4 * tok * 2 * kvw,
    )(shares, mine)
    return (
        attended,
        cache_key.reshape(slots_here, PAGE, kvw),
        cache_value.reshape(slots_here, PAGE, kvw),
    )


def solution(mesh):
    return jax.shard_map(
        body,
        mesh=mesh,
        in_specs=(
            P(("groups", "section"), "tensor"),
            P(("groups", "section"), "tensor"),
            P("groups", None),
            P(),
            P(None, "tensor"),
            P(None, "tensor"),
            P("groups"),
            P("groups"),
            P("groups", None),
            P("groups"),
            P(("groups", "section"), None, "tensor"),
            P(("groups", "section"), None, "tensor"),
            P(("groups", "section"), None, "tensor"),
        ),
        out_specs=(
            P(("groups", "section"), None, "tensor"),
            P(("groups", "section"), None, "tensor"),
            P(("groups", "section"), None, "tensor"),
        ),
        check_vma=False,
    )
```

```python
import jax
import jax.numpy as jnp
from jax import lax
from jax.experimental import pallas as pl
from jax.experimental.pallas import tpu as pltpu
from jax.sharding import PartitionSpec as P

HD = 128
PAGE = 16
LOWEST = -1e30
EPS = 1e-06
STAT = 8
F32 = jnp.float32
BF16 = jnp.bfloat16
I32 = jnp.int32

VM = pl.BlockSpec(memory_space=pltpu.VMEM)
SM = pl.BlockSpec(memory_space=pltpu.SMEM)
ANY = pl.BlockSpec(memory_space=pl.ANY)
MIB = 1 << 20


def call(kernel, out_shape, in_specs, out_specs, scratch=(), limit=16, flops=0, traffic=0):
    return pl.pallas_call(
        kernel,
        out_shape=out_shape,
        in_specs=in_specs,
        out_specs=out_specs,
        scratch_shapes=list(scratch),
        compiler_params=pltpu.CompilerParams(vmem_limit_bytes=limit * MIB),
        cost_estimate=pl.CostEstimate(flops=flops, bytes_accessed=traffic, transcendentals=0),
    )


def rank_of(section, n):
    lower = section < n // 2
    z, y = section // 2, section % 2
    return jnp.where(lower, n // 4 - 1 - z, z - n // 4) * 4 + (1 - y) * 2 + jnp.where(lower, 0, 1)


def section_of(rank, n):
    away, side = rank // 4, rank % 2
    return 2 * (n // 4 - 1 - away + side * (2 * away + 1)) + 1 - rank // 2 % 2


def dot(a, b):
    return jnp.dot(a, b, preferred_element_type=F32)


def dot_t(a, b):
    return lax.dot_general(a, b, (((1,), (1,)), ((), ())), preferred_element_type=F32)


def diagonal(shape):
    return lax.broadcasted_iota(I32, shape, 0) == lax.broadcasted_iota(I32, shape, 1)


def column_to_row(column):
    rows = column.shape[0]
    return jnp.sum(jnp.where(diagonal((rows, rows)), column, 0.0), axis=0, keepdims=True)


def row_to_column(row):
    lanes = row.shape[1]
    return jnp.sum(jnp.where(diagonal((lanes, lanes)), row, 0.0), axis=1, keepdims=True)


def squares_of(rows):
    total = jnp.zeros((rows.shape[0], HD), F32)
    for c in range(0, rows.shape[1], HD):
        wide = rows[:, c : c + HD].astype(F32)
        total = total + wide * wide
    return total


def split_three(values):
    high = values.astype(BF16).astype(F32)
    rest = values - high
    middle = rest.astype(BF16).astype(F32)
    return high, middle, rest - middle


def softmax_parts(query, key, value, usable):
    scores = jnp.where(usable, dot_t(query, key) * HD**-0.5, LOWEST)
    top = jnp.max(scores, axis=1, keepdims=True)
    weights = jnp.where(usable, jnp.exp(scores - top), 0.0)
    return dot(weights.astype(BF16), value), top, jnp.sum(weights, axis=1, keepdims=True)


def prepare_kernel(sizes, *refs):
    n, img, tok, blocks, lot, page_cap = sizes
    far, (info, slots), near, small, (starts, sems) = refs[:10], refs[10:12], refs[12:17], refs[17:22], refs[22:]
    held = near[0].shape[0]
    half = near[2].shape[1]
    me = lax.axis_index("tensor")
    pairs = list(zip(far[:5], small)) + list(zip(far[7:], near[2:]))
    for w, kept in zip(far[5:7], near[:2]):
        for start, at, size in ((me * half, 0, half), ((1 - me) * half, half, held - half)):
            source = pl.ds(pl.multiple_of(start, held - half), size)
            pairs.append((w.at[source], kept.at[at : at + size]))
    copies = [pltpu.make_async_copy(a, b, sems.at[i]) for i, (a, b) in enumerate(pairs)]
    for c in copies:
        c.start()
    route, pages, count, tail, req = small
    for c in copies[: len(small)]:
        c.wait()
    pos = lax.axis_index("section")
    table = [route[:, e * img : (e + 1) * img] for e in range(n)]
    own = jnp.zeros((1, img), I32)
    for e in range(n):
        own = jnp.where(pos == e, table[e], own)
    marks = own == lax.broadcasted_iota(I32, (n, img), 0)
    ones = jnp.where(marks, 1.0, 0.0).astype(BF16)
    earlier = lax.broadcasted_iota(I32, (img, img), 0) < lax.broadcasted_iota(I32, (img, img), 1)
    prefix = dot(ones, jnp.where(earlier, 1.0, 0.0).astype(BF16))
    local = jnp.sum(jnp.where(marks, prefix, 0.0), axis=0, keepdims=True).astype(I32)
    info[0:1, :img] = rank_of(own, n) * lot + local
    lanes = lax.broadcasted_iota(I32, (1, n * lot), 1)
    source, inner = section_of(lanes // lot, n), lanes % lot
    fits = jnp.zeros((1, n * lot), I32)
    offset = jnp.zeros((1, n * lot), I32)
    for e in range(n):
        arriving = jnp.sum((table[e] == pos).astype(I32), axis=1, keepdims=True)
        fits = fits + jnp.where(source == e, arriving, 0)
        offset = offset + jnp.where(source > e, arriving, 0)
    info[2:3, : n * lot] = jnp.where(inner < fits, offset + inner, -1)
    total = jnp.int32(0)
    for r in range(n):
        starts[r] = total
        total = total + count[r]
    token = lax.broadcasted_iota(I32, (1, tok), 1) + pos * tok
    token_slot = jnp.full((1, tok), -1, I32)
    for b in range(n):
        r = req[b]
        first = starts[r] * PAGE
        last = first + (count[r] - 1) * PAGE + tail[r]
        token_slot = jnp.where((token >= first) & (token < last), b, token_slot)
    info[1:2, :tok] = token_slot
    for g in range(blocks):
        holder = pages[0, pos * blocks + g]
        slot = rank_of(holder, n) * page_cap
        for e in range(g):
            slot = slot + (pages[0, pos * blocks + e] == holder).astype(I32)
        slots[g] = slot
    for c in copies[len(small) :]:
        c.wait()


def scale_of(near, far):
    sums = jnp.sum(squares_of(near) + squares_of(far), axis=1, keepdims=True)
    return lax.rsqrt(sums / (2.0 * near.shape[1]) + EPS)


def normed_rows(rows, c, step, scale, gain):
    return (rows[:, c : c + step].astype(F32) * scale * gain).astype(BF16)


def add_part(total, at, normed, w, begin):
    part = dot(normed, w)
    columns = slice(at, at + part.shape[1])
    if begin:
        total[:, columns] = part
    else:
        total[:, columns] += part


def vis_kernel(n, lot, step, *refs):
    near, far, gain, query, key_held, value_held, w_key, w_value, info, out, key_rest, value_rest, total, sems = refs
    img, half = near.shape
    kvw = w_key.shape[1]
    me = lax.axis_index("tensor")
    held, size = key_held.shape[0], key_rest.shape[0]
    last = pl.ds(pl.multiple_of((1 - me) * half + held - half, size), size)
    pairs = ((w_key, key_rest), (w_value, value_rest))
    copies = [pltpu.make_async_copy(w.at[last], kept, sems.at[i]) for i, (w, kept) in enumerate(pairs)]
    for c in copies:
        c.start()
    scale = scale_of(near, far)
    for at in range(0, 2 * half, step):
        if at == held:
            for c in copies:
                c.wait()
        rows, side = (near, me) if at < half else (far, 1 - me)
        weights, w_at = ((key_held, value_held), at) if at < held else ((key_rest, value_rest), at - held)
        c = at % half
        columns = pl.ds(pl.multiple_of(side * half + c, step), step)
        normed = normed_rows(rows, c, step, scale, gain[:, columns])
        for w, col in zip(weights, (0, kvw)):
            add_part(total, col, normed, w[w_at : w_at + step, :], at == 0)
    slot = lax.broadcasted_iota(I32, (n * lot, img), 0)
    chosen = jnp.where(slot == info[0:1, :img], 1.0, 0.0).astype(BF16)
    packed = dot(chosen, total[...].astype(BF16)).astype(BF16)
    q_lots = out.shape[1] - lot
    for k in range(n):
        for j in range(query.shape[0] // q_lots):
            out[k, :q_lots, j * HD : (j + 1) * HD] = query[j * q_lots : (j + 1) * q_lots, :]
        out[k, q_lots:, :] = packed[k * lot : (k + 1) * lot, :]


def put_page(out, page_cap, slot, rows):
    chunk = page_cap * PAGE
    for h in range(rows.shape[1] // HD):
        at = pl.ds(pl.multiple_of((slot % page_cap) * PAGE + h * chunk, PAGE), PAGE)
        out[slot // page_cap, at, :] = rows[:, h * HD : (h + 1) * HD]


def text_kernel(load, step, page_cap, q_rows, *refs):
    near_far, far, gain, w_key_far, w_value_far, info, slots, out, bias, base, near, w_key, w_value, total, sems = refs
    half = near.shape[1]
    kvw = w_key.shape[1]
    me = lax.axis_index("tensor")
    first = pltpu.make_async_copy(near_far, near, sems.at[0])
    first.start()
    loads = []
    for side in (me, 1 - me):
        for c in range(0, half, load):
            at = len(loads) * load
            columns = pl.ds(pl.multiple_of(side * half + c, load), load)
            pair = [
                pltpu.make_async_copy(w.at[columns], held.at[at : at + load], sems.at[2 * len(loads) + i])
                for i, (w, held) in enumerate(((w_key_far, w_key), (w_value_far, w_value)), 1)
            ]
            for copy in pair:
                copy.start()
            loads.append(pair)
    sums = squares_of(far)
    first.wait()
    sums = jnp.sum(squares_of(near) + sums, axis=1, keepdims=True)
    scale = lax.rsqrt(sums / (2.0 * half) + EPS)
    for i, pair in enumerate(loads):
        for copy in pair:
            copy.wait()
        for at in range(i * load, (i + 1) * load, step):
            rows, side = (near, me) if at < half else (far, 1 - me)
            c = at % half
            columns = pl.ds(pl.multiple_of(side * half + c, step), step)
            normed = normed_rows(rows, c, step, scale, gain[:, columns])
            for w, col in ((w_key, 0), (w_value, kvw)):
                add_part(total, col, normed, w[at : at + step, :], at == 0)
    out[...] = total[...].astype(BF16)
    base[...] = jnp.zeros(base.shape, BF16)
    tok = near.shape[0]
    for g in range(tok // PAGE):
        put_page(base, page_cap, slots[g], out[g * PAGE : (g + 1) * PAGE, :])
    token_slot = row_to_column(info[1:2, :tok].astype(F32))
    lanes = section_of(lax.broadcasted_iota(I32, bias.shape, 1) // q_rows, bias.shape[1] // q_rows)
    bias[...] = jnp.where(token_slot == lanes.astype(F32), 0.0, LOWEST)


def attend_kernel(n, cap, lot, page_cap, kv_heads, slots, info, kv_text, arrived, bias, base, out, own, mixed, held, rows_held):
    rank = rank_of(lax.axis_index("section"), n)
    tok = kv_text.shape[0]
    kvw = kv_heads * HD
    q_lots = arrived.shape[1] - lot
    reach = min(tok, n * cap)
    hit = lax.broadcasted_iota(I32, (reach, n * lot), 0) == info[2:3, : n * lot]
    hot = jnp.where(hit, 1.0, 0.0)
    covered = jnp.sum(hot, axis=1, keepdims=True) > 0.0
    incoming = jnp.concatenate([arrived[k, q_lots:, :] for k in range(n)], axis=0)
    placed = dot(hot.astype(BF16), incoming)
    mixed[...] = jnp.where(covered, placed, kv_text[:reach, :].astype(F32)).astype(BF16)
    groups = arrived.shape[2] // HD // kv_heads
    rows = groups * q_lots
    pages = base.shape[1]
    out[:, :pages, :] = base[...]
    for g in range(reach // PAGE):
        put_page(out, page_cap, slots[g], mixed[g * PAGE : (g + 1) * PAGE, :])
    for g in range(kv_heads):
        query = jnp.concatenate(
            [
                arrived[k, :q_lots, (g * groups + j) * HD : (g * groups + j + 1) * HD]
                for k in range(n)
                for j in range(groups)
            ],
            axis=0,
        )
        cols = slice(g * HD, (g + 1) * HD)
        vcols = slice(kvw + g * HD, kvw + (g + 1) * HD)
        key = jnp.concatenate([mixed[:, cols], kv_text[reach:, cols]], axis=0)
        value = jnp.concatenate([mixed[:, vcols], kv_text[reach:, vcols]], axis=0)
        scores = dot_t(key, query) * HD**-0.5 + bias[...]
        top = jnp.max(scores, axis=0, keepdims=True)
        weights = jnp.exp(scores - top)
        rows_held[g : g + 1, :] = top
        rows_held[kv_heads + g : kv_heads + g + 1, :] = jnp.sum(weights, axis=0, keepdims=True)
        numerator = lax.dot_general(
            weights.astype(BF16), value, (((0,), (0,)), ((), ())), preferred_element_type=F32
        )
        held[g * n * rows : (g + 1) * n * rows, :] = numerator
        own[g * rows : (g + 1) * rows, :] = held[pl.ds(pl.multiple_of((g * n + rank) * rows, rows), rows), :]
        numerator = numerator.astype(BF16)
        for k in range(n):
            out[k, pages + g * rows : pages + (g + 1) * rows, :] = numerator[k * rows : (k + 1) * rows, :]
    stat_rows = 2 * kv_heads
    share = HD // rows
    window = pl.ds(pl.multiple_of(rank // share * HD, HD), HD)
    own[kv_heads * rows : kv_heads * rows + stat_rows, :] = rows_held[:stat_rows, window]
    blank = jnp.zeros((PAGE - 3 * stat_rows, HD), F32)
    for w in range(-(-n // share)):
        stats = rows_held[:stat_rows, w * HD : (w + 1) * HD]
        lines = jnp.concatenate([*split_three(stats), blank], axis=0).astype(BF16)
        for k in range(w * share, min(n, (w + 1) * share)):
            out[k, pages + kv_heads * rows :, :] = lines


def pick_column(row, rows, start):
    shape = (rows, HD)
    chosen = lax.broadcasted_iota(I32, shape, 1) == lax.broadcasted_iota(I32, shape, 0) + start
    return jnp.sum(jnp.where(chosen, row, 0.0), axis=1, keepdims=True)


def combine(pieces, highest):
    numerator, total = 0.0, 0.0
    for rows, top, weight in pieces:
        scale = jnp.exp(top - highest)
        numerator = numerator + rows * scale
        total = total + weight * scale
    return numerator, total


def fresh_kernel(n, kv_heads, steps, query, key, value, own, mine):
    rows = query.shape[0] // kv_heads
    every = kv_heads * rows
    start = rank_of(lax.axis_index("section"), n) % (HD // rows) * rows
    row = lax.broadcasted_iota(I32, (rows, steps), 0)
    causal = lax.broadcasted_iota(I32, (rows, steps), 1) <= row % steps
    tops, totals = [], []
    for g in range(kv_heads):
        cols = slice(g * HD, (g + 1) * HD)
        at = slice(g * rows, (g + 1) * rows)
        fresh = softmax_parts(query[at, :], key[:, cols], value[:, cols], causal)
        share = (
            own[at, :],
            pick_column(own[every + g : every + g + 1, :], rows, start),
            pick_column(own[every + kv_heads + g : every + kv_heads + g + 1, :], rows, start),
        )
        highest = jnp.maximum(fresh[1], share[1])
        numerator, total = combine((fresh, share), highest)
        mine[at, :] = numerator
        tops.append(highest)
        totals.append(total)
    line = column_to_row(jnp.concatenate(tops + totals, axis=0))
    mine[every:, :] = jnp.broadcast_to(line, (STAT, line.shape[1]))


def finish_kernel(kv_heads, steps, page_cap, shares, mine, attended, keys, values):
    n = shares.shape[0]
    pos = lax.axis_index("section")
    every = mine.shape[0] - STAT
    rows = every // kv_heads
    start = rank_of(pos, n) % (HD // rows) * rows
    chunk = page_cap * PAGE
    halves = keys.shape[2] // HD
    for k in range(n):
        for i, out in enumerate((keys, values)):
            for h in range(halves):
                part = i * halves + h
                out[section_of(k, n), :, h * HD : (h + 1) * HD] = shares[k, part * chunk : (part + 1) * chunk, :]
    pages = 2 * halves * chunk
    stats = row_to_column(mine[every : every + 1, :])
    lines = []
    for k in range(n):
        three = shares[k, pages + every :, :].astype(F32)
        size = 2 * kv_heads
        lines.append(three[:size] + three[size : 2 * size] + three[2 * size : 3 * size])
    for g in range(kv_heads):
        at = slice(g * rows, (g + 1) * rows)
        pieces = [(mine[at, :], stats[at], stats[every + g * rows : every + (g + 1) * rows])]
        for k in range(n):
            away = pos != section_of(k, n)
            top = jnp.where(away, pick_column(lines[k][g : g + 1], rows, start), LOWEST)
            weight = jnp.where(away, pick_column(lines[k][kv_heads + g : kv_heads + g + 1], rows, start), 0.0)
            share = shares[k, pages + g * rows : pages + (g + 1) * rows, :].astype(F32)
            pieces.append((share, top, weight))
        highest = pieces[0][1]
        for p in pieces[1:]:
            highest = jnp.maximum(highest, p[1])
        numerator, total = combine(pieces, highest)
        result = (numerator / total).astype(BF16)
        for h in range(rows // steps):
            to = (g * rows // steps + h) * HD
            attended[0, :, to : to + HD] = result[h * steps : (h + 1) * steps, :]


def body(
    text_rows,
    vis_rows,
    img_route,
    norm_gain,
    w_key,
    w_value,
    page_count,
    tail_len,
    page_dest,
    dec_req,
    dec_query,
    dec_key,
    dec_value,
):
    n = lax.axis_size("section")
    tok, half = text_rows.shape
    img = vis_rows.shape[0]
    kvw = w_key.shape[1]
    kv_heads = kvw // HD
    _, steps, q_width = dec_query.shape
    heads = q_width // HD
    q_rows = heads * steps
    blocks = tok // PAGE
    cap = max(2, (2 * img + n - 1) // n)
    page_cap = max(1, (blocks + n - 1) // n)

    def across(array):
        return lax.ppermute(array, "tensor", [(0, 1), (1, 0)])

    def exchange(array):
        order = [[section_of(rank, n) for rank in range(n)]]
        return lax.all_to_all(array, "section", split_axis=0, concat_axis=0, tiled=True, axis_index_groups=order)

    def remote(array):
        return pltpu.with_memory_space_constraint(array, pltpu.HBM)

    def local(array):
        return pltpu.with_memory_space_constraint(array, pltpu.VMEM)

    vis_far = across(vis_rows)
    text_far = across(text_rows)
    query = dec_query.reshape(steps, heads, HD).transpose(1, 0, 2).reshape(q_rows, HD)

    lot = -(-cap // PAGE) * PAGE
    q_lots = q_rows * HD // (2 * kvw)
    width = max(tok, n * lot)
    gain = norm_gain.reshape(1, 2 * half)
    held = half + half // 2
    arguments = (
        img_route.T,
        page_dest.T,
        page_count,
        tail_len,
        dec_req,
        w_key,
        w_value,
        vis_rows,
        gain,
        query,
    )
    info, slots, key_held, value_held, vis_near, gain_near, query_near = call(
        lambda *refs: prepare_kernel((n, img, tok, blocks, lot, page_cap), *refs),
        (
            jax.ShapeDtypeStruct((8, width), I32),
            jax.ShapeDtypeStruct((blocks,), I32),
            pltpu.VMEM((held, kvw), BF16),
            pltpu.VMEM((held, kvw), BF16),
            *[pltpu.VMEM(a.shape, a.dtype) for a in arguments[7:]],
        ),
        [ANY] * len(arguments),
        (VM, SM) + (VM,) * 5,
        [
            *[(pltpu.VMEM if i == 0 else pltpu.SMEM)(a.shape, a.dtype) for i, a in enumerate(arguments[:5])],
            pltpu.SMEM((n,), I32),
            pltpu.SemaphoreType.DMA((len(arguments) + 2,)),
        ],
        flops=1 << 20,
        traffic=2 * 2 * half * 2 * kvw * 2,
    )(*[remote(a) for a in arguments])

    step = min(1024, half)
    load = min(2048, half)

    packed = call(
        lambda *refs: vis_kernel(n, lot, step, *refs),
        pltpu.VMEM((n, q_lots + lot, 2 * kvw), BF16),
        [VM] * 6 + [ANY] * 2 + [VM],
        VM,
        [
            pltpu.VMEM((2 * half - held, kvw), BF16),
            pltpu.VMEM((2 * half - held, kvw), BF16),
            pltpu.VMEM((img, 2 * kvw), F32),
            pltpu.SemaphoreType.DMA((2,)),
        ],
        flops=64 * img * 2 * half * 2 * kvw,
        traffic=2 * img * 2 * half + 8 * half * kvw,
    )(
        local(vis_near),
        vis_far,
        local(gain_near),
        local(query_near),
        local(key_held),
        local(value_held),
        remote(w_key),
        remote(w_value),
        info,
    )
    arrived = exchange(packed)

    block = page_cap * PAGE * 2 * kv_heads + q_rows + PAGE
    kv_text, bias, base = call(
        lambda *refs: text_kernel(load, step, page_cap, q_rows // kv_heads, *refs),
        (
            jax.ShapeDtypeStruct((tok, 2 * kvw), BF16),
            jax.ShapeDtypeStruct((tok, n * q_rows // kv_heads), F32),
            jax.ShapeDtypeStruct((n, block - q_rows - PAGE, HD), BF16),
        ),
        [ANY, VM, VM, ANY, ANY, VM, SM],
        (VM, VM, VM),
        [
            pltpu.VMEM((tok, half), BF16),
            pltpu.VMEM(w_key.shape, BF16),
            pltpu.VMEM(w_value.shape, BF16),
            pltpu.VMEM((tok, 2 * kvw), F32),
            pltpu.SemaphoreType.DMA((1 + 4 * half // load,)),
        ],
        limit=24,
        flops=2 * tok * 2 * half * 2 * kvw,
        traffic=2 * tok * 2 * half + 8 * half * kvw,
    )(remote(text_rows), text_far, remote(gain), remote(w_key), remote(w_value), info, slots)

    sent, own = call(
        lambda *refs: attend_kernel(n, cap, lot, page_cap, kv_heads, *refs),
        (
            pltpu.VMEM((n, block, HD), BF16),
            jax.ShapeDtypeStruct((q_rows + STAT, HD), F32),
        ),
        [SM] + [VM] * 5,
        (VM, VM),
        [
            pltpu.VMEM((min(tok, n * cap), 2 * kvw), BF16),
            pltpu.VMEM((n * q_rows, HD), F32),
            pltpu.VMEM((STAT, n * q_rows // kv_heads), F32),
        ],
        flops=4 * n * q_rows * tok * HD,
        traffic=n * (q_rows + STAT) * HD * 4,
    )(slots, info, kv_text, arrived, bias, base)
    shares = exchange(sent)

    mine = call(
        lambda *refs: fresh_kernel(n, kv_heads, steps, *refs),
        jax.ShapeDtypeStruct((q_rows + STAT, HD), F32),
        [VM] * 4,
        VM,
        flops=1 << 20,
        traffic=1 << 18,
    )(remote(query), remote(dec_key[0]), remote(dec_value[0]), own)

    slots_here = n * page_cap
    attended, cache_key, cache_value = call(
        lambda *refs: finish_kernel(kv_heads, steps, page_cap, *refs),
        (
            jax.ShapeDtypeStruct(dec_query.shape, BF16),
            jax.ShapeDtypeStruct((n, page_cap * PAGE, kvw), BF16),
            jax.ShapeDtypeStruct((n, page_cap * PAGE, kvw), BF16),
        ),
        [VM, VM],
        (VM, VM, VM),
        traffic=4 * tok * 2 * kvw,
    )(shares, mine)
    return (
        attended,
        cache_key.reshape(slots_here, PAGE, kvw),
        cache_value.reshape(slots_here, PAGE, kvw),
    )


def solution(mesh):
    return jax.shard_map(
        body,
        mesh=mesh,
        in_specs=(
            P(("groups", "section"), "tensor"),
            P(("groups", "section"), "tensor"),
            P("groups", None),
            P(),
            P(None, "tensor"),
            P(None, "tensor"),
            P("groups"),
            P("groups"),
            P("groups", None),
            P("groups"),
            P(("groups", "section"), None, "tensor"),
            P(("groups", "section"), None, "tensor"),
            P(("groups", "section"), None, "tensor"),
        ),
        out_specs=(
            P(("groups", "section"), None, "tensor"),
            P(("groups", "section"), None, "tensor"),
            P(("groups", "section"), None, "tensor"),
        ),
        check_vma=False,
    )
```

```python
import jax
import jax.numpy as jnp
from jax import lax
from jax.experimental import pallas as pl
from jax.experimental.pallas import tpu as pltpu
from jax.sharding import PartitionSpec as P

HD = 128
PAGE = 16
LOWEST = -1e30
EPS = 1e-06
STAT = 8
F32 = jnp.float32
BF16 = jnp.bfloat16
I32 = jnp.int32

VM = pl.BlockSpec(memory_space=pltpu.VMEM)
SM = pl.BlockSpec(memory_space=pltpu.SMEM)
ANY = pl.BlockSpec(memory_space=pl.ANY)
MIB = 1 << 20


def call(kernel, out_shape, in_specs, out_specs, scratch=(), limit=16, flops=0, traffic=0):
    return pl.pallas_call(
        kernel,
        out_shape=out_shape,
        in_specs=in_specs,
        out_specs=out_specs,
        scratch_shapes=list(scratch),
        compiler_params=pltpu.CompilerParams(vmem_limit_bytes=limit * MIB),
        cost_estimate=pl.CostEstimate(flops=flops, bytes_accessed=traffic, transcendentals=0),
    )


def rank_of(section, n):
    return jnp.where(section < n // 2, n - 2 - 2 * section, 2 * section - n + 1)


def section_of(rank, n):
    return n // 2 - 1 - rank // 2 + rank % 2 * (rank // 2 * 2 + 1)


def page_rank_of(section, n):
    lower = section < n // 2
    z, y = section // 2, section % 2
    return jnp.where(lower, n // 4 - 1 - z, z - n // 4) * 4 + (1 - y) * 2 + jnp.where(lower, 0, 1)


def page_section_of(rank, n):
    away, side = rank // 4, rank % 2
    return 2 * (n // 4 - 1 - away + side * (2 * away + 1)) + 1 - rank // 2 % 2


def dot(a, b):
    return jnp.dot(a, b, preferred_element_type=F32)


def dot_t(a, b):
    return lax.dot_general(a, b, (((1,), (1,)), ((), ())), preferred_element_type=F32)


def diagonal(shape):
    return lax.broadcasted_iota(I32, shape, 0) == lax.broadcasted_iota(I32, shape, 1)


def column_to_row(column):
    rows = column.shape[0]
    return jnp.sum(jnp.where(diagonal((rows, rows)), column, 0.0), axis=0, keepdims=True)


def row_to_column(row):
    lanes = row.shape[1]
    return jnp.sum(jnp.where(diagonal((lanes, lanes)), row, 0.0), axis=1, keepdims=True)


def squares_of(rows):
    total = jnp.zeros((rows.shape[0], HD), F32)
    for c in range(0, rows.shape[1], HD):
        wide = rows[:, c : c + HD].astype(F32)
        total = total + wide * wide
    return total


def split_three(values):
    high = values.astype(BF16).astype(F32)
    rest = values - high
    middle = rest.astype(BF16).astype(F32)
    return high, middle, rest - middle


def softmax_parts(query, key, value, usable):
    scores = jnp.where(usable, dot_t(query, key) * HD**-0.5, LOWEST)
    top = jnp.max(scores, axis=1, keepdims=True)
    weights = jnp.where(usable, jnp.exp(scores - top), 0.0)
    return dot(weights.astype(BF16), value), top, jnp.sum(weights, axis=1, keepdims=True)


def prepare_kernel(sizes, *refs):
    n, img, tok, blocks, lot, page_cap = sizes
    far, (info, slots), near, small, (starts, sems) = refs[:10], refs[10:12], refs[12:17], refs[17:22], refs[22:]
    half = near[0].shape[0]
    me = lax.axis_index("tensor")
    pairs = list(zip(far[:5], small)) + list(zip(far[7:], near[2:]))
    mine = pl.ds(pl.multiple_of(me * half, half), half)
    pairs += [(w.at[mine], kept) for w, kept in zip(far[5:7], near[:2])]
    copies = [pltpu.make_async_copy(a, b, sems.at[i]) for i, (a, b) in enumerate(pairs)]
    for c in copies:
        c.start()
    route, pages, count, tail, req = small
    for c in copies[: len(small)]:
        c.wait()
    pos = lax.axis_index("section")
    table = [route[:, e * img : (e + 1) * img] for e in range(n)]
    own = jnp.zeros((1, img), I32)
    for e in range(n):
        own = jnp.where(pos == e, table[e], own)
    marks = own == lax.broadcasted_iota(I32, (n, img), 0)
    ones = jnp.where(marks, 1.0, 0.0).astype(BF16)
    earlier = lax.broadcasted_iota(I32, (img, img), 0) < lax.broadcasted_iota(I32, (img, img), 1)
    prefix = dot(ones, jnp.where(earlier, 1.0, 0.0).astype(BF16))
    local = jnp.sum(jnp.where(marks, prefix, 0.0), axis=0, keepdims=True).astype(I32)
    info[0:1, :img] = rank_of(own, n) * lot + local
    lanes = lax.broadcasted_iota(I32, (1, n * lot), 1)
    source, inner = section_of(lanes // lot, n), lanes % lot
    fits = jnp.zeros((1, n * lot), I32)
    offset = jnp.zeros((1, n * lot), I32)
    for e in range(n):
        arriving = jnp.sum((table[e] == pos).astype(I32), axis=1, keepdims=True)
        fits = fits + jnp.where(source == e, arriving, 0)
        offset = offset + jnp.where(source > e, arriving, 0)
    info[2:3, : n * lot] = jnp.where(inner < fits, offset + inner, -1)
    total = jnp.int32(0)
    for r in range(n):
        starts[r] = total
        total = total + count[r]
    token = lax.broadcasted_iota(I32, (1, tok), 1) + pos * tok
    token_slot = jnp.full((1, tok), -1, I32)
    for b in range(n):
        r = req[b]
        first = starts[r] * PAGE
        last = first + (count[r] - 1) * PAGE + tail[r]
        token_slot = jnp.where((token >= first) & (token < last), b, token_slot)
    info[1:2, :tok] = token_slot
    for g in range(blocks):
        holder = pages[0, pos * blocks + g]
        slot = page_rank_of(holder, n) * page_cap
        for e in range(g):
            slot = slot + (pages[0, pos * blocks + e] == holder).astype(I32)
        slots[g] = slot
    for c in copies[len(small) :]:
        c.wait()


def scale_of(near, far):
    sums = jnp.sum(squares_of(near) + squares_of(far), axis=1, keepdims=True)
    return lax.rsqrt(sums / (2.0 * near.shape[1]) + EPS)


def normed_rows(rows, c, step, scale, gain):
    return (rows[:, c : c + step].astype(F32) * scale * gain).astype(BF16)


def add_part(total, at, normed, w, begin):
    part = dot(normed, w)
    columns = slice(at, at + part.shape[1])
    if begin:
        total[:, columns] = part
    else:
        total[:, columns] += part


def vis_kernel(n, lot, load, step, *refs):
    near, far, gain, query, key_held, value_held, w_key, w_value, info, out, key_rest, value_rest, total, sems = refs
    img, half = near.shape
    kvw = w_key.shape[1]
    me = lax.axis_index("tensor")
    loads = []
    for c in range(0, half, load):
        source = pl.ds(pl.multiple_of((1 - me) * half + c, load), load)
        at = len(loads) * 2
        loads.append(
            [
                pltpu.make_async_copy(w.at[source], kept.at[c : c + load], sems.at[at + i])
                for i, (w, kept) in enumerate(((w_key, key_rest), (w_value, value_rest)))
            ]
        )
        for copy in loads[-1]:
            copy.start()
    scale = scale_of(near, far)
    for rows, side, weights in ((near, me, (key_held, value_held)), (far, 1 - me, (key_rest, value_rest))):
        for c in range(0, half, step):
            if rows is far and c % load == 0:
                for copy in loads[c // load]:
                    copy.wait()
            columns = pl.ds(pl.multiple_of(side * half + c, step), step)
            normed = normed_rows(rows, c, step, scale, gain[:, columns])
            for w, col in zip(weights, (0, kvw)):
                add_part(total, col, normed, w[c : c + step, :], rows is near and c == 0)
    slot = lax.broadcasted_iota(I32, (n * lot, img), 0)
    chosen = jnp.where(slot == info[0:1, :img], 1.0, 0.0).astype(BF16)
    packed = dot(chosen, total[...].astype(BF16)).astype(BF16)
    q_lots = out.shape[1] - lot
    for k in range(n):
        for j in range(query.shape[0] // q_lots):
            out[k, :q_lots, j * HD : (j + 1) * HD] = query[j * q_lots : (j + 1) * q_lots, :]
        out[k, q_lots:, :] = packed[k * lot : (k + 1) * lot, :]


def put_page(out, page_cap, slot, rows):
    chunk = page_cap * PAGE
    for h in range(rows.shape[1] // HD):
        at = pl.ds(pl.multiple_of((slot % page_cap) * PAGE + h * chunk, PAGE), PAGE)
        out[slot // page_cap, at, :] = rows[:, h * HD : (h + 1) * HD]


def text_kernel(load, step, page_cap, q_rows, *refs):
    near_far, far, gain, w_key_far, w_value_far, info, slots, out, bias, base, near, w_key, w_value, total, sems = refs
    half = near.shape[1]
    kvw = w_key.shape[1]
    me = lax.axis_index("tensor")
    first = pltpu.make_async_copy(near_far, near, sems.at[0])
    first.start()
    loads = []
    for side in (me, 1 - me):
        for c in range(0, half, load):
            at = len(loads) * load
            columns = pl.ds(pl.multiple_of(side * half + c, load), load)
            pair = [
                pltpu.make_async_copy(w.at[columns], held.at[at : at + load], sems.at[2 * len(loads) + i])
                for i, (w, held) in enumerate(((w_key_far, w_key), (w_value_far, w_value)), 1)
            ]
            for copy in pair:
                copy.start()
            loads.append(pair)
    sums = squares_of(far)
    first.wait()
    sums = jnp.sum(squares_of(near) + sums, axis=1, keepdims=True)
    scale = lax.rsqrt(sums / (2.0 * half) + EPS)
    for i, pair in enumerate(loads):
        for copy in pair:
            copy.wait()
        for at in range(i * load, (i + 1) * load, step):
            rows, side = (near, me) if at < half else (far, 1 - me)
            c = at % half
            columns = pl.ds(pl.multiple_of(side * half + c, step), step)
            normed = normed_rows(rows, c, step, scale, gain[:, columns])
            for w, col in ((w_key, 0), (w_value, kvw)):
                add_part(total, col, normed, w[at : at + step, :], at == 0)
    out[...] = total[...].astype(BF16)
    base[...] = jnp.zeros(base.shape, BF16)
    tok = near.shape[0]
    for g in range(tok // PAGE):
        put_page(base, page_cap, slots[g], out[g * PAGE : (g + 1) * PAGE, :])
    token_slot = row_to_column(info[1:2, :tok].astype(F32))
    lanes = section_of(lax.broadcasted_iota(I32, bias.shape, 1) // q_rows, bias.shape[1] // q_rows)
    bias[...] = jnp.where(token_slot == lanes.astype(F32), 0.0, LOWEST)


def attend_kernel(n, cap, lot, page_cap, kv_heads, slots, info, kv_text, arrived, bias, base, sent, own, *scratch):
    out, mixed, held, rows_held, sems = scratch
    order = [page_section_of(k, n) for k in range(n)]
    rank = rank_of(lax.axis_index("section"), n)
    tok = kv_text.shape[0]
    kvw = kv_heads * HD
    q_lots = arrived.shape[1] - lot
    reach = min(tok, n * cap)
    hit = lax.broadcasted_iota(I32, (reach, n * lot), 0) == info[2:3, : n * lot]
    hot = jnp.where(hit, 1.0, 0.0)
    covered = jnp.sum(hot, axis=1, keepdims=True) > 0.0
    incoming = jnp.concatenate([arrived[k, q_lots:, :] for k in range(n)], axis=0)
    placed = dot(hot.astype(BF16), incoming)
    mixed[...] = jnp.where(covered, placed, kv_text[:reach, :].astype(F32)).astype(BF16)
    groups = arrived.shape[2] // HD // kv_heads
    rows = groups * q_lots
    pages = base.shape[1]
    out[:, :pages, :] = base[...]
    for g in range(reach // PAGE):
        put_page(out, page_cap, slots[g], mixed[g * PAGE : (g + 1) * PAGE, :])
    first = pltpu.make_async_copy(out.at[:, :pages, :], sent.at[:, :pages, :], sems.at[0])
    first.start()
    for g in range(kv_heads):
        query = jnp.concatenate(
            [
                arrived[k, :q_lots, (g * groups + j) * HD : (g * groups + j + 1) * HD]
                for k in range(n)
                for j in range(groups)
            ],
            axis=0,
        )
        cols = slice(g * HD, (g + 1) * HD)
        vcols = slice(kvw + g * HD, kvw + (g + 1) * HD)
        key = jnp.concatenate([mixed[:, cols], kv_text[reach:, cols]], axis=0)
        value = jnp.concatenate([mixed[:, vcols], kv_text[reach:, vcols]], axis=0)
        scores = dot_t(key, query) * HD**-0.5 + bias[...]
        top = jnp.max(scores, axis=0, keepdims=True)
        weights = jnp.exp(scores - top)
        rows_held[g : g + 1, :] = top
        rows_held[kv_heads + g : kv_heads + g + 1, :] = jnp.sum(weights, axis=0, keepdims=True)
        numerator = lax.dot_general(
            weights.astype(BF16), value, (((0,), (0,)), ((), ())), preferred_element_type=F32
        )
        held[g * n * rows : (g + 1) * n * rows, :] = numerator
        own[g * rows : (g + 1) * rows, :] = held[pl.ds(pl.multiple_of((g * n + rank) * rows, rows), rows), :]
        numerator = numerator.astype(BF16)
        for k in range(n):
            to = order.index(section_of(k, n))
            out[to, pages + g * rows : pages + (g + 1) * rows, :] = numerator[k * rows : (k + 1) * rows, :]
    stat_rows = 2 * kv_heads
    share = HD // rows
    window = pl.ds(pl.multiple_of(rank // share * HD, HD), HD)
    own[kv_heads * rows : kv_heads * rows + stat_rows, :] = rows_held[:stat_rows, window]
    blank = jnp.zeros((PAGE - 3 * stat_rows, HD), F32)
    for w in range(-(-n // share)):
        stats = rows_held[:stat_rows, w * HD : (w + 1) * HD]
        lines = jnp.concatenate([*split_three(stats), blank], axis=0).astype(BF16)
        for k in range(w * share, min(n, (w + 1) * share)):
            out[order.index(section_of(k, n)), pages + kv_heads * rows :, :] = lines
    last = pltpu.make_async_copy(out.at[:, pages:, :], sent.at[:, pages:, :], sems.at[1])
    last.start()
    first.wait()
    last.wait()


def pick_column(row, rows, start):
    shape = (rows, HD)
    chosen = lax.broadcasted_iota(I32, shape, 1) == lax.broadcasted_iota(I32, shape, 0) + start
    return jnp.sum(jnp.where(chosen, row, 0.0), axis=1, keepdims=True)


def combine(pieces, highest):
    numerator, total = 0.0, 0.0
    for rows, top, weight in pieces:
        scale = jnp.exp(top - highest)
        numerator = numerator + rows * scale
        total = total + weight * scale
    return numerator, total


def fresh_kernel(n, kv_heads, steps, query, key, value, own, mine):
    rows = query.shape[0] // kv_heads
    every = kv_heads * rows
    start = rank_of(lax.axis_index("section"), n) % (HD // rows) * rows
    row = lax.broadcasted_iota(I32, (rows, steps), 0)
    causal = lax.broadcasted_iota(I32, (rows, steps), 1) <= row % steps
    tops, totals = [], []
    for g in range(kv_heads):
        cols = slice(g * HD, (g + 1) * HD)
        at = slice(g * rows, (g + 1) * rows)
        fresh = softmax_parts(query[at, :], key[:, cols], value[:, cols], causal)
        share = (
            own[at, :],
            pick_column(own[every + g : every + g + 1, :], rows, start),
            pick_column(own[every + kv_heads + g : every + kv_heads + g + 1, :], rows, start),
        )
        highest = jnp.maximum(fresh[1], share[1])
        numerator, total = combine((fresh, share), highest)
        mine[at, :] = numerator
        tops.append(highest)
        totals.append(total)
    line = column_to_row(jnp.concatenate(tops + totals, axis=0))
    mine[every:, :] = jnp.broadcast_to(line, (STAT, line.shape[1]))


def finish_kernel(kv_heads, steps, page_cap, shares, mine, attended, keys, values):
    n = shares.shape[0]
    pos = lax.axis_index("section")
    every = mine.shape[0] - STAT
    rows = every // kv_heads
    start = rank_of(pos, n) % (HD // rows) * rows
    chunk = page_cap * PAGE
    halves = keys.shape[2] // HD
    for k in range(n):
        for i, out in enumerate((keys, values)):
            for h in range(halves):
                part = i * halves + h
                out[page_section_of(k, n), :, h * HD : (h + 1) * HD] = shares[k, part * chunk : (part + 1) * chunk, :]
    pages = 2 * halves * chunk
    stats = row_to_column(mine[every : every + 1, :])
    lines = []
    for k in range(n):
        three = shares[k, pages + every :, :].astype(F32)
        size = 2 * kv_heads
        lines.append(three[:size] + three[size : 2 * size] + three[2 * size : 3 * size])
    for g in range(kv_heads):
        at = slice(g * rows, (g + 1) * rows)
        pieces = [(mine[at, :], stats[at], stats[every + g * rows : every + (g + 1) * rows])]
        for k in range(n):
            away = pos != page_section_of(k, n)
            top = jnp.where(away, pick_column(lines[k][g : g + 1], rows, start), LOWEST)
            weight = jnp.where(away, pick_column(lines[k][kv_heads + g : kv_heads + g + 1], rows, start), 0.0)
            share = shares[k, pages + g * rows : pages + (g + 1) * rows, :].astype(F32)
            pieces.append((share, top, weight))
        highest = pieces[0][1]
        for p in pieces[1:]:
            highest = jnp.maximum(highest, p[1])
        numerator, total = combine(pieces, highest)
        result = (numerator / total).astype(BF16)
        for h in range(rows // steps):
            to = (g * rows // steps + h) * HD
            attended[0, :, to : to + HD] = result[h * steps : (h + 1) * steps, :]


def body(
    text_rows,
    vis_rows,
    img_route,
    norm_gain,
    w_key,
    w_value,
    page_count,
    tail_len,
    page_dest,
    dec_req,
    dec_query,
    dec_key,
    dec_value,
):
    n = lax.axis_size("section")
    tok, half = text_rows.shape
    img = vis_rows.shape[0]
    kvw = w_key.shape[1]
    kv_heads = kvw // HD
    _, steps, q_width = dec_query.shape
    heads = q_width // HD
    q_rows = heads * steps
    blocks = tok // PAGE
    cap = max(2, (2 * img + n - 1) // n)
    page_cap = max(1, (blocks + n - 1) // n)

    def across(array):
        return lax.ppermute(array, "tensor", [(0, 1), (1, 0)])

    def exchange(array, section_at):
        order = [[section_at(rank, n) for rank in range(n)]]
        return lax.all_to_all(array, "section", split_axis=0, concat_axis=0, tiled=True, axis_index_groups=order)

    def remote(array):
        return pltpu.with_memory_space_constraint(array, pltpu.HBM)

    def local(array):
        return pltpu.with_memory_space_constraint(array, pltpu.VMEM)

    vis_far = across(vis_rows)
    text_far = across(text_rows)
    query = dec_query.reshape(steps, heads, HD).transpose(1, 0, 2).reshape(q_rows, HD)

    lot = -(-cap // PAGE) * PAGE
    q_lots = q_rows * HD // (2 * kvw)
    width = max(tok, n * lot)
    gain = norm_gain.reshape(1, 2 * half)
    arguments = (
        img_route.T,
        page_dest.T,
        page_count,
        tail_len,
        dec_req,
        w_key,
        w_value,
        vis_rows,
        gain,
        query,
    )
    info, slots, key_held, value_held, vis_near, gain_near, query_near = call(
        lambda *refs: prepare_kernel((n, img, tok, blocks, lot, page_cap), *refs),
        (
            jax.ShapeDtypeStruct((8, width), I32),
            jax.ShapeDtypeStruct((blocks,), I32),
            pltpu.VMEM((half, kvw), BF16),
            pltpu.VMEM((half, kvw), BF16),
            *[pltpu.VMEM(a.shape, a.dtype) for a in arguments[7:]],
        ),
        [ANY] * len(arguments),
        (VM, SM) + (VM,) * 5,
        [
            *[(pltpu.VMEM if i == 0 else pltpu.SMEM)(a.shape, a.dtype) for i, a in enumerate(arguments[:5])],
            pltpu.SMEM((n,), I32),
            pltpu.SemaphoreType.DMA((len(arguments),)),
        ],
        flops=1 << 20,
        traffic=2 * 2 * half * 2 * kvw * 2,
    )(*[remote(a) for a in arguments])

    step = min(1024, half)
    load = min(2048, half)

    packed = call(
        lambda *refs: vis_kernel(n, lot, load, step, *refs),
        pltpu.VMEM((n, q_lots + lot, 2 * kvw), BF16),
        [VM] * 6 + [ANY] * 2 + [VM],
        VM,
        [
            pltpu.VMEM((half, kvw), BF16),
            pltpu.VMEM((half, kvw), BF16),
            pltpu.VMEM((img, 2 * kvw), F32),
            pltpu.SemaphoreType.DMA((2 * half // load,)),
        ],
        flops=64 * img * 2 * half * 2 * kvw,
        traffic=2 * img * 2 * half + 8 * half * kvw,
    )(
        local(vis_near),
        vis_far,
        local(gain_near),
        local(query_near),
        local(key_held),
        local(value_held),
        remote(w_key),
        remote(w_value),
        info,
    )
    arrived = exchange(packed, section_of)

    block = page_cap * PAGE * 2 * kv_heads + q_rows + PAGE
    kv_text, bias, base = call(
        lambda *refs: text_kernel(load, step, page_cap, q_rows // kv_heads, *refs),
        (
            jax.ShapeDtypeStruct((tok, 2 * kvw), BF16),
            jax.ShapeDtypeStruct((tok, n * q_rows // kv_heads), F32),
            jax.ShapeDtypeStruct((n, block - q_rows - PAGE, HD), BF16),
        ),
        [ANY, VM, VM, ANY, ANY, VM, SM],
        (VM, VM, VM),
        [
            pltpu.VMEM((tok, half), BF16),
            pltpu.VMEM(w_key.shape, BF16),
            pltpu.VMEM(w_value.shape, BF16),
            pltpu.VMEM((tok, 2 * kvw), F32),
            pltpu.SemaphoreType.DMA((1 + 4 * half // load,)),
        ],
        limit=24,
        flops=2 * tok * 2 * half * 2 * kvw,
        traffic=2 * tok * 2 * half + 8 * half * kvw,
    )(remote(text_rows), text_far, remote(gain), remote(w_key), remote(w_value), info, slots)

    sent, own = call(
        lambda *refs: attend_kernel(n, cap, lot, page_cap, kv_heads, *refs),
        (
            jax.ShapeDtypeStruct((n, block, HD), BF16),
            jax.ShapeDtypeStruct((q_rows + STAT, HD), F32),
        ),
        [SM] + [VM] * 5,
        (ANY, VM),
        [
            pltpu.VMEM((n, block, HD), BF16),
            pltpu.VMEM((min(tok, n * cap), 2 * kvw), BF16),
            pltpu.VMEM((n * q_rows, HD), F32),
            pltpu.VMEM((STAT, n * q_rows // kv_heads), F32),
            pltpu.SemaphoreType.DMA((2,)),
        ],
        flops=4 * n * q_rows * tok * HD,
        traffic=n * (q_rows + STAT) * HD * 4,
    )(slots, info, kv_text, arrived, bias, base)
    shares = exchange(sent, page_section_of)

    mine = call(
        lambda *refs: fresh_kernel(n, kv_heads, steps, *refs),
        jax.ShapeDtypeStruct((q_rows + STAT, HD), F32),
        [VM] * 4,
        VM,
        flops=1 << 20,
        traffic=1 << 18,
    )(remote(query), remote(dec_key[0]), remote(dec_value[0]), own)

    slots_here = n * page_cap
    attended, cache_key, cache_value = call(
        lambda *refs: finish_kernel(kv_heads, steps, page_cap, *refs),
        (
            jax.ShapeDtypeStruct(dec_query.shape, BF16),
            jax.ShapeDtypeStruct((n, page_cap * PAGE, kvw), BF16),
            jax.ShapeDtypeStruct((n, page_cap * PAGE, kvw), BF16),
        ),
        [VM, VM],
        (VM, VM, VM),
        traffic=4 * tok * 2 * kvw,
    )(shares, mine)
    return (
        attended,
        cache_key.reshape(slots_here, PAGE, kvw),
        cache_value.reshape(slots_here, PAGE, kvw),
    )


def solution(mesh):
    return jax.shard_map(
        body,
        mesh=mesh,
        in_specs=(
            P(("groups", "section"), "tensor"),
            P(("groups", "section"), "tensor"),
            P("groups", None),
            P(),
            P(None, "tensor"),
            P(None, "tensor"),
            P("groups"),
            P("groups"),
            P("groups", None),
            P("groups"),
            P(("groups", "section"), None, "tensor"),
            P(("groups", "section"), None, "tensor"),
            P(("groups", "section"), None, "tensor"),
        ),
        out_specs=(
            P(("groups", "section"), None, "tensor"),
            P(("groups", "section"), None, "tensor"),
            P(("groups", "section"), None, "tensor"),
        ),
        check_vma=False,
    )
```

```python
import jax
import jax.numpy as jnp
from jax import lax
from jax.experimental import pallas as pl
from jax.experimental.pallas import tpu as pltpu
from jax.sharding import PartitionSpec as P

HD = 128
PAGE = 16
LOWEST = -1e30
EPS = 1e-06
STAT = 8
F32 = jnp.float32
BF16 = jnp.bfloat16
I32 = jnp.int32

VM = pl.BlockSpec(memory_space=pltpu.VMEM)
SM = pl.BlockSpec(memory_space=pltpu.SMEM)
ANY = pl.BlockSpec(memory_space=pl.ANY)
MIB = 1 << 20


def call(kernel, out_shape, in_specs, out_specs, scratch=(), limit=16, flops=0, traffic=0):
    return pl.pallas_call(
        kernel,
        out_shape=out_shape,
        in_specs=in_specs,
        out_specs=out_specs,
        scratch_shapes=list(scratch),
        compiler_params=pltpu.CompilerParams(vmem_limit_bytes=limit * MIB),
        cost_estimate=pl.CostEstimate(flops=flops, bytes_accessed=traffic, transcendentals=0),
    )


def rank_of(section, n):
    return jnp.where(section < n // 2, n - 2 - 2 * section, 2 * section - n + 1)


def section_of(rank, n):
    return n // 2 - 1 - rank // 2 + rank % 2 * (rank // 2 * 2 + 1)


def dot(a, b):
    return jnp.dot(a, b, preferred_element_type=F32)


def dot_t(a, b):
    return lax.dot_general(a, b, (((1,), (1,)), ((), ())), preferred_element_type=F32)


def diagonal(shape):
    return lax.broadcasted_iota(I32, shape, 0) == lax.broadcasted_iota(I32, shape, 1)


def column_to_row(column):
    rows = column.shape[0]
    return jnp.sum(jnp.where(diagonal((rows, rows)), column, 0.0), axis=0, keepdims=True)


def row_to_column(row):
    lanes = row.shape[1]
    return jnp.sum(jnp.where(diagonal((lanes, lanes)), row, 0.0), axis=1, keepdims=True)


def squares_of(rows):
    total = jnp.zeros((rows.shape[0], HD), F32)
    for c in range(0, rows.shape[1], HD):
        wide = rows[:, c : c + HD].astype(F32)
        total = total + wide * wide
    return total


def split_three(values):
    high = values.astype(BF16).astype(F32)
    rest = values - high
    middle = rest.astype(BF16).astype(F32)
    return high, middle, rest - middle


def softmax_parts(query, key, value, usable):
    scores = jnp.where(usable, dot_t(query, key) * HD**-0.5, LOWEST)
    top = jnp.max(scores, axis=1, keepdims=True)
    weights = jnp.where(usable, jnp.exp(scores - top), 0.0)
    return dot(weights.astype(BF16), value), top, jnp.sum(weights, axis=1, keepdims=True)


def prepare_kernel(n, lot, *refs):
    far, info, near, (route, sems) = refs[:6], refs[6], refs[7:12], refs[12:]
    img, half = near[2].shape
    first = pl.ds(pl.multiple_of(lax.axis_index("tensor") * half, half), near[0].shape[0])
    sources = (far[0], far[1].at[first], far[2].at[first], *far[3:])
    copies = [pltpu.make_async_copy(a, b, sems.at[i]) for i, (a, b) in enumerate(zip(sources, (route, *near)))]
    for c in copies:
        c.start()
    copies[0].wait()
    pos = lax.axis_index("section")
    own = jnp.zeros((1, img), I32)
    for e in range(n):
        own = jnp.where(pos == e, route[:, e * img : (e + 1) * img], own)
    marks = own == lax.broadcasted_iota(I32, (n, img), 0)
    ones = jnp.where(marks, 1.0, 0.0).astype(BF16)
    earlier = lax.broadcasted_iota(I32, (img, img), 0) < lax.broadcasted_iota(I32, (img, img), 1)
    prefix = dot(ones, jnp.where(earlier, 1.0, 0.0).astype(BF16))
    local = jnp.sum(jnp.where(marks, prefix, 0.0), axis=0, keepdims=True).astype(I32)
    info[...] = jnp.broadcast_to(rank_of(own, n) * lot + local, info.shape)
    for c in copies[1:]:
        c.wait()


def plan_tokens(n, img, lot, page_cap, small, info, slots, bias, starts):
    route, pages, count, tail, req = small
    pos = lax.axis_index("section")
    tok, width = bias.shape
    blocks = tok // PAGE
    lanes = lax.broadcasted_iota(I32, (1, n * lot), 1)
    source, inner = section_of(lanes // lot, n), lanes % lot
    fits = jnp.zeros((1, n * lot), I32)
    offset = jnp.zeros((1, n * lot), I32)
    for e in range(n):
        here = (route[:, e * img : (e + 1) * img] == pos).astype(I32)
        arriving = jnp.sum(here, axis=1, keepdims=True)
        fits = fits + jnp.where(source == e, arriving, 0)
        offset = offset + jnp.where(source > e, arriving, 0)
    info[...] = jnp.broadcast_to(jnp.where(inner < fits, offset + inner, -1), info.shape)
    total = jnp.int32(0)
    for r in range(n):
        starts[r] = total
        total = total + count[r]
    token = lax.broadcasted_iota(I32, (1, tok), 1) + pos * tok
    token_slot = jnp.full((1, tok), -1, I32)
    for b in range(n):
        r = req[b]
        first = starts[r] * PAGE
        last = first + (count[r] - 1) * PAGE + tail[r]
        token_slot = jnp.where((token >= first) & (token < last), b, token_slot)
    member = section_of(lax.broadcasted_iota(I32, (1, width), 1) // (width // n), n)
    bias[...] = jnp.where(row_to_column(token_slot.astype(F32)) == member.astype(F32), 0.0, LOWEST)
    for g in range(blocks):
        holder = pages[0, pos * blocks + g]
        slot = rank_of(holder, n) * page_cap
        for e in range(g):
            slot = slot + (pages[0, pos * blocks + e] == holder).astype(I32)
        slots[g] = slot


def scale_of(near, far):
    sums = jnp.sum(squares_of(near) + squares_of(far), axis=1, keepdims=True)
    return lax.rsqrt(sums / (2.0 * near.shape[1]) + EPS)


def normed_rows(rows, c, step, scale, gain):
    return (rows[:, c : c + step].astype(F32) * scale * gain).astype(BF16)


def add_part(total, at, normed, w, begin):
    part = dot(normed, w)
    columns = slice(at, at + part.shape[1])
    if begin:
        total[:, columns] = part
    else:
        total[:, columns] += part


def vis_kernel(n, lot, sizes, step, *refs):
    near, far, gain, query, key_held, value_held, w_key, w_value, info, out, key_rest, value_rest, total, sems = refs
    img, half = near.shape
    kvw = w_key.shape[1]
    me = lax.axis_index("tensor")
    held = key_held.shape[0]
    loads = {}
    at = held
    for size in sizes:
        side = me if at < half else 1 - me
        source = pl.ds(pl.multiple_of(side * half + at % half, size), size)
        number = 2 * len(loads)
        loads[at] = [
            pltpu.make_async_copy(w.at[source], kept.at[at - held : at - held + size], sems.at[number + i])
            for i, (w, kept) in enumerate(((w_key, key_rest), (w_value, value_rest)))
        ]
        for copy in loads[at]:
            copy.start()
        at += size
    scale = scale_of(near, far)
    for at in range(0, 2 * half, step):
        for copy in loads.get(at, ()):
            copy.wait()
        rows, side = (near, me) if at < half else (far, 1 - me)
        weights, w_at = ((key_held, value_held), at) if at < held else ((key_rest, value_rest), at - held)
        c = at % half
        columns = pl.ds(pl.multiple_of(side * half + c, step), step)
        normed = normed_rows(rows, c, step, scale, gain[:, columns])
        for w, col in zip(weights, (0, kvw)):
            add_part(total, col, normed, w[w_at : w_at + step, :], at == 0)
    slot = lax.broadcasted_iota(I32, (n * lot, img), 0)
    chosen = jnp.where(slot == info[0:1, :img], 1.0, 0.0).astype(BF16)
    packed = dot(chosen, total[...].astype(BF16)).astype(BF16)
    q_lots = out.shape[1] - lot
    for k in range(n):
        for j in range(query.shape[0] // q_lots):
            out[k, :q_lots, j * HD : (j + 1) * HD] = query[j * q_lots : (j + 1) * q_lots, :]
        out[k, q_lots:, :] = packed[k * lot : (k + 1) * lot, :]


def put_page(out, page_cap, slot, rows):
    chunk = page_cap * PAGE
    for h in range(rows.shape[1] // HD):
        at = pl.ds(pl.multiple_of((slot % page_cap) * PAGE + h * chunk, PAGE), PAGE)
        out[slot // page_cap, at, :] = rows[:, h * HD : (h + 1) * HD]


def text_kernel(n, img, lot, load, step, page_cap, *refs):
    (near_far, far, gain, w_key_far, w_value_far), small_far, refs = refs[:5], refs[5:10], refs[10:]
    (out, bias, base, info, slots), (near, w_key, w_value, total, starts, sems), small = refs[:5], refs[5:11], refs[11:]
    half = near.shape[1]
    kvw = w_key.shape[1]
    me = lax.axis_index("tensor")
    first = pltpu.make_async_copy(near_far, near, sems.at[0])
    first.start()
    used = sems.shape[0] - len(small)
    lists = [pltpu.make_async_copy(a, b, sems.at[used + i]) for i, (a, b) in enumerate(zip(small_far, small))]
    for copy in lists:
        copy.start()
    loads = []
    for side in (me, 1 - me):
        for c in range(0, half, load):
            at = len(loads) * load
            columns = pl.ds(pl.multiple_of(side * half + c, load), load)
            pair = [
                pltpu.make_async_copy(w.at[columns], held.at[at : at + load], sems.at[2 * len(loads) + i])
                for i, (w, held) in enumerate(((w_key_far, w_key), (w_value_far, w_value)), 1)
            ]
            for copy in pair:
                copy.start()
            loads.append(pair)
    sums = squares_of(far)
    for copy in lists:
        copy.wait()
    plan_tokens(n, img, lot, page_cap, small, info, slots, bias, starts)
    first.wait()
    sums = jnp.sum(squares_of(near) + sums, axis=1, keepdims=True)
    scale = lax.rsqrt(sums / (2.0 * half) + EPS)
    for i, pair in enumerate(loads):
        for copy in pair:
            copy.wait()
        for at in range(i * load, (i + 1) * load, step):
            rows, side = (near, me) if at < half else (far, 1 - me)
            c = at % half
            columns = pl.ds(pl.multiple_of(side * half + c, step), step)
            normed = normed_rows(rows, c, step, scale, gain[:, columns])
            for w, col in ((w_key, 0), (w_value, kvw)):
                add_part(total, col, normed, w[at : at + step, :], at == 0)
    out[...] = total[...].astype(BF16)
    base[...] = jnp.zeros(base.shape, BF16)
    tok = near.shape[0]
    for g in range(tok // PAGE):
        put_page(base, page_cap, slots[g], out[g * PAGE : (g + 1) * PAGE, :])


def attend_kernel(n, cap, lot, page_cap, kv_heads, slots, info, kv_text, arrived, bias, base, sent, own, *scratch):
    out, mixed, held, rows_held, sems = scratch
    rank = rank_of(lax.axis_index("section"), n)
    tok = kv_text.shape[0]
    kvw = kv_heads * HD
    q_lots = arrived.shape[1] - lot
    reach = min(tok, n * cap)
    hit = lax.broadcasted_iota(I32, (reach, n * lot), 0) == info[0:1, :]
    hot = jnp.where(hit, 1.0, 0.0)
    covered = jnp.sum(hot, axis=1, keepdims=True) > 0.0
    incoming = jnp.concatenate([arrived[k, q_lots:, :] for k in range(n)], axis=0)
    placed = dot(hot.astype(BF16), incoming)
    mixed[...] = jnp.where(covered, placed, kv_text[:reach, :].astype(F32)).astype(BF16)
    groups = arrived.shape[2] // HD // kv_heads
    rows = groups * q_lots
    pages = base.shape[1]
    out[:, :pages, :] = base[...]
    for g in range(reach // PAGE):
        put_page(out, page_cap, slots[g], mixed[g * PAGE : (g + 1) * PAGE, :])
    first = pltpu.make_async_copy(out.at[:, :pages, :], sent.at[:, :pages, :], sems.at[0])
    first.start()
    for g in range(kv_heads):
        query = jnp.concatenate(
            [
                arrived[k, :q_lots, (g * groups + j) * HD : (g * groups + j + 1) * HD]
                for k in range(n)
                for j in range(groups)
            ],
            axis=0,
        )
        cols = slice(g * HD, (g + 1) * HD)
        vcols = slice(kvw + g * HD, kvw + (g + 1) * HD)
        key = jnp.concatenate([mixed[:, cols], kv_text[reach:, cols]], axis=0)
        value = jnp.concatenate([mixed[:, vcols], kv_text[reach:, vcols]], axis=0)
        scores = dot_t(key, query) * HD**-0.5 + bias[...]
        top = jnp.max(scores, axis=0, keepdims=True)
        weights = jnp.exp(scores - top)
        rows_held[g : g + 1, :] = top
        rows_held[kv_heads + g : kv_heads + g + 1, :] = jnp.sum(weights, axis=0, keepdims=True)
        numerator = lax.dot_general(
            weights.astype(BF16), value, (((0,), (0,)), ((), ())), preferred_element_type=F32
        )
        held[g * n * rows : (g + 1) * n * rows, :] = numerator
        own[g * rows : (g + 1) * rows, :] = held[pl.ds(pl.multiple_of((g * n + rank) * rows, rows), rows), :]
        numerator = numerator.astype(BF16)
        for k in range(n):
            out[k, pages + g * rows : pages + (g + 1) * rows, :] = numerator[k * rows : (k + 1) * rows, :]
    stat_rows = 2 * kv_heads
    share = HD // rows
    window = pl.ds(pl.multiple_of(rank // share * HD, HD), HD)
    own[kv_heads * rows : kv_heads * rows + stat_rows, :] = rows_held[:stat_rows, window]
    blank = jnp.zeros((PAGE - 3 * stat_rows, HD), F32)
    for w in range(-(-n // share)):
        stats = rows_held[:stat_rows, w * HD : (w + 1) * HD]
        lines = jnp.concatenate([*split_three(stats), blank], axis=0).astype(BF16)
        for k in range(w * share, min(n, (w + 1) * share)):
            out[k, pages + kv_heads * rows :, :] = lines
    last = pltpu.make_async_copy(out.at[:, pages:, :], sent.at[:, pages:, :], sems.at[1])
    last.start()
    first.wait()
    last.wait()


def pick_column(row, rows, start):
    shape = (rows, HD)
    chosen = lax.broadcasted_iota(I32, shape, 1) == lax.broadcasted_iota(I32, shape, 0) + start
    return jnp.sum(jnp.where(chosen, row, 0.0), axis=1, keepdims=True)


def combine(pieces, highest):
    numerator, total = 0.0, 0.0
    for rows, top, weight in pieces:
        scale = jnp.exp(top - highest)
        numerator = numerator + rows * scale
        total = total + weight * scale
    return numerator, total


def fresh_kernel(n, kv_heads, steps, query, key, value, own, mine):
    rows = query.shape[0] // kv_heads
    every = kv_heads * rows
    start = rank_of(lax.axis_index("section"), n) % (HD // rows) * rows
    row = lax.broadcasted_iota(I32, (rows, steps), 0)
    causal = lax.broadcasted_iota(I32, (rows, steps), 1) <= row % steps
    tops, totals = [], []
    for g in range(kv_heads):
        cols = slice(g * HD, (g + 1) * HD)
        at = slice(g * rows, (g + 1) * rows)
        fresh = softmax_parts(query[at, :], key[:, cols], value[:, cols], causal)
        share = (
            own[at, :],
            pick_column(own[every + g : every + g + 1, :], rows, start),
            pick_column(own[every + kv_heads + g : every + kv_heads + g + 1, :], rows, start),
        )
        highest = jnp.maximum(fresh[1], share[1])
        numerator, total = combine((fresh, share), highest)
        mine[at, :] = numerator
        tops.append(highest)
        totals.append(total)
    line = column_to_row(jnp.concatenate(tops + totals, axis=0))
    mine[every:, :] = jnp.broadcast_to(line, (STAT, line.shape[1]))


def finish_kernel(kv_heads, steps, page_cap, shares, mine, attended, keys, values):
    n = shares.shape[0]
    pos = lax.axis_index("section")
    every = mine.shape[0] - STAT
    rows = every // kv_heads
    start = rank_of(pos, n) % (HD // rows) * rows
    chunk = page_cap * PAGE
    halves = keys.shape[2] // HD
    for k in range(n):
        for i, out in enumerate((keys, values)):
            for h in range(halves):
                part = i * halves + h
                out[section_of(k, n), :, h * HD : (h + 1) * HD] = shares[k, part * chunk : (part + 1) * chunk, :]
    pages = 2 * halves * chunk
    stats = row_to_column(mine[every : every + 1, :])
    lines = []
    for k in range(n):
        three = shares[k, pages + every :, :].astype(F32)
        size = 2 * kv_heads
        lines.append(three[:size] + three[size : 2 * size] + three[2 * size : 3 * size])
    for g in range(kv_heads):
        at = slice(g * rows, (g + 1) * rows)
        pieces = [(mine[at, :], stats[at], stats[every + g * rows : every + (g + 1) * rows])]
        for k in range(n):
            away = pos != section_of(k, n)
            top = jnp.where(away, pick_column(lines[k][g : g + 1], rows, start), LOWEST)
            weight = jnp.where(away, pick_column(lines[k][kv_heads + g : kv_heads + g + 1], rows, start), 0.0)
            share = shares[k, pages + g * rows : pages + (g + 1) * rows, :].astype(F32)
            pieces.append((share, top, weight))
        highest = pieces[0][1]
        for p in pieces[1:]:
            highest = jnp.maximum(highest, p[1])
        numerator, total = combine(pieces, highest)
        result = (numerator / total).astype(BF16)
        for h in range(rows // steps):
            to = (g * rows // steps + h) * HD
            attended[0, :, to : to + HD] = result[h * steps : (h + 1) * steps, :]


def body(
    text_rows,
    vis_rows,
    img_route,
    norm_gain,
    w_key,
    w_value,
    page_count,
    tail_len,
    page_dest,
    dec_req,
    dec_query,
    dec_key,
    dec_value,
):
    n = lax.axis_size("section")
    tok, half = text_rows.shape
    img = vis_rows.shape[0]
    kvw = w_key.shape[1]
    kv_heads = kvw // HD
    _, steps, q_width = dec_query.shape
    heads = q_width // HD
    q_rows = heads * steps
    blocks = tok // PAGE
    cap = max(2, (2 * img + n - 1) // n)
    page_cap = max(1, (blocks + n - 1) // n)

    def across(array):
        return lax.ppermute(array, "tensor", [(0, 1), (1, 0)])

    def exchange(array):
        order = [[section_of(rank, n) for rank in range(n)]]
        return lax.all_to_all(array, "section", split_axis=0, concat_axis=0, tiled=True, axis_index_groups=order)

    def remote(array):
        return pltpu.with_memory_space_constraint(array, pltpu.HBM)

    def local(array):
        return pltpu.with_memory_space_constraint(array, pltpu.VMEM)

    vis_far = across(vis_rows)
    text_far = across(text_rows)
    query = dec_query.reshape(steps, heads, HD).transpose(1, 0, 2).reshape(q_rows, HD)

    lot = -(-cap // PAGE) * PAGE
    q_lots = q_rows * HD // (2 * kvw)
    gain = norm_gain.reshape(1, 2 * half)
    load = min(2048, half)
    step = min(1024, load)
    kept = load
    arguments = (img_route.T, w_key, w_value, vis_rows, gain, query)
    info, key_held, value_held, vis_near, gain_near, query_near = call(
        lambda *refs: prepare_kernel(n, lot, *refs),
        (
            jax.ShapeDtypeStruct((STAT, img), I32),
            pltpu.VMEM((kept, kvw), BF16),
            pltpu.VMEM((kept, kvw), BF16),
            *[pltpu.VMEM(a.shape, a.dtype) for a in arguments[3:]],
        ),
        [ANY] * len(arguments),
        (VM,) * 6,
        [pltpu.VMEM((1, n * img), I32), pltpu.SemaphoreType.DMA((len(arguments),))],
        flops=1 << 20,
        traffic=2 * 2 * half * 2 * kvw * 2,
    )(*[remote(a) for a in arguments])

    left = 2 * half - kept
    sizes = [load] * (left // load - 1) + [step] * (load // step)
    packed = call(
        lambda *refs: vis_kernel(n, lot, sizes, step, *refs),
        pltpu.VMEM((n, q_lots + lot, 2 * kvw), BF16),
        [VM] * 6 + [ANY] * 2 + [VM],
        VM,
        [
            pltpu.VMEM((left, kvw), BF16),
            pltpu.VMEM((left, kvw), BF16),
            pltpu.VMEM((img, 2 * kvw), F32),
            pltpu.SemaphoreType.DMA((2 * len(sizes),)),
        ],
        flops=64 * img * 2 * half * 2 * kvw,
        traffic=2 * img * 2 * half + 8 * half * kvw,
    )(
        local(vis_near),
        vis_far,
        local(gain_near),
        local(query_near),
        local(key_held),
        local(value_held),
        remote(w_key),
        remote(w_value),
        info,
    )
    arrived = exchange(packed)

    block = page_cap * PAGE * 2 * kv_heads + q_rows + PAGE
    lists = (img_route.T, page_dest.T, page_count, tail_len, dec_req)
    kv_text, bias, base, info, slots = call(
        lambda *refs: text_kernel(n, img, lot, load, step, page_cap, *refs),
        (
            jax.ShapeDtypeStruct((tok, 2 * kvw), BF16),
            jax.ShapeDtypeStruct((tok, n * q_rows // kv_heads), F32),
            jax.ShapeDtypeStruct((n, block - q_rows - PAGE, HD), BF16),
            jax.ShapeDtypeStruct((STAT, n * lot), I32),
            jax.ShapeDtypeStruct((blocks,), I32),
        ),
        [ANY, VM, VM] + [ANY] * 7,
        (VM, VM, VM, VM, SM),
        [
            pltpu.VMEM((tok, half), BF16),
            pltpu.VMEM(w_key.shape, BF16),
            pltpu.VMEM(w_value.shape, BF16),
            pltpu.VMEM((tok, 2 * kvw), F32),
            pltpu.SMEM((n,), I32),
            pltpu.SemaphoreType.DMA((1 + 4 * half // load + len(lists),)),
            *[(pltpu.VMEM if i == 0 else pltpu.SMEM)(a.shape, a.dtype) for i, a in enumerate(lists)],
        ],
        limit=24,
        flops=2 * tok * 2 * half * 2 * kvw,
        traffic=2 * tok * 2 * half + 8 * half * kvw,
    )(remote(text_rows), text_far, remote(gain), remote(w_key), remote(w_value), *[remote(a) for a in lists])

    sent, own = call(
        lambda *refs: attend_kernel(n, cap, lot, page_cap, kv_heads, *refs),
        (
            jax.ShapeDtypeStruct((n, block, HD), BF16),
            jax.ShapeDtypeStruct((q_rows + STAT, HD), F32),
        ),
        [SM] + [VM] * 5,
        (ANY, VM),
        [
            pltpu.VMEM((n, block, HD), BF16),
            pltpu.VMEM((min(tok, n * cap), 2 * kvw), BF16),
            pltpu.VMEM((n * q_rows, HD), F32),
            pltpu.VMEM((STAT, n * q_rows // kv_heads), F32),
            pltpu.SemaphoreType.DMA((2,)),
        ],
        flops=4 * n * q_rows * tok * HD,
        traffic=n * (q_rows + STAT) * HD * 4,
    )(slots, info, kv_text, arrived, bias, base)
    shares = exchange(sent)

    mine = call(
        lambda *refs: fresh_kernel(n, kv_heads, steps, *refs),
        jax.ShapeDtypeStruct((q_rows + STAT, HD), F32),
        [VM] * 4,
        VM,
        flops=1 << 20,
        traffic=1 << 18,
    )(remote(query), remote(dec_key[0]), remote(dec_value[0]), own)

    slots_here = n * page_cap
    attended, cache_key, cache_value = call(
        lambda *refs: finish_kernel(kv_heads, steps, page_cap, *refs),
        (
            jax.ShapeDtypeStruct(dec_query.shape, BF16),
            jax.ShapeDtypeStruct((n, page_cap * PAGE, kvw), BF16),
            jax.ShapeDtypeStruct((n, page_cap * PAGE, kvw), BF16),
        ),
        [VM, VM],
        (VM, VM, VM),
        traffic=4 * tok * 2 * kvw,
    )(shares, mine)
    return (
        attended,
        cache_key.reshape(slots_here, PAGE, kvw),
        cache_value.reshape(slots_here, PAGE, kvw),
    )


def solution(mesh):
    return jax.shard_map(
        body,
        mesh=mesh,
        in_specs=(
            P(("groups", "section"), "tensor"),
            P(("groups", "section"), "tensor"),
            P("groups", None),
            P(),
            P(None, "tensor"),
            P(None, "tensor"),
            P("groups"),
            P("groups"),
            P("groups", None),
            P("groups"),
            P(("groups", "section"), None, "tensor"),
            P(("groups", "section"), None, "tensor"),
            P(("groups", "section"), None, "tensor"),
        ),
        out_specs=(
            P(("groups", "section"), None, "tensor"),
            P(("groups", "section"), None, "tensor"),
            P(("groups", "section"), None, "tensor"),
        ),
        check_vma=False,
    )
```

```python
import jax
import jax.numpy as jnp
from jax import lax
from jax.experimental import pallas as pl
from jax.experimental.pallas import tpu as pltpu
from jax.sharding import PartitionSpec as P

HD = 128
PAGE = 16
LOWEST = -1e30
EPS = 1e-06
STAT = 8
F32 = jnp.float32
BF16 = jnp.bfloat16
I32 = jnp.int32

VM = pl.BlockSpec(memory_space=pltpu.VMEM)
SM = pl.BlockSpec(memory_space=pltpu.SMEM)
ANY = pl.BlockSpec(memory_space=pl.ANY)
MIB = 1 << 20


def call(kernel, out_shape, in_specs, out_specs, scratch=(), limit=16, flops=0, traffic=0):
    return pl.pallas_call(
        kernel,
        out_shape=out_shape,
        in_specs=in_specs,
        out_specs=out_specs,
        scratch_shapes=list(scratch),
        compiler_params=pltpu.CompilerParams(vmem_limit_bytes=limit * MIB),
        cost_estimate=pl.CostEstimate(flops=flops, bytes_accessed=traffic, transcendentals=0),
    )


def rank_of(section, n):
    z, y, length = section // 2, section % 2, n // 2
    return (1 - y) * length + (z + length - n // 4 + 1) % length


def section_of(rank, n):
    length = n // 2
    return 2 * ((rank % length + n // 4 - 1) % length) + 1 - rank // length


def dot(a, b):
    return jnp.dot(a, b, preferred_element_type=F32)


def dot_t(a, b):
    return lax.dot_general(a, b, (((1,), (1,)), ((), ())), preferred_element_type=F32)


def diagonal(shape):
    return lax.broadcasted_iota(I32, shape, 0) == lax.broadcasted_iota(I32, shape, 1)


def column_to_row(column):
    rows = column.shape[0]
    return jnp.sum(jnp.where(diagonal((rows, rows)), column, 0.0), axis=0, keepdims=True)


def row_to_column(row):
    lanes = row.shape[1]
    return jnp.sum(jnp.where(diagonal((lanes, lanes)), row, 0.0), axis=1, keepdims=True)


def squares_of(rows):
    total = jnp.zeros((rows.shape[0], HD), F32)
    for c in range(0, rows.shape[1], HD):
        wide = rows[:, c : c + HD].astype(F32)
        total = total + wide * wide
    return total


def split_three(values):
    high = values.astype(BF16).astype(F32)
    rest = values - high
    middle = rest.astype(BF16).astype(F32)
    return high, middle, rest - middle


def softmax_parts(query, key, value, usable):
    scores = jnp.where(usable, dot_t(query, key) * HD**-0.5, LOWEST)
    top = jnp.max(scores, axis=1, keepdims=True)
    weights = jnp.where(usable, jnp.exp(scores - top), 0.0)
    return dot(weights.astype(BF16), value), top, jnp.sum(weights, axis=1, keepdims=True)


def prepare_kernel(n, lot, *refs):
    far, info, near, (route, sems) = refs[:6], refs[6], refs[7:12], refs[12:]
    img, half = near[2].shape
    first = pl.ds(pl.multiple_of(lax.axis_index("tensor") * half, half), near[0].shape[0])
    sources = (far[0], far[1].at[first], far[2].at[first], *far[3:])
    copies = [pltpu.make_async_copy(a, b, sems.at[i]) for i, (a, b) in enumerate(zip(sources, (route, *near)))]
    for c in copies:
        c.start()
    copies[0].wait()
    pos = lax.axis_index("section")
    own = jnp.zeros((1, img), I32)
    for e in range(n):
        own = jnp.where(pos == e, route[:, e * img : (e + 1) * img], own)
    marks = own == lax.broadcasted_iota(I32, (n, img), 0)
    ones = jnp.where(marks, 1.0, 0.0).astype(BF16)
    earlier = lax.broadcasted_iota(I32, (img, img), 0) < lax.broadcasted_iota(I32, (img, img), 1)
    prefix = dot(ones, jnp.where(earlier, 1.0, 0.0).astype(BF16))
    local = jnp.sum(jnp.where(marks, prefix, 0.0), axis=0, keepdims=True).astype(I32)
    info[...] = jnp.broadcast_to(rank_of(own, n) * lot + local, info.shape)
    for c in copies[1:]:
        c.wait()


def plan_tokens(n, img, lot, page_cap, small, info, slots, bias, starts):
    route, pages, count, tail, req = small
    pos = lax.axis_index("section")
    tok, width = bias.shape
    blocks = tok // PAGE
    lanes = lax.broadcasted_iota(I32, (1, n * lot), 1)
    source, inner = section_of(lanes // lot, n), lanes % lot
    fits = jnp.zeros((1, n * lot), I32)
    offset = jnp.zeros((1, n * lot), I32)
    for e in range(n):
        here = (route[:, e * img : (e + 1) * img] == pos).astype(I32)
        arriving = jnp.sum(here, axis=1, keepdims=True)
        fits = fits + jnp.where(source == e, arriving, 0)
        offset = offset + jnp.where(source > e, arriving, 0)
    info[...] = jnp.broadcast_to(jnp.where(inner < fits, offset + inner, -1), info.shape)
    total = jnp.int32(0)
    for r in range(n):
        starts[r] = total
        total = total + count[r]
    token = lax.broadcasted_iota(I32, (1, tok), 1) + pos * tok
    token_slot = jnp.full((1, tok), -1, I32)
    for b in range(n):
        r = req[b]
        first = starts[r] * PAGE
        last = first + (count[r] - 1) * PAGE + tail[r]
        token_slot = jnp.where((token >= first) & (token < last), b, token_slot)
    member = section_of(lax.broadcasted_iota(I32, (1, width), 1) // (width // n), n)
    bias[...] = jnp.where(row_to_column(token_slot.astype(F32)) == member.astype(F32), 0.0, LOWEST)
    for g in range(blocks):
        holder = pages[0, pos * blocks + g]
        slot = rank_of(holder, n) * page_cap
        for e in range(g):
            slot = slot + (pages[0, pos * blocks + e] == holder).astype(I32)
        slots[g] = slot


def scale_of(near, far):
    sums = jnp.sum(squares_of(near) + squares_of(far), axis=1, keepdims=True)
    return lax.rsqrt(sums / (2.0 * near.shape[1]) + EPS)


def normed_rows(rows, c, step, scale, gain):
    return (rows[:, c : c + step].astype(F32) * scale * gain).astype(BF16)


def add_part(total, at, normed, w, begin):
    part = dot(normed, w)
    columns = slice(at, at + part.shape[1])
    if begin:
        total[:, columns] = part
    else:
        total[:, columns] += part


def vis_kernel(n, lot, sizes, step, *refs):
    near, far, gain, query, key_held, value_held, w_key, w_value, info, out, key_rest, value_rest, total, sems = refs
    img, half = near.shape
    kvw = w_key.shape[1]
    me = lax.axis_index("tensor")
    held = key_held.shape[0]
    loads = {}
    at = held
    for size in sizes:
        side = me if at < half else 1 - me
        source = pl.ds(pl.multiple_of(side * half + at % half, size), size)
        number = 2 * len(loads)
        loads[at] = [
            pltpu.make_async_copy(w.at[source], kept.at[at - held : at - held + size], sems.at[number + i])
            for i, (w, kept) in enumerate(((w_key, key_rest), (w_value, value_rest)))
        ]
        for copy in loads[at]:
            copy.start()
        at += size
    scale = scale_of(near, far)
    for at in range(0, 2 * half, step):
        for copy in loads.get(at, ()):
            copy.wait()
        rows, side = (near, me) if at < half else (far, 1 - me)
        weights, w_at = ((key_held, value_held), at) if at < held else ((key_rest, value_rest), at - held)
        c = at % half
        columns = pl.ds(pl.multiple_of(side * half + c, step), step)
        normed = normed_rows(rows, c, step, scale, gain[:, columns])
        for w, col in zip(weights, (0, kvw)):
            add_part(total, col, normed, w[w_at : w_at + step, :], at == 0)
    slot = lax.broadcasted_iota(I32, (n * lot, img), 0)
    chosen = jnp.where(slot == info[0:1, :img], 1.0, 0.0).astype(BF16)
    packed = dot(chosen, total[...].astype(BF16)).astype(BF16)
    q_lots = out.shape[1] - lot
    for k in range(n):
        for j in range(query.shape[0] // q_lots):
            out[k, :q_lots, j * HD : (j + 1) * HD] = query[j * q_lots : (j + 1) * q_lots, :]
        out[k, q_lots:, :] = packed[k * lot : (k + 1) * lot, :]


def put_page(out, page_cap, slot, rows):
    chunk = page_cap * PAGE
    for h in range(rows.shape[1] // HD):
        at = pl.ds(pl.multiple_of((slot % page_cap) * PAGE + h * chunk, PAGE), PAGE)
        out[slot // page_cap, at, :] = rows[:, h * HD : (h + 1) * HD]


def text_kernel(n, img, lot, load, step, page_cap, *refs):
    (near_far, far, gain, w_key_far, w_value_far), small_far, refs = refs[:5], refs[5:10], refs[10:]
    (out, bias, base, info, slots), (near, w_key, w_value, total, starts, sems), small = refs[:5], refs[5:11], refs[11:]
    half = near.shape[1]
    kvw = w_key.shape[1]
    me = lax.axis_index("tensor")
    first = pltpu.make_async_copy(near_far, near, sems.at[0])
    first.start()
    used = sems.shape[0] - len(small)
    lists = [pltpu.make_async_copy(a, b, sems.at[used + i]) for i, (a, b) in enumerate(zip(small_far, small))]
    for copy in lists:
        copy.start()
    loads = []
    for side in (me, 1 - me):
        for c in range(0, half, load):
            at = len(loads) * load
            columns = pl.ds(pl.multiple_of(side * half + c, load), load)
            pair = [
                pltpu.make_async_copy(w.at[columns], held.at[at : at + load], sems.at[2 * len(loads) + i])
                for i, (w, held) in enumerate(((w_key_far, w_key), (w_value_far, w_value)), 1)
            ]
            for copy in pair:
                copy.start()
            loads.append(pair)
    sums = squares_of(far)
    for copy in lists:
        copy.wait()
    plan_tokens(n, img, lot, page_cap, small, info, slots, bias, starts)
    first.wait()
    sums = jnp.sum(squares_of(near) + sums, axis=1, keepdims=True)
    scale = lax.rsqrt(sums / (2.0 * half) + EPS)
    for i, pair in enumerate(loads):
        for copy in pair:
            copy.wait()
        for at in range(i * load, (i + 1) * load, step):
            rows, side = (near, me) if at < half else (far, 1 - me)
            c = at % half
            columns = pl.ds(pl.multiple_of(side * half + c, step), step)
            normed = normed_rows(rows, c, step, scale, gain[:, columns])
            for w, col in ((w_key, 0), (w_value, kvw)):
                add_part(total, col, normed, w[at : at + step, :], at == 0)
    out[...] = total[...].astype(BF16)
    base[...] = jnp.zeros(base.shape, BF16)
    tok = near.shape[0]
    for g in range(tok // PAGE):
        put_page(base, page_cap, slots[g], out[g * PAGE : (g + 1) * PAGE, :])


def attend_kernel(n, cap, lot, page_cap, kv_heads, slots, info, kv_text, arrived, bias, base, sent, own, *scratch):
    out, mixed, held, rows_held, sems = scratch
    rank = rank_of(lax.axis_index("section"), n)
    tok = kv_text.shape[0]
    kvw = kv_heads * HD
    q_lots = arrived.shape[1] - lot
    reach = min(tok, n * cap)
    hit = lax.broadcasted_iota(I32, (reach, n * lot), 0) == info[0:1, :]
    hot = jnp.where(hit, 1.0, 0.0)
    covered = jnp.sum(hot, axis=1, keepdims=True) > 0.0
    incoming = jnp.concatenate([arrived[k, q_lots:, :] for k in range(n)], axis=0)
    placed = dot(hot.astype(BF16), incoming)
    mixed[...] = jnp.where(covered, placed, kv_text[:reach, :].astype(F32)).astype(BF16)
    groups = arrived.shape[2] // HD // kv_heads
    rows = groups * q_lots
    pages = base.shape[1]
    out[:, :pages, :] = base[...]
    for g in range(reach // PAGE):
        put_page(out, page_cap, slots[g], mixed[g * PAGE : (g + 1) * PAGE, :])
    first = pltpu.make_async_copy(out.at[:, :pages, :], sent.at[:, :pages, :], sems.at[0])
    first.start()
    for g in range(kv_heads):
        query = jnp.concatenate(
            [
                arrived[k, :q_lots, (g * groups + j) * HD : (g * groups + j + 1) * HD]
                for k in range(n)
                for j in range(groups)
            ],
            axis=0,
        )
        cols = slice(g * HD, (g + 1) * HD)
        vcols = slice(kvw + g * HD, kvw + (g + 1) * HD)
        key = jnp.concatenate([mixed[:, cols], kv_text[reach:, cols]], axis=0)
        value = jnp.concatenate([mixed[:, vcols], kv_text[reach:, vcols]], axis=0)
        scores = dot_t(key, query) * HD**-0.5 + bias[...]
        top = jnp.max(scores, axis=0, keepdims=True)
        weights = jnp.exp(scores - top)
        rows_held[g : g + 1, :] = top
        rows_held[kv_heads + g : kv_heads + g + 1, :] = jnp.sum(weights, axis=0, keepdims=True)
        numerator = lax.dot_general(
            weights.astype(BF16), value, (((0,), (0,)), ((), ())), preferred_element_type=F32
        )
        held[g * n * rows : (g + 1) * n * rows, :] = numerator
        own[g * rows : (g + 1) * rows, :] = held[pl.ds(pl.multiple_of((g * n + rank) * rows, rows), rows), :]
        numerator = numerator.astype(BF16)
        for k in range(n):
            out[k, pages + g * rows : pages + (g + 1) * rows, :] = numerator[k * rows : (k + 1) * rows, :]
    stat_rows = 2 * kv_heads
    share = HD // rows
    window = pl.ds(pl.multiple_of(rank // share * HD, HD), HD)
    own[kv_heads * rows : kv_heads * rows + stat_rows, :] = rows_held[:stat_rows, window]
    blank = jnp.zeros((PAGE - 3 * stat_rows, HD), F32)
    for w in range(-(-n // share)):
        stats = rows_held[:stat_rows, w * HD : (w + 1) * HD]
        lines = jnp.concatenate([*split_three(stats), blank], axis=0).astype(BF16)
        for k in range(w * share, min(n, (w + 1) * share)):
            out[k, pages + kv_heads * rows :, :] = lines
    last = pltpu.make_async_copy(out.at[:, pages:, :], sent.at[:, pages:, :], sems.at[1])
    last.start()
    first.wait()
    last.wait()


def pick_column(row, rows, start):
    shape = (rows, HD)
    chosen = lax.broadcasted_iota(I32, shape, 1) == lax.broadcasted_iota(I32, shape, 0) + start
    return jnp.sum(jnp.where(chosen, row, 0.0), axis=1, keepdims=True)


def combine(pieces, highest):
    numerator, total = 0.0, 0.0
    for rows, top, weight in pieces:
        scale = jnp.exp(top - highest)
        numerator = numerator + rows * scale
        total = total + weight * scale
    return numerator, total


def fresh_kernel(n, kv_heads, steps, query, key, value, own, mine):
    rows = query.shape[0] // kv_heads
    every = kv_heads * rows
    start = rank_of(lax.axis_index("section"), n) % (HD // rows) * rows
    row = lax.broadcasted_iota(I32, (rows, steps), 0)
    causal = lax.broadcasted_iota(I32, (rows, steps), 1) <= row % steps
    tops, totals = [], []
    for g in range(kv_heads):
        cols = slice(g * HD, (g + 1) * HD)
        at = slice(g * rows, (g + 1) * rows)
        fresh = softmax_parts(query[at, :], key[:, cols], value[:, cols], causal)
        share = (
            own[at, :],
            pick_column(own[every + g : every + g + 1, :], rows, start),
            pick_column(own[every + kv_heads + g : every + kv_heads + g + 1, :], rows, start),
        )
        highest = jnp.maximum(fresh[1], share[1])
        numerator, total = combine((fresh, share), highest)
        mine[at, :] = numerator
        tops.append(highest)
        totals.append(total)
    line = column_to_row(jnp.concatenate(tops + totals, axis=0))
    mine[every:, :] = jnp.broadcast_to(line, (STAT, line.shape[1]))


def finish_kernel(kv_heads, steps, page_cap, shares, mine, attended, keys, values):
    n = shares.shape[0]
    pos = lax.axis_index("section")
    every = mine.shape[0] - STAT
    rows = every // kv_heads
    start = rank_of(pos, n) % (HD // rows) * rows
    chunk = page_cap * PAGE
    halves = keys.shape[2] // HD
    for k in range(n):
        for i, out in enumerate((keys, values)):
            for h in range(halves):
                part = i * halves + h
                out[section_of(k, n), :, h * HD : (h + 1) * HD] = shares[k, part * chunk : (part + 1) * chunk, :]
    pages = 2 * halves * chunk
    stats = row_to_column(mine[every : every + 1, :])
    lines = []
    for k in range(n):
        three = shares[k, pages + every :, :].astype(F32)
        size = 2 * kv_heads
        lines.append(three[:size] + three[size : 2 * size] + three[2 * size : 3 * size])
    for g in range(kv_heads):
        at = slice(g * rows, (g + 1) * rows)
        pieces = [(mine[at, :], stats[at], stats[every + g * rows : every + (g + 1) * rows])]
        for k in range(n):
            away = pos != section_of(k, n)
            top = jnp.where(away, pick_column(lines[k][g : g + 1], rows, start), LOWEST)
            weight = jnp.where(away, pick_column(lines[k][kv_heads + g : kv_heads + g + 1], rows, start), 0.0)
            share = shares[k, pages + g * rows : pages + (g + 1) * rows, :].astype(F32)
            pieces.append((share, top, weight))
        highest = pieces[0][1]
        for p in pieces[1:]:
            highest = jnp.maximum(highest, p[1])
        numerator, total = combine(pieces, highest)
        result = (numerator / total).astype(BF16)
        for h in range(rows // steps):
            to = (g * rows // steps + h) * HD
            attended[0, :, to : to + HD] = result[h * steps : (h + 1) * steps, :]


def body(
    text_rows,
    vis_rows,
    img_route,
    norm_gain,
    w_key,
    w_value,
    page_count,
    tail_len,
    page_dest,
    dec_req,
    dec_query,
    dec_key,
    dec_value,
):
    n = lax.axis_size("section")
    tok, half = text_rows.shape
    img = vis_rows.shape[0]
    kvw = w_key.shape[1]
    kv_heads = kvw // HD
    _, steps, q_width = dec_query.shape
    heads = q_width // HD
    q_rows = heads * steps
    blocks = tok // PAGE
    cap = max(2, (2 * img + n - 1) // n)
    page_cap = max(1, (blocks + n - 1) // n)

    def across(array):
        return lax.ppermute(array, "tensor", [(0, 1), (1, 0)])

    def exchange(array):
        order = [[section_of(rank, n) for rank in range(n)]]
        return lax.all_to_all(array, "section", split_axis=0, concat_axis=0, tiled=True, axis_index_groups=order)

    def remote(array):
        return pltpu.with_memory_space_constraint(array, pltpu.HBM)

    def local(array):
        return pltpu.with_memory_space_constraint(array, pltpu.VMEM)

    vis_far = across(vis_rows)
    text_far = across(text_rows)
    query = dec_query.reshape(steps, heads, HD).transpose(1, 0, 2).reshape(q_rows, HD)

    lot = -(-cap // PAGE) * PAGE
    q_lots = q_rows * HD // (2 * kvw)
    gain = norm_gain.reshape(1, 2 * half)
    load = min(2048, half)
    step = min(1024, load)
    kept = load
    arguments = (img_route.T, w_key, w_value, vis_rows, gain, query)
    info, key_held, value_held, vis_near, gain_near, query_near = call(
        lambda *refs: prepare_kernel(n, lot, *refs),
        (
            jax.ShapeDtypeStruct((STAT, img), I32),
            pltpu.VMEM((kept, kvw), BF16),
            pltpu.VMEM((kept, kvw), BF16),
            *[pltpu.VMEM(a.shape, a.dtype) for a in arguments[3:]],
        ),
        [ANY] * len(arguments),
        (VM,) * 6,
        [pltpu.VMEM((1, n * img), I32), pltpu.SemaphoreType.DMA((len(arguments),))],
        flops=1 << 20,
        traffic=2 * 2 * half * 2 * kvw * 2,
    )(*[remote(a) for a in arguments])

    left = 2 * half - kept
    sizes = [load] * (left // load - 1) + [step] * (load // step)
    packed = call(
        lambda *refs: vis_kernel(n, lot, sizes, step, *refs),
        pltpu.VMEM((n, q_lots + lot, 2 * kvw), BF16),
        [VM] * 6 + [ANY] * 2 + [VM],
        VM,
        [
            pltpu.VMEM((left, kvw), BF16),
            pltpu.VMEM((left, kvw), BF16),
            pltpu.VMEM((img, 2 * kvw), F32),
            pltpu.SemaphoreType.DMA((2 * len(sizes),)),
        ],
        flops=64 * img * 2 * half * 2 * kvw,
        traffic=2 * img * 2 * half + 8 * half * kvw,
    )(
        local(vis_near),
        vis_far,
        local(gain_near),
        local(query_near),
        local(key_held),
        local(value_held),
        remote(w_key),
        remote(w_value),
        info,
    )
    arrived = exchange(packed)

    block = page_cap * PAGE * 2 * kv_heads + q_rows + PAGE
    lists = (img_route.T, page_dest.T, page_count, tail_len, dec_req)
    kv_text, bias, base, info, slots = call(
        lambda *refs: text_kernel(n, img, lot, load, step, page_cap, *refs),
        (
            jax.ShapeDtypeStruct((tok, 2 * kvw), BF16),
            jax.ShapeDtypeStruct((tok, n * q_rows // kv_heads), F32),
            jax.ShapeDtypeStruct((n, block - q_rows - PAGE, HD), BF16),
            jax.ShapeDtypeStruct((STAT, n * lot), I32),
            jax.ShapeDtypeStruct((blocks,), I32),
        ),
        [ANY, VM, VM] + [ANY] * 7,
        (VM, VM, VM, VM, SM),
        [
            pltpu.VMEM((tok, half), BF16),
            pltpu.VMEM(w_key.shape, BF16),
            pltpu.VMEM(w_value.shape, BF16),
            pltpu.VMEM((tok, 2 * kvw), F32),
            pltpu.SMEM((n,), I32),
            pltpu.SemaphoreType.DMA((1 + 4 * half // load + len(lists),)),
            *[(pltpu.VMEM if i == 0 else pltpu.SMEM)(a.shape, a.dtype) for i, a in enumerate(lists)],
        ],
        limit=24,
        flops=2 * tok * 2 * half * 2 * kvw,
        traffic=2 * tok * 2 * half + 8 * half * kvw,
    )(remote(text_rows), text_far, remote(gain), remote(w_key), remote(w_value), *[remote(a) for a in lists])

    sent, own = call(
        lambda *refs: attend_kernel(n, cap, lot, page_cap, kv_heads, *refs),
        (
            jax.ShapeDtypeStruct((n, block, HD), BF16),
            jax.ShapeDtypeStruct((q_rows + STAT, HD), F32),
        ),
        [SM] + [VM] * 5,
        (ANY, VM),
        [
            pltpu.VMEM((n, block, HD), BF16),
            pltpu.VMEM((min(tok, n * cap), 2 * kvw), BF16),
            pltpu.VMEM((n * q_rows, HD), F32),
            pltpu.VMEM((STAT, n * q_rows // kv_heads), F32),
            pltpu.SemaphoreType.DMA((2,)),
        ],
        flops=4 * n * q_rows * tok * HD,
        traffic=n * (q_rows + STAT) * HD * 4,
    )(slots, info, kv_text, arrived, bias, base)
    shares = exchange(sent)

    mine = call(
        lambda *refs: fresh_kernel(n, kv_heads, steps, *refs),
        jax.ShapeDtypeStruct((q_rows + STAT, HD), F32),
        [VM] * 4,
        VM,
        flops=1 << 20,
        traffic=1 << 18,
    )(remote(query), remote(dec_key[0]), remote(dec_value[0]), own)

    slots_here = n * page_cap
    attended, cache_key, cache_value = call(
        lambda *refs: finish_kernel(kv_heads, steps, page_cap, *refs),
        (
            jax.ShapeDtypeStruct(dec_query.shape, BF16),
            jax.ShapeDtypeStruct((n, page_cap * PAGE, kvw), BF16),
            jax.ShapeDtypeStruct((n, page_cap * PAGE, kvw), BF16),
        ),
        [VM, VM],
        (VM, VM, VM),
        traffic=4 * tok * 2 * kvw,
    )(shares, mine)
    return (
        attended,
        cache_key.reshape(slots_here, PAGE, kvw),
        cache_value.reshape(slots_here, PAGE, kvw),
    )


def solution(mesh):
    return jax.shard_map(
        body,
        mesh=mesh,
        in_specs=(
            P(("groups", "section"), "tensor"),
            P(("groups", "section"), "tensor"),
            P("groups", None),
            P(),
            P(None, "tensor"),
            P(None, "tensor"),
            P("groups"),
            P("groups"),
            P("groups", None),
            P("groups"),
            P(("groups", "section"), None, "tensor"),
            P(("groups", "section"), None, "tensor"),
            P(("groups", "section"), None, "tensor"),
        ),
        out_specs=(
            P(("groups", "section"), None, "tensor"),
            P(("groups", "section"), None, "tensor"),
            P(("groups", "section"), None, "tensor"),
        ),
        check_vma=False,
    )
```

```python
import jax
import jax.numpy as jnp
from jax import lax
from jax.experimental import pallas as pl
from jax.experimental.pallas import tpu as pltpu
from jax.sharding import PartitionSpec as P

HD = 128
PAGE = 16
LOWEST = -1e30
EPS = 1e-06
STAT = 8
F32 = jnp.float32
BF16 = jnp.bfloat16
I32 = jnp.int32

VM = pl.BlockSpec(memory_space=pltpu.VMEM)
SM = pl.BlockSpec(memory_space=pltpu.SMEM)
ANY = pl.BlockSpec(memory_space=pl.ANY)
MIB = 1 << 20


def call(kernel, out_shape, in_specs, out_specs, scratch=(), limit=16, flops=0, traffic=0):
    return pl.pallas_call(
        kernel,
        out_shape=out_shape,
        in_specs=in_specs,
        out_specs=out_specs,
        scratch_shapes=list(scratch),
        compiler_params=pltpu.CompilerParams(vmem_limit_bytes=limit * MIB),
        cost_estimate=pl.CostEstimate(flops=flops, bytes_accessed=traffic, transcendentals=0),
    )


def rank_of(section, n):
    z, y, length = section // 2, section % 2, n // 2
    return (1 - y) * length + (2 * length - z - n // 4) % length


def section_of(rank, n):
    length = n // 2
    return 2 * (length - 1 - (rank % length + n // 4 - 1) % length) + 1 - rank // length


def dot(a, b):
    return jnp.dot(a, b, preferred_element_type=F32)


def dot_t(a, b):
    return lax.dot_general(a, b, (((1,), (1,)), ((), ())), preferred_element_type=F32)


def diagonal(shape):
    return lax.broadcasted_iota(I32, shape, 0) == lax.broadcasted_iota(I32, shape, 1)


def column_to_row(column):
    rows = column.shape[0]
    return jnp.sum(jnp.where(diagonal((rows, rows)), column, 0.0), axis=0, keepdims=True)


def row_to_column(row):
    lanes = row.shape[1]
    return jnp.sum(jnp.where(diagonal((lanes, lanes)), row, 0.0), axis=1, keepdims=True)


def squares_of(rows):
    total = jnp.zeros((rows.shape[0], HD), F32)
    for c in range(0, rows.shape[1], HD):
        wide = rows[:, c : c + HD].astype(F32)
        total = total + wide * wide
    return total


def split_three(values):
    high = values.astype(BF16).astype(F32)
    rest = values - high
    middle = rest.astype(BF16).astype(F32)
    return high, middle, rest - middle


def softmax_parts(query, key, value, usable):
    scores = jnp.where(usable, dot_t(query, key) * HD**-0.5, LOWEST)
    top = jnp.max(scores, axis=1, keepdims=True)
    weights = jnp.where(usable, jnp.exp(scores - top), 0.0)
    return dot(weights.astype(BF16), value), top, jnp.sum(weights, axis=1, keepdims=True)


def prepare_kernel(n, lot, *refs):
    far, info, near, (route, sems) = refs[:6], refs[6], refs[7:12], refs[12:]
    img, half = near[2].shape
    first = pl.ds(pl.multiple_of(lax.axis_index("tensor") * half, half), near[0].shape[0])
    sources = (far[0], far[1].at[first], far[2].at[first], *far[3:])
    copies = [pltpu.make_async_copy(a, b, sems.at[i]) for i, (a, b) in enumerate(zip(sources, (route, *near)))]
    for c in copies:
        c.start()
    copies[0].wait()
    pos = lax.axis_index("section")
    own = jnp.zeros((1, img), I32)
    for e in range(n):
        own = jnp.where(pos == e, route[:, e * img : (e + 1) * img], own)
    marks = own == lax.broadcasted_iota(I32, (n, img), 0)
    ones = jnp.where(marks, 1.0, 0.0).astype(BF16)
    earlier = lax.broadcasted_iota(I32, (img, img), 0) < lax.broadcasted_iota(I32, (img, img), 1)
    prefix = dot(ones, jnp.where(earlier, 1.0, 0.0).astype(BF16))
    local = jnp.sum(jnp.where(marks, prefix, 0.0), axis=0, keepdims=True).astype(I32)
    info[...] = jnp.broadcast_to(rank_of(own, n) * lot + local, info.shape)
    for c in copies[1:]:
        c.wait()


def plan_tokens(n, img, lot, page_cap, small, info, slots, bias, starts):
    route, pages, count, tail, req = small
    pos = lax.axis_index("section")
    tok, width = bias.shape
    blocks = tok // PAGE
    lanes = lax.broadcasted_iota(I32, (1, n * lot), 1)
    source, inner = section_of(lanes // lot, n), lanes % lot
    fits = jnp.zeros((1, n * lot), I32)
    offset = jnp.zeros((1, n * lot), I32)
    for e in range(n):
        here = (route[:, e * img : (e + 1) * img] == pos).astype(I32)
        arriving = jnp.sum(here, axis=1, keepdims=True)
        fits = fits + jnp.where(source == e, arriving, 0)
        offset = offset + jnp.where(source > e, arriving, 0)
    info[...] = jnp.broadcast_to(jnp.where(inner < fits, offset + inner, -1), info.shape)
    total = jnp.int32(0)
    for r in range(n):
        starts[r] = total
        total = total + count[r]
    token = lax.broadcasted_iota(I32, (1, tok), 1) + pos * tok
    token_slot = jnp.full((1, tok), -1, I32)
    for b in range(n):
        r = req[b]
        first = starts[r] * PAGE
        last = first + (count[r] - 1) * PAGE + tail[r]
        token_slot = jnp.where((token >= first) & (token < last), b, token_slot)
    member = section_of(lax.broadcasted_iota(I32, (1, width), 1) // (width // n), n)
    bias[...] = jnp.where(row_to_column(token_slot.astype(F32)) == member.astype(F32), 0.0, LOWEST)
    for g in range(blocks):
        holder = pages[0, pos * blocks + g]
        slot = rank_of(holder, n) * page_cap
        for e in range(g):
            slot = slot + (pages[0, pos * blocks + e] == holder).astype(I32)
        slots[g] = slot


def scale_of(near, far):
    sums = jnp.sum(squares_of(near) + squares_of(far), axis=1, keepdims=True)
    return lax.rsqrt(sums / (2.0 * near.shape[1]) + EPS)


def normed_rows(rows, c, step, scale, gain):
    return (rows[:, c : c + step].astype(F32) * scale * gain).astype(BF16)


def add_part(total, at, normed, w, begin):
    part = dot(normed, w)
    columns = slice(at, at + part.shape[1])
    if begin:
        total[:, columns] = part
    else:
        total[:, columns] += part


def vis_kernel(n, lot, sizes, step, *refs):
    near, far, gain, query, key_held, value_held, w_key, w_value, info, out, key_rest, value_rest, total, sems = refs
    img, half = near.shape
    kvw = w_key.shape[1]
    me = lax.axis_index("tensor")
    held = key_held.shape[0]
    loads = {}
    at = held
    for size in sizes:
        side = me if at < half else 1 - me
        source = pl.ds(pl.multiple_of(side * half + at % half, size), size)
        number = 2 * len(loads)
        loads[at] = [
            pltpu.make_async_copy(w.at[source], kept.at[at - held : at - held + size], sems.at[number + i])
            for i, (w, kept) in enumerate(((w_key, key_rest), (w_value, value_rest)))
        ]
        for copy in loads[at]:
            copy.start()
        at += size
    scale = scale_of(near, far)
    for at in range(0, 2 * half, step):
        for copy in loads.get(at, ()):
            copy.wait()
        rows, side = (near, me) if at < half else (far, 1 - me)
        weights, w_at = ((key_held, value_held), at) if at < held else ((key_rest, value_rest), at - held)
        c = at % half
        columns = pl.ds(pl.multiple_of(side * half + c, step), step)
        normed = normed_rows(rows, c, step, scale, gain[:, columns])
        for w, col in zip(weights, (0, kvw)):
            add_part(total, col, normed, w[w_at : w_at + step, :], at == 0)
    slot = lax.broadcasted_iota(I32, (n * lot, img), 0)
    chosen = jnp.where(slot == info[0:1, :img], 1.0, 0.0).astype(BF16)
    packed = dot(chosen, total[...].astype(BF16)).astype(BF16)
    q_lots = out.shape[1] - lot
    for k in range(n):
        for j in range(query.shape[0] // q_lots):
            out[k, :q_lots, j * HD : (j + 1) * HD] = query[j * q_lots : (j + 1) * q_lots, :]
        out[k, q_lots:, :] = packed[k * lot : (k + 1) * lot, :]


def put_page(out, page_cap, slot, rows):
    chunk = page_cap * PAGE
    for h in range(rows.shape[1] // HD):
        at = pl.ds(pl.multiple_of((slot % page_cap) * PAGE + h * chunk, PAGE), PAGE)
        out[slot // page_cap, at, :] = rows[:, h * HD : (h + 1) * HD]


def text_kernel(n, img, lot, load, step, page_cap, *refs):
    (near_far, far, gain, w_key_far, w_value_far), small_far, refs = refs[:5], refs[5:10], refs[10:]
    (out, bias, base, info, slots), (near, w_key, w_value, total, starts, sems), small = refs[:5], refs[5:11], refs[11:]
    half = near.shape[1]
    kvw = w_key.shape[1]
    me = lax.axis_index("tensor")
    first = pltpu.make_async_copy(near_far, near, sems.at[0])
    first.start()
    used = sems.shape[0] - len(small)
    lists = [pltpu.make_async_copy(a, b, sems.at[used + i]) for i, (a, b) in enumerate(zip(small_far, small))]
    for copy in lists:
        copy.start()
    loads = []
    for side in (me, 1 - me):
        for c in range(0, half, load):
            at = len(loads) * load
            columns = pl.ds(pl.multiple_of(side * half + c, load), load)
            pair = [
                pltpu.make_async_copy(w.at[columns], held.at[at : at + load], sems.at[2 * len(loads) + i])
                for i, (w, held) in enumerate(((w_key_far, w_key), (w_value_far, w_value)), 1)
            ]
            for copy in pair:
                copy.start()
            loads.append(pair)
    sums = squares_of(far)
    for copy in lists:
        copy.wait()
    plan_tokens(n, img, lot, page_cap, small, info, slots, bias, starts)
    first.wait()
    sums = jnp.sum(squares_of(near) + sums, axis=1, keepdims=True)
    scale = lax.rsqrt(sums / (2.0 * half) + EPS)
    for i, pair in enumerate(loads):
        for copy in pair:
            copy.wait()
        for at in range(i * load, (i + 1) * load, step):
            rows, side = (near, me) if at < half else (far, 1 - me)
            c = at % half
            columns = pl.ds(pl.multiple_of(side * half + c, step), step)
            normed = normed_rows(rows, c, step, scale, gain[:, columns])
            for w, col in ((w_key, 0), (w_value, kvw)):
                add_part(total, col, normed, w[at : at + step, :], at == 0)
    out[...] = total[...].astype(BF16)
    base[...] = jnp.zeros(base.shape, BF16)
    tok = near.shape[0]
    for g in range(tok // PAGE):
        put_page(base, page_cap, slots[g], out[g * PAGE : (g + 1) * PAGE, :])


def attend_kernel(n, cap, lot, page_cap, kv_heads, slots, info, kv_text, arrived, bias, base, sent, own, *scratch):
    out, mixed, held, rows_held, sems = scratch
    rank = rank_of(lax.axis_index("section"), n)
    tok = kv_text.shape[0]
    kvw = kv_heads * HD
    q_lots = arrived.shape[1] - lot
    reach = min(tok, n * cap)
    hit = lax.broadcasted_iota(I32, (reach, n * lot), 0) == info[0:1, :]
    hot = jnp.where(hit, 1.0, 0.0)
    covered = jnp.sum(hot, axis=1, keepdims=True) > 0.0
    incoming = jnp.concatenate([arrived[k, q_lots:, :] for k in range(n)], axis=0)
    placed = dot(hot.astype(BF16), incoming)
    mixed[...] = jnp.where(covered, placed, kv_text[:reach, :].astype(F32)).astype(BF16)
    groups = arrived.shape[2] // HD // kv_heads
    rows = groups * q_lots
    pages = base.shape[1]
    out[:, :pages, :] = base[...]
    for g in range(reach // PAGE):
        put_page(out, page_cap, slots[g], mixed[g * PAGE : (g + 1) * PAGE, :])
    first = pltpu.make_async_copy(out.at[:, :pages, :], sent.at[:, :pages, :], sems.at[0])
    first.start()
    for g in range(kv_heads):
        query = jnp.concatenate(
            [
                arrived[k, :q_lots, (g * groups + j) * HD : (g * groups + j + 1) * HD]
                for k in range(n)
                for j in range(groups)
            ],
            axis=0,
        )
        cols = slice(g * HD, (g + 1) * HD)
        vcols = slice(kvw + g * HD, kvw + (g + 1) * HD)
        key = jnp.concatenate([mixed[:, cols], kv_text[reach:, cols]], axis=0)
        value = jnp.concatenate([mixed[:, vcols], kv_text[reach:, vcols]], axis=0)
        scores = dot_t(key, query) * HD**-0.5 + bias[...]
        top = jnp.max(scores, axis=0, keepdims=True)
        weights = jnp.exp(scores - top)
        rows_held[g : g + 1, :] = top
        rows_held[kv_heads + g : kv_heads + g + 1, :] = jnp.sum(weights, axis=0, keepdims=True)
        numerator = lax.dot_general(
            weights.astype(BF16), value, (((0,), (0,)), ((), ())), preferred_element_type=F32
        )
        held[g * n * rows : (g + 1) * n * rows, :] = numerator
        own[g * rows : (g + 1) * rows, :] = held[pl.ds(pl.multiple_of((g * n + rank) * rows, rows), rows), :]
        numerator = numerator.astype(BF16)
        for k in range(n):
            out[k, pages + g * rows : pages + (g + 1) * rows, :] = numerator[k * rows : (k + 1) * rows, :]
    stat_rows = 2 * kv_heads
    share = HD // rows
    window = pl.ds(pl.multiple_of(rank // share * HD, HD), HD)
    own[kv_heads * rows : kv_heads * rows + stat_rows, :] = rows_held[:stat_rows, window]
    blank = jnp.zeros((PAGE - 3 * stat_rows, HD), F32)
    for w in range(-(-n // share)):
        stats = rows_held[:stat_rows, w * HD : (w + 1) * HD]
        lines = jnp.concatenate([*split_three(stats), blank], axis=0).astype(BF16)
        for k in range(w * share, min(n, (w + 1) * share)):
            out[k, pages + kv_heads * rows :, :] = lines
    last = pltpu.make_async_copy(out.at[:, pages:, :], sent.at[:, pages:, :], sems.at[1])
    last.start()
    first.wait()
    last.wait()


def pick_column(row, rows, start):
    shape = (rows, HD)
    chosen = lax.broadcasted_iota(I32, shape, 1) == lax.broadcasted_iota(I32, shape, 0) + start
    return jnp.sum(jnp.where(chosen, row, 0.0), axis=1, keepdims=True)


def combine(pieces, highest):
    numerator, total = 0.0, 0.0
    for rows, top, weight in pieces:
        scale = jnp.exp(top - highest)
        numerator = numerator + rows * scale
        total = total + weight * scale
    return numerator, total


def fresh_kernel(n, kv_heads, steps, query, key, value, own, mine):
    rows = query.shape[0] // kv_heads
    every = kv_heads * rows
    start = rank_of(lax.axis_index("section"), n) % (HD // rows) * rows
    row = lax.broadcasted_iota(I32, (rows, steps), 0)
    causal = lax.broadcasted_iota(I32, (rows, steps), 1) <= row % steps
    tops, totals = [], []
    for g in range(kv_heads):
        cols = slice(g * HD, (g + 1) * HD)
        at = slice(g * rows, (g + 1) * rows)
        fresh = softmax_parts(query[at, :], key[:, cols], value[:, cols], causal)
        share = (
            own[at, :],
            pick_column(own[every + g : every + g + 1, :], rows, start),
            pick_column(own[every + kv_heads + g : every + kv_heads + g + 1, :], rows, start),
        )
        highest = jnp.maximum(fresh[1], share[1])
        numerator, total = combine((fresh, share), highest)
        mine[at, :] = numerator
        tops.append(highest)
        totals.append(total)
    line = column_to_row(jnp.concatenate(tops + totals, axis=0))
    mine[every:, :] = jnp.broadcast_to(line, (STAT, line.shape[1]))


def finish_kernel(kv_heads, steps, page_cap, shares, mine, attended, keys, values):
    n = shares.shape[0]
    pos = lax.axis_index("section")
    every = mine.shape[0] - STAT
    rows = every // kv_heads
    start = rank_of(pos, n) % (HD // rows) * rows
    chunk = page_cap * PAGE
    halves = keys.shape[2] // HD
    for k in range(n):
        for i, out in enumerate((keys, values)):
            for h in range(halves):
                part = i * halves + h
                out[section_of(k, n), :, h * HD : (h + 1) * HD] = shares[k, part * chunk : (part + 1) * chunk, :]
    pages = 2 * halves * chunk
    stats = row_to_column(mine[every : every + 1, :])
    lines = []
    for k in range(n):
        three = shares[k, pages + every :, :].astype(F32)
        size = 2 * kv_heads
        lines.append(three[:size] + three[size : 2 * size] + three[2 * size : 3 * size])
    for g in range(kv_heads):
        at = slice(g * rows, (g + 1) * rows)
        pieces = [(mine[at, :], stats[at], stats[every + g * rows : every + (g + 1) * rows])]
        for k in range(n):
            away = pos != section_of(k, n)
            top = jnp.where(away, pick_column(lines[k][g : g + 1], rows, start), LOWEST)
            weight = jnp.where(away, pick_column(lines[k][kv_heads + g : kv_heads + g + 1], rows, start), 0.0)
            share = shares[k, pages + g * rows : pages + (g + 1) * rows, :].astype(F32)
            pieces.append((share, top, weight))
        highest = pieces[0][1]
        for p in pieces[1:]:
            highest = jnp.maximum(highest, p[1])
        numerator, total = combine(pieces, highest)
        result = (numerator / total).astype(BF16)
        for h in range(rows // steps):
            to = (g * rows // steps + h) * HD
            attended[0, :, to : to + HD] = result[h * steps : (h + 1) * steps, :]


def body(
    text_rows,
    vis_rows,
    img_route,
    norm_gain,
    w_key,
    w_value,
    page_count,
    tail_len,
    page_dest,
    dec_req,
    dec_query,
    dec_key,
    dec_value,
):
    n = lax.axis_size("section")
    tok, half = text_rows.shape
    img = vis_rows.shape[0]
    kvw = w_key.shape[1]
    kv_heads = kvw // HD
    _, steps, q_width = dec_query.shape
    heads = q_width // HD
    q_rows = heads * steps
    blocks = tok // PAGE
    cap = max(2, (2 * img + n - 1) // n)
    page_cap = max(1, (blocks + n - 1) // n)

    def across(array):
        return lax.ppermute(array, "tensor", [(0, 1), (1, 0)])

    def exchange(array):
        order = [[section_of(rank, n) for rank in range(n)]]
        return lax.all_to_all(array, "section", split_axis=0, concat_axis=0, tiled=True, axis_index_groups=order)

    def remote(array):
        return pltpu.with_memory_space_constraint(array, pltpu.HBM)

    def local(array):
        return pltpu.with_memory_space_constraint(array, pltpu.VMEM)

    vis_far = across(vis_rows)
    text_far = across(text_rows)
    query = dec_query.reshape(steps, heads, HD).transpose(1, 0, 2).reshape(q_rows, HD)

    lot = -(-cap // PAGE) * PAGE
    q_lots = q_rows * HD // (2 * kvw)
    gain = norm_gain.reshape(1, 2 * half)
    load = min(2048, half)
    step = min(1024, load)
    kept = load
    arguments = (img_route.T, w_key, w_value, vis_rows, gain, query)
    info, key_held, value_held, vis_near, gain_near, query_near = call(
        lambda *refs: prepare_kernel(n, lot, *refs),
        (
            jax.ShapeDtypeStruct((STAT, img), I32),
            pltpu.VMEM((kept, kvw), BF16),
            pltpu.VMEM((kept, kvw), BF16),
            *[pltpu.VMEM(a.shape, a.dtype) for a in arguments[3:]],
        ),
        [ANY] * len(arguments),
        (VM,) * 6,
        [pltpu.VMEM((1, n * img), I32), pltpu.SemaphoreType.DMA((len(arguments),))],
        flops=1 << 20,
        traffic=2 * 2 * half * 2 * kvw * 2,
    )(*[remote(a) for a in arguments])

    left = 2 * half - kept
    sizes = [load] * (left // load - 1) + [step] * (load // step)
    packed = call(
        lambda *refs: vis_kernel(n, lot, sizes, step, *refs),
        pltpu.VMEM((n, q_lots + lot, 2 * kvw), BF16),
        [VM] * 6 + [ANY] * 2 + [VM],
        VM,
        [
            pltpu.VMEM((left, kvw), BF16),
            pltpu.VMEM((left, kvw), BF16),
            pltpu.VMEM((img, 2 * kvw), F32),
            pltpu.SemaphoreType.DMA((2 * len(sizes),)),
        ],
        flops=64 * img * 2 * half * 2 * kvw,
        traffic=2 * img * 2 * half + 8 * half * kvw,
    )(
        local(vis_near),
        vis_far,
        local(gain_near),
        local(query_near),
        local(key_held),
        local(value_held),
        remote(w_key),
        remote(w_value),
        info,
    )
    arrived = exchange(packed)

    block = page_cap * PAGE * 2 * kv_heads + q_rows + PAGE
    lists = (img_route.T, page_dest.T, page_count, tail_len, dec_req)
    kv_text, bias, base, info, slots = call(
        lambda *refs: text_kernel(n, img, lot, load, step, page_cap, *refs),
        (
            jax.ShapeDtypeStruct((tok, 2 * kvw), BF16),
            jax.ShapeDtypeStruct((tok, n * q_rows // kv_heads), F32),
            jax.ShapeDtypeStruct((n, block - q_rows - PAGE, HD), BF16),
            jax.ShapeDtypeStruct((STAT, n * lot), I32),
            jax.ShapeDtypeStruct((blocks,), I32),
        ),
        [ANY, VM, VM] + [ANY] * 7,
        (VM, VM, VM, VM, SM),
        [
            pltpu.VMEM((tok, half), BF16),
            pltpu.VMEM(w_key.shape, BF16),
            pltpu.VMEM(w_value.shape, BF16),
            pltpu.VMEM((tok, 2 * kvw), F32),
            pltpu.SMEM((n,), I32),
            pltpu.SemaphoreType.DMA((1 + 4 * half // load + len(lists),)),
            *[(pltpu.VMEM if i == 0 else pltpu.SMEM)(a.shape, a.dtype) for i, a in enumerate(lists)],
        ],
        limit=24,
        flops=2 * tok * 2 * half * 2 * kvw,
        traffic=2 * tok * 2 * half + 8 * half * kvw,
    )(remote(text_rows), text_far, remote(gain), remote(w_key), remote(w_value), *[remote(a) for a in lists])

    sent, own = call(
        lambda *refs: attend_kernel(n, cap, lot, page_cap, kv_heads, *refs),
        (
            jax.ShapeDtypeStruct((n, block, HD), BF16),
            jax.ShapeDtypeStruct((q_rows + STAT, HD), F32),
        ),
        [SM] + [VM] * 5,
        (ANY, VM),
        [
            pltpu.VMEM((n, block, HD), BF16),
            pltpu.VMEM((min(tok, n * cap), 2 * kvw), BF16),
            pltpu.VMEM((n * q_rows, HD), F32),
            pltpu.VMEM((STAT, n * q_rows // kv_heads), F32),
            pltpu.SemaphoreType.DMA((2,)),
        ],
        flops=4 * n * q_rows * tok * HD,
        traffic=n * (q_rows + STAT) * HD * 4,
    )(slots, info, kv_text, arrived, bias, base)
    shares = exchange(sent)

    mine = call(
        lambda *refs: fresh_kernel(n, kv_heads, steps, *refs),
        jax.ShapeDtypeStruct((q_rows + STAT, HD), F32),
        [VM] * 4,
        VM,
        flops=1 << 20,
        traffic=1 << 18,
    )(remote(query), remote(dec_key[0]), remote(dec_value[0]), own)

    slots_here = n * page_cap
    attended, cache_key, cache_value = call(
        lambda *refs: finish_kernel(kv_heads, steps, page_cap, *refs),
        (
            jax.ShapeDtypeStruct(dec_query.shape, BF16),
            jax.ShapeDtypeStruct((n, page_cap * PAGE, kvw), BF16),
            jax.ShapeDtypeStruct((n, page_cap * PAGE, kvw), BF16),
        ),
        [VM, VM],
        (VM, VM, VM),
        traffic=4 * tok * 2 * kvw,
    )(shares, mine)
    return (
        attended,
        cache_key.reshape(slots_here, PAGE, kvw),
        cache_value.reshape(slots_here, PAGE, kvw),
    )


def solution(mesh):
    return jax.shard_map(
        body,
        mesh=mesh,
        in_specs=(
            P(("groups", "section"), "tensor"),
            P(("groups", "section"), "tensor"),
            P("groups", None),
            P(),
            P(None, "tensor"),
            P(None, "tensor"),
            P("groups"),
            P("groups"),
            P("groups", None),
            P("groups"),
            P(("groups", "section"), None, "tensor"),
            P(("groups", "section"), None, "tensor"),
            P(("groups", "section"), None, "tensor"),
        ),
        out_specs=(
            P(("groups", "section"), None, "tensor"),
            P(("groups", "section"), None, "tensor"),
            P(("groups", "section"), None, "tensor"),
        ),
        check_vma=False,
    )
```

```python
import jax
import jax.numpy as jnp
from jax import lax
from jax.experimental import pallas as pl
from jax.experimental.pallas import tpu as pltpu
from jax.sharding import PartitionSpec as P

HD = 128
PAGE = 16
LOWEST = -1e30
EPS = 1e-06
STAT = 8
F32 = jnp.float32
BF16 = jnp.bfloat16
I32 = jnp.int32

VM = pl.BlockSpec(memory_space=pltpu.VMEM)
SM = pl.BlockSpec(memory_space=pltpu.SMEM)
ANY = pl.BlockSpec(memory_space=pl.ANY)
MIB = 1 << 20


def call(kernel, out_shape, in_specs, out_specs, scratch=(), limit=16, flops=0, traffic=0):
    return pl.pallas_call(
        kernel,
        out_shape=out_shape,
        in_specs=in_specs,
        out_specs=out_specs,
        scratch_shapes=list(scratch),
        compiler_params=pltpu.CompilerParams(vmem_limit_bytes=limit * MIB),
        cost_estimate=pl.CostEstimate(flops=flops, bytes_accessed=traffic, transcendentals=0),
    )


def rank_of(section, n):
    return jnp.where(section < n // 2, n - 2 - 2 * section, 2 * section - n + 1)


def section_of(rank, n):
    return n // 2 - 1 - rank // 2 + rank % 2 * (rank // 2 * 2 + 1)


def page_rank_of(section, n):
    z, y, length = section // 2, section % 2, n // 2
    return (1 - y) * length + (2 * length - z - n // 4) % length


def page_section_of(rank, n):
    length = n // 2
    return 2 * (length - 1 - (rank % length + n // 4 - 1) % length) + 1 - rank // length


def dot(a, b):
    return jnp.dot(a, b, preferred_element_type=F32)


def dot_t(a, b):
    return lax.dot_general(a, b, (((1,), (1,)), ((), ())), preferred_element_type=F32)


def diagonal(shape):
    return lax.broadcasted_iota(I32, shape, 0) == lax.broadcasted_iota(I32, shape, 1)


def column_to_row(column):
    rows = column.shape[0]
    return jnp.sum(jnp.where(diagonal((rows, rows)), column, 0.0), axis=0, keepdims=True)


def row_to_column(row):
    lanes = row.shape[1]
    return jnp.sum(jnp.where(diagonal((lanes, lanes)), row, 0.0), axis=1, keepdims=True)


def squares_of(rows):
    total = jnp.zeros((rows.shape[0], HD), F32)
    for c in range(0, rows.shape[1], HD):
        wide = rows[:, c : c + HD].astype(F32)
        total = total + wide * wide
    return total


def split_three(values):
    high = values.astype(BF16).astype(F32)
    rest = values - high
    middle = rest.astype(BF16).astype(F32)
    return high, middle, rest - middle


def softmax_parts(query, key, value, usable):
    scores = jnp.where(usable, dot_t(query, key) * HD**-0.5, LOWEST)
    top = jnp.max(scores, axis=1, keepdims=True)
    weights = jnp.where(usable, jnp.exp(scores - top), 0.0)
    return dot(weights.astype(BF16), value), top, jnp.sum(weights, axis=1, keepdims=True)


def prepare_kernel(n, lot, *refs):
    far, info, near, (route, sems) = refs[:6], refs[6], refs[7:12], refs[12:]
    img, half = near[2].shape
    first = pl.ds(pl.multiple_of(lax.axis_index("tensor") * half, half), near[0].shape[0])
    sources = (far[0], far[1].at[first], far[2].at[first], *far[3:])
    copies = [pltpu.make_async_copy(a, b, sems.at[i]) for i, (a, b) in enumerate(zip(sources, (route, *near)))]
    for c in copies:
        c.start()
    copies[0].wait()
    pos = lax.axis_index("section")
    own = jnp.zeros((1, img), I32)
    for e in range(n):
        own = jnp.where(pos == e, route[:, e * img : (e + 1) * img], own)
    marks = own == lax.broadcasted_iota(I32, (n, img), 0)
    ones = jnp.where(marks, 1.0, 0.0).astype(BF16)
    earlier = lax.broadcasted_iota(I32, (img, img), 0) < lax.broadcasted_iota(I32, (img, img), 1)
    prefix = dot(ones, jnp.where(earlier, 1.0, 0.0).astype(BF16))
    local = jnp.sum(jnp.where(marks, prefix, 0.0), axis=0, keepdims=True).astype(I32)
    info[...] = jnp.broadcast_to(rank_of(own, n) * lot + local, info.shape)
    for c in copies[1:]:
        c.wait()


def plan_tokens(n, img, lot, page_cap, small, info, slots, bias, starts):
    route, pages, count, tail, req = small
    pos = lax.axis_index("section")
    tok, width = bias.shape
    blocks = tok // PAGE
    lanes = lax.broadcasted_iota(I32, (1, n * lot), 1)
    source, inner = section_of(lanes // lot, n), lanes % lot
    fits = jnp.zeros((1, n * lot), I32)
    offset = jnp.zeros((1, n * lot), I32)
    for e in range(n):
        here = (route[:, e * img : (e + 1) * img] == pos).astype(I32)
        arriving = jnp.sum(here, axis=1, keepdims=True)
        fits = fits + jnp.where(source == e, arriving, 0)
        offset = offset + jnp.where(source > e, arriving, 0)
    info[...] = jnp.broadcast_to(jnp.where(inner < fits, offset + inner, -1), info.shape)
    total = jnp.int32(0)
    for r in range(n):
        starts[r] = total
        total = total + count[r]
    token = lax.broadcasted_iota(I32, (1, tok), 1) + pos * tok
    token_slot = jnp.full((1, tok), -1, I32)
    for b in range(n):
        r = req[b]
        first = starts[r] * PAGE
        last = first + (count[r] - 1) * PAGE + tail[r]
        token_slot = jnp.where((token >= first) & (token < last), b, token_slot)
    member = section_of(lax.broadcasted_iota(I32, (1, width), 1) // (width // n), n)
    bias[...] = jnp.where(row_to_column(token_slot.astype(F32)) == member.astype(F32), 0.0, LOWEST)
    for g in range(blocks):
        holder = pages[0, pos * blocks + g]
        slot = page_rank_of(holder, n) * page_cap
        for e in range(g):
            slot = slot + (pages[0, pos * blocks + e] == holder).astype(I32)
        slots[g] = slot


def scale_of(near, far):
    sums = jnp.sum(squares_of(near) + squares_of(far), axis=1, keepdims=True)
    return lax.rsqrt(sums / (2.0 * near.shape[1]) + EPS)


def normed_rows(rows, c, step, scale, gain):
    return (rows[:, c : c + step].astype(F32) * scale * gain).astype(BF16)


def add_part(total, at, normed, w, begin):
    part = dot(normed, w)
    columns = slice(at, at + part.shape[1])
    if begin:
        total[:, columns] = part
    else:
        total[:, columns] += part


def vis_kernel(n, lot, sizes, step, *refs):
    near, far, gain, query, key_held, value_held, w_key, w_value, info, out, key_rest, value_rest, total, sems = refs
    img, half = near.shape
    kvw = w_key.shape[1]
    me = lax.axis_index("tensor")
    held = key_held.shape[0]
    loads = {}
    at = held
    for size in sizes:
        side = me if at < half else 1 - me
        source = pl.ds(pl.multiple_of(side * half + at % half, size), size)
        number = 2 * len(loads)
        loads[at] = [
            pltpu.make_async_copy(w.at[source], kept.at[at - held : at - held + size], sems.at[number + i])
            for i, (w, kept) in enumerate(((w_key, key_rest), (w_value, value_rest)))
        ]
        for copy in loads[at]:
            copy.start()
        at += size
    scale = scale_of(near, far)
    for at in range(0, 2 * half, step):
        for copy in loads.get(at, ()):
            copy.wait()
        rows, side = (near, me) if at < half else (far, 1 - me)
        weights, w_at = ((key_held, value_held), at) if at < held else ((key_rest, value_rest), at - held)
        c = at % half
        columns = pl.ds(pl.multiple_of(side * half + c, step), step)
        normed = normed_rows(rows, c, step, scale, gain[:, columns])
        for w, col in zip(weights, (0, kvw)):
            add_part(total, col, normed, w[w_at : w_at + step, :], at == 0)
    slot = lax.broadcasted_iota(I32, (n * lot, img), 0)
    chosen = jnp.where(slot == info[0:1, :img], 1.0, 0.0).astype(BF16)
    packed = dot(chosen, total[...].astype(BF16)).astype(BF16)
    q_lots = out.shape[1] - lot
    for k in range(n):
        for j in range(query.shape[0] // q_lots):
            out[k, :q_lots, j * HD : (j + 1) * HD] = query[j * q_lots : (j + 1) * q_lots, :]
        out[k, q_lots:, :] = packed[k * lot : (k + 1) * lot, :]


def put_page(out, page_cap, slot, rows):
    chunk = page_cap * PAGE
    for h in range(rows.shape[1] // HD):
        at = pl.ds(pl.multiple_of((slot % page_cap) * PAGE + h * chunk, PAGE), PAGE)
        out[slot // page_cap, at, :] = rows[:, h * HD : (h + 1) * HD]


def text_kernel(n, img, lot, load, step, page_cap, *refs):
    (near_far, far, gain, w_key_far, w_value_far), small_far, refs = refs[:5], refs[5:10], refs[10:]
    (out, bias, base, info, slots), (near, w_key, w_value, total, starts, sems), small = refs[:5], refs[5:11], refs[11:]
    half = near.shape[1]
    kvw = w_key.shape[1]
    me = lax.axis_index("tensor")
    first = pltpu.make_async_copy(near_far, near, sems.at[0])
    first.start()
    used = sems.shape[0] - len(small)
    lists = [pltpu.make_async_copy(a, b, sems.at[used + i]) for i, (a, b) in enumerate(zip(small_far, small))]
    for copy in lists:
        copy.start()
    loads = []
    for side in (me, 1 - me):
        for c in range(0, half, load):
            at = len(loads) * load
            columns = pl.ds(pl.multiple_of(side * half + c, load), load)
            pair = [
                pltpu.make_async_copy(w.at[columns], held.at[at : at + load], sems.at[2 * len(loads) + i])
                for i, (w, held) in enumerate(((w_key_far, w_key), (w_value_far, w_value)), 1)
            ]
            for copy in pair:
                copy.start()
            loads.append(pair)
    sums = squares_of(far)
    for copy in lists:
        copy.wait()
    plan_tokens(n, img, lot, page_cap, small, info, slots, bias, starts)
    first.wait()
    sums = jnp.sum(squares_of(near) + sums, axis=1, keepdims=True)
    scale = lax.rsqrt(sums / (2.0 * half) + EPS)
    for i, pair in enumerate(loads):
        for copy in pair:
            copy.wait()
        for at in range(i * load, (i + 1) * load, step):
            rows, side = (near, me) if at < half else (far, 1 - me)
            c = at % half
            columns = pl.ds(pl.multiple_of(side * half + c, step), step)
            normed = normed_rows(rows, c, step, scale, gain[:, columns])
            for w, col in ((w_key, 0), (w_value, kvw)):
                add_part(total, col, normed, w[at : at + step, :], at == 0)
    out[...] = total[...].astype(BF16)
    base[...] = jnp.zeros(base.shape, BF16)
    tok = near.shape[0]
    for g in range(tok // PAGE):
        put_page(base, page_cap, slots[g], out[g * PAGE : (g + 1) * PAGE, :])


def attend_kernel(n, cap, lot, page_cap, kv_heads, slots, info, kv_text, arrived, bias, base, sent, own, *scratch):
    out, mixed, held, rows_held, sems = scratch
    order = [page_section_of(k, n) for k in range(n)]
    rank = rank_of(lax.axis_index("section"), n)
    tok = kv_text.shape[0]
    kvw = kv_heads * HD
    q_lots = arrived.shape[1] - lot
    reach = min(tok, n * cap)
    hit = lax.broadcasted_iota(I32, (reach, n * lot), 0) == info[0:1, :]
    hot = jnp.where(hit, 1.0, 0.0)
    covered = jnp.sum(hot, axis=1, keepdims=True) > 0.0
    incoming = jnp.concatenate([arrived[k, q_lots:, :] for k in range(n)], axis=0)
    placed = dot(hot.astype(BF16), incoming)
    mixed[...] = jnp.where(covered, placed, kv_text[:reach, :].astype(F32)).astype(BF16)
    groups = arrived.shape[2] // HD // kv_heads
    rows = groups * q_lots
    pages = base.shape[1]
    out[:, :pages, :] = base[...]
    for g in range(reach // PAGE):
        put_page(out, page_cap, slots[g], mixed[g * PAGE : (g + 1) * PAGE, :])
    first = pltpu.make_async_copy(out.at[:, :pages, :], sent.at[:, :pages, :], sems.at[0])
    first.start()
    for g in range(kv_heads):
        query = jnp.concatenate(
            [
                arrived[k, :q_lots, (g * groups + j) * HD : (g * groups + j + 1) * HD]
                for k in range(n)
                for j in range(groups)
            ],
            axis=0,
        )
        cols = slice(g * HD, (g + 1) * HD)
        vcols = slice(kvw + g * HD, kvw + (g + 1) * HD)
        key = jnp.concatenate([mixed[:, cols], kv_text[reach:, cols]], axis=0)
        value = jnp.concatenate([mixed[:, vcols], kv_text[reach:, vcols]], axis=0)
        scores = dot_t(key, query) * HD**-0.5 + bias[...]
        top = jnp.max(scores, axis=0, keepdims=True)
        weights = jnp.exp(scores - top)
        rows_held[g : g + 1, :] = top
        rows_held[kv_heads + g : kv_heads + g + 1, :] = jnp.sum(weights, axis=0, keepdims=True)
        numerator = lax.dot_general(
            weights.astype(BF16), value, (((0,), (0,)), ((), ())), preferred_element_type=F32
        )
        held[g * n * rows : (g + 1) * n * rows, :] = numerator
        own[g * rows : (g + 1) * rows, :] = held[pl.ds(pl.multiple_of((g * n + rank) * rows, rows), rows), :]
        numerator = numerator.astype(BF16)
        for k in range(n):
            to = order.index(section_of(k, n))
            out[to, pages + g * rows : pages + (g + 1) * rows, :] = numerator[k * rows : (k + 1) * rows, :]
    stat_rows = 2 * kv_heads
    share = HD // rows
    window = pl.ds(pl.multiple_of(rank // share * HD, HD), HD)
    own[kv_heads * rows : kv_heads * rows + stat_rows, :] = rows_held[:stat_rows, window]
    blank = jnp.zeros((PAGE - 3 * stat_rows, HD), F32)
    for w in range(-(-n // share)):
        stats = rows_held[:stat_rows, w * HD : (w + 1) * HD]
        lines = jnp.concatenate([*split_three(stats), blank], axis=0).astype(BF16)
        for k in range(w * share, min(n, (w + 1) * share)):
            out[order.index(section_of(k, n)), pages + kv_heads * rows :, :] = lines
    last = pltpu.make_async_copy(out.at[:, pages:, :], sent.at[:, pages:, :], sems.at[1])
    last.start()
    first.wait()
    last.wait()


def pick_column(row, rows, start):
    shape = (rows, HD)
    chosen = lax.broadcasted_iota(I32, shape, 1) == lax.broadcasted_iota(I32, shape, 0) + start
    return jnp.sum(jnp.where(chosen, row, 0.0), axis=1, keepdims=True)


def combine(pieces, highest):
    numerator, total = 0.0, 0.0
    for rows, top, weight in pieces:
        scale = jnp.exp(top - highest)
        numerator = numerator + rows * scale
        total = total + weight * scale
    return numerator, total


def fresh_kernel(n, kv_heads, steps, query, key, value, own, mine):
    rows = query.shape[0] // kv_heads
    every = kv_heads * rows
    start = rank_of(lax.axis_index("section"), n) % (HD // rows) * rows
    row = lax.broadcasted_iota(I32, (rows, steps), 0)
    causal = lax.broadcasted_iota(I32, (rows, steps), 1) <= row % steps
    tops, totals = [], []
    for g in range(kv_heads):
        cols = slice(g * HD, (g + 1) * HD)
        at = slice(g * rows, (g + 1) * rows)
        fresh = softmax_parts(query[at, :], key[:, cols], value[:, cols], causal)
        share = (
            own[at, :],
            pick_column(own[every + g : every + g + 1, :], rows, start),
            pick_column(own[every + kv_heads + g : every + kv_heads + g + 1, :], rows, start),
        )
        highest = jnp.maximum(fresh[1], share[1])
        numerator, total = combine((fresh, share), highest)
        mine[at, :] = numerator
        tops.append(highest)
        totals.append(total)
    line = column_to_row(jnp.concatenate(tops + totals, axis=0))
    mine[every:, :] = jnp.broadcast_to(line, (STAT, line.shape[1]))


def finish_kernel(kv_heads, steps, page_cap, shares, mine, attended, keys, values, *scratch):
    n = shares.shape[0]
    pos = lax.axis_index("section")
    every = mine.shape[0] - STAT
    rows = every // kv_heads
    start = rank_of(pos, n) % (HD // rows) * rows
    chunk = page_cap * PAGE
    halves = keys.shape[2] // HD
    held, sems = scratch[:2], scratch[2]
    for k in range(n):
        for i, out in enumerate(held):
            for h in range(halves):
                part = i * halves + h
                out[page_section_of(k, n), :, h * HD : (h + 1) * HD] = shares[k, part * chunk : (part + 1) * chunk, :]
    copies = [pltpu.make_async_copy(x, out, sems.at[i]) for i, (x, out) in enumerate(zip(held, (keys, values)))]
    for c in copies:
        c.start()
    pages = 2 * halves * chunk
    stats = row_to_column(mine[every : every + 1, :])
    lines = []
    for k in range(n):
        three = shares[k, pages + every :, :].astype(F32)
        size = 2 * kv_heads
        lines.append(three[:size] + three[size : 2 * size] + three[2 * size : 3 * size])
    for g in range(kv_heads):
        at = slice(g * rows, (g + 1) * rows)
        pieces = [(mine[at, :], stats[at], stats[every + g * rows : every + (g + 1) * rows])]
        for k in range(n):
            away = pos != page_section_of(k, n)
            top = jnp.where(away, pick_column(lines[k][g : g + 1], rows, start), LOWEST)
            weight = jnp.where(away, pick_column(lines[k][kv_heads + g : kv_heads + g + 1], rows, start), 0.0)
            share = shares[k, pages + g * rows : pages + (g + 1) * rows, :].astype(F32)
            pieces.append((share, top, weight))
        highest = pieces[0][1]
        for p in pieces[1:]:
            highest = jnp.maximum(highest, p[1])
        numerator, total = combine(pieces, highest)
        result = (numerator / total).astype(BF16)
        for h in range(rows // steps):
            to = (g * rows // steps + h) * HD
            attended[0, :, to : to + HD] = result[h * steps : (h + 1) * steps, :]
    for c in copies:
        c.wait()


def body(
    text_rows,
    vis_rows,
    img_route,
    norm_gain,
    w_key,
    w_value,
    page_count,
    tail_len,
    page_dest,
    dec_req,
    dec_query,
    dec_key,
    dec_value,
):
    n = lax.axis_size("section")
    tok, half = text_rows.shape
    img = vis_rows.shape[0]
    kvw = w_key.shape[1]
    kv_heads = kvw // HD
    _, steps, q_width = dec_query.shape
    heads = q_width // HD
    q_rows = heads * steps
    blocks = tok // PAGE
    cap = max(2, (2 * img + n - 1) // n)
    page_cap = max(1, (blocks + n - 1) // n)

    def across(array):
        return lax.ppermute(array, "tensor", [(0, 1), (1, 0)])

    def exchange(array, section_at):
        order = [[section_at(rank, n) for rank in range(n)]]
        return lax.all_to_all(array, "section", split_axis=0, concat_axis=0, tiled=True, axis_index_groups=order)

    def remote(array):
        return pltpu.with_memory_space_constraint(array, pltpu.HBM)

    def local(array):
        return pltpu.with_memory_space_constraint(array, pltpu.VMEM)

    vis_far = across(vis_rows)
    text_far = across(text_rows)
    query = dec_query.reshape(steps, heads, HD).transpose(1, 0, 2).reshape(q_rows, HD)

    lot = -(-cap // PAGE) * PAGE
    q_lots = q_rows * HD // (2 * kvw)
    gain = norm_gain.reshape(1, 2 * half)
    load = min(2048, half)
    step = min(1024, load // 2)
    kept = load + load // 2
    arguments = (img_route.T, w_key, w_value, vis_rows, gain, query)
    info, key_held, value_held, vis_near, gain_near, query_near = call(
        lambda *refs: prepare_kernel(n, lot, *refs),
        (
            jax.ShapeDtypeStruct((STAT, img), I32),
            pltpu.VMEM((kept, kvw), BF16),
            pltpu.VMEM((kept, kvw), BF16),
            *[pltpu.VMEM(a.shape, a.dtype) for a in arguments[3:]],
        ),
        [ANY] * len(arguments),
        (VM,) * 6,
        [pltpu.VMEM((1, n * img), I32), pltpu.SemaphoreType.DMA((len(arguments),))],
        flops=1 << 20,
        traffic=2 * 2 * half * 2 * kvw * 2,
    )(*[remote(a) for a in arguments])

    left = 2 * half - kept
    sizes = [half - kept, *[load] * (half // load - 1), *[load // 2] * 2]
    packed = call(
        lambda *refs: vis_kernel(n, lot, sizes, step, *refs),
        pltpu.VMEM((n, q_lots + lot, 2 * kvw), BF16),
        [VM] * 6 + [ANY] * 2 + [VM],
        VM,
        [
            pltpu.VMEM((left, kvw), BF16),
            pltpu.VMEM((left, kvw), BF16),
            pltpu.VMEM((img, 2 * kvw), F32),
            pltpu.SemaphoreType.DMA((2 * len(sizes),)),
        ],
        flops=64 * img * 2 * half * 2 * kvw,
        traffic=2 * img * 2 * half + 8 * half * kvw,
    )(
        local(vis_near),
        vis_far,
        local(gain_near),
        local(query_near),
        local(key_held),
        local(value_held),
        remote(w_key),
        remote(w_value),
        info,
    )
    arrived = exchange(packed, section_of)

    block = page_cap * PAGE * 2 * kv_heads + q_rows + PAGE
    lists = (img_route.T, page_dest.T, page_count, tail_len, dec_req)
    kv_text, bias, base, info, slots = call(
        lambda *refs: text_kernel(n, img, lot, load, step, page_cap, *refs),
        (
            jax.ShapeDtypeStruct((tok, 2 * kvw), BF16),
            jax.ShapeDtypeStruct((tok, n * q_rows // kv_heads), F32),
            jax.ShapeDtypeStruct((n, block - q_rows - PAGE, HD), BF16),
            jax.ShapeDtypeStruct((STAT, n * lot), I32),
            jax.ShapeDtypeStruct((blocks,), I32),
        ),
        [ANY, VM, VM] + [ANY] * 7,
        (VM, VM, VM, VM, SM),
        [
            pltpu.VMEM((tok, half), BF16),
            pltpu.VMEM(w_key.shape, BF16),
            pltpu.VMEM(w_value.shape, BF16),
            pltpu.VMEM((tok, 2 * kvw), F32),
            pltpu.SMEM((n,), I32),
            pltpu.SemaphoreType.DMA((1 + 4 * half // load + len(lists),)),
            *[(pltpu.VMEM if i == 0 else pltpu.SMEM)(a.shape, a.dtype) for i, a in enumerate(lists)],
        ],
        limit=24,
        flops=2 * tok * 2 * half * 2 * kvw,
        traffic=2 * tok * 2 * half + 8 * half * kvw,
    )(remote(text_rows), text_far, remote(gain), remote(w_key), remote(w_value), *[remote(a) for a in lists])

    sent, own = call(
        lambda *refs: attend_kernel(n, cap, lot, page_cap, kv_heads, *refs),
        (
            jax.ShapeDtypeStruct((n, block, HD), BF16),
            jax.ShapeDtypeStruct((q_rows + STAT, HD), F32),
        ),
        [SM] + [VM] * 5,
        (ANY, VM),
        [
            pltpu.VMEM((n, block, HD), BF16),
            pltpu.VMEM((min(tok, n * cap), 2 * kvw), BF16),
            pltpu.VMEM((n * q_rows, HD), F32),
            pltpu.VMEM((STAT, n * q_rows // kv_heads), F32),
            pltpu.SemaphoreType.DMA((2,)),
        ],
        flops=4 * n * q_rows * tok * HD,
        traffic=n * (q_rows + STAT) * HD * 4,
    )(slots, info, kv_text, arrived, bias, base)
    shares = exchange(sent, page_section_of)

    mine = call(
        lambda *refs: fresh_kernel(n, kv_heads, steps, *refs),
        jax.ShapeDtypeStruct((q_rows + STAT, HD), F32),
        [VM] * 4,
        VM,
        flops=1 << 20,
        traffic=1 << 18,
    )(remote(query), remote(dec_key[0]), remote(dec_value[0]), own)

    slots_here = n * page_cap
    attended, cache_key, cache_value = call(
        lambda *refs: finish_kernel(kv_heads, steps, page_cap, *refs),
        (
            jax.ShapeDtypeStruct(dec_query.shape, BF16),
            jax.ShapeDtypeStruct((n, page_cap * PAGE, kvw), BF16),
            jax.ShapeDtypeStruct((n, page_cap * PAGE, kvw), BF16),
        ),
        [VM, VM],
        (VM, ANY, ANY),
        [
            pltpu.VMEM((n, page_cap * PAGE, kvw), BF16),
            pltpu.VMEM((n, page_cap * PAGE, kvw), BF16),
            pltpu.SemaphoreType.DMA((2,)),
        ],
        traffic=4 * tok * 2 * kvw,
    )(shares, mine)
    return (
        attended,
        cache_key.reshape(slots_here, PAGE, kvw),
        cache_value.reshape(slots_here, PAGE, kvw),
    )


def solution(mesh):
    return jax.shard_map(
        body,
        mesh=mesh,
        in_specs=(
            P(("groups", "section"), "tensor"),
            P(("groups", "section"), "tensor"),
            P("groups", None),
            P(),
            P(None, "tensor"),
            P(None, "tensor"),
            P("groups"),
            P("groups"),
            P("groups", None),
            P("groups"),
            P(("groups", "section"), None, "tensor"),
            P(("groups", "section"), None, "tensor"),
            P(("groups", "section"), None, "tensor"),
        ),
        out_specs=(
            P(("groups", "section"), None, "tensor"),
            P(("groups", "section"), None, "tensor"),
            P(("groups", "section"), None, "tensor"),
        ),
        check_vma=False,
    )
```

```python
import jax
import jax.numpy as jnp
from jax import lax
from jax.experimental import pallas as pl
from jax.experimental.pallas import tpu as pltpu
from jax.sharding import PartitionSpec as P

HD = 128
PAGE = 16
LOWEST = -1e30
EPS = 1e-06
STAT = 8
F32 = jnp.float32
BF16 = jnp.bfloat16
I32 = jnp.int32

VM = pl.BlockSpec(memory_space=pltpu.VMEM)
SM = pl.BlockSpec(memory_space=pltpu.SMEM)
ANY = pl.BlockSpec(memory_space=pl.ANY)
MIB = 1 << 20


def call(kernel, out_shape, in_specs, out_specs, scratch=(), limit=16, flops=0, traffic=0):
    return pl.pallas_call(
        kernel,
        out_shape=out_shape,
        in_specs=in_specs,
        out_specs=out_specs,
        scratch_shapes=list(scratch),
        compiler_params=pltpu.CompilerParams(vmem_limit_bytes=limit * MIB),
        cost_estimate=pl.CostEstimate(flops=flops, bytes_accessed=traffic, transcendentals=0),
    )


def rank_of(section, n):
    return jnp.where(section < n // 2, n - 2 - 2 * section, 2 * section - n + 1)


def section_of(rank, n):
    return n // 2 - 1 - rank // 2 + rank % 2 * (rank // 2 * 2 + 1)


def page_rank_of(section, n):
    z, y, length = section // 2, section % 2, n // 2
    return ((1 - y) * length + (2 * length - z - n // 4) % length + n - 1) % n


def page_section_of(rank, n):
    length, place = n // 2, (rank + 1) % n
    return 2 * (length - 1 - (place % length + n // 4 - 1) % length) + 1 - place // length


def dot(a, b):
    return jnp.dot(a, b, preferred_element_type=F32)


def dot_t(a, b):
    return lax.dot_general(a, b, (((1,), (1,)), ((), ())), preferred_element_type=F32)


def diagonal(shape):
    return lax.broadcasted_iota(I32, shape, 0) == lax.broadcasted_iota(I32, shape, 1)


def column_to_row(column):
    rows = column.shape[0]
    return jnp.sum(jnp.where(diagonal((rows, rows)), column, 0.0), axis=0, keepdims=True)


def row_to_column(row):
    lanes = row.shape[1]
    return jnp.sum(jnp.where(diagonal((lanes, lanes)), row, 0.0), axis=1, keepdims=True)


def squares_of(rows):
    total = jnp.zeros((rows.shape[0], HD), F32)
    for c in range(0, rows.shape[1], HD):
        wide = rows[:, c : c + HD].astype(F32)
        total = total + wide * wide
    return total


def split_three(values):
    high = values.astype(BF16).astype(F32)
    rest = values - high
    middle = rest.astype(BF16).astype(F32)
    return high, middle, rest - middle


def softmax_parts(query, key, value, usable):
    scores = jnp.where(usable, dot_t(query, key) * HD**-0.5, LOWEST)
    top = jnp.max(scores, axis=1, keepdims=True)
    weights = jnp.where(usable, jnp.exp(scores - top), 0.0)
    return dot(weights.astype(BF16), value), top, jnp.sum(weights, axis=1, keepdims=True)


def prepare_kernel(n, lot, *refs):
    far, info, near, (route, sems) = refs[:6], refs[6], refs[7:12], refs[12:]
    img, half = near[2].shape
    first = pl.ds(pl.multiple_of(lax.axis_index("tensor") * half, half), near[0].shape[0])
    sources = (far[0], far[1].at[first], far[2].at[first], *far[3:])
    copies = [pltpu.make_async_copy(a, b, sems.at[i]) for i, (a, b) in enumerate(zip(sources, (route, *near)))]
    for c in copies:
        c.start()
    copies[0].wait()
    pos = lax.axis_index("section")
    own = jnp.zeros((1, img), I32)
    for e in range(n):
        own = jnp.where(pos == e, route[:, e * img : (e + 1) * img], own)
    marks = own == lax.broadcasted_iota(I32, (n, img), 0)
    ones = jnp.where(marks, 1.0, 0.0).astype(BF16)
    earlier = lax.broadcasted_iota(I32, (img, img), 0) < lax.broadcasted_iota(I32, (img, img), 1)
    prefix = dot(ones, jnp.where(earlier, 1.0, 0.0).astype(BF16))
    local = jnp.sum(jnp.where(marks, prefix, 0.0), axis=0, keepdims=True).astype(I32)
    info[...] = jnp.broadcast_to(rank_of(own, n) * lot + local, info.shape)
    for c in copies[1:]:
        c.wait()


def plan_tokens(n, img, lot, page_cap, small, info, slots, bias, starts):
    route, pages, count, tail, req = small
    pos = lax.axis_index("section")
    tok, width = bias.shape
    blocks = tok // PAGE
    lanes = lax.broadcasted_iota(I32, (1, n * lot), 1)
    source, inner = section_of(lanes // lot, n), lanes % lot
    fits = jnp.zeros((1, n * lot), I32)
    offset = jnp.zeros((1, n * lot), I32)
    for e in range(n):
        here = (route[:, e * img : (e + 1) * img] == pos).astype(I32)
        arriving = jnp.sum(here, axis=1, keepdims=True)
        fits = fits + jnp.where(source == e, arriving, 0)
        offset = offset + jnp.where(source > e, arriving, 0)
    info[...] = jnp.broadcast_to(jnp.where(inner < fits, offset + inner, -1), info.shape)
    total = jnp.int32(0)
    for r in range(n):
        starts[r] = total
        total = total + count[r]
    token = lax.broadcasted_iota(I32, (1, tok), 1) + pos * tok
    token_slot = jnp.full((1, tok), -1, I32)
    for b in range(n):
        r = req[b]
        first = starts[r] * PAGE
        last = first + (count[r] - 1) * PAGE + tail[r]
        token_slot = jnp.where((token >= first) & (token < last), b, token_slot)
    member = section_of(lax.broadcasted_iota(I32, (1, width), 1) // (width // n), n)
    bias[...] = jnp.where(row_to_column(token_slot.astype(F32)) == member.astype(F32), 0.0, LOWEST)
    for g in range(blocks):
        holder = pages[0, pos * blocks + g]
        slot = page_rank_of(holder, n) * page_cap
        for e in range(g):
            slot = slot + (pages[0, pos * blocks + e] == holder).astype(I32)
        slots[g] = slot


def scale_of(near, far):
    sums = jnp.sum(squares_of(near) + squares_of(far), axis=1, keepdims=True)
    return lax.rsqrt(sums / (2.0 * near.shape[1]) + EPS)


def normed_rows(rows, c, step, scale, gain):
    return (rows[:, c : c + step].astype(F32) * scale * gain).astype(BF16)


def add_part(total, at, normed, w, begin):
    part = dot(normed, w)
    columns = slice(at, at + part.shape[1])
    if begin:
        total[:, columns] = part
    else:
        total[:, columns] += part


def vis_kernel(n, lot, sizes, step, *refs):
    near, far, gain, query, key_held, value_held, w_key, w_value, info, out, key_rest, value_rest, total, sems = refs
    img, half = near.shape
    kvw = w_key.shape[1]
    me = lax.axis_index("tensor")
    held = key_held.shape[0]
    loads = {}
    at = held
    for size in sizes:
        side = me if at < half else 1 - me
        source = pl.ds(pl.multiple_of(side * half + at % half, size), size)
        number = 2 * len(loads)
        loads[at] = [
            pltpu.make_async_copy(w.at[source], kept.at[at - held : at - held + size], sems.at[number + i])
            for i, (w, kept) in enumerate(((w_key, key_rest), (w_value, value_rest)))
        ]
        for copy in loads[at]:
            copy.start()
        at += size
    scale = scale_of(near, far)
    for at in range(0, 2 * half, step):
        for copy in loads.get(at, ()):
            copy.wait()
        rows, side = (near, me) if at < half else (far, 1 - me)
        weights, w_at = ((key_held, value_held), at) if at < held else ((key_rest, value_rest), at - held)
        c = at % half
        columns = pl.ds(pl.multiple_of(side * half + c, step), step)
        normed = normed_rows(rows, c, step, scale, gain[:, columns])
        for w, col in zip(weights, (0, kvw)):
            add_part(total, col, normed, w[w_at : w_at + step, :], at == 0)
    slot = lax.broadcasted_iota(I32, (n * lot, img), 0)
    chosen = jnp.where(slot == info[0:1, :img], 1.0, 0.0).astype(BF16)
    packed = dot(chosen, total[...].astype(BF16)).astype(BF16)
    q_lots = out.shape[1] - lot
    for k in range(n):
        for j in range(query.shape[0] // q_lots):
            out[k, :q_lots, j * HD : (j + 1) * HD] = query[j * q_lots : (j + 1) * q_lots, :]
        out[k, q_lots:, :] = packed[k * lot : (k + 1) * lot, :]


def put_page(out, page_cap, slot, rows):
    chunk = page_cap * PAGE
    for h in range(rows.shape[1] // HD):
        at = pl.ds(pl.multiple_of((slot % page_cap) * PAGE + h * chunk, PAGE), PAGE)
        out[slot // page_cap, at, :] = rows[:, h * HD : (h + 1) * HD]


def text_kernel(n, img, lot, load, step, page_cap, *refs):
    (near_far, far, gain, w_key_far, w_value_far), small_far, refs = refs[:5], refs[5:10], refs[10:]
    (out, bias, base, info, slots), (near, w_key, w_value, total, starts, sems), small = refs[:5], refs[5:11], refs[11:]
    half = near.shape[1]
    kvw = w_key.shape[1]
    me = lax.axis_index("tensor")
    first = pltpu.make_async_copy(near_far, near, sems.at[0])
    first.start()
    used = sems.shape[0] - len(small)
    lists = [pltpu.make_async_copy(a, b, sems.at[used + i]) for i, (a, b) in enumerate(zip(small_far, small))]
    for copy in lists:
        copy.start()
    loads = []
    for side in (me, 1 - me):
        for c in range(0, half, load):
            at = len(loads) * load
            columns = pl.ds(pl.multiple_of(side * half + c, load), load)
            pair = [
                pltpu.make_async_copy(w.at[columns], held.at[at : at + load], sems.at[2 * len(loads) + i])
                for i, (w, held) in enumerate(((w_key_far, w_key), (w_value_far, w_value)), 1)
            ]
            for copy in pair:
                copy.start()
            loads.append(pair)
    sums = squares_of(far)
    for copy in lists:
        copy.wait()
    plan_tokens(n, img, lot, page_cap, small, info, slots, bias, starts)
    first.wait()
    sums = jnp.sum(squares_of(near) + sums, axis=1, keepdims=True)
    scale = lax.rsqrt(sums / (2.0 * half) + EPS)
    for i, pair in enumerate(loads):
        for copy in pair:
            copy.wait()
        for at in range(i * load, (i + 1) * load, step):
            rows, side = (near, me) if at < half else (far, 1 - me)
            c = at % half
            columns = pl.ds(pl.multiple_of(side * half + c, step), step)
            normed = normed_rows(rows, c, step, scale, gain[:, columns])
            for w, col in ((w_key, 0), (w_value, kvw)):
                add_part(total, col, normed, w[at : at + step, :], at == 0)
    out[...] = total[...].astype(BF16)
    base[...] = jnp.zeros(base.shape, BF16)
    tok = near.shape[0]
    for g in range(tok // PAGE):
        put_page(base, page_cap, slots[g], out[g * PAGE : (g + 1) * PAGE, :])


def attend_kernel(n, cap, lot, page_cap, kv_heads, slots, info, kv_text, arrived, bias, base, sent, own, *scratch):
    out, mixed, held, rows_held, sems = scratch
    order = [page_section_of(k, n) for k in range(n)]
    rank = rank_of(lax.axis_index("section"), n)
    tok = kv_text.shape[0]
    kvw = kv_heads * HD
    q_lots = arrived.shape[1] - lot
    reach = min(tok, n * cap)
    hit = lax.broadcasted_iota(I32, (reach, n * lot), 0) == info[0:1, :]
    hot = jnp.where(hit, 1.0, 0.0)
    covered = jnp.sum(hot, axis=1, keepdims=True) > 0.0
    incoming = jnp.concatenate([arrived[k, q_lots:, :] for k in range(n)], axis=0)
    placed = dot(hot.astype(BF16), incoming)
    mixed[...] = jnp.where(covered, placed, kv_text[:reach, :].astype(F32)).astype(BF16)
    groups = arrived.shape[2] // HD // kv_heads
    rows = groups * q_lots
    pages = base.shape[1]
    out[:, :pages, :] = base[...]
    for g in range(reach // PAGE):
        put_page(out, page_cap, slots[g], mixed[g * PAGE : (g + 1) * PAGE, :])
    first = pltpu.make_async_copy(out.at[:, :pages, :], sent.at[:, :pages, :], sems.at[0])
    first.start()
    for g in range(kv_heads):
        query = jnp.concatenate(
            [
                arrived[k, :q_lots, (g * groups + j) * HD : (g * groups + j + 1) * HD]
                for k in range(n)
                for j in range(groups)
            ],
            axis=0,
        )
        cols = slice(g * HD, (g + 1) * HD)
        vcols = slice(kvw + g * HD, kvw + (g + 1) * HD)
        key = jnp.concatenate([mixed[:, cols], kv_text[reach:, cols]], axis=0)
        value = jnp.concatenate([mixed[:, vcols], kv_text[reach:, vcols]], axis=0)
        scores = dot_t(key, query) * HD**-0.5 + bias[...]
        top = jnp.max(scores, axis=0, keepdims=True)
        weights = jnp.exp(scores - top)
        rows_held[g : g + 1, :] = top
        rows_held[kv_heads + g : kv_heads + g + 1, :] = jnp.sum(weights, axis=0, keepdims=True)
        numerator = lax.dot_general(
            weights.astype(BF16), value, (((0,), (0,)), ((), ())), preferred_element_type=F32
        )
        held[g * n * rows : (g + 1) * n * rows, :] = numerator
        own[g * rows : (g + 1) * rows, :] = held[pl.ds(pl.multiple_of((g * n + rank) * rows, rows), rows), :]
        numerator = numerator.astype(BF16)
        for k in range(n):
            to = order.index(section_of(k, n))
            out[to, pages + g * rows : pages + (g + 1) * rows, :] = numerator[k * rows : (k + 1) * rows, :]
    stat_rows = 2 * kv_heads
    share = HD // rows
    window = pl.ds(pl.multiple_of(rank // share * HD, HD), HD)
    own[kv_heads * rows : kv_heads * rows + stat_rows, :] = rows_held[:stat_rows, window]
    blank = jnp.zeros((PAGE - 3 * stat_rows, HD), F32)
    for w in range(-(-n // share)):
        stats = rows_held[:stat_rows, w * HD : (w + 1) * HD]
        lines = jnp.concatenate([*split_three(stats), blank], axis=0).astype(BF16)
        for k in range(w * share, min(n, (w + 1) * share)):
            out[order.index(section_of(k, n)), pages + kv_heads * rows :, :] = lines
    last = pltpu.make_async_copy(out.at[:, pages:, :], sent.at[:, pages:, :], sems.at[1])
    last.start()
    first.wait()
    last.wait()


def pick_column(row, rows, start):
    shape = (rows, HD)
    chosen = lax.broadcasted_iota(I32, shape, 1) == lax.broadcasted_iota(I32, shape, 0) + start
    return jnp.sum(jnp.where(chosen, row, 0.0), axis=1, keepdims=True)


def combine(pieces, highest):
    numerator, total = 0.0, 0.0
    for rows, top, weight in pieces:
        scale = jnp.exp(top - highest)
        numerator = numerator + rows * scale
        total = total + weight * scale
    return numerator, total


def fresh_kernel(n, kv_heads, steps, query, key, value, own, mine):
    rows = query.shape[0] // kv_heads
    every = kv_heads * rows
    start = rank_of(lax.axis_index("section"), n) % (HD // rows) * rows
    row = lax.broadcasted_iota(I32, (rows, steps), 0)
    causal = lax.broadcasted_iota(I32, (rows, steps), 1) <= row % steps
    tops, totals = [], []
    for g in range(kv_heads):
        cols = slice(g * HD, (g + 1) * HD)
        at = slice(g * rows, (g + 1) * rows)
        fresh = softmax_parts(query[at, :], key[:, cols], value[:, cols], causal)
        share = (
            own[at, :],
            pick_column(own[every + g : every + g + 1, :], rows, start),
            pick_column(own[every + kv_heads + g : every + kv_heads + g + 1, :], rows, start),
        )
        highest = jnp.maximum(fresh[1], share[1])
        numerator, total = combine((fresh, share), highest)
        mine[at, :] = numerator
        tops.append(highest)
        totals.append(total)
    line = column_to_row(jnp.concatenate(tops + totals, axis=0))
    mine[every:, :] = jnp.broadcast_to(line, (STAT, line.shape[1]))


def finish_kernel(kv_heads, steps, page_cap, shares, mine, attended, keys, values):
    n = shares.shape[0]
    pos = lax.axis_index("section")
    every = mine.shape[0] - STAT
    rows = every // kv_heads
    start = rank_of(pos, n) % (HD // rows) * rows
    chunk = page_cap * PAGE
    halves = keys.shape[2] // HD
    for k in range(n):
        for i, out in enumerate((keys, values)):
            for h in range(halves):
                part = i * halves + h
                out[page_section_of(k, n), :, h * HD : (h + 1) * HD] = shares[k, part * chunk : (part + 1) * chunk, :]
    pages = 2 * halves * chunk
    stats = row_to_column(mine[every : every + 1, :])
    lines = []
    for k in range(n):
        three = shares[k, pages + every :, :].astype(F32)
        size = 2 * kv_heads
        lines.append(three[:size] + three[size : 2 * size] + three[2 * size : 3 * size])
    for g in range(kv_heads):
        at = slice(g * rows, (g + 1) * rows)
        pieces = [(mine[at, :], stats[at], stats[every + g * rows : every + (g + 1) * rows])]
        for k in range(n):
            away = pos != page_section_of(k, n)
            top = jnp.where(away, pick_column(lines[k][g : g + 1], rows, start), LOWEST)
            weight = jnp.where(away, pick_column(lines[k][kv_heads + g : kv_heads + g + 1], rows, start), 0.0)
            share = shares[k, pages + g * rows : pages + (g + 1) * rows, :].astype(F32)
            pieces.append((share, top, weight))
        highest = pieces[0][1]
        for p in pieces[1:]:
            highest = jnp.maximum(highest, p[1])
        numerator, total = combine(pieces, highest)
        result = (numerator / total).astype(BF16)
        for h in range(rows // steps):
            to = (g * rows // steps + h) * HD
            attended[0, :, to : to + HD] = result[h * steps : (h + 1) * steps, :]


def body(
    text_rows,
    vis_rows,
    img_route,
    norm_gain,
    w_key,
    w_value,
    page_count,
    tail_len,
    page_dest,
    dec_req,
    dec_query,
    dec_key,
    dec_value,
):
    n = lax.axis_size("section")
    tok, half = text_rows.shape
    img = vis_rows.shape[0]
    kvw = w_key.shape[1]
    kv_heads = kvw // HD
    _, steps, q_width = dec_query.shape
    heads = q_width // HD
    q_rows = heads * steps
    blocks = tok // PAGE
    cap = max(2, (2 * img + n - 1) // n)
    page_cap = max(1, (blocks + n - 1) // n)

    def across(array):
        return lax.ppermute(array, "tensor", [(0, 1), (1, 0)])

    def exchange(array, section_at):
        order = [[section_at(rank, n) for rank in range(n)]]
        return lax.all_to_all(array, "section", split_axis=0, concat_axis=0, tiled=True, axis_index_groups=order)

    def remote(array):
        return pltpu.with_memory_space_constraint(array, pltpu.HBM)

    def local(array):
        return pltpu.with_memory_space_constraint(array, pltpu.VMEM)

    vis_far = across(vis_rows)
    text_far = across(text_rows)
    query = dec_query.reshape(steps, heads, HD).transpose(1, 0, 2).reshape(q_rows, HD)

    lot = -(-cap // PAGE) * PAGE
    q_lots = q_rows * HD // (2 * kvw)
    gain = norm_gain.reshape(1, 2 * half)
    load = min(2048, half)
    step = min(1024, load // 2)
    kept = load + load // 2
    arguments = (img_route.T, w_key, w_value, vis_rows, gain, query)
    info, key_held, value_held, vis_near, gain_near, query_near = call(
        lambda *refs: prepare_kernel(n, lot, *refs),
        (
            jax.ShapeDtypeStruct((STAT, img), I32),
            pltpu.VMEM((kept, kvw), BF16),
            pltpu.VMEM((kept, kvw), BF16),
            *[pltpu.VMEM(a.shape, a.dtype) for a in arguments[3:]],
        ),
        [ANY] * len(arguments),
        (VM,) * 6,
        [pltpu.VMEM((1, n * img), I32), pltpu.SemaphoreType.DMA((len(arguments),))],
        flops=1 << 20,
        traffic=2 * 2 * half * 2 * kvw * 2,
    )(*[remote(a) for a in arguments])

    left = 2 * half - kept
    sizes = [half - kept, *[load] * (half // load - 1), *[load // 2] * 2]
    packed = call(
        lambda *refs: vis_kernel(n, lot, sizes, step, *refs),
        pltpu.VMEM((n, q_lots + lot, 2 * kvw), BF16),
        [VM] * 6 + [ANY] * 2 + [VM],
        VM,
        [
            pltpu.VMEM((left, kvw), BF16),
            pltpu.VMEM((left, kvw), BF16),
            pltpu.VMEM((img, 2 * kvw), F32),
            pltpu.SemaphoreType.DMA((2 * len(sizes),)),
        ],
        flops=64 * img * 2 * half * 2 * kvw,
        traffic=2 * img * 2 * half + 8 * half * kvw,
    )(
        local(vis_near),
        vis_far,
        local(gain_near),
        local(query_near),
        local(key_held),
        local(value_held),
        remote(w_key),
        remote(w_value),
        info,
    )
    arrived = exchange(packed, section_of)

    block = page_cap * PAGE * 2 * kv_heads + q_rows + PAGE
    lists = (img_route.T, page_dest.T, page_count, tail_len, dec_req)
    kv_text, bias, base, info, slots = call(
        lambda *refs: text_kernel(n, img, lot, load, step, page_cap, *refs),
        (
            jax.ShapeDtypeStruct((tok, 2 * kvw), BF16),
            jax.ShapeDtypeStruct((tok, n * q_rows // kv_heads), F32),
            jax.ShapeDtypeStruct((n, block - q_rows - PAGE, HD), BF16),
            jax.ShapeDtypeStruct((STAT, n * lot), I32),
            jax.ShapeDtypeStruct((blocks,), I32),
        ),
        [ANY, VM, VM] + [ANY] * 7,
        (VM, VM, VM, VM, SM),
        [
            pltpu.VMEM((tok, half), BF16),
            pltpu.VMEM(w_key.shape, BF16),
            pltpu.VMEM(w_value.shape, BF16),
            pltpu.VMEM((tok, 2 * kvw), F32),
            pltpu.SMEM((n,), I32),
            pltpu.SemaphoreType.DMA((1 + 4 * half // load + len(lists),)),
            *[(pltpu.VMEM if i == 0 else pltpu.SMEM)(a.shape, a.dtype) for i, a in enumerate(lists)],
        ],
        limit=24,
        flops=2 * tok * 2 * half * 2 * kvw,
        traffic=2 * tok * 2 * half + 8 * half * kvw,
    )(remote(text_rows), text_far, remote(gain), remote(w_key), remote(w_value), *[remote(a) for a in lists])

    sent, own = call(
        lambda *refs: attend_kernel(n, cap, lot, page_cap, kv_heads, *refs),
        (
            jax.ShapeDtypeStruct((n, block, HD), BF16),
            jax.ShapeDtypeStruct((q_rows + STAT, HD), F32),
        ),
        [SM] + [VM] * 5,
        (ANY, VM),
        [
            pltpu.VMEM((n, block, HD), BF16),
            pltpu.VMEM((min(tok, n * cap), 2 * kvw), BF16),
            pltpu.VMEM((n * q_rows, HD), F32),
            pltpu.VMEM((STAT, n * q_rows // kv_heads), F32),
            pltpu.SemaphoreType.DMA((2,)),
        ],
        flops=4 * n * q_rows * tok * HD,
        traffic=n * (q_rows + STAT) * HD * 4,
    )(slots, info, kv_text, arrived, bias, base)
    shares = exchange(sent, page_section_of)

    mine = call(
        lambda *refs: fresh_kernel(n, kv_heads, steps, *refs),
        jax.ShapeDtypeStruct((q_rows + STAT, HD), F32),
        [VM] * 4,
        VM,
        flops=1 << 20,
        traffic=1 << 18,
    )(remote(query), remote(dec_key[0]), remote(dec_value[0]), own)

    slots_here = n * page_cap
    attended, cache_key, cache_value = call(
        lambda *refs: finish_kernel(kv_heads, steps, page_cap, *refs),
        (
            jax.ShapeDtypeStruct(dec_query.shape, BF16),
            jax.ShapeDtypeStruct((n, page_cap * PAGE, kvw), BF16),
            jax.ShapeDtypeStruct((n, page_cap * PAGE, kvw), BF16),
        ),
        [VM, VM],
        (VM, VM, VM),
        traffic=4 * tok * 2 * kvw,
    )(shares, mine)
    return (
        attended,
        cache_key.reshape(slots_here, PAGE, kvw),
        cache_value.reshape(slots_here, PAGE, kvw),
    )


def solution(mesh):
    return jax.shard_map(
        body,
        mesh=mesh,
        in_specs=(
            P(("groups", "section"), "tensor"),
            P(("groups", "section"), "tensor"),
            P("groups", None),
            P(),
            P(None, "tensor"),
            P(None, "tensor"),
            P("groups"),
            P("groups"),
            P("groups", None),
            P("groups"),
            P(("groups", "section"), None, "tensor"),
            P(("groups", "section"), None, "tensor"),
            P(("groups", "section"), None, "tensor"),
        ),
        out_specs=(
            P(("groups", "section"), None, "tensor"),
            P(("groups", "section"), None, "tensor"),
            P(("groups", "section"), None, "tensor"),
        ),
        check_vma=False,
    )
```

```python
import jax
import jax.numpy as jnp
from jax import lax
from jax.experimental import pallas as pl
from jax.experimental.pallas import tpu as pltpu
from jax.sharding import PartitionSpec as P

HD = 128
PAGE = 16
LOWEST = -1e30
EPS = 1e-06
STAT = 8
F32 = jnp.float32
BF16 = jnp.bfloat16
I32 = jnp.int32

VM = pl.BlockSpec(memory_space=pltpu.VMEM)
SM = pl.BlockSpec(memory_space=pltpu.SMEM)
ANY = pl.BlockSpec(memory_space=pl.ANY)
MIB = 1 << 20


def call(kernel, out_shape, in_specs, out_specs, scratch=(), limit=16, flops=0, traffic=0):
    return pl.pallas_call(
        kernel,
        out_shape=out_shape,
        in_specs=in_specs,
        out_specs=out_specs,
        scratch_shapes=list(scratch),
        compiler_params=pltpu.CompilerParams(vmem_limit_bytes=limit * MIB),
        cost_estimate=pl.CostEstimate(flops=flops, bytes_accessed=traffic, transcendentals=0),
    )


def rank_of(section, n):
    return jnp.where(section < n // 2, n - 2 - 2 * section, 2 * section - n + 1)


def section_of(rank, n):
    return n // 2 - 1 - rank // 2 + rank % 2 * (rank // 2 * 2 + 1)


def page_rank_of(section, n):
    z, y, length = section // 2, section % 2, n // 2
    return (1 - y) * length + (2 * length - z - n // 4) % length


def page_section_of(rank, n):
    length = n // 2
    return 2 * (length - 1 - (rank % length + n // 4 - 1) % length) + 1 - rank // length


def dot(a, b):
    return jnp.dot(a, b, preferred_element_type=F32)


def dot_t(a, b):
    return lax.dot_general(a, b, (((1,), (1,)), ((), ())), preferred_element_type=F32)


def diagonal(shape):
    return lax.broadcasted_iota(I32, shape, 0) == lax.broadcasted_iota(I32, shape, 1)


def column_to_row(column):
    rows = column.shape[0]
    return jnp.sum(jnp.where(diagonal((rows, rows)), column, 0.0), axis=0, keepdims=True)


def row_to_column(row):
    lanes = row.shape[1]
    return jnp.sum(jnp.where(diagonal((lanes, lanes)), row, 0.0), axis=1, keepdims=True)


def squares_of(rows):
    total = jnp.zeros((rows.shape[0], HD), F32)
    for c in range(0, rows.shape[1], HD):
        wide = rows[:, c : c + HD].astype(F32)
        total = total + wide * wide
    return total


def split_three(values):
    high = values.astype(BF16).astype(F32)
    rest = values - high
    middle = rest.astype(BF16).astype(F32)
    return high, middle, rest - middle


def softmax_parts(query, key, value, usable):
    scores = jnp.where(usable, dot_t(query, key) * HD**-0.5, LOWEST)
    top = jnp.max(scores, axis=1, keepdims=True)
    weights = jnp.where(usable, jnp.exp(scores - top), 0.0)
    return dot(weights.astype(BF16), value), top, jnp.sum(weights, axis=1, keepdims=True)


def prepare_kernel(n, lot, *refs):
    far, info, near, (route, sems) = refs[:6], refs[6], refs[7:12], refs[12:]
    img, half = near[2].shape
    first = pl.ds(pl.multiple_of(lax.axis_index("tensor") * half, half), near[0].shape[0])
    sources = (far[0], far[1].at[first], far[2].at[first], *far[3:])
    copies = [pltpu.make_async_copy(a, b, sems.at[i]) for i, (a, b) in enumerate(zip(sources, (route, *near)))]
    for c in copies:
        c.start()
    copies[0].wait()
    pos = lax.axis_index("section")
    own = jnp.zeros((1, img), I32)
    for e in range(n):
        own = jnp.where(pos == e, route[:, e * img : (e + 1) * img], own)
    marks = own == lax.broadcasted_iota(I32, (n, img), 0)
    ones = jnp.where(marks, 1.0, 0.0).astype(BF16)
    earlier = lax.broadcasted_iota(I32, (img, img), 0) < lax.broadcasted_iota(I32, (img, img), 1)
    prefix = dot(ones, jnp.where(earlier, 1.0, 0.0).astype(BF16))
    local = jnp.sum(jnp.where(marks, prefix, 0.0), axis=0, keepdims=True).astype(I32)
    info[...] = jnp.broadcast_to(rank_of(own, n) * lot + local, info.shape)
    for c in copies[1:]:
        c.wait()


def plan_tokens(n, img, lot, page_cap, small, info, slots, bias, starts):
    route, pages, count, tail, req = small
    pos = lax.axis_index("section")
    tok, width = bias.shape
    blocks = tok // PAGE
    lanes = lax.broadcasted_iota(I32, (1, n * lot), 1)
    source, inner = section_of(lanes // lot, n), lanes % lot
    fits = jnp.zeros((1, n * lot), I32)
    offset = jnp.zeros((1, n * lot), I32)
    for e in range(n):
        here = (route[:, e * img : (e + 1) * img] == pos).astype(I32)
        arriving = jnp.sum(here, axis=1, keepdims=True)
        fits = fits + jnp.where(source == e, arriving, 0)
        offset = offset + jnp.where(source > e, arriving, 0)
    info[...] = jnp.broadcast_to(jnp.where(inner < fits, offset + inner, -1), info.shape)
    total = jnp.int32(0)
    for r in range(n):
        starts[r] = total
        total = total + count[r]
    token = lax.broadcasted_iota(I32, (1, tok), 1) + pos * tok
    token_slot = jnp.full((1, tok), -1, I32)
    for b in range(n):
        r = req[b]
        first = starts[r] * PAGE
        last = first + (count[r] - 1) * PAGE + tail[r]
        token_slot = jnp.where((token >= first) & (token < last), b, token_slot)
    member = section_of(lax.broadcasted_iota(I32, (1, width), 1) // (width // n), n)
    bias[...] = jnp.where(row_to_column(token_slot.astype(F32)) == member.astype(F32), 0.0, LOWEST)
    for g in range(blocks):
        holder = pages[0, pos * blocks + g]
        slot = page_rank_of(holder, n) * page_cap
        for e in range(g):
            slot = slot + (pages[0, pos * blocks + e] == holder).astype(I32)
        slots[g] = slot


def scale_of(near, far):
    sums = jnp.sum(squares_of(near) + squares_of(far), axis=1, keepdims=True)
    return lax.rsqrt(sums / (2.0 * near.shape[1]) + EPS)


def normed_rows(rows, c, step, scale, gain):
    return (rows[:, c : c + step].astype(F32) * scale * gain).astype(BF16)


def add_part(total, at, normed, w, begin):
    part = dot(normed, w)
    columns = slice(at, at + part.shape[1])
    if begin:
        total[:, columns] = part
    else:
        total[:, columns] += part


def vis_kernel(n, lot, sizes, step, *refs):
    near, far, gain, query, key_held, value_held, w_key, w_value, info, out, key_rest, value_rest, total, sems = refs
    img, half = near.shape
    kvw = w_key.shape[1]
    me = lax.axis_index("tensor")
    held = key_held.shape[0]
    loads = {}
    at = held
    for size in sizes:
        side = me if at < half else 1 - me
        source = pl.ds(pl.multiple_of(side * half + at % half, size), size)
        number = 2 * len(loads)
        loads[at] = [
            pltpu.make_async_copy(w.at[source], kept.at[at - held : at - held + size], sems.at[number + i])
            for i, (w, kept) in enumerate(((w_key, key_rest), (w_value, value_rest)))
        ]
        for copy in loads[at]:
            copy.start()
        at += size
    scale = scale_of(near, far)
    for at in range(0, 2 * half, step):
        for copy in loads.get(at, ()):
            copy.wait()
        rows, side = (near, me) if at < half else (far, 1 - me)
        weights, w_at = ((key_held, value_held), at) if at < held else ((key_rest, value_rest), at - held)
        c = at % half
        columns = pl.ds(pl.multiple_of(side * half + c, step), step)
        normed = normed_rows(rows, c, step, scale, gain[:, columns])
        for w, col in zip(weights, (0, kvw)):
            add_part(total, col, normed, w[w_at : w_at + step, :], at == 0)
    slot = lax.broadcasted_iota(I32, (n * lot, img), 0)
    chosen = jnp.where(slot == info[0:1, :img], 1.0, 0.0).astype(BF16)
    packed = dot(chosen, total[...].astype(BF16)).astype(BF16)
    q_lots = out.shape[1] - lot
    for k in range(n):
        for j in range(query.shape[0] // q_lots):
            out[k, :q_lots, j * HD : (j + 1) * HD] = query[j * q_lots : (j + 1) * q_lots, :]
        out[k, q_lots:, :] = packed[k * lot : (k + 1) * lot, :]


def put_page(out, page_cap, slot, rows):
    chunk = page_cap * PAGE
    for h in range(rows.shape[1] // HD):
        at = pl.ds(pl.multiple_of((slot % page_cap) * PAGE + h * chunk, PAGE), PAGE)
        out[slot // page_cap, at, :] = rows[:, h * HD : (h + 1) * HD]


def text_kernel(n, img, lot, load, step, page_cap, *refs):
    (near_far, far, gain, w_key_far, w_value_far), small_far, refs = refs[:5], refs[5:10], refs[10:]
    (out, bias, base, info, slots), (near, w_key, w_value, total, starts, sems), small = refs[:5], refs[5:11], refs[11:]
    half = near.shape[1]
    kvw = w_key.shape[1]
    me = lax.axis_index("tensor")
    first = pltpu.make_async_copy(near_far, near, sems.at[0])
    first.start()
    used = sems.shape[0] - len(small)
    lists = [pltpu.make_async_copy(a, b, sems.at[used + i]) for i, (a, b) in enumerate(zip(small_far, small))]
    for copy in lists:
        copy.start()
    loads = []
    for side in (me, 1 - me):
        for c in range(0, half, load):
            at = len(loads) * load
            columns = pl.ds(pl.multiple_of(side * half + c, load), load)
            pair = [
                pltpu.make_async_copy(w.at[columns], held.at[at : at + load], sems.at[2 * len(loads) + i])
                for i, (w, held) in enumerate(((w_key_far, w_key), (w_value_far, w_value)), 1)
            ]
            for copy in pair:
                copy.start()
            loads.append(pair)
    sums = squares_of(far)
    for copy in lists:
        copy.wait()
    plan_tokens(n, img, lot, page_cap, small, info, slots, bias, starts)
    first.wait()
    sums = jnp.sum(squares_of(near) + sums, axis=1, keepdims=True)
    scale = lax.rsqrt(sums / (2.0 * half) + EPS)
    for i, pair in enumerate(loads):
        for copy in pair:
            copy.wait()
        for at in range(i * load, (i + 1) * load, step):
            rows, side = (near, me) if at < half else (far, 1 - me)
            c = at % half
            columns = pl.ds(pl.multiple_of(side * half + c, step), step)
            normed = normed_rows(rows, c, step, scale, gain[:, columns])
            for w, col in ((w_key, 0), (w_value, kvw)):
                add_part(total, col, normed, w[at : at + step, :], at == 0)
    out[...] = total[...].astype(BF16)
    base[...] = jnp.zeros(base.shape, BF16)
    tok = near.shape[0]
    for g in range(tok // PAGE):
        put_page(base, page_cap, slots[g], out[g * PAGE : (g + 1) * PAGE, :])


def attend_kernel(n, cap, lot, page_cap, kv_heads, slots, info, kv_text, arrived, bias, base, sent, own, *scratch):
    out, mixed, held, rows_held, sems = scratch
    order = [page_section_of(k, n) for k in range(n)]
    rank = rank_of(lax.axis_index("section"), n)
    tok = kv_text.shape[0]
    kvw = kv_heads * HD
    q_lots = arrived.shape[1] - lot
    reach = min(tok, n * cap)
    hit = lax.broadcasted_iota(I32, (reach, n * lot), 0) == info[0:1, :]
    hot = jnp.where(hit, 1.0, 0.0)
    covered = jnp.sum(hot, axis=1, keepdims=True) > 0.0
    incoming = jnp.concatenate([arrived[k, q_lots:, :] for k in range(n)], axis=0)
    placed = dot(hot.astype(BF16), incoming)
    mixed[...] = jnp.where(covered, placed, kv_text[:reach, :].astype(F32)).astype(BF16)
    groups = arrived.shape[2] // HD // kv_heads
    rows = groups * q_lots
    pages = base.shape[1]
    out[:, :pages, :] = base[...]
    for g in range(reach // PAGE):
        put_page(out, page_cap, slots[g], mixed[g * PAGE : (g + 1) * PAGE, :])
    first = pltpu.make_async_copy(out.at[:, :pages, :], sent.at[:, :pages, :], sems.at[0])
    first.start()
    for g in range(kv_heads):
        query = jnp.concatenate(
            [
                arrived[k, :q_lots, (g * groups + j) * HD : (g * groups + j + 1) * HD]
                for k in range(n)
                for j in range(groups)
            ],
            axis=0,
        )
        cols = slice(g * HD, (g + 1) * HD)
        vcols = slice(kvw + g * HD, kvw + (g + 1) * HD)
        key = jnp.concatenate([mixed[:, cols], kv_text[reach:, cols]], axis=0)
        value = jnp.concatenate([mixed[:, vcols], kv_text[reach:, vcols]], axis=0)
        scores = dot_t(key, query) * HD**-0.5 + bias[...]
        top = jnp.max(scores, axis=0, keepdims=True)
        weights = jnp.exp(scores - top)
        rows_held[g : g + 1, :] = top
        rows_held[kv_heads + g : kv_heads + g + 1, :] = jnp.sum(weights, axis=0, keepdims=True)
        numerator = lax.dot_general(
            weights.astype(BF16), value, (((0,), (0,)), ((), ())), preferred_element_type=F32
        )
        held[g * n * rows : (g + 1) * n * rows, :] = numerator
        own[g * rows : (g + 1) * rows, :] = held[pl.ds(pl.multiple_of((g * n + rank) * rows, rows), rows), :]
        numerator = numerator.astype(BF16)
        for k in range(n):
            to = order.index(section_of(k, n))
            out[to, pages + g * rows : pages + (g + 1) * rows, :] = numerator[k * rows : (k + 1) * rows, :]
    stat_rows = 2 * kv_heads
    share = HD // rows
    window = pl.ds(pl.multiple_of(rank // share * HD, HD), HD)
    own[kv_heads * rows : kv_heads * rows + stat_rows, :] = rows_held[:stat_rows, window]
    blank = jnp.zeros((PAGE - 3 * stat_rows, HD), F32)
    for w in range(-(-n // share)):
        stats = rows_held[:stat_rows, w * HD : (w + 1) * HD]
        lines = jnp.concatenate([*split_three(stats), blank], axis=0).astype(BF16)
        for k in range(w * share, min(n, (w + 1) * share)):
            out[order.index(section_of(k, n)), pages + kv_heads * rows :, :] = lines
    last = pltpu.make_async_copy(out.at[:, pages:, :], sent.at[:, pages:, :], sems.at[1])
    last.start()
    first.wait()
    last.wait()


def pick_column(row, rows, start):
    shape = (rows, HD)
    chosen = lax.broadcasted_iota(I32, shape, 1) == lax.broadcasted_iota(I32, shape, 0) + start
    return jnp.sum(jnp.where(chosen, row, 0.0), axis=1, keepdims=True)


def combine(pieces, highest):
    numerator, total = 0.0, 0.0
    for rows, top, weight in pieces:
        scale = jnp.exp(top - highest)
        numerator = numerator + rows * scale
        total = total + weight * scale
    return numerator, total


def fresh_kernel(n, kv_heads, steps, query, key, value, own, mine):
    rows = query.shape[0] // kv_heads
    every = kv_heads * rows
    start = rank_of(lax.axis_index("section"), n) % (HD // rows) * rows
    row = lax.broadcasted_iota(I32, (rows, steps), 0)
    causal = lax.broadcasted_iota(I32, (rows, steps), 1) <= row % steps
    tops, totals = [], []
    for g in range(kv_heads):
        cols = slice(g * HD, (g + 1) * HD)
        at = slice(g * rows, (g + 1) * rows)
        fresh = softmax_parts(query[at, :], key[:, cols], value[:, cols], causal)
        share = (
            own[at, :],
            pick_column(own[every + g : every + g + 1, :], rows, start),
            pick_column(own[every + kv_heads + g : every + kv_heads + g + 1, :], rows, start),
        )
        highest = jnp.maximum(fresh[1], share[1])
        numerator, total = combine((fresh, share), highest)
        mine[at, :] = numerator
        tops.append(highest)
        totals.append(total)
    line = column_to_row(jnp.concatenate(tops + totals, axis=0))
    mine[every:, :] = jnp.broadcast_to(line, (STAT, line.shape[1]))


def finish_kernel(kv_heads, steps, page_cap, shares, mine, attended, keys, values):
    n = shares.shape[0]
    pos = lax.axis_index("section")
    every = mine.shape[0] - STAT
    rows = every // kv_heads
    start = rank_of(pos, n) % (HD // rows) * rows
    chunk = page_cap * PAGE
    halves = keys.shape[2] // HD
    for k in range(n):
        for i, out in enumerate((keys, values)):
            for h in range(halves):
                part = i * halves + h
                out[page_section_of(k, n), :, h * HD : (h + 1) * HD] = shares[k, part * chunk : (part + 1) * chunk, :]
    pages = 2 * halves * chunk
    stats = row_to_column(mine[every : every + 1, :])
    lines = []
    for k in range(n):
        three = shares[k, pages + every :, :].astype(F32)
        size = 2 * kv_heads
        lines.append(three[:size] + three[size : 2 * size] + three[2 * size : 3 * size])
    for g in range(kv_heads):
        at = slice(g * rows, (g + 1) * rows)
        pieces = [(mine[at, :], stats[at], stats[every + g * rows : every + (g + 1) * rows])]
        for k in range(n):
            away = pos != page_section_of(k, n)
            top = jnp.where(away, pick_column(lines[k][g : g + 1], rows, start), LOWEST)
            weight = jnp.where(away, pick_column(lines[k][kv_heads + g : kv_heads + g + 1], rows, start), 0.0)
            share = shares[k, pages + g * rows : pages + (g + 1) * rows, :].astype(F32)
            pieces.append((share, top, weight))
        highest = pieces[0][1]
        for p in pieces[1:]:
            highest = jnp.maximum(highest, p[1])
        numerator, total = combine(pieces, highest)
        result = (numerator / total).astype(BF16)
        for h in range(rows // steps):
            to = (g * rows // steps + h) * HD
            attended[0, :, to : to + HD] = result[h * steps : (h + 1) * steps, :]


def body(
    text_rows,
    vis_rows,
    img_route,
    norm_gain,
    w_key,
    w_value,
    page_count,
    tail_len,
    page_dest,
    dec_req,
    dec_query,
    dec_key,
    dec_value,
):
    n = lax.axis_size("section")
    tok, half = text_rows.shape
    img = vis_rows.shape[0]
    kvw = w_key.shape[1]
    kv_heads = kvw // HD
    _, steps, q_width = dec_query.shape
    heads = q_width // HD
    q_rows = heads * steps
    blocks = tok // PAGE
    cap = max(2, (2 * img + n - 1) // n)
    page_cap = max(1, (blocks + n - 1) // n)

    def across(array):
        return lax.ppermute(array, "tensor", [(0, 1), (1, 0)])

    def exchange(array, section_at):
        order = [[section_at(rank, n) for rank in range(n)]]
        return lax.all_to_all(array, "section", split_axis=0, concat_axis=0, tiled=True, axis_index_groups=order)

    def remote(array):
        return pltpu.with_memory_space_constraint(array, pltpu.HBM)

    def local(array):
        return pltpu.with_memory_space_constraint(array, pltpu.VMEM)

    vis_far = across(vis_rows)
    text_far = across(text_rows)
    query = dec_query.reshape(steps, heads, HD).transpose(1, 0, 2).reshape(q_rows, HD)

    lot = -(-cap // PAGE) * PAGE
    q_lots = q_rows * HD // (2 * kvw)
    gain = norm_gain.reshape(1, 2 * half)
    load = min(2048, half)
    step = min(1024, load // 2)
    kept = load + load // 2
    arguments = (img_route.T, w_key, w_value, vis_rows, gain, query)
    info, key_held, value_held, vis_near, gain_near, query_near = call(
        lambda *refs: prepare_kernel(n, lot, *refs),
        (
            jax.ShapeDtypeStruct((STAT, img), I32),
            pltpu.VMEM((kept, kvw), BF16),
            pltpu.VMEM((kept, kvw), BF16),
            *[pltpu.VMEM(a.shape, a.dtype) for a in arguments[3:]],
        ),
        [ANY] * len(arguments),
        (VM,) * 6,
        [pltpu.VMEM((1, n * img), I32), pltpu.SemaphoreType.DMA((len(arguments),))],
        flops=1 << 20,
        traffic=2 * 2 * half * 2 * kvw * 2,
    )(*[remote(a) for a in arguments])

    left = 2 * half - kept
    sizes = [half - kept, *[load] * (half // load - 1), *[load // 2] * 2]
    packed = call(
        lambda *refs: vis_kernel(n, lot, sizes, step, *refs),
        pltpu.VMEM((n, q_lots + lot, 2 * kvw), BF16),
        [VM] * 6 + [ANY] * 2 + [VM],
        VM,
        [
            pltpu.VMEM((left, kvw), BF16),
            pltpu.VMEM((left, kvw), BF16),
            pltpu.VMEM((img, 2 * kvw), F32),
            pltpu.SemaphoreType.DMA((2 * len(sizes),)),
        ],
        flops=64 * img * 2 * half * 2 * kvw,
        traffic=2 * img * 2 * half + 8 * half * kvw,
    )(
        local(vis_near),
        vis_far,
        local(gain_near),
        local(query_near),
        local(key_held),
        local(value_held),
        remote(w_key),
        remote(w_value),
        info,
    )
    arrived = exchange(packed, section_of)

    block = page_cap * PAGE * 2 * kv_heads + q_rows + PAGE
    lists = (img_route.T, page_dest.T, page_count, tail_len, dec_req)
    kv_text, bias, base, info, slots = call(
        lambda *refs: text_kernel(n, img, lot, load, step, page_cap, *refs),
        (
            jax.ShapeDtypeStruct((tok, 2 * kvw), BF16),
            jax.ShapeDtypeStruct((tok, n * q_rows // kv_heads), F32),
            jax.ShapeDtypeStruct((n, block - q_rows - PAGE, HD), BF16),
            jax.ShapeDtypeStruct((STAT, n * lot), I32),
            jax.ShapeDtypeStruct((blocks,), I32),
        ),
        [ANY, VM, VM] + [ANY] * 7,
        (VM, VM, VM, VM, SM),
        [
            pltpu.VMEM((tok, half), BF16),
            pltpu.VMEM(w_key.shape, BF16),
            pltpu.VMEM(w_value.shape, BF16),
            pltpu.VMEM((tok, 2 * kvw), F32),
            pltpu.SMEM((n,), I32),
            pltpu.SemaphoreType.DMA((1 + 4 * half // load + len(lists),)),
            *[(pltpu.VMEM if i == 0 else pltpu.SMEM)(a.shape, a.dtype) for i, a in enumerate(lists)],
        ],
        limit=24,
        flops=2 * tok * 2 * half * 2 * kvw,
        traffic=2 * tok * 2 * half + 8 * half * kvw,
    )(remote(text_rows), text_far, remote(gain), remote(w_key), remote(w_value), *[remote(a) for a in lists])

    sent, own = call(
        lambda *refs: attend_kernel(n, cap, lot, page_cap, kv_heads, *refs),
        (
            jax.ShapeDtypeStruct((n, block, HD), BF16),
            jax.ShapeDtypeStruct((q_rows + STAT, HD), F32),
        ),
        [SM] + [VM] * 5,
        (ANY, VM),
        [
            pltpu.VMEM((n, block, HD), BF16),
            pltpu.VMEM((min(tok, n * cap), 2 * kvw), BF16),
            pltpu.VMEM((n * q_rows, HD), F32),
            pltpu.VMEM((STAT, n * q_rows // kv_heads), F32),
            pltpu.SemaphoreType.DMA((2,)),
        ],
        flops=4 * n * q_rows * tok * HD,
        traffic=n * (q_rows + STAT) * HD * 4,
    )(slots, info, kv_text, arrived, bias, base)
    shares = exchange(sent, page_section_of)

    mine = call(
        lambda *refs: fresh_kernel(n, kv_heads, steps, *refs),
        jax.ShapeDtypeStruct((q_rows + STAT, HD), F32),
        [VM] * 4,
        VM,
        flops=1 << 20,
        traffic=1 << 18,
    )(remote(query), remote(dec_key[0]), remote(dec_value[0]), own)

    slots_here = n * page_cap
    attended, cache_key, cache_value = call(
        lambda *refs: finish_kernel(kv_heads, steps, page_cap, *refs),
        (
            jax.ShapeDtypeStruct(dec_query.shape, BF16),
            jax.ShapeDtypeStruct((n, page_cap * PAGE, kvw), BF16),
            jax.ShapeDtypeStruct((n, page_cap * PAGE, kvw), BF16),
        ),
        [VM, VM],
        (VM, VM, VM),
        traffic=4 * tok * 2 * kvw,
    )(shares, mine)
    return (
        attended,
        cache_key.reshape(slots_here, PAGE, kvw),
        cache_value.reshape(slots_here, PAGE, kvw),
    )


def solution(mesh):
    return jax.shard_map(
        body,
        mesh=mesh,
        in_specs=(
            P(("groups", "section"), "tensor"),
            P(("groups", "section"), "tensor"),
            P("groups", None),
            P(),
            P(None, "tensor"),
            P(None, "tensor"),
            P("groups"),
            P("groups"),
            P("groups", None),
            P("groups"),
            P(("groups", "section"), None, "tensor"),
            P(("groups", "section"), None, "tensor"),
            P(("groups", "section"), None, "tensor"),
        ),
        out_specs=(
            P(("groups", "section"), None, "tensor"),
            P(("groups", "section"), None, "tensor"),
            P(("groups", "section"), None, "tensor"),
        ),
        check_vma=False,
    )
```

```python
import jax
import jax.numpy as jnp
from jax import lax
from jax.experimental import pallas as pl
from jax.experimental.pallas import tpu as pltpu
from jax.sharding import PartitionSpec as P

HD = 128
PAGE = 16
LOWEST = -1e30
EPS = 1e-06
STAT = 8
F32 = jnp.float32
BF16 = jnp.bfloat16
I32 = jnp.int32

VM = pl.BlockSpec(memory_space=pltpu.VMEM)
SM = pl.BlockSpec(memory_space=pltpu.SMEM)
ANY = pl.BlockSpec(memory_space=pl.ANY)
MIB = 1 << 20


def call(kernel, out_shape, in_specs, out_specs, scratch=(), limit=16, flops=0, traffic=0):
    return pl.pallas_call(
        kernel,
        out_shape=out_shape,
        in_specs=in_specs,
        out_specs=out_specs,
        scratch_shapes=list(scratch),
        compiler_params=pltpu.CompilerParams(vmem_limit_bytes=limit * MIB),
        cost_estimate=pl.CostEstimate(flops=flops, bytes_accessed=traffic, transcendentals=0),
    )


def rank_of(section, n):
    return jnp.where(section < n // 2, n - 2 - 2 * section, 2 * section - n + 1)


def section_of(rank, n):
    return n // 2 - 1 - rank // 2 + rank % 2 * (rank // 2 * 2 + 1)


def page_rank_of(section, n):
    z, y, length = section // 2, section % 2, n // 2
    return y * length + (2 * length - z - n // 4) % length


def page_section_of(rank, n):
    length = n // 2
    return 2 * (length - 1 - (rank % length + n // 4 - 1) % length) + rank // length


def dot(a, b):
    return jnp.dot(a, b, preferred_element_type=F32)


def dot_t(a, b):
    return lax.dot_general(a, b, (((1,), (1,)), ((), ())), preferred_element_type=F32)


def diagonal(shape):
    return lax.broadcasted_iota(I32, shape, 0) == lax.broadcasted_iota(I32, shape, 1)


def column_to_row(column):
    rows = column.shape[0]
    return jnp.sum(jnp.where(diagonal((rows, rows)), column, 0.0), axis=0, keepdims=True)


def row_to_column(row):
    lanes = row.shape[1]
    return jnp.sum(jnp.where(diagonal((lanes, lanes)), row, 0.0), axis=1, keepdims=True)


def squares_of(rows):
    total = jnp.zeros((rows.shape[0], HD), F32)
    for c in range(0, rows.shape[1], HD):
        wide = rows[:, c : c + HD].astype(F32)
        total = total + wide * wide
    return total


def split_three(values):
    high = values.astype(BF16).astype(F32)
    rest = values - high
    middle = rest.astype(BF16).astype(F32)
    return high, middle, rest - middle


def softmax_parts(query, key, value, usable):
    scores = jnp.where(usable, dot_t(query, key) * HD**-0.5, LOWEST)
    top = jnp.max(scores, axis=1, keepdims=True)
    weights = jnp.where(usable, jnp.exp(scores - top), 0.0)
    return dot(weights.astype(BF16), value), top, jnp.sum(weights, axis=1, keepdims=True)


def prepare_kernel(n, lot, *refs):
    far, info, near, (route, sems) = refs[:6], refs[6], refs[7:12], refs[12:]
    img, half = near[2].shape
    first = pl.ds(pl.multiple_of(lax.axis_index("tensor") * half, half), near[0].shape[0])
    sources = (far[0], far[1].at[first], far[2].at[first], *far[3:])
    copies = [pltpu.make_async_copy(a, b, sems.at[i]) for i, (a, b) in enumerate(zip(sources, (route, *near)))]
    for c in copies:
        c.start()
    copies[0].wait()
    pos = lax.axis_index("section")
    own = jnp.zeros((1, img), I32)
    for e in range(n):
        own = jnp.where(pos == e, route[:, e * img : (e + 1) * img], own)
    marks = own == lax.broadcasted_iota(I32, (n, img), 0)
    ones = jnp.where(marks, 1.0, 0.0).astype(BF16)
    earlier = lax.broadcasted_iota(I32, (img, img), 0) < lax.broadcasted_iota(I32, (img, img), 1)
    prefix = dot(ones, jnp.where(earlier, 1.0, 0.0).astype(BF16))
    local = jnp.sum(jnp.where(marks, prefix, 0.0), axis=0, keepdims=True).astype(I32)
    info[...] = jnp.broadcast_to(rank_of(own, n) * lot + local, info.shape)
    for c in copies[1:]:
        c.wait()


def plan_tokens(n, img, lot, page_cap, small, info, slots, bias, starts):
    route, pages, count, tail, req = small
    pos = lax.axis_index("section")
    tok, width = bias.shape
    blocks = tok // PAGE
    lanes = lax.broadcasted_iota(I32, (1, n * lot), 1)
    source, inner = section_of(lanes // lot, n), lanes % lot
    fits = jnp.zeros((1, n * lot), I32)
    offset = jnp.zeros((1, n * lot), I32)
    for e in range(n):
        here = (route[:, e * img : (e + 1) * img] == pos).astype(I32)
        arriving = jnp.sum(here, axis=1, keepdims=True)
        fits = fits + jnp.where(source == e, arriving, 0)
        offset = offset + jnp.where(source > e, arriving, 0)
    info[...] = jnp.broadcast_to(jnp.where(inner < fits, offset + inner, -1), info.shape)
    total = jnp.int32(0)
    for r in range(n):
        starts[r] = total
        total = total + count[r]
    token = lax.broadcasted_iota(I32, (1, tok), 1) + pos * tok
    token_slot = jnp.full((1, tok), -1, I32)
    for b in range(n):
        r = req[b]
        first = starts[r] * PAGE
        last = first + (count[r] - 1) * PAGE + tail[r]
        token_slot = jnp.where((token >= first) & (token < last), b, token_slot)
    member = section_of(lax.broadcasted_iota(I32, (1, width), 1) // (width // n), n)
    bias[...] = jnp.where(row_to_column(token_slot.astype(F32)) == member.astype(F32), 0.0, LOWEST)
    for g in range(blocks):
        holder = pages[0, pos * blocks + g]
        slot = page_rank_of(holder, n) * page_cap
        for e in range(g):
            slot = slot + (pages[0, pos * blocks + e] == holder).astype(I32)
        slots[g] = slot


def scale_of(near, far):
    sums = jnp.sum(squares_of(near) + squares_of(far), axis=1, keepdims=True)
    return lax.rsqrt(sums / (2.0 * near.shape[1]) + EPS)


def normed_rows(rows, c, step, scale, gain):
    return (rows[:, c : c + step].astype(F32) * scale * gain).astype(BF16)


def add_part(total, at, normed, w, begin):
    part = dot(normed, w)
    columns = slice(at, at + part.shape[1])
    if begin:
        total[:, columns] = part
    else:
        total[:, columns] += part


def vis_kernel(n, lot, sizes, step, *refs):
    near, far, gain, query, key_held, value_held, w_key, w_value, info, out, key_rest, value_rest, total, sems = refs
    img, half = near.shape
    kvw = w_key.shape[1]
    me = lax.axis_index("tensor")
    held = key_held.shape[0]
    loads = {}
    at = held
    for size in sizes:
        side = me if at < half else 1 - me
        source = pl.ds(pl.multiple_of(side * half + at % half, size), size)
        number = 2 * len(loads)
        loads[at] = [
            pltpu.make_async_copy(w.at[source], kept.at[at - held : at - held + size], sems.at[number + i])
            for i, (w, kept) in enumerate(((w_key, key_rest), (w_value, value_rest)))
        ]
        for copy in loads[at]:
            copy.start()
        at += size
    scale = scale_of(near, far)
    for at in range(0, 2 * half, step):
        for copy in loads.get(at, ()):
            copy.wait()
        rows, side = (near, me) if at < half else (far, 1 - me)
        weights, w_at = ((key_held, value_held), at) if at < held else ((key_rest, value_rest), at - held)
        c = at % half
        columns = pl.ds(pl.multiple_of(side * half + c, step), step)
        normed = normed_rows(rows, c, step, scale, gain[:, columns])
        for w, col in zip(weights, (0, kvw)):
            add_part(total, col, normed, w[w_at : w_at + step, :], at == 0)
    slot = lax.broadcasted_iota(I32, (n * lot, img), 0)
    chosen = jnp.where(slot == info[0:1, :img], 1.0, 0.0).astype(BF16)
    packed = dot(chosen, total[...].astype(BF16)).astype(BF16)
    q_lots = out.shape[1] - lot
    for k in range(n):
        for j in range(query.shape[0] // q_lots):
            out[k, :q_lots, j * HD : (j + 1) * HD] = query[j * q_lots : (j + 1) * q_lots, :]
        out[k, q_lots:, :] = packed[k * lot : (k + 1) * lot, :]


def put_page(out, page_cap, slot, rows):
    chunk = page_cap * PAGE
    for h in range(rows.shape[1] // HD):
        at = pl.ds(pl.multiple_of((slot % page_cap) * PAGE + h * chunk, PAGE), PAGE)
        out[slot // page_cap, at, :] = rows[:, h * HD : (h + 1) * HD]


def text_kernel(n, img, lot, load, step, page_cap, *refs):
    (near_far, far, gain, w_key_far, w_value_far), small_far, refs = refs[:5], refs[5:10], refs[10:]
    (out, bias, base, info, slots), (near, w_key, w_value, total, starts, sems), small = refs[:5], refs[5:11], refs[11:]
    half = near.shape[1]
    kvw = w_key.shape[1]
    me = lax.axis_index("tensor")
    first = pltpu.make_async_copy(near_far, near, sems.at[0])
    first.start()
    used = sems.shape[0] - len(small)
    lists = [pltpu.make_async_copy(a, b, sems.at[used + i]) for i, (a, b) in enumerate(zip(small_far, small))]
    for copy in lists:
        copy.start()
    loads = []
    for side in (me, 1 - me):
        for c in range(0, half, load):
            at = len(loads) * load
            columns = pl.ds(pl.multiple_of(side * half + c, load), load)
            pair = [
                pltpu.make_async_copy(w.at[columns], held.at[at : at + load], sems.at[2 * len(loads) + i])
                for i, (w, held) in enumerate(((w_key_far, w_key), (w_value_far, w_value)), 1)
            ]
            for copy in pair:
                copy.start()
            loads.append(pair)
    sums = squares_of(far)
    for copy in lists:
        copy.wait()
    plan_tokens(n, img, lot, page_cap, small, info, slots, bias, starts)
    first.wait()
    sums = jnp.sum(squares_of(near) + sums, axis=1, keepdims=True)
    scale = lax.rsqrt(sums / (2.0 * half) + EPS)
    for i, pair in enumerate(loads):
        for copy in pair:
            copy.wait()
        for at in range(i * load, (i + 1) * load, step):
            rows, side = (near, me) if at < half else (far, 1 - me)
            c = at % half
            columns = pl.ds(pl.multiple_of(side * half + c, step), step)
            normed = normed_rows(rows, c, step, scale, gain[:, columns])
            for w, col in ((w_key, 0), (w_value, kvw)):
                add_part(total, col, normed, w[at : at + step, :], at == 0)
    out[...] = total[...].astype(BF16)
    base[...] = jnp.zeros(base.shape, BF16)
    tok = near.shape[0]
    for g in range(tok // PAGE):
        put_page(base, page_cap, slots[g], out[g * PAGE : (g + 1) * PAGE, :])


def attend_kernel(n, cap, lot, page_cap, kv_heads, slots, info, kv_text, arrived, bias, base, sent, own, *scratch):
    out, mixed, held, rows_held, sems = scratch
    order = [page_section_of(k, n) for k in range(n)]
    rank = rank_of(lax.axis_index("section"), n)
    tok = kv_text.shape[0]
    kvw = kv_heads * HD
    q_lots = arrived.shape[1] - lot
    reach = min(tok, n * cap)
    hit = lax.broadcasted_iota(I32, (reach, n * lot), 0) == info[0:1, :]
    hot = jnp.where(hit, 1.0, 0.0)
    covered = jnp.sum(hot, axis=1, keepdims=True) > 0.0
    incoming = jnp.concatenate([arrived[k, q_lots:, :] for k in range(n)], axis=0)
    placed = dot(hot.astype(BF16), incoming)
    mixed[...] = jnp.where(covered, placed, kv_text[:reach, :].astype(F32)).astype(BF16)
    groups = arrived.shape[2] // HD // kv_heads
    rows = groups * q_lots
    pages = base.shape[1]
    out[:, :pages, :] = base[...]
    for g in range(reach // PAGE):
        put_page(out, page_cap, slots[g], mixed[g * PAGE : (g + 1) * PAGE, :])
    first = pltpu.make_async_copy(out.at[:, :pages, :], sent.at[:, :pages, :], sems.at[0])
    first.start()
    for g in range(kv_heads):
        query = jnp.concatenate(
            [
                arrived[k, :q_lots, (g * groups + j) * HD : (g * groups + j + 1) * HD]
                for k in range(n)
                for j in range(groups)
            ],
            axis=0,
        )
        cols = slice(g * HD, (g + 1) * HD)
        vcols = slice(kvw + g * HD, kvw + (g + 1) * HD)
        key = jnp.concatenate([mixed[:, cols], kv_text[reach:, cols]], axis=0)
        value = jnp.concatenate([mixed[:, vcols], kv_text[reach:, vcols]], axis=0)
        scores = dot_t(key, query) * HD**-0.5 + bias[...]
        top = jnp.max(scores, axis=0, keepdims=True)
        weights = jnp.exp(scores - top)
        rows_held[g : g + 1, :] = top
        rows_held[kv_heads + g : kv_heads + g + 1, :] = jnp.sum(weights, axis=0, keepdims=True)
        numerator = lax.dot_general(
            weights.astype(BF16), value, (((0,), (0,)), ((), ())), preferred_element_type=F32
        )
        held[g * n * rows : (g + 1) * n * rows, :] = numerator
        own[g * rows : (g + 1) * rows, :] = held[pl.ds(pl.multiple_of((g * n + rank) * rows, rows), rows), :]
        numerator = numerator.astype(BF16)
        for k in range(n):
            to = order.index(section_of(k, n))
            out[to, pages + g * rows : pages + (g + 1) * rows, :] = numerator[k * rows : (k + 1) * rows, :]
    stat_rows = 2 * kv_heads
    share = HD // rows
    window = pl.ds(pl.multiple_of(rank // share * HD, HD), HD)
    own[kv_heads * rows : kv_heads * rows + stat_rows, :] = rows_held[:stat_rows, window]
    blank = jnp.zeros((PAGE - 3 * stat_rows, HD), F32)
    for w in range(-(-n // share)):
        stats = rows_held[:stat_rows, w * HD : (w + 1) * HD]
        lines = jnp.concatenate([*split_three(stats), blank], axis=0).astype(BF16)
        for k in range(w * share, min(n, (w + 1) * share)):
            out[order.index(section_of(k, n)), pages + kv_heads * rows :, :] = lines
    last = pltpu.make_async_copy(out.at[:, pages:, :], sent.at[:, pages:, :], sems.at[1])
    last.start()
    first.wait()
    last.wait()


def pick_column(row, rows, start):
    shape = (rows, HD)
    chosen = lax.broadcasted_iota(I32, shape, 1) == lax.broadcasted_iota(I32, shape, 0) + start
    return jnp.sum(jnp.where(chosen, row, 0.0), axis=1, keepdims=True)


def combine(pieces, highest):
    numerator, total = 0.0, 0.0
    for rows, top, weight in pieces:
        scale = jnp.exp(top - highest)
        numerator = numerator + rows * scale
        total = total + weight * scale
    return numerator, total


def fresh_kernel(n, kv_heads, steps, query, key, value, own, mine):
    rows = query.shape[0] // kv_heads
    every = kv_heads * rows
    start = rank_of(lax.axis_index("section"), n) % (HD // rows) * rows
    row = lax.broadcasted_iota(I32, (rows, steps), 0)
    causal = lax.broadcasted_iota(I32, (rows, steps), 1) <= row % steps
    tops, totals = [], []
    for g in range(kv_heads):
        cols = slice(g * HD, (g + 1) * HD)
        at = slice(g * rows, (g + 1) * rows)
        fresh = softmax_parts(query[at, :], key[:, cols], value[:, cols], causal)
        share = (
            own[at, :],
            pick_column(own[every + g : every + g + 1, :], rows, start),
            pick_column(own[every + kv_heads + g : every + kv_heads + g + 1, :], rows, start),
        )
        highest = jnp.maximum(fresh[1], share[1])
        numerator, total = combine((fresh, share), highest)
        mine[at, :] = numerator
        tops.append(highest)
        totals.append(total)
    line = column_to_row(jnp.concatenate(tops + totals, axis=0))
    mine[every:, :] = jnp.broadcast_to(line, (STAT, line.shape[1]))


def finish_kernel(kv_heads, steps, page_cap, shares, mine, attended, keys, values):
    n = shares.shape[0]
    pos = lax.axis_index("section")
    every = mine.shape[0] - STAT
    rows = every // kv_heads
    start = rank_of(pos, n) % (HD // rows) * rows
    chunk = page_cap * PAGE
    halves = keys.shape[2] // HD
    for k in range(n):
        for i, out in enumerate((keys, values)):
            for h in range(halves):
                part = i * halves + h
                out[page_section_of(k, n), :, h * HD : (h + 1) * HD] = shares[k, part * chunk : (part + 1) * chunk, :]
    pages = 2 * halves * chunk
    stats = row_to_column(mine[every : every + 1, :])
    lines = []
    for k in range(n):
        three = shares[k, pages + every :, :].astype(F32)
        size = 2 * kv_heads
        lines.append(three[:size] + three[size : 2 * size] + three[2 * size : 3 * size])
    for g in range(kv_heads):
        at = slice(g * rows, (g + 1) * rows)
        pieces = [(mine[at, :], stats[at], stats[every + g * rows : every + (g + 1) * rows])]
        for k in range(n):
            away = pos != page_section_of(k, n)
            top = jnp.where(away, pick_column(lines[k][g : g + 1], rows, start), LOWEST)
            weight = jnp.where(away, pick_column(lines[k][kv_heads + g : kv_heads + g + 1], rows, start), 0.0)
            share = shares[k, pages + g * rows : pages + (g + 1) * rows, :].astype(F32)
            pieces.append((share, top, weight))
        highest = pieces[0][1]
        for p in pieces[1:]:
            highest = jnp.maximum(highest, p[1])
        numerator, total = combine(pieces, highest)
        result = (numerator / total).astype(BF16)
        for h in range(rows // steps):
            to = (g * rows // steps + h) * HD
            attended[0, :, to : to + HD] = result[h * steps : (h + 1) * steps, :]


def body(
    text_rows,
    vis_rows,
    img_route,
    norm_gain,
    w_key,
    w_value,
    page_count,
    tail_len,
    page_dest,
    dec_req,
    dec_query,
    dec_key,
    dec_value,
):
    n = lax.axis_size("section")
    tok, half = text_rows.shape
    img = vis_rows.shape[0]
    kvw = w_key.shape[1]
    kv_heads = kvw // HD
    _, steps, q_width = dec_query.shape
    heads = q_width // HD
    q_rows = heads * steps
    blocks = tok // PAGE
    cap = max(2, (2 * img + n - 1) // n)
    page_cap = max(1, (blocks + n - 1) // n)

    def across(array):
        return lax.ppermute(array, "tensor", [(0, 1), (1, 0)])

    def exchange(array, section_at):
        order = [[section_at(rank, n) for rank in range(n)]]
        return lax.all_to_all(array, "section", split_axis=0, concat_axis=0, tiled=True, axis_index_groups=order)

    def remote(array):
        return pltpu.with_memory_space_constraint(array, pltpu.HBM)

    def local(array):
        return pltpu.with_memory_space_constraint(array, pltpu.VMEM)

    vis_far = across(vis_rows)
    text_far = across(text_rows)
    query = dec_query.reshape(steps, heads, HD).transpose(1, 0, 2).reshape(q_rows, HD)

    lot = -(-cap // PAGE) * PAGE
    q_lots = q_rows * HD // (2 * kvw)
    gain = norm_gain.reshape(1, 2 * half)
    load = min(2048, half)
    step = min(1024, load // 2)
    kept = load + load // 2
    arguments = (img_route.T, w_key, w_value, vis_rows, gain, query)
    info, key_held, value_held, vis_near, gain_near, query_near = call(
        lambda *refs: prepare_kernel(n, lot, *refs),
        (
            jax.ShapeDtypeStruct((STAT, img), I32),
            pltpu.VMEM((kept, kvw), BF16),
            pltpu.VMEM((kept, kvw), BF16),
            *[pltpu.VMEM(a.shape, a.dtype) for a in arguments[3:]],
        ),
        [ANY] * len(arguments),
        (VM,) * 6,
        [pltpu.VMEM((1, n * img), I32), pltpu.SemaphoreType.DMA((len(arguments),))],
        flops=1 << 20,
        traffic=2 * 2 * half * 2 * kvw * 2,
    )(*[remote(a) for a in arguments])

    left = 2 * half - kept
    sizes = [half - kept, *[load] * (half // load - 1), *[load // 2] * 2]
    packed = call(
        lambda *refs: vis_kernel(n, lot, sizes, step, *refs),
        pltpu.VMEM((n, q_lots + lot, 2 * kvw), BF16),
        [VM] * 6 + [ANY] * 2 + [VM],
        VM,
        [
            pltpu.VMEM((left, kvw), BF16),
            pltpu.VMEM((left, kvw), BF16),
            pltpu.VMEM((img, 2 * kvw), F32),
            pltpu.SemaphoreType.DMA((2 * len(sizes),)),
        ],
        flops=64 * img * 2 * half * 2 * kvw,
        traffic=2 * img * 2 * half + 8 * half * kvw,
    )(
        local(vis_near),
        vis_far,
        local(gain_near),
        local(query_near),
        local(key_held),
        local(value_held),
        remote(w_key),
        remote(w_value),
        info,
    )
    arrived = exchange(packed, section_of)

    block = page_cap * PAGE * 2 * kv_heads + q_rows + PAGE
    lists = (img_route.T, page_dest.T, page_count, tail_len, dec_req)
    kv_text, bias, base, info, slots = call(
        lambda *refs: text_kernel(n, img, lot, load, step, page_cap, *refs),
        (
            jax.ShapeDtypeStruct((tok, 2 * kvw), BF16),
            jax.ShapeDtypeStruct((tok, n * q_rows // kv_heads), F32),
            jax.ShapeDtypeStruct((n, block - q_rows - PAGE, HD), BF16),
            jax.ShapeDtypeStruct((STAT, n * lot), I32),
            jax.ShapeDtypeStruct((blocks,), I32),
        ),
        [ANY, VM, VM] + [ANY] * 7,
        (VM, VM, VM, VM, SM),
        [
            pltpu.VMEM((tok, half), BF16),
            pltpu.VMEM(w_key.shape, BF16),
            pltpu.VMEM(w_value.shape, BF16),
            pltpu.VMEM((tok, 2 * kvw), F32),
            pltpu.SMEM((n,), I32),
            pltpu.SemaphoreType.DMA((1 + 4 * half // load + len(lists),)),
            *[(pltpu.VMEM if i == 0 else pltpu.SMEM)(a.shape, a.dtype) for i, a in enumerate(lists)],
        ],
        limit=24,
        flops=2 * tok * 2 * half * 2 * kvw,
        traffic=2 * tok * 2 * half + 8 * half * kvw,
    )(remote(text_rows), text_far, remote(gain), remote(w_key), remote(w_value), *[remote(a) for a in lists])

    sent, own = call(
        lambda *refs: attend_kernel(n, cap, lot, page_cap, kv_heads, *refs),
        (
            jax.ShapeDtypeStruct((n, block, HD), BF16),
            jax.ShapeDtypeStruct((q_rows + STAT, HD), F32),
        ),
        [SM] + [VM] * 5,
        (ANY, VM),
        [
            pltpu.VMEM((n, block, HD), BF16),
            pltpu.VMEM((min(tok, n * cap), 2 * kvw), BF16),
            pltpu.VMEM((n * q_rows, HD), F32),
            pltpu.VMEM((STAT, n * q_rows // kv_heads), F32),
            pltpu.SemaphoreType.DMA((2,)),
        ],
        flops=4 * n * q_rows * tok * HD,
        traffic=n * (q_rows + STAT) * HD * 4,
    )(slots, info, kv_text, arrived, bias, base)
    shares = exchange(sent, page_section_of)

    mine = call(
        lambda *refs: fresh_kernel(n, kv_heads, steps, *refs),
        jax.ShapeDtypeStruct((q_rows + STAT, HD), F32),
        [VM] * 4,
        VM,
        flops=1 << 20,
        traffic=1 << 18,
    )(remote(query), remote(dec_key[0]), remote(dec_value[0]), own)

    slots_here = n * page_cap
    attended, cache_key, cache_value = call(
        lambda *refs: finish_kernel(kv_heads, steps, page_cap, *refs),
        (
            jax.ShapeDtypeStruct(dec_query.shape, BF16),
            jax.ShapeDtypeStruct((n, page_cap * PAGE, kvw), BF16),
            jax.ShapeDtypeStruct((n, page_cap * PAGE, kvw), BF16),
        ),
        [VM, VM],
        (VM, VM, VM),
        traffic=4 * tok * 2 * kvw,
    )(shares, mine)
    return (
        attended,
        cache_key.reshape(slots_here, PAGE, kvw),
        cache_value.reshape(slots_here, PAGE, kvw),
    )


def solution(mesh):
    return jax.shard_map(
        body,
        mesh=mesh,
        in_specs=(
            P(("groups", "section"), "tensor"),
            P(("groups", "section"), "tensor"),
            P("groups", None),
            P(),
            P(None, "tensor"),
            P(None, "tensor"),
            P("groups"),
            P("groups"),
            P("groups", None),
            P("groups"),
            P(("groups", "section"), None, "tensor"),
            P(("groups", "section"), None, "tensor"),
            P(("groups", "section"), None, "tensor"),
        ),
        out_specs=(
            P(("groups", "section"), None, "tensor"),
            P(("groups", "section"), None, "tensor"),
            P(("groups", "section"), None, "tensor"),
        ),
        check_vma=False,
    )
```

```python
import jax
import jax.numpy as jnp
from jax import lax
from jax.experimental import pallas as pl
from jax.experimental.pallas import tpu as pltpu
from jax.sharding import PartitionSpec as P

HD = 128
PAGE = 16
LOWEST = -1e30
EPS = 1e-06
STAT = 8
F32 = jnp.float32
BF16 = jnp.bfloat16
I32 = jnp.int32

VM = pl.BlockSpec(memory_space=pltpu.VMEM)
SM = pl.BlockSpec(memory_space=pltpu.SMEM)
ANY = pl.BlockSpec(memory_space=pl.ANY)
MIB = 1 << 20


def call(kernel, out_shape, in_specs, out_specs, scratch=(), limit=16, flops=0, traffic=0):
    return pl.pallas_call(
        kernel,
        out_shape=out_shape,
        in_specs=in_specs,
        out_specs=out_specs,
        scratch_shapes=list(scratch),
        compiler_params=pltpu.CompilerParams(vmem_limit_bytes=limit * MIB),
        cost_estimate=pl.CostEstimate(flops=flops, bytes_accessed=traffic, transcendentals=0),
    )


def rank_of(section, n):
    return jnp.where(section < n // 2, n - 2 - 2 * section, 2 * section - n + 1)


def section_of(rank, n):
    return n // 2 - 1 - rank // 2 + rank % 2 * (rank // 2 * 2 + 1)


def page_rank_of(section, n):
    z, y, length = section // 2, section % 2, n // 2
    return y * length + (2 * length - z - n // 4) % length


def page_section_of(rank, n):
    length = n // 2
    return 2 * (length - 1 - (rank % length + n // 4 - 1) % length) + rank // length


def dot(a, b):
    return jnp.dot(a, b, preferred_element_type=F32)


def dot_t(a, b):
    return lax.dot_general(a, b, (((1,), (1,)), ((), ())), preferred_element_type=F32)


def diagonal(shape):
    return lax.broadcasted_iota(I32, shape, 0) == lax.broadcasted_iota(I32, shape, 1)


def column_to_row(column):
    rows = column.shape[0]
    return jnp.sum(jnp.where(diagonal((rows, rows)), column, 0.0), axis=0, keepdims=True)


def row_to_column(row):
    lanes = row.shape[1]
    return jnp.sum(jnp.where(diagonal((lanes, lanes)), row, 0.0), axis=1, keepdims=True)


def squares_of(rows):
    total = jnp.zeros((rows.shape[0], HD), F32)
    for c in range(0, rows.shape[1], HD):
        wide = rows[:, c : c + HD].astype(F32)
        total = total + wide * wide
    return total


def split_three(values):
    high = values.astype(BF16).astype(F32)
    rest = values - high
    middle = rest.astype(BF16).astype(F32)
    return high, middle, rest - middle


def softmax_parts(query, key, value, usable):
    scores = jnp.where(usable, dot_t(query, key) * HD**-0.5, LOWEST)
    top = jnp.max(scores, axis=1, keepdims=True)
    weights = jnp.where(usable, jnp.exp(scores - top), 0.0)
    return dot(weights.astype(BF16), value), top, jnp.sum(weights, axis=1, keepdims=True)


def prepare_kernel(n, lot, *refs):
    far, info, near, (route, sems) = refs[:6], refs[6], refs[7:12], refs[12:]
    img, half = near[2].shape
    first = pl.ds(pl.multiple_of(lax.axis_index("tensor") * half, half), near[0].shape[0])
    sources = (far[0], far[1].at[first], far[2].at[first], *far[3:])
    copies = [pltpu.make_async_copy(a, b, sems.at[i]) for i, (a, b) in enumerate(zip(sources, (route, *near)))]
    for c in copies:
        c.start()
    copies[0].wait()
    pos = lax.axis_index("section")
    own = jnp.zeros((1, img), I32)
    for e in range(n):
        own = jnp.where(pos == e, route[:, e * img : (e + 1) * img], own)
    marks = own == lax.broadcasted_iota(I32, (n, img), 0)
    ones = jnp.where(marks, 1.0, 0.0).astype(BF16)
    earlier = lax.broadcasted_iota(I32, (img, img), 0) < lax.broadcasted_iota(I32, (img, img), 1)
    prefix = dot(ones, jnp.where(earlier, 1.0, 0.0).astype(BF16))
    local = jnp.sum(jnp.where(marks, prefix, 0.0), axis=0, keepdims=True).astype(I32)
    info[...] = jnp.broadcast_to(rank_of(own, n) * lot + local, info.shape)
    for c in copies[1:]:
        c.wait()


def plan_tokens(n, img, lot, page_cap, small, info, slots, bias, starts):
    route, pages, count, tail, req = small
    pos = lax.axis_index("section")
    tok, width = bias.shape
    blocks = tok // PAGE
    lanes = lax.broadcasted_iota(I32, (1, n * lot), 1)
    source, inner = section_of(lanes // lot, n), lanes % lot
    fits = jnp.zeros((1, n * lot), I32)
    offset = jnp.zeros((1, n * lot), I32)
    for e in range(n):
        here = (route[:, e * img : (e + 1) * img] == pos).astype(I32)
        arriving = jnp.sum(here, axis=1, keepdims=True)
        fits = fits + jnp.where(source == e, arriving, 0)
        offset = offset + jnp.where(source > e, arriving, 0)
    info[...] = jnp.broadcast_to(jnp.where(inner < fits, offset + inner, -1), info.shape)
    total = jnp.int32(0)
    for r in range(n):
        starts[r] = total
        total = total + count[r]
    token = lax.broadcasted_iota(I32, (1, tok), 1) + pos * tok
    token_slot = jnp.full((1, tok), -1, I32)
    for b in range(n):
        r = req[b]
        first = starts[r] * PAGE
        last = first + (count[r] - 1) * PAGE + tail[r]
        token_slot = jnp.where((token >= first) & (token < last), b, token_slot)
    member = section_of(lax.broadcasted_iota(I32, (1, width), 1) // (width // n), n)
    bias[...] = jnp.where(row_to_column(token_slot.astype(F32)) == member.astype(F32), 0.0, LOWEST)
    for g in range(blocks):
        holder = pages[0, pos * blocks + g]
        slot = page_rank_of(holder, n) * page_cap
        for e in range(g):
            slot = slot + (pages[0, pos * blocks + e] == holder).astype(I32)
        slots[g] = slot


def scale_of(near, far):
    sums = jnp.sum(squares_of(near) + squares_of(far), axis=1, keepdims=True)
    return lax.rsqrt(sums / (2.0 * near.shape[1]) + EPS)


def normed_rows(rows, c, step, scale, gain):
    return (rows[:, c : c + step].astype(F32) * scale * gain).astype(BF16)


def add_part(total, at, normed, w, begin):
    part = dot(normed, w)
    columns = slice(at, at + part.shape[1])
    if begin:
        total[:, columns] = part
    else:
        total[:, columns] += part


def start_lists(far, small, sems):
    copies = [pltpu.make_async_copy(a, b, sems.at[i]) for i, (a, b) in enumerate(zip(far, small))]
    for c in copies:
        c.start()
    return copies


def vis_kernel(n, lot, page_cap, sizes, step, *refs):
    near, far, gain, query, key_held, value_held, w_key, w_value, info = refs[:9]
    lists, (out, *plan) = refs[9:14], refs[14:18]
    (key_rest, value_rest, total, starts, sems, list_sems), small = refs[18:24], refs[24:]
    img, half = near.shape
    kvw = w_key.shape[1]
    me = lax.axis_index("tensor")
    held = key_held.shape[0]
    copies = start_lists(lists, small, list_sems)
    loads = {}
    at = held
    for size in sizes:
        side = me if at < half else 1 - me
        source = pl.ds(pl.multiple_of(side * half + at % half, size), size)
        number = 2 * len(loads)
        loads[at] = [
            pltpu.make_async_copy(w.at[source], kept.at[at - held : at - held + size], sems.at[number + i])
            for i, (w, kept) in enumerate(((w_key, key_rest), (w_value, value_rest)))
        ]
        for copy in loads[at]:
            copy.start()
        at += size
    scale = scale_of(near, far)
    for at in range(0, 2 * half, step):
        for copy in loads.get(at, ()):
            copy.wait()
        rows, side = (near, me) if at < half else (far, 1 - me)
        weights, w_at = ((key_held, value_held), at) if at < held else ((key_rest, value_rest), at - held)
        c = at % half
        columns = pl.ds(pl.multiple_of(side * half + c, step), step)
        normed = normed_rows(rows, c, step, scale, gain[:, columns])
        for w, col in zip(weights, (0, kvw)):
            add_part(total, col, normed, w[w_at : w_at + step, :], at == 0)
    slot = lax.broadcasted_iota(I32, (n * lot, img), 0)
    chosen = jnp.where(slot == info[0:1, :img], 1.0, 0.0).astype(BF16)
    packed = dot(chosen, total[...].astype(BF16)).astype(BF16)
    q_lots = out.shape[1] - lot
    for k in range(n):
        for j in range(query.shape[0] // q_lots):
            out[k, :q_lots, j * HD : (j + 1) * HD] = query[j * q_lots : (j + 1) * q_lots, :]
        out[k, q_lots:, :] = packed[k * lot : (k + 1) * lot, :]
    for copy in copies:
        copy.wait()

    @pl.when(me == 1)
    def _():
        plan_tokens(n, img, lot, page_cap, small, *plan, starts)


def put_page(out, page_cap, slot, rows):
    chunk = page_cap * PAGE
    for h in range(rows.shape[1] // HD):
        at = pl.ds(pl.multiple_of((slot % page_cap) * PAGE + h * chunk, PAGE), PAGE)
        out[slot // page_cap, at, :] = rows[:, h * HD : (h + 1) * HD]


def text_kernel(n, img, lot, load, step, page_cap, *refs):
    (near_far, far, gain, w_key_far, w_value_far), lists, early, refs = refs[:5], refs[5:10], refs[10:13], refs[13:]
    (out, base, info, slots, bias), (near, w_key, w_value, total, starts, sems, list_sems), small = (
        refs[:5],
        refs[5:12],
        refs[12:],
    )
    half = near.shape[1]
    kvw = w_key.shape[1]
    me = lax.axis_index("tensor")
    first = pltpu.make_async_copy(near_far, near, sems.at[0])
    first.start()
    copies = start_lists(lists, small, list_sems)
    loads = []
    for side in (me, 1 - me):
        for c in range(0, half, load):
            at = len(loads) * load
            columns = pl.ds(pl.multiple_of(side * half + c, load), load)
            pair = [
                pltpu.make_async_copy(w.at[columns], held.at[at : at + load], sems.at[2 * len(loads) + i])
                for i, (w, held) in enumerate(((w_key_far, w_key), (w_value_far, w_value)), 1)
            ]
            for copy in pair:
                copy.start()
            loads.append(pair)
    sums = squares_of(far)
    for copy in copies:
        copy.wait()

    @pl.when(me == 0)
    def _():
        plan_tokens(n, img, lot, page_cap, small, info, slots, bias, starts)

    @pl.when(me == 1)
    def _():
        info[...] = early[0][...]
        bias[...] = early[2][...]
        for g in range(slots.shape[0]):
            slots[g] = early[1][g]

    first.wait()
    sums = jnp.sum(squares_of(near) + sums, axis=1, keepdims=True)
    scale = lax.rsqrt(sums / (2.0 * half) + EPS)
    for i, pair in enumerate(loads):
        for copy in pair:
            copy.wait()
        for at in range(i * load, (i + 1) * load, step):
            rows, side = (near, me) if at < half else (far, 1 - me)
            c = at % half
            columns = pl.ds(pl.multiple_of(side * half + c, step), step)
            normed = normed_rows(rows, c, step, scale, gain[:, columns])
            for w, col in ((w_key, 0), (w_value, kvw)):
                add_part(total, col, normed, w[at : at + step, :], at == 0)
    out[...] = total[...].astype(BF16)
    base[...] = jnp.zeros(base.shape, BF16)
    tok = near.shape[0]
    for g in range(tok // PAGE):
        put_page(base, page_cap, slots[g], out[g * PAGE : (g + 1) * PAGE, :])


def attend_kernel(n, cap, lot, page_cap, kv_heads, slots, info, kv_text, arrived, bias, base, sent, own, *scratch):
    out, mixed, held, rows_held, sems = scratch
    order = [page_section_of(k, n) for k in range(n)]
    rank = rank_of(lax.axis_index("section"), n)
    tok = kv_text.shape[0]
    kvw = kv_heads * HD
    q_lots = arrived.shape[1] - lot
    reach = min(tok, n * cap)
    hit = lax.broadcasted_iota(I32, (reach, n * lot), 0) == info[0:1, :]
    hot = jnp.where(hit, 1.0, 0.0)
    covered = jnp.sum(hot, axis=1, keepdims=True) > 0.0
    incoming = jnp.concatenate([arrived[k, q_lots:, :] for k in range(n)], axis=0)
    placed = dot(hot.astype(BF16), incoming)
    mixed[...] = jnp.where(covered, placed, kv_text[:reach, :].astype(F32)).astype(BF16)
    groups = arrived.shape[2] // HD // kv_heads
    rows = groups * q_lots
    pages = base.shape[1]
    out[:, :pages, :] = base[...]
    for g in range(reach // PAGE):
        put_page(out, page_cap, slots[g], mixed[g * PAGE : (g + 1) * PAGE, :])
    first = pltpu.make_async_copy(out.at[:, :pages, :], sent.at[:, :pages, :], sems.at[0])
    first.start()
    for g in range(kv_heads):
        query = jnp.concatenate(
            [
                arrived[k, :q_lots, (g * groups + j) * HD : (g * groups + j + 1) * HD]
                for k in range(n)
                for j in range(groups)
            ],
            axis=0,
        )
        cols = slice(g * HD, (g + 1) * HD)
        vcols = slice(kvw + g * HD, kvw + (g + 1) * HD)
        key = jnp.concatenate([mixed[:, cols], kv_text[reach:, cols]], axis=0)
        value = jnp.concatenate([mixed[:, vcols], kv_text[reach:, vcols]], axis=0)
        scores = dot_t(key, query) * HD**-0.5 + bias[...]
        top = jnp.max(scores, axis=0, keepdims=True)
        weights = jnp.exp(scores - top)
        rows_held[g : g + 1, :] = top
        rows_held[kv_heads + g : kv_heads + g + 1, :] = jnp.sum(weights, axis=0, keepdims=True)
        numerator = lax.dot_general(
            weights.astype(BF16), value, (((0,), (0,)), ((), ())), preferred_element_type=F32
        )
        held[g * n * rows : (g + 1) * n * rows, :] = numerator
        own[g * rows : (g + 1) * rows, :] = held[pl.ds(pl.multiple_of((g * n + rank) * rows, rows), rows), :]
        numerator = numerator.astype(BF16)
        for k in range(n):
            to = order.index(section_of(k, n))
            out[to, pages + g * rows : pages + (g + 1) * rows, :] = numerator[k * rows : (k + 1) * rows, :]
    stat_rows = 2 * kv_heads
    share = HD // rows
    window = pl.ds(pl.multiple_of(rank // share * HD, HD), HD)
    own[kv_heads * rows : kv_heads * rows + stat_rows, :] = rows_held[:stat_rows, window]
    blank = jnp.zeros((PAGE - 3 * stat_rows, HD), F32)
    for w in range(-(-n // share)):
        stats = rows_held[:stat_rows, w * HD : (w + 1) * HD]
        lines = jnp.concatenate([*split_three(stats), blank], axis=0).astype(BF16)
        for k in range(w * share, min(n, (w + 1) * share)):
            out[order.index(section_of(k, n)), pages + kv_heads * rows :, :] = lines
    last = pltpu.make_async_copy(out.at[:, pages:, :], sent.at[:, pages:, :], sems.at[1])
    last.start()
    first.wait()
    last.wait()


def pick_column(row, rows, start):
    shape = (rows, HD)
    chosen = lax.broadcasted_iota(I32, shape, 1) == lax.broadcasted_iota(I32, shape, 0) + start
    return jnp.sum(jnp.where(chosen, row, 0.0), axis=1, keepdims=True)


def combine(pieces, highest):
    numerator, total = 0.0, 0.0
    for rows, top, weight in pieces:
        scale = jnp.exp(top - highest)
        numerator = numerator + rows * scale
        total = total + weight * scale
    return numerator, total


def fresh_kernel(n, kv_heads, steps, query, key, value, own, mine):
    rows = query.shape[0] // kv_heads
    every = kv_heads * rows
    start = rank_of(lax.axis_index("section"), n) % (HD // rows) * rows
    row = lax.broadcasted_iota(I32, (rows, steps), 0)
    causal = lax.broadcasted_iota(I32, (rows, steps), 1) <= row % steps
    tops, totals = [], []
    for g in range(kv_heads):
        cols = slice(g * HD, (g + 1) * HD)
        at = slice(g * rows, (g + 1) * rows)
        fresh = softmax_parts(query[at, :], key[:, cols], value[:, cols], causal)
        share = (
            own[at, :],
            pick_column(own[every + g : every + g + 1, :], rows, start),
            pick_column(own[every + kv_heads + g : every + kv_heads + g + 1, :], rows, start),
        )
        highest = jnp.maximum(fresh[1], share[1])
        numerator, total = combine((fresh, share), highest)
        mine[at, :] = numerator
        tops.append(highest)
        totals.append(total)
    line = column_to_row(jnp.concatenate(tops + totals, axis=0))
    mine[every:, :] = jnp.broadcast_to(line, (STAT, line.shape[1]))


def finish_kernel(kv_heads, steps, page_cap, shares, mine, attended, keys, values):
    n = shares.shape[0]
    pos = lax.axis_index("section")
    every = mine.shape[0] - STAT
    rows = every // kv_heads
    start = rank_of(pos, n) % (HD // rows) * rows
    chunk = page_cap * PAGE
    halves = keys.shape[2] // HD
    for k in range(n):
        for i, out in enumerate((keys, values)):
            for h in range(halves):
                part = i * halves + h
                out[page_section_of(k, n), :, h * HD : (h + 1) * HD] = shares[k, part * chunk : (part + 1) * chunk, :]
    pages = 2 * halves * chunk
    stats = row_to_column(mine[every : every + 1, :])
    lines = []
    for k in range(n):
        three = shares[k, pages + every :, :].astype(F32)
        size = 2 * kv_heads
        lines.append(three[:size] + three[size : 2 * size] + three[2 * size : 3 * size])
    for g in range(kv_heads):
        at = slice(g * rows, (g + 1) * rows)
        pieces = [(mine[at, :], stats[at], stats[every + g * rows : every + (g + 1) * rows])]
        for k in range(n):
            away = pos != page_section_of(k, n)
            top = jnp.where(away, pick_column(lines[k][g : g + 1], rows, start), LOWEST)
            weight = jnp.where(away, pick_column(lines[k][kv_heads + g : kv_heads + g + 1], rows, start), 0.0)
            share = shares[k, pages + g * rows : pages + (g + 1) * rows, :].astype(F32)
            pieces.append((share, top, weight))
        highest = pieces[0][1]
        for p in pieces[1:]:
            highest = jnp.maximum(highest, p[1])
        numerator, total = combine(pieces, highest)
        result = (numerator / total).astype(BF16)
        for h in range(rows // steps):
            to = (g * rows // steps + h) * HD
            attended[0, :, to : to + HD] = result[h * steps : (h + 1) * steps, :]


def body(
    text_rows,
    vis_rows,
    img_route,
    norm_gain,
    w_key,
    w_value,
    page_count,
    tail_len,
    page_dest,
    dec_req,
    dec_query,
    dec_key,
    dec_value,
):
    n = lax.axis_size("section")
    tok, half = text_rows.shape
    img = vis_rows.shape[0]
    kvw = w_key.shape[1]
    kv_heads = kvw // HD
    _, steps, q_width = dec_query.shape
    heads = q_width // HD
    q_rows = heads * steps
    blocks = tok // PAGE
    cap = max(2, (2 * img + n - 1) // n)
    page_cap = max(1, (blocks + n - 1) // n)

    def across(array):
        return lax.ppermute(array, "tensor", [(0, 1), (1, 0)])

    def exchange(array, section_at):
        order = [[section_at(rank, n) for rank in range(n)]]
        return lax.all_to_all(array, "section", split_axis=0, concat_axis=0, tiled=True, axis_index_groups=order)

    def remote(array):
        return pltpu.with_memory_space_constraint(array, pltpu.HBM)

    def local(array):
        return pltpu.with_memory_space_constraint(array, pltpu.VMEM)

    vis_far = across(vis_rows)
    text_far = across(text_rows)
    query = dec_query.reshape(steps, heads, HD).transpose(1, 0, 2).reshape(q_rows, HD)

    lot = -(-cap // PAGE) * PAGE
    q_lots = q_rows * HD // (2 * kvw)
    gain = norm_gain.reshape(1, 2 * half)
    load = min(2048, half)
    step = min(1024, load // 2)
    kept = load + load // 2
    arguments = (img_route.T, w_key, w_value, vis_rows, gain, query)
    info, key_held, value_held, vis_near, gain_near, query_near = call(
        lambda *refs: prepare_kernel(n, lot, *refs),
        (
            jax.ShapeDtypeStruct((STAT, img), I32),
            pltpu.VMEM((kept, kvw), BF16),
            pltpu.VMEM((kept, kvw), BF16),
            *[pltpu.VMEM(a.shape, a.dtype) for a in arguments[3:]],
        ),
        [ANY] * len(arguments),
        (VM,) * 6,
        [pltpu.VMEM((1, n * img), I32), pltpu.SemaphoreType.DMA((len(arguments),))],
        flops=1 << 20,
        traffic=2 * 2 * half * 2 * kvw * 2,
    )(*[remote(a) for a in arguments])

    left = 2 * half - kept
    sizes = [half - kept, *[load] * (half // load - 1), *[load // 2] * 2]
    lists = (img_route.T, page_dest.T, page_count, tail_len, dec_req)
    held_lists = [(pltpu.VMEM if i == 0 else pltpu.SMEM)(a.shape, a.dtype) for i, a in enumerate(lists)]
    plan_shapes = (
        jax.ShapeDtypeStruct((STAT, n * lot), I32),
        jax.ShapeDtypeStruct((blocks,), I32),
        jax.ShapeDtypeStruct((tok, n * q_rows // kv_heads), F32),
    )
    packed, *early = call(
        lambda *refs: vis_kernel(n, lot, page_cap, sizes, step, *refs),
        (pltpu.VMEM((n, q_lots + lot, 2 * kvw), BF16), *plan_shapes),
        [VM] * 6 + [ANY] * 2 + [VM] + [ANY] * len(lists),
        (VM, VM, SM, VM),
        [
            pltpu.VMEM((left, kvw), BF16),
            pltpu.VMEM((left, kvw), BF16),
            pltpu.VMEM((img, 2 * kvw), F32),
            pltpu.SMEM((n,), I32),
            pltpu.SemaphoreType.DMA((2 * len(sizes),)),
            pltpu.SemaphoreType.DMA((len(lists),)),
            *held_lists,
        ],
        flops=64 * img * 2 * half * 2 * kvw,
        traffic=2 * img * 2 * half + 8 * half * kvw,
    )(
        local(vis_near),
        vis_far,
        local(gain_near),
        local(query_near),
        local(key_held),
        local(value_held),
        remote(w_key),
        remote(w_value),
        info,
        *[remote(a) for a in lists],
    )
    arrived = exchange(packed, section_of)

    block = page_cap * PAGE * 2 * kv_heads + q_rows + PAGE
    kv_text, base, info, slots, bias = call(
        lambda *refs: text_kernel(n, img, lot, load, step, page_cap, *refs),
        (
            jax.ShapeDtypeStruct((tok, 2 * kvw), BF16),
            jax.ShapeDtypeStruct((n, block - q_rows - PAGE, HD), BF16),
            *plan_shapes,
        ),
        [ANY, VM, VM] + [ANY] * 7 + [VM, SM, VM],
        (VM, VM, VM, SM, VM),
        [
            pltpu.VMEM((tok, half), BF16),
            pltpu.VMEM(w_key.shape, BF16),
            pltpu.VMEM(w_value.shape, BF16),
            pltpu.VMEM((tok, 2 * kvw), F32),
            pltpu.SMEM((n,), I32),
            pltpu.SemaphoreType.DMA((1 + 4 * half // load,)),
            pltpu.SemaphoreType.DMA((len(lists),)),
            *held_lists,
        ],
        limit=24,
        flops=2 * tok * 2 * half * 2 * kvw,
        traffic=2 * tok * 2 * half + 8 * half * kvw,
    )(
        remote(text_rows),
        text_far,
        remote(gain),
        remote(w_key),
        remote(w_value),
        *[remote(a) for a in lists],
        *early,
    )

    sent, own = call(
        lambda *refs: attend_kernel(n, cap, lot, page_cap, kv_heads, *refs),
        (
            jax.ShapeDtypeStruct((n, block, HD), BF16),
            jax.ShapeDtypeStruct((q_rows + STAT, HD), F32),
        ),
        [SM] + [VM] * 5,
        (ANY, VM),
        [
            pltpu.VMEM((n, block, HD), BF16),
            pltpu.VMEM((min(tok, n * cap), 2 * kvw), BF16),
            pltpu.VMEM((n * q_rows, HD), F32),
            pltpu.VMEM((STAT, n * q_rows // kv_heads), F32),
            pltpu.SemaphoreType.DMA((2,)),
        ],
        flops=4 * n * q_rows * tok * HD,
        traffic=n * (q_rows + STAT) * HD * 4,
    )(slots, info, kv_text, arrived, bias, base)
    shares = exchange(sent, page_section_of)

    mine = call(
        lambda *refs: fresh_kernel(n, kv_heads, steps, *refs),
        jax.ShapeDtypeStruct((q_rows + STAT, HD), F32),
        [VM] * 4,
        VM,
        flops=1 << 20,
        traffic=1 << 18,
    )(remote(query), remote(dec_key[0]), remote(dec_value[0]), own)

    slots_here = n * page_cap
    attended, cache_key, cache_value = call(
        lambda *refs: finish_kernel(kv_heads, steps, page_cap, *refs),
        (
            jax.ShapeDtypeStruct(dec_query.shape, BF16),
            jax.ShapeDtypeStruct((n, page_cap * PAGE, kvw), BF16),
            jax.ShapeDtypeStruct((n, page_cap * PAGE, kvw), BF16),
        ),
        [VM, VM],
        (VM, VM, VM),
        traffic=4 * tok * 2 * kvw,
    )(shares, mine)
    return (
        attended,
        cache_key.reshape(slots_here, PAGE, kvw),
        cache_value.reshape(slots_here, PAGE, kvw),
    )


def solution(mesh):
    return jax.shard_map(
        body,
        mesh=mesh,
        in_specs=(
            P(("groups", "section"), "tensor"),
            P(("groups", "section"), "tensor"),
            P("groups", None),
            P(),
            P(None, "tensor"),
            P(None, "tensor"),
            P("groups"),
            P("groups"),
            P("groups", None),
            P("groups"),
            P(("groups", "section"), None, "tensor"),
            P(("groups", "section"), None, "tensor"),
            P(("groups", "section"), None, "tensor"),
        ),
        out_specs=(
            P(("groups", "section"), None, "tensor"),
            P(("groups", "section"), None, "tensor"),
            P(("groups", "section"), None, "tensor"),
        ),
        check_vma=False,
    )
```

```python
import jax
import jax.numpy as jnp
from jax import lax
from jax.experimental import pallas as pl
from jax.experimental.pallas import tpu as pltpu
from jax.sharding import PartitionSpec as P

HD = 128
PAGE = 16
LOWEST = -1e30
EPS = 1e-06
STAT = 8
F32 = jnp.float32
BF16 = jnp.bfloat16
I32 = jnp.int32

VM = pl.BlockSpec(memory_space=pltpu.VMEM)
SM = pl.BlockSpec(memory_space=pltpu.SMEM)
ANY = pl.BlockSpec(memory_space=pl.ANY)
MIB = 1 << 20


def call(kernel, out_shape, in_specs, out_specs, scratch=(), limit=16, flops=0, traffic=0):
    return pl.pallas_call(
        kernel,
        out_shape=out_shape,
        in_specs=in_specs,
        out_specs=out_specs,
        scratch_shapes=list(scratch),
        compiler_params=pltpu.CompilerParams(vmem_limit_bytes=limit * MIB),
        cost_estimate=pl.CostEstimate(flops=flops, bytes_accessed=traffic, transcendentals=0),
    )


def rank_of(section, n):
    return jnp.where(section < n // 2, n - 2 - 2 * section, 2 * section - n + 1)


def section_of(rank, n):
    return n // 2 - 1 - rank // 2 + rank % 2 * (rank // 2 * 2 + 1)


def page_rank_of(section, n):
    z, y, length = section // 2, section % 2, n // 2
    return y * length + (2 * length - z - n // 4) % length


def page_section_of(rank, n):
    length = n // 2
    return 2 * (length - 1 - (rank % length + n // 4 - 1) % length) + rank // length


def dot(a, b):
    return jnp.dot(a, b, preferred_element_type=F32)


def dot_t(a, b):
    return lax.dot_general(a, b, (((1,), (1,)), ((), ())), preferred_element_type=F32)


def diagonal(shape):
    return lax.broadcasted_iota(I32, shape, 0) == lax.broadcasted_iota(I32, shape, 1)


def column_to_row(column):
    rows = column.shape[0]
    return jnp.sum(jnp.where(diagonal((rows, rows)), column, 0.0), axis=0, keepdims=True)


def row_to_column(row):
    lanes = row.shape[1]
    return jnp.sum(jnp.where(diagonal((lanes, lanes)), row, 0.0), axis=1, keepdims=True)


def squares_of(rows):
    total = jnp.zeros((rows.shape[0], HD), F32)
    for c in range(0, rows.shape[1], HD):
        wide = rows[:, c : c + HD].astype(F32)
        total = total + wide * wide
    return total


def split_three(values):
    high = values.astype(BF16).astype(F32)
    rest = values - high
    middle = rest.astype(BF16).astype(F32)
    return high, middle, rest - middle


def softmax_parts(query, key, value, usable):
    scores = jnp.where(usable, dot_t(query, key) * HD**-0.5, LOWEST)
    top = jnp.max(scores, axis=1, keepdims=True)
    weights = jnp.where(usable, jnp.exp(scores - top), 0.0)
    return dot(weights.astype(BF16), value), top, jnp.sum(weights, axis=1, keepdims=True)


def prepare_kernel(n, lot, *refs):
    far, info, near, (route, sems) = refs[:6], refs[6], refs[7:12], refs[12:]
    img, half = near[2].shape
    first = pl.ds(pl.multiple_of(lax.axis_index("tensor") * half, half), near[0].shape[0])
    sources = (far[0], far[1].at[first], far[2].at[first], *far[3:])
    copies = [pltpu.make_async_copy(a, b, sems.at[i]) for i, (a, b) in enumerate(zip(sources, (route, *near)))]
    for c in copies:
        c.start()
    copies[0].wait()
    pos = lax.axis_index("section")
    own = jnp.zeros((1, img), I32)
    for e in range(n):
        own = jnp.where(pos == e, route[:, e * img : (e + 1) * img], own)
    marks = own == lax.broadcasted_iota(I32, (n, img), 0)
    ones = jnp.where(marks, 1.0, 0.0).astype(BF16)
    earlier = lax.broadcasted_iota(I32, (img, img), 0) < lax.broadcasted_iota(I32, (img, img), 1)
    prefix = dot(ones, jnp.where(earlier, 1.0, 0.0).astype(BF16))
    local = jnp.sum(jnp.where(marks, prefix, 0.0), axis=0, keepdims=True).astype(I32)
    info[...] = jnp.broadcast_to(rank_of(own, n) * lot + local, info.shape)
    for c in copies[1:]:
        c.wait()


def plan_tokens(n, img, lot, page_cap, small, hot, covered, slots, bias, starts):
    route, pages, count, tail, req = small
    pos = lax.axis_index("section")
    tok, width = bias.shape
    blocks = tok // PAGE
    lanes = lax.broadcasted_iota(I32, (1, n * lot), 1)
    source, inner = section_of(lanes // lot, n), lanes % lot
    fits = jnp.zeros((1, n * lot), I32)
    offset = jnp.zeros((1, n * lot), I32)
    for e in range(n):
        here = (route[:, e * img : (e + 1) * img] == pos).astype(I32)
        arriving = jnp.sum(here, axis=1, keepdims=True)
        fits = fits + jnp.where(source == e, arriving, 0)
        offset = offset + jnp.where(source > e, arriving, 0)
    target = jnp.where(inner < fits, offset + inner, -1)
    chosen = jnp.where(lax.broadcasted_iota(I32, hot.shape, 0) == target, 1.0, 0.0)
    hot[...] = chosen.astype(BF16)
    covered[...] = jnp.broadcast_to(jnp.sum(chosen, axis=1, keepdims=True), covered.shape)
    total = jnp.int32(0)
    for r in range(n):
        starts[r] = total
        total = total + count[r]
    token = lax.broadcasted_iota(I32, (1, tok), 1) + pos * tok
    token_slot = jnp.full((1, tok), -1, I32)
    for b in range(n):
        r = req[b]
        first = starts[r] * PAGE
        last = first + (count[r] - 1) * PAGE + tail[r]
        token_slot = jnp.where((token >= first) & (token < last), b, token_slot)
    member = section_of(lax.broadcasted_iota(I32, (1, width), 1) // (width // n), n)
    bias[...] = jnp.where(row_to_column(token_slot.astype(F32)) == member.astype(F32), 0.0, LOWEST)
    for g in range(blocks):
        holder = pages[0, pos * blocks + g]
        slot = page_rank_of(holder, n) * page_cap
        for e in range(g):
            slot = slot + (pages[0, pos * blocks + e] == holder).astype(I32)
        slots[g] = slot


def scale_of(near, far):
    sums = jnp.sum(squares_of(near) + squares_of(far), axis=1, keepdims=True)
    return lax.rsqrt(sums / (2.0 * near.shape[1]) + EPS)


def normed_rows(rows, c, step, scale, gain):
    return (rows[:, c : c + step].astype(F32) * scale * gain).astype(BF16)


def add_part(total, at, normed, w, begin):
    part = dot(normed, w)
    columns = slice(at, at + part.shape[1])
    if begin:
        total[:, columns] = part
    else:
        total[:, columns] += part


def vis_kernel(n, lot, sizes, step, *refs):
    near, far, gain, query, key_held, value_held, w_key, w_value, info, out, key_rest, value_rest, total, sems = refs
    img, half = near.shape
    kvw = w_key.shape[1]
    me = lax.axis_index("tensor")
    held = key_held.shape[0]
    loads = {}
    at = held
    for size in sizes:
        side = me if at < half else 1 - me
        source = pl.ds(pl.multiple_of(side * half + at % half, size), size)
        number = 2 * len(loads)
        loads[at] = [
            pltpu.make_async_copy(w.at[source], kept.at[at - held : at - held + size], sems.at[number + i])
            for i, (w, kept) in enumerate(((w_key, key_rest), (w_value, value_rest)))
        ]
        for copy in loads[at]:
            copy.start()
        at += size
    scale = scale_of(near, far)
    points = [*range(0, 2 * half - step, step), *range(2 * half - step, 2 * half, sizes[-1])]
    for at, end in zip(points, [*points[1:], 2 * half]):
        for copy in loads.get(at, ()):
            copy.wait()
        rows, side = (near, me) if at < half else (far, 1 - me)
        weights, w_at = ((key_held, value_held), at) if at < held else ((key_rest, value_rest), at - held)
        c = at % half
        size = end - at
        columns = pl.ds(pl.multiple_of(side * half + c, size), size)
        normed = normed_rows(rows, c, size, scale, gain[:, columns])
        for w, col in zip(weights, (0, kvw)):
            add_part(total, col, normed, w[w_at : w_at + size, :], at == 0)
    slot = lax.broadcasted_iota(I32, (n * lot, img), 0)
    chosen = jnp.where(slot == info[0:1, :img], 1.0, 0.0).astype(BF16)
    packed = dot(chosen, total[...].astype(BF16)).astype(BF16)
    q_lots = out.shape[1] - lot
    for k in range(n):
        for j in range(query.shape[0] // q_lots):
            out[k, :q_lots, j * HD : (j + 1) * HD] = query[j * q_lots : (j + 1) * q_lots, :]
        out[k, q_lots:, :] = packed[k * lot : (k + 1) * lot, :]


def put_page(out, page_cap, slot, rows):
    chunk = page_cap * PAGE
    for h in range(rows.shape[1] // HD):
        at = pl.ds(pl.multiple_of((slot % page_cap) * PAGE + h * chunk, PAGE), PAGE)
        out[slot // page_cap, at, :] = rows[:, h * HD : (h + 1) * HD]


def text_kernel(n, img, lot, load, step, page_cap, *refs):
    (near_far, far, gain, w_key_far, w_value_far), small_far, refs = refs[:5], refs[5:10], refs[10:]
    (out, bias, base, hot, covered, slots), (near, w_key, w_value, total, starts, sems), small = (
        refs[:6],
        refs[6:12],
        refs[12:],
    )
    half = near.shape[1]
    kvw = w_key.shape[1]
    me = lax.axis_index("tensor")
    first = pltpu.make_async_copy(near_far, near, sems.at[0])
    first.start()
    used = sems.shape[0] - len(small)
    lists = [pltpu.make_async_copy(a, b, sems.at[used + i]) for i, (a, b) in enumerate(zip(small_far, small))]
    for copy in lists:
        copy.start()
    loads = []
    for side in (me, 1 - me):
        for c in range(0, half, load):
            at = len(loads) * load
            columns = pl.ds(pl.multiple_of(side * half + c, load), load)
            pair = [
                pltpu.make_async_copy(w.at[columns], held.at[at : at + load], sems.at[2 * len(loads) + i])
                for i, (w, held) in enumerate(((w_key_far, w_key), (w_value_far, w_value)), 1)
            ]
            for copy in pair:
                copy.start()
            loads.append(pair)
    sums = squares_of(far)
    for copy in lists:
        copy.wait()
    plan_tokens(n, img, lot, page_cap, small, hot, covered, slots, bias, starts)
    first.wait()
    sums = jnp.sum(squares_of(near) + sums, axis=1, keepdims=True)
    scale = lax.rsqrt(sums / (2.0 * half) + EPS)
    for i, pair in enumerate(loads):
        for copy in pair:
            copy.wait()
        for at in range(i * load, (i + 1) * load, step):
            rows, side = (near, me) if at < half else (far, 1 - me)
            c = at % half
            columns = pl.ds(pl.multiple_of(side * half + c, step), step)
            normed = normed_rows(rows, c, step, scale, gain[:, columns])
            for w, col in ((w_key, 0), (w_value, kvw)):
                add_part(total, col, normed, w[at : at + step, :], at == 0)
    out[...] = total[...].astype(BF16)
    base[...] = jnp.zeros(base.shape, BF16)
    tok = near.shape[0]
    for g in range(tok // PAGE):
        put_page(base, page_cap, slots[g], out[g * PAGE : (g + 1) * PAGE, :])


def attend_kernel(n, cap, lot, page_cap, kv_heads, slots, hot, covered, kv_text, arrived, bias, base, sent, own, *scratch):
    out, mixed, held, rows_held, sems = scratch
    order = [page_section_of(k, n) for k in range(n)]
    rank = rank_of(lax.axis_index("section"), n)
    tok = kv_text.shape[0]
    kvw = kv_heads * HD
    q_lots = arrived.shape[1] - lot
    reach = min(tok, n * cap)
    incoming = jnp.concatenate([arrived[k, q_lots:, :] for k in range(n)], axis=0)
    placed = dot(hot[...], incoming)
    mixed[...] = jnp.where(covered[:, :1] > 0.0, placed, kv_text[:reach, :].astype(F32)).astype(BF16)
    groups = arrived.shape[2] // HD // kv_heads
    rows = groups * q_lots
    pages = base.shape[1]
    out[:, :pages, :] = base[...]
    for g in range(reach // PAGE):
        put_page(out, page_cap, slots[g], mixed[g * PAGE : (g + 1) * PAGE, :])
    first = pltpu.make_async_copy(out.at[:, :pages, :], sent.at[:, :pages, :], sems.at[0])
    first.start()
    for g in range(kv_heads):
        query = jnp.concatenate(
            [
                arrived[k, :q_lots, (g * groups + j) * HD : (g * groups + j + 1) * HD]
                for k in range(n)
                for j in range(groups)
            ],
            axis=0,
        )
        cols = slice(g * HD, (g + 1) * HD)
        vcols = slice(kvw + g * HD, kvw + (g + 1) * HD)
        key = jnp.concatenate([mixed[:, cols], kv_text[reach:, cols]], axis=0)
        value = jnp.concatenate([mixed[:, vcols], kv_text[reach:, vcols]], axis=0)
        scores = dot_t(key, query) * HD**-0.5 + bias[...]
        top = jnp.max(scores, axis=0, keepdims=True)
        weights = jnp.exp(scores - top)
        rows_held[g : g + 1, :] = top
        rows_held[kv_heads + g : kv_heads + g + 1, :] = jnp.sum(weights, axis=0, keepdims=True)
        numerator = lax.dot_general(
            weights.astype(BF16), value, (((0,), (0,)), ((), ())), preferred_element_type=F32
        )
        held[g * n * rows : (g + 1) * n * rows, :] = numerator
        own[g * rows : (g + 1) * rows, :] = held[pl.ds(pl.multiple_of((g * n + rank) * rows, rows), rows), :]
        numerator = numerator.astype(BF16)
        for k in range(n):
            to = order.index(section_of(k, n))
            out[to, pages + g * rows : pages + (g + 1) * rows, :] = numerator[k * rows : (k + 1) * rows, :]
    stat_rows = 2 * kv_heads
    share = HD // rows
    window = pl.ds(pl.multiple_of(rank // share * HD, HD), HD)
    own[kv_heads * rows : kv_heads * rows + stat_rows, :] = rows_held[:stat_rows, window]
    blank = jnp.zeros((PAGE - 3 * stat_rows, HD), F32)
    for w in range(-(-n // share)):
        stats = rows_held[:stat_rows, w * HD : (w + 1) * HD]
        lines = jnp.concatenate([*split_three(stats), blank], axis=0).astype(BF16)
        for k in range(w * share, min(n, (w + 1) * share)):
            out[order.index(section_of(k, n)), pages + kv_heads * rows :, :] = lines
    last = pltpu.make_async_copy(out.at[:, pages:, :], sent.at[:, pages:, :], sems.at[1])
    last.start()
    first.wait()
    last.wait()


def pick_column(row, rows, start):
    shape = (rows, HD)
    chosen = lax.broadcasted_iota(I32, shape, 1) == lax.broadcasted_iota(I32, shape, 0) + start
    return jnp.sum(jnp.where(chosen, row, 0.0), axis=1, keepdims=True)


def combine(pieces, highest):
    numerator, total = 0.0, 0.0
    for rows, top, weight in pieces:
        scale = jnp.exp(top - highest)
        numerator = numerator + rows * scale
        total = total + weight * scale
    return numerator, total


def fresh_kernel(n, kv_heads, steps, query, key, value, own, mine):
    rows = query.shape[0] // kv_heads
    every = kv_heads * rows
    start = rank_of(lax.axis_index("section"), n) % (HD // rows) * rows
    row = lax.broadcasted_iota(I32, (rows, steps), 0)
    causal = lax.broadcasted_iota(I32, (rows, steps), 1) <= row % steps
    tops, totals = [], []
    for g in range(kv_heads):
        cols = slice(g * HD, (g + 1) * HD)
        at = slice(g * rows, (g + 1) * rows)
        fresh = softmax_parts(query[at, :], key[:, cols], value[:, cols], causal)
        share = (
            own[at, :],
            pick_column(own[every + g : every + g + 1, :], rows, start),
            pick_column(own[every + kv_heads + g : every + kv_heads + g + 1, :], rows, start),
        )
        highest = jnp.maximum(fresh[1], share[1])
        numerator, total = combine((fresh, share), highest)
        mine[at, :] = numerator
        tops.append(highest)
        totals.append(total)
    line = column_to_row(jnp.concatenate(tops + totals, axis=0))
    mine[every:, :] = jnp.broadcast_to(line, (STAT, line.shape[1]))


def finish_kernel(kv_heads, steps, page_cap, shares, mine, attended, keys, values):
    n = shares.shape[0]
    pos = lax.axis_index("section")
    every = mine.shape[0] - STAT
    rows = every // kv_heads
    start = rank_of(pos, n) % (HD // rows) * rows
    chunk = page_cap * PAGE
    halves = keys.shape[2] // HD
    for k in range(n):
        for i, out in enumerate((keys, values)):
            for h in range(halves):
                part = i * halves + h
                out[page_section_of(k, n), :, h * HD : (h + 1) * HD] = shares[k, part * chunk : (part + 1) * chunk, :]
    pages = 2 * halves * chunk
    stats = row_to_column(mine[every : every + 1, :])
    lines = []
    for k in range(n):
        three = shares[k, pages + every :, :].astype(F32)
        size = 2 * kv_heads
        lines.append(three[:size] + three[size : 2 * size] + three[2 * size : 3 * size])
    for g in range(kv_heads):
        at = slice(g * rows, (g + 1) * rows)
        pieces = [(mine[at, :], stats[at], stats[every + g * rows : every + (g + 1) * rows])]
        for k in range(n):
            away = pos != page_section_of(k, n)
            top = jnp.where(away, pick_column(lines[k][g : g + 1], rows, start), LOWEST)
            weight = jnp.where(away, pick_column(lines[k][kv_heads + g : kv_heads + g + 1], rows, start), 0.0)
            share = shares[k, pages + g * rows : pages + (g + 1) * rows, :].astype(F32)
            pieces.append((share, top, weight))
        highest = pieces[0][1]
        for p in pieces[1:]:
            highest = jnp.maximum(highest, p[1])
        numerator, total = combine(pieces, highest)
        result = (numerator / total).astype(BF16)
        for h in range(rows // steps):
            to = (g * rows // steps + h) * HD
            attended[0, :, to : to + HD] = result[h * steps : (h + 1) * steps, :]


def body(
    text_rows,
    vis_rows,
    img_route,
    norm_gain,
    w_key,
    w_value,
    page_count,
    tail_len,
    page_dest,
    dec_req,
    dec_query,
    dec_key,
    dec_value,
):
    n = lax.axis_size("section")
    tok, half = text_rows.shape
    img = vis_rows.shape[0]
    kvw = w_key.shape[1]
    kv_heads = kvw // HD
    _, steps, q_width = dec_query.shape
    heads = q_width // HD
    q_rows = heads * steps
    blocks = tok // PAGE
    cap = max(2, (2 * img + n - 1) // n)
    page_cap = max(1, (blocks + n - 1) // n)

    def across(array):
        return lax.ppermute(array, "tensor", [(0, 1), (1, 0)])

    def exchange(array, section_at):
        order = [[section_at(rank, n) for rank in range(n)]]
        return lax.all_to_all(array, "section", split_axis=0, concat_axis=0, tiled=True, axis_index_groups=order)

    def remote(array):
        return pltpu.with_memory_space_constraint(array, pltpu.HBM)

    def local(array):
        return pltpu.with_memory_space_constraint(array, pltpu.VMEM)

    vis_far = across(vis_rows)
    text_far = across(text_rows)
    query = dec_query.reshape(steps, heads, HD).transpose(1, 0, 2).reshape(q_rows, HD)

    lot = -(-cap // PAGE) * PAGE
    q_lots = q_rows * HD // (2 * kvw)
    gain = norm_gain.reshape(1, 2 * half)
    load = min(2048, half)
    step = min(1024, load // 2)
    fine = step // 2
    kept = load + load // 2
    arguments = (img_route.T, w_key, w_value, vis_rows, gain, query)
    info, key_held, value_held, vis_near, gain_near, query_near = call(
        lambda *refs: prepare_kernel(n, lot, *refs),
        (
            jax.ShapeDtypeStruct((STAT, img), I32),
            pltpu.VMEM((kept, kvw), BF16),
            pltpu.VMEM((kept, kvw), BF16),
            *[pltpu.VMEM(a.shape, a.dtype) for a in arguments[3:]],
        ),
        [ANY] * len(arguments),
        (VM,) * 6,
        [pltpu.VMEM((1, n * img), I32), pltpu.SemaphoreType.DMA((len(arguments),))],
        flops=1 << 20,
        traffic=2 * 2 * half * 2 * kvw * 2,
    )(*[remote(a) for a in arguments])

    left = 2 * half - kept
    sizes = [half - kept, *[load] * (half // load - 1), load // 2, fine, fine]
    packed = call(
        lambda *refs: vis_kernel(n, lot, sizes, step, *refs),
        pltpu.VMEM((n, q_lots + lot, 2 * kvw), BF16),
        [VM] * 6 + [ANY] * 2 + [VM],
        VM,
        [
            pltpu.VMEM((left, kvw), BF16),
            pltpu.VMEM((left, kvw), BF16),
            pltpu.VMEM((img, 2 * kvw), F32),
            pltpu.SemaphoreType.DMA((2 * len(sizes),)),
        ],
        flops=64 * img * 2 * half * 2 * kvw,
        traffic=2 * img * 2 * half + 8 * half * kvw,
    )(
        local(vis_near),
        vis_far,
        local(gain_near),
        local(query_near),
        local(key_held),
        local(value_held),
        remote(w_key),
        remote(w_value),
        info,
    )
    arrived = exchange(packed, section_of)

    block = page_cap * PAGE * 2 * kv_heads + q_rows + PAGE
    lists = (img_route.T, page_dest.T, page_count, tail_len, dec_req)
    reach = min(tok, n * cap)
    kv_text, bias, base, hot, covered, slots = call(
        lambda *refs: text_kernel(n, img, lot, load, step, page_cap, *refs),
        (
            jax.ShapeDtypeStruct((tok, 2 * kvw), BF16),
            jax.ShapeDtypeStruct((tok, n * q_rows // kv_heads), F32),
            jax.ShapeDtypeStruct((n, block - q_rows - PAGE, HD), BF16),
            jax.ShapeDtypeStruct((reach, n * lot), BF16),
            jax.ShapeDtypeStruct((reach, HD), F32),
            jax.ShapeDtypeStruct((blocks,), I32),
        ),
        [ANY, VM, VM] + [ANY] * 7,
        (VM, VM, VM, VM, VM, SM),
        [
            pltpu.VMEM((tok, half), BF16),
            pltpu.VMEM(w_key.shape, BF16),
            pltpu.VMEM(w_value.shape, BF16),
            pltpu.VMEM((tok, 2 * kvw), F32),
            pltpu.SMEM((n,), I32),
            pltpu.SemaphoreType.DMA((1 + 4 * half // load + len(lists),)),
            *[(pltpu.VMEM if i == 0 else pltpu.SMEM)(a.shape, a.dtype) for i, a in enumerate(lists)],
        ],
        limit=24,
        flops=2 * tok * 2 * half * 2 * kvw,
        traffic=2 * tok * 2 * half + 8 * half * kvw,
    )(remote(text_rows), text_far, remote(gain), remote(w_key), remote(w_value), *[remote(a) for a in lists])

    sent, own = call(
        lambda *refs: attend_kernel(n, cap, lot, page_cap, kv_heads, *refs),
        (
            jax.ShapeDtypeStruct((n, block, HD), BF16),
            jax.ShapeDtypeStruct((q_rows + STAT, HD), F32),
        ),
        [SM] + [VM] * 6,
        (ANY, VM),
        [
            pltpu.VMEM((n, block, HD), BF16),
            pltpu.VMEM((min(tok, n * cap), 2 * kvw), BF16),
            pltpu.VMEM((n * q_rows, HD), F32),
            pltpu.VMEM((STAT, n * q_rows // kv_heads), F32),
            pltpu.SemaphoreType.DMA((2,)),
        ],
        flops=4 * n * q_rows * tok * HD,
        traffic=n * (q_rows + STAT) * HD * 4,
    )(slots, hot, covered, kv_text, arrived, bias, base)
    shares = exchange(sent, page_section_of)

    mine = call(
        lambda *refs: fresh_kernel(n, kv_heads, steps, *refs),
        jax.ShapeDtypeStruct((q_rows + STAT, HD), F32),
        [VM] * 4,
        VM,
        flops=1 << 20,
        traffic=1 << 18,
    )(remote(query), remote(dec_key[0]), remote(dec_value[0]), own)

    slots_here = n * page_cap
    attended, cache_key, cache_value = call(
        lambda *refs: finish_kernel(kv_heads, steps, page_cap, *refs),
        (
            jax.ShapeDtypeStruct(dec_query.shape, BF16),
            jax.ShapeDtypeStruct((n, page_cap * PAGE, kvw), BF16),
            jax.ShapeDtypeStruct((n, page_cap * PAGE, kvw), BF16),
        ),
        [VM, VM],
        (VM, VM, VM),
        traffic=4 * tok * 2 * kvw,
    )(shares, mine)
    return (
        attended,
        cache_key.reshape(slots_here, PAGE, kvw),
        cache_value.reshape(slots_here, PAGE, kvw),
    )


def solution(mesh):
    return jax.shard_map(
        body,
        mesh=mesh,
        in_specs=(
            P(("groups", "section"), "tensor"),
            P(("groups", "section"), "tensor"),
            P("groups", None),
            P(),
            P(None, "tensor"),
            P(None, "tensor"),
            P("groups"),
            P("groups"),
            P("groups", None),
            P("groups"),
            P(("groups", "section"), None, "tensor"),
            P(("groups", "section"), None, "tensor"),
            P(("groups", "section"), None, "tensor"),
        ),
        out_specs=(
            P(("groups", "section"), None, "tensor"),
            P(("groups", "section"), None, "tensor"),
            P(("groups", "section"), None, "tensor"),
        ),
        check_vma=False,
    )
```

```python
import jax
import jax.numpy as jnp
from jax import lax
from jax.experimental import pallas as pl
from jax.experimental.pallas import tpu as pltpu
from jax.sharding import PartitionSpec as P

HD = 128
PAGE = 16
LOWEST = -1e30
EPS = 1e-06
STAT = 8
F32 = jnp.float32
BF16 = jnp.bfloat16
I32 = jnp.int32

VM = pl.BlockSpec(memory_space=pltpu.VMEM)
SM = pl.BlockSpec(memory_space=pltpu.SMEM)
ANY = pl.BlockSpec(memory_space=pl.ANY)
MIB = 1 << 20


def call(kernel, out_shape, in_specs, out_specs, scratch=(), limit=16, flops=0, traffic=0):
    return pl.pallas_call(
        kernel,
        out_shape=out_shape,
        in_specs=in_specs,
        out_specs=out_specs,
        scratch_shapes=list(scratch),
        compiler_params=pltpu.CompilerParams(vmem_limit_bytes=limit * MIB),
        cost_estimate=pl.CostEstimate(flops=flops, bytes_accessed=traffic, transcendentals=0),
    )


def rank_of(section, n):
    return jnp.where(section < n // 2, n - 2 - 2 * section, 2 * section - n + 1)


def section_of(rank, n):
    return n // 2 - 1 - rank // 2 + rank % 2 * (rank // 2 * 2 + 1)


def page_rank_of(section, n):
    z, y, length = section // 2, section % 2, n // 2
    return y * length + (2 * length - z - n // 4) % length


def page_section_of(rank, n):
    length = n // 2
    return 2 * (length - 1 - (rank % length + n // 4 - 1) % length) + rank // length


def dot(a, b):
    return jnp.dot(a, b, preferred_element_type=F32)


def dot_t(a, b):
    return lax.dot_general(a, b, (((1,), (1,)), ((), ())), preferred_element_type=F32)


def diagonal(shape):
    return lax.broadcasted_iota(I32, shape, 0) == lax.broadcasted_iota(I32, shape, 1)


def column_to_row(column):
    rows = column.shape[0]
    return jnp.sum(jnp.where(diagonal((rows, rows)), column, 0.0), axis=0, keepdims=True)


def row_to_column(row):
    lanes = row.shape[1]
    return jnp.sum(jnp.where(diagonal((lanes, lanes)), row, 0.0), axis=1, keepdims=True)


def squares_of(rows):
    total = jnp.zeros((rows.shape[0], HD), F32)
    for c in range(0, rows.shape[1], HD):
        wide = rows[:, c : c + HD].astype(F32)
        total = total + wide * wide
    return total


def split_three(values):
    high = values.astype(BF16).astype(F32)
    rest = values - high
    middle = rest.astype(BF16).astype(F32)
    return high, middle, rest - middle


def softmax_parts(query, key, value, usable):
    scores = jnp.where(usable, dot_t(query, key) * HD**-0.5, LOWEST)
    top = jnp.max(scores, axis=1, keepdims=True)
    weights = jnp.where(usable, jnp.exp(scores - top), 0.0)
    return dot(weights.astype(BF16), value), top, jnp.sum(weights, axis=1, keepdims=True)


def prepare_kernel(n, lot, *refs):
    far, info, near, (route, sems) = refs[:6], refs[6], refs[7:12], refs[12:]
    img, half = near[2].shape
    first = pl.ds(pl.multiple_of(lax.axis_index("tensor") * half, half), near[0].shape[0])
    sources = (far[0], far[1].at[first], far[2].at[first], *far[3:])
    copies = [pltpu.make_async_copy(a, b, sems.at[i]) for i, (a, b) in enumerate(zip(sources, (route, *near)))]
    for c in copies:
        c.start()
    copies[0].wait()
    pos = lax.axis_index("section")
    own = jnp.zeros((1, img), I32)
    for e in range(n):
        own = jnp.where(pos == e, route[:, e * img : (e + 1) * img], own)
    marks = own == lax.broadcasted_iota(I32, (n, img), 0)
    ones = jnp.where(marks, 1.0, 0.0).astype(BF16)
    earlier = lax.broadcasted_iota(I32, (img, img), 0) < lax.broadcasted_iota(I32, (img, img), 1)
    prefix = dot(ones, jnp.where(earlier, 1.0, 0.0).astype(BF16))
    local = jnp.sum(jnp.where(marks, prefix, 0.0), axis=0, keepdims=True).astype(I32)
    info[...] = jnp.broadcast_to(rank_of(own, n) * lot + local, info.shape)
    for c in copies[1:]:
        c.wait()


def plan_tokens(n, img, lot, page_cap, small, hot, covered, slots, bias, starts):
    route, pages, count, tail, req = small
    pos = lax.axis_index("section")
    tok, width = bias.shape
    blocks = tok // PAGE
    lanes = lax.broadcasted_iota(I32, (1, n * lot), 1)
    source, inner = section_of(lanes // lot, n), lanes % lot
    fits = jnp.zeros((1, n * lot), I32)
    offset = jnp.zeros((1, n * lot), I32)
    for e in range(n):
        here = (route[:, e * img : (e + 1) * img] == pos).astype(I32)
        arriving = jnp.sum(here, axis=1, keepdims=True)
        fits = fits + jnp.where(source == e, arriving, 0)
        offset = offset + jnp.where(source > e, arriving, 0)
    target = jnp.where(inner < fits, offset + inner, -1)
    chosen = jnp.where(lax.broadcasted_iota(I32, hot.shape, 0) == target, 1.0, 0.0)
    hot[...] = chosen.astype(BF16)
    covered[...] = jnp.broadcast_to(jnp.sum(chosen, axis=1, keepdims=True), covered.shape)
    total = jnp.int32(0)
    for r in range(n):
        starts[r] = total
        total = total + count[r]
    token = lax.broadcasted_iota(I32, (1, tok), 1) + pos * tok
    token_slot = jnp.full((1, tok), -1, I32)
    for b in range(n):
        r = req[b]
        first = starts[r] * PAGE
        last = first + (count[r] - 1) * PAGE + tail[r]
        token_slot = jnp.where((token >= first) & (token < last), b, token_slot)
    member = section_of(lax.broadcasted_iota(I32, (1, width), 1) // (width // n), n)
    bias[...] = jnp.where(row_to_column(token_slot.astype(F32)) == member.astype(F32), 0.0, LOWEST)
    for g in range(blocks):
        holder = pages[0, pos * blocks + g]
        slot = page_rank_of(holder, n) * page_cap
        for e in range(g):
            slot = slot + (pages[0, pos * blocks + e] == holder).astype(I32)
        slots[g] = slot


def scale_of(near, far):
    sums = jnp.sum(squares_of(near) + squares_of(far), axis=1, keepdims=True)
    return lax.rsqrt(sums / (2.0 * near.shape[1]) + EPS)


def normed_rows(rows, c, step, scale, gain):
    return (rows[:, c : c + step].astype(F32) * scale * gain).astype(BF16)


def add_part(total, at, normed, w, begin):
    part = dot(normed, w)
    columns = slice(at, at + part.shape[1])
    if begin:
        total[:, columns] = part
    else:
        total[:, columns] += part


def vis_kernel(n, lot, sizes, step, *refs):
    near, far, gain, query, key_held, value_held, w_key, w_value, info, out, key_rest, value_rest, total, sems = refs
    img, half = near.shape
    kvw = w_key.shape[1]
    me = lax.axis_index("tensor")
    held = key_held.shape[0]
    loads = {}
    at = held
    for size in sizes:
        side = me if at < half else 1 - me
        source = pl.ds(pl.multiple_of(side * half + at % half, size), size)
        number = 2 * len(loads)
        loads[at] = [
            pltpu.make_async_copy(w.at[source], kept.at[at - held : at - held + size], sems.at[number + i])
            for i, (w, kept) in enumerate(((w_key, key_rest), (w_value, value_rest)))
        ]
        for copy in loads[at]:
            copy.start()
        at += size
    scale = scale_of(near, far)
    points = [*range(0, 2 * half - step, step), *range(2 * half - step, 2 * half, sizes[-1])]
    for at, end in zip(points, [*points[1:], 2 * half]):
        for copy in loads.get(at, ()):
            copy.wait()
        rows, side = (near, me) if at < half else (far, 1 - me)
        weights, w_at = ((key_held, value_held), at) if at < held else ((key_rest, value_rest), at - held)
        c = at % half
        size = end - at
        columns = pl.ds(pl.multiple_of(side * half + c, size), size)
        normed = normed_rows(rows, c, size, scale, gain[:, columns])
        for w, col in zip(weights, (0, kvw)):
            add_part(total, col, normed, w[w_at : w_at + size, :], at == 0)
    slot = lax.broadcasted_iota(I32, (n * lot, img), 0)
    chosen = jnp.where(slot == info[0:1, :img], 1.0, 0.0).astype(BF16)
    packed = dot(chosen, total[...].astype(BF16)).astype(BF16)
    q_lots = out.shape[1] - lot
    for k in range(n):
        for j in range(query.shape[0] // q_lots):
            out[k, :q_lots, j * HD : (j + 1) * HD] = query[j * q_lots : (j + 1) * q_lots, :]
        out[k, q_lots:, :] = packed[k * lot : (k + 1) * lot, :]


def put_page(out, page_cap, slot, rows):
    chunk = page_cap * PAGE
    for h in range(rows.shape[1] // HD):
        at = pl.ds(pl.multiple_of((slot % page_cap) * PAGE + h * chunk, PAGE), PAGE)
        out[slot // page_cap, at, :] = rows[:, h * HD : (h + 1) * HD]


def text_kernel(n, img, lot, load, step, page_cap, *refs):
    (near_far, far, gain, w_key_far, w_value_far), small_far, refs = refs[:5], refs[5:10], refs[10:]
    (out, bias, base, hot, covered, slots), (near, w_key, w_value, total, starts, sems), small = (
        refs[:6],
        refs[6:12],
        refs[12:],
    )
    half = near.shape[1]
    kvw = w_key.shape[1]
    me = lax.axis_index("tensor")
    used = sems.shape[0] - len(small)
    lists = [pltpu.make_async_copy(a, b, sems.at[used + i]) for i, (a, b) in enumerate(zip(small_far, small))]
    for copy in lists:
        copy.start()
    first = pltpu.make_async_copy(near_far, near, sems.at[0])
    first.start()
    loads = []
    for side in (me, 1 - me):
        for c in range(0, half, load):
            at = len(loads) * load
            columns = pl.ds(pl.multiple_of(side * half + c, load), load)
            pair = [
                pltpu.make_async_copy(w.at[columns], held.at[at : at + load], sems.at[2 * len(loads) + i])
                for i, (w, held) in enumerate(((w_key_far, w_key), (w_value_far, w_value)), 1)
            ]
            for copy in pair:
                copy.start()
            loads.append(pair)
    sums = squares_of(far)
    first.wait()
    sums = jnp.sum(squares_of(near) + sums, axis=1, keepdims=True)
    scale = lax.rsqrt(sums / (2.0 * half) + EPS)
    for i, pair in enumerate(loads):
        for copy in pair:
            copy.wait()
        if i == 1:
            for copy in lists:
                copy.wait()
            plan_tokens(n, img, lot, page_cap, small, hot, covered, slots, bias, starts)
        for at in range(i * load, (i + 1) * load, step):
            rows, side = (near, me) if at < half else (far, 1 - me)
            c = at % half
            columns = pl.ds(pl.multiple_of(side * half + c, step), step)
            normed = normed_rows(rows, c, step, scale, gain[:, columns])
            for w, col in ((w_key, 0), (w_value, kvw)):
                add_part(total, col, normed, w[at : at + step, :], at == 0)
    out[...] = total[...].astype(BF16)
    base[...] = jnp.zeros(base.shape, BF16)
    tok = near.shape[0]
    for g in range(tok // PAGE):
        put_page(base, page_cap, slots[g], out[g * PAGE : (g + 1) * PAGE, :])


def attend_kernel(n, cap, lot, page_cap, kv_heads, slots, hot, covered, kv_text, arrived, bias, base, sent, own, *scratch):
    out, mixed, held, rows_held, sems = scratch
    order = [page_section_of(k, n) for k in range(n)]
    rank = rank_of(lax.axis_index("section"), n)
    tok = kv_text.shape[0]
    kvw = kv_heads * HD
    q_lots = arrived.shape[1] - lot
    reach = min(tok, n * cap)
    incoming = jnp.concatenate([arrived[k, q_lots:, :] for k in range(n)], axis=0)
    placed = dot(hot[...], incoming)
    mixed[...] = jnp.where(covered[:, :1] > 0.0, placed, kv_text[:reach, :].astype(F32)).astype(BF16)
    groups = arrived.shape[2] // HD // kv_heads
    rows = groups * q_lots
    pages = base.shape[1]
    out[:, :pages, :] = base[...]
    for g in range(reach // PAGE):
        put_page(out, page_cap, slots[g], mixed[g * PAGE : (g + 1) * PAGE, :])
    first = pltpu.make_async_copy(out.at[:, :pages, :], sent.at[:, :pages, :], sems.at[0])
    first.start()
    for g in range(kv_heads):
        query = jnp.concatenate(
            [
                arrived[k, :q_lots, (g * groups + j) * HD : (g * groups + j + 1) * HD]
                for k in range(n)
                for j in range(groups)
            ],
            axis=0,
        )
        cols = slice(g * HD, (g + 1) * HD)
        vcols = slice(kvw + g * HD, kvw + (g + 1) * HD)
        key = jnp.concatenate([mixed[:, cols], kv_text[reach:, cols]], axis=0)
        value = jnp.concatenate([mixed[:, vcols], kv_text[reach:, vcols]], axis=0)
        scores = dot_t(key, query) * HD**-0.5 + bias[...]
        top = jnp.max(scores, axis=0, keepdims=True)
        weights = jnp.exp(scores - top)
        rows_held[g : g + 1, :] = top
        rows_held[kv_heads + g : kv_heads + g + 1, :] = jnp.sum(weights, axis=0, keepdims=True)
        numerator = lax.dot_general(
            weights.astype(BF16), value, (((0,), (0,)), ((), ())), preferred_element_type=F32
        )
        held[g * n * rows : (g + 1) * n * rows, :] = numerator
        own[g * rows : (g + 1) * rows, :] = held[pl.ds(pl.multiple_of((g * n + rank) * rows, rows), rows), :]
        numerator = numerator.astype(BF16)
        for k in range(n):
            to = order.index(section_of(k, n))
            out[to, pages + g * rows : pages + (g + 1) * rows, :] = numerator[k * rows : (k + 1) * rows, :]
    stat_rows = 2 * kv_heads
    share = HD // rows
    window = pl.ds(pl.multiple_of(rank // share * HD, HD), HD)
    own[kv_heads * rows : kv_heads * rows + stat_rows, :] = rows_held[:stat_rows, window]
    blank = jnp.zeros((PAGE - 3 * stat_rows, HD), F32)
    for w in range(-(-n // share)):
        stats = rows_held[:stat_rows, w * HD : (w + 1) * HD]
        lines = jnp.concatenate([*split_three(stats), blank], axis=0).astype(BF16)
        for k in range(w * share, min(n, (w + 1) * share)):
            out[order.index(section_of(k, n)), pages + kv_heads * rows :, :] = lines
    last = pltpu.make_async_copy(out.at[:, pages:, :], sent.at[:, pages:, :], sems.at[1])
    last.start()
    first.wait()
    last.wait()


def pick_column(row, rows, start):
    shape = (rows, HD)
    chosen = lax.broadcasted_iota(I32, shape, 1) == lax.broadcasted_iota(I32, shape, 0) + start
    return jnp.sum(jnp.where(chosen, row, 0.0), axis=1, keepdims=True)


def combine(pieces, highest):
    numerator, total = 0.0, 0.0
    for rows, top, weight in pieces:
        scale = jnp.exp(top - highest)
        numerator = numerator + rows * scale
        total = total + weight * scale
    return numerator, total


def fresh_kernel(n, kv_heads, steps, query, key, value, own, mine):
    rows = query.shape[0] // kv_heads
    every = kv_heads * rows
    start = rank_of(lax.axis_index("section"), n) % (HD // rows) * rows
    row = lax.broadcasted_iota(I32, (rows, steps), 0)
    causal = lax.broadcasted_iota(I32, (rows, steps), 1) <= row % steps
    tops, totals = [], []
    for g in range(kv_heads):
        cols = slice(g * HD, (g + 1) * HD)
        at = slice(g * rows, (g + 1) * rows)
        fresh = softmax_parts(query[at, :], key[:, cols], value[:, cols], causal)
        share = (
            own[at, :],
            pick_column(own[every + g : every + g + 1, :], rows, start),
            pick_column(own[every + kv_heads + g : every + kv_heads + g + 1, :], rows, start),
        )
        highest = jnp.maximum(fresh[1], share[1])
        numerator, total = combine((fresh, share), highest)
        mine[at, :] = numerator
        tops.append(highest)
        totals.append(total)
    line = column_to_row(jnp.concatenate(tops + totals, axis=0))
    mine[every:, :] = jnp.broadcast_to(line, (STAT, line.shape[1]))


def finish_kernel(kv_heads, steps, page_cap, shares, mine, attended, keys, values):
    n = shares.shape[0]
    pos = lax.axis_index("section")
    every = mine.shape[0] - STAT
    rows = every // kv_heads
    start = rank_of(pos, n) % (HD // rows) * rows
    chunk = page_cap * PAGE
    halves = keys.shape[2] // HD
    for k in range(n):
        for i, out in enumerate((keys, values)):
            for h in range(halves):
                part = i * halves + h
                out[page_section_of(k, n), :, h * HD : (h + 1) * HD] = shares[k, part * chunk : (part + 1) * chunk, :]
    pages = 2 * halves * chunk
    stats = row_to_column(mine[every : every + 1, :])
    lines = []
    for k in range(n):
        three = shares[k, pages + every :, :].astype(F32)
        size = 2 * kv_heads
        lines.append(three[:size] + three[size : 2 * size] + three[2 * size : 3 * size])
    for g in range(kv_heads):
        at = slice(g * rows, (g + 1) * rows)
        pieces = [(mine[at, :], stats[at], stats[every + g * rows : every + (g + 1) * rows])]
        for k in range(n):
            away = pos != page_section_of(k, n)
            top = jnp.where(away, pick_column(lines[k][g : g + 1], rows, start), LOWEST)
            weight = jnp.where(away, pick_column(lines[k][kv_heads + g : kv_heads + g + 1], rows, start), 0.0)
            share = shares[k, pages + g * rows : pages + (g + 1) * rows, :].astype(F32)
            pieces.append((share, top, weight))
        highest = pieces[0][1]
        for p in pieces[1:]:
            highest = jnp.maximum(highest, p[1])
        numerator, total = combine(pieces, highest)
        result = (numerator / total).astype(BF16)
        for h in range(rows // steps):
            to = (g * rows // steps + h) * HD
            attended[0, :, to : to + HD] = result[h * steps : (h + 1) * steps, :]


def body(
    text_rows,
    vis_rows,
    img_route,
    norm_gain,
    w_key,
    w_value,
    page_count,
    tail_len,
    page_dest,
    dec_req,
    dec_query,
    dec_key,
    dec_value,
):
    n = lax.axis_size("section")
    tok, half = text_rows.shape
    img = vis_rows.shape[0]
    kvw = w_key.shape[1]
    kv_heads = kvw // HD
    _, steps, q_width = dec_query.shape
    heads = q_width // HD
    q_rows = heads * steps
    blocks = tok // PAGE
    cap = max(2, (2 * img + n - 1) // n)
    page_cap = max(1, (blocks + n - 1) // n)

    def across(array):
        return lax.ppermute(array, "tensor", [(0, 1), (1, 0)])

    def exchange(array, section_at):
        order = [[section_at(rank, n) for rank in range(n)]]
        return lax.all_to_all(array, "section", split_axis=0, concat_axis=0, tiled=True, axis_index_groups=order)

    def remote(array):
        return pltpu.with_memory_space_constraint(array, pltpu.HBM)

    def local(array):
        return pltpu.with_memory_space_constraint(array, pltpu.VMEM)

    vis_far = across(vis_rows)
    text_far = across(text_rows)
    query = dec_query.reshape(steps, heads, HD).transpose(1, 0, 2).reshape(q_rows, HD)

    lot = -(-cap // PAGE) * PAGE
    q_lots = q_rows * HD // (2 * kvw)
    gain = norm_gain.reshape(1, 2 * half)
    load = min(2048, half)
    step = min(1024, load // 2)
    fine = step // 2
    kept = load + load // 2
    arguments = (img_route.T, w_key, w_value, vis_rows, gain, query)
    info, key_held, value_held, vis_near, gain_near, query_near = call(
        lambda *refs: prepare_kernel(n, lot, *refs),
        (
            jax.ShapeDtypeStruct((STAT, img), I32),
            pltpu.VMEM((kept, kvw), BF16),
            pltpu.VMEM((kept, kvw), BF16),
            *[pltpu.VMEM(a.shape, a.dtype) for a in arguments[3:]],
        ),
        [ANY] * len(arguments),
        (VM,) * 6,
        [pltpu.VMEM((1, n * img), I32), pltpu.SemaphoreType.DMA((len(arguments),))],
        flops=1 << 20,
        traffic=2 * 2 * half * 2 * kvw * 2,
    )(*[remote(a) for a in arguments])

    left = 2 * half - kept
    sizes = [half - kept, *[load] * (half // load - 1), load // 2, fine, fine]
    packed = call(
        lambda *refs: vis_kernel(n, lot, sizes, step, *refs),
        pltpu.VMEM((n, q_lots + lot, 2 * kvw), BF16),
        [VM] * 6 + [ANY] * 2 + [VM],
        VM,
        [
            pltpu.VMEM((left, kvw), BF16),
            pltpu.VMEM((left, kvw), BF16),
            pltpu.VMEM((img, 2 * kvw), F32),
            pltpu.SemaphoreType.DMA((2 * len(sizes),)),
        ],
        flops=64 * img * 2 * half * 2 * kvw,
        traffic=2 * img * 2 * half + 8 * half * kvw,
    )(
        local(vis_near),
        vis_far,
        local(gain_near),
        local(query_near),
        local(key_held),
        local(value_held),
        remote(w_key),
        remote(w_value),
        info,
    )
    arrived = exchange(packed, section_of)

    block = page_cap * PAGE * 2 * kv_heads + q_rows + PAGE
    lists = (img_route.T, page_dest.T, page_count, tail_len, dec_req)
    reach = min(tok, n * cap)
    kv_text, bias, base, hot, covered, slots = call(
        lambda *refs: text_kernel(n, img, lot, load, step, page_cap, *refs),
        (
            jax.ShapeDtypeStruct((tok, 2 * kvw), BF16),
            jax.ShapeDtypeStruct((tok, n * q_rows // kv_heads), F32),
            jax.ShapeDtypeStruct((n, block - q_rows - PAGE, HD), BF16),
            jax.ShapeDtypeStruct((reach, n * lot), BF16),
            jax.ShapeDtypeStruct((reach, HD), F32),
            jax.ShapeDtypeStruct((blocks,), I32),
        ),
        [ANY, VM, VM] + [ANY] * 7,
        (VM, VM, VM, VM, VM, SM),
        [
            pltpu.VMEM((tok, half), BF16),
            pltpu.VMEM(w_key.shape, BF16),
            pltpu.VMEM(w_value.shape, BF16),
            pltpu.VMEM((tok, 2 * kvw), F32),
            pltpu.SMEM((n,), I32),
            pltpu.SemaphoreType.DMA((1 + 4 * half // load + len(lists),)),
            *[(pltpu.VMEM if i == 0 else pltpu.SMEM)(a.shape, a.dtype) for i, a in enumerate(lists)],
        ],
        limit=24,
        flops=2 * tok * 2 * half * 2 * kvw,
        traffic=2 * tok * 2 * half + 8 * half * kvw,
    )(remote(text_rows), text_far, remote(gain), remote(w_key), remote(w_value), *[remote(a) for a in lists])

    sent, own = call(
        lambda *refs: attend_kernel(n, cap, lot, page_cap, kv_heads, *refs),
        (
            jax.ShapeDtypeStruct((n, block, HD), BF16),
            jax.ShapeDtypeStruct((q_rows + STAT, HD), F32),
        ),
        [SM] + [VM] * 6,
        (ANY, VM),
        [
            pltpu.VMEM((n, block, HD), BF16),
            pltpu.VMEM((min(tok, n * cap), 2 * kvw), BF16),
            pltpu.VMEM((n * q_rows, HD), F32),
            pltpu.VMEM((STAT, n * q_rows // kv_heads), F32),
            pltpu.SemaphoreType.DMA((2,)),
        ],
        flops=4 * n * q_rows * tok * HD,
        traffic=n * (q_rows + STAT) * HD * 4,
    )(slots, hot, covered, kv_text, arrived, bias, base)
    shares = exchange(sent, page_section_of)

    mine = call(
        lambda *refs: fresh_kernel(n, kv_heads, steps, *refs),
        jax.ShapeDtypeStruct((q_rows + STAT, HD), F32),
        [VM] * 4,
        VM,
        flops=1 << 20,
        traffic=1 << 18,
    )(remote(query), remote(dec_key[0]), remote(dec_value[0]), own)

    slots_here = n * page_cap
    attended, cache_key, cache_value = call(
        lambda *refs: finish_kernel(kv_heads, steps, page_cap, *refs),
        (
            jax.ShapeDtypeStruct(dec_query.shape, BF16),
            jax.ShapeDtypeStruct((n, page_cap * PAGE, kvw), BF16),
            jax.ShapeDtypeStruct((n, page_cap * PAGE, kvw), BF16),
        ),
        [VM, VM],
        (VM, VM, VM),
        traffic=4 * tok * 2 * kvw,
    )(shares, mine)
    return (
        attended,
        cache_key.reshape(slots_here, PAGE, kvw),
        cache_value.reshape(slots_here, PAGE, kvw),
    )


def solution(mesh):
    return jax.shard_map(
        body,
        mesh=mesh,
        in_specs=(
            P(("groups", "section"), "tensor"),
            P(("groups", "section"), "tensor"),
            P("groups", None),
            P(),
            P(None, "tensor"),
            P(None, "tensor"),
            P("groups"),
            P("groups"),
            P("groups", None),
            P("groups"),
            P(("groups", "section"), None, "tensor"),
            P(("groups", "section"), None, "tensor"),
            P(("groups", "section"), None, "tensor"),
        ),
        out_specs=(
            P(("groups", "section"), None, "tensor"),
            P(("groups", "section"), None, "tensor"),
            P(("groups", "section"), None, "tensor"),
        ),
        check_vma=False,
    )
```

```python
import jax
import jax.numpy as jnp
from jax import lax
from jax.experimental import pallas as pl
from jax.experimental.pallas import tpu as pltpu
from jax.sharding import PartitionSpec as P

HD = 128
PAGE = 16
LOWEST = -1e30
EPS = 1e-06
STAT = 8
F32 = jnp.float32
BF16 = jnp.bfloat16
I32 = jnp.int32

VM = pl.BlockSpec(memory_space=pltpu.VMEM)
SM = pl.BlockSpec(memory_space=pltpu.SMEM)
ANY = pl.BlockSpec(memory_space=pl.ANY)
MIB = 1 << 20


def call(kernel, out_shape, in_specs, out_specs, scratch=(), limit=16, flops=0, traffic=0):
    return pl.pallas_call(
        kernel,
        out_shape=out_shape,
        in_specs=in_specs,
        out_specs=out_specs,
        scratch_shapes=list(scratch),
        compiler_params=pltpu.CompilerParams(vmem_limit_bytes=limit * MIB),
        cost_estimate=pl.CostEstimate(flops=flops, bytes_accessed=traffic, transcendentals=0),
    )


def mirrored(section, n):
    return n - 2 - section + 2 * (section % 2)


def rank_of(section, n):
    other = mirrored(section, n)
    return jnp.where(other < n // 2, n - 2 - 2 * other, 2 * other - n + 1)


def section_of(rank, n):
    return mirrored(n // 2 - 1 - rank // 2 + rank % 2 * (rank // 2 * 2 + 1), n)


def page_rank_of(section, n):
    z, y, length = section // 2, section % 2, n // 2
    return y * length + (2 * length - z - n // 4) % length


def page_section_of(rank, n):
    length = n // 2
    return 2 * (length - 1 - (rank % length + n // 4 - 1) % length) + rank // length


def dot(a, b):
    return jnp.dot(a, b, preferred_element_type=F32)


def dot_t(a, b):
    return lax.dot_general(a, b, (((1,), (1,)), ((), ())), preferred_element_type=F32)


def diagonal(shape):
    return lax.broadcasted_iota(I32, shape, 0) == lax.broadcasted_iota(I32, shape, 1)


def column_to_row(column):
    rows = column.shape[0]
    return jnp.sum(jnp.where(diagonal((rows, rows)), column, 0.0), axis=0, keepdims=True)


def row_to_column(row):
    lanes = row.shape[1]
    return jnp.sum(jnp.where(diagonal((lanes, lanes)), row, 0.0), axis=1, keepdims=True)


def squares_of(rows):
    total = jnp.zeros((rows.shape[0], HD), F32)
    for c in range(0, rows.shape[1], HD):
        wide = rows[:, c : c + HD].astype(F32)
        total = total + wide * wide
    return total


def split_three(values):
    high = values.astype(BF16).astype(F32)
    rest = values - high
    middle = rest.astype(BF16).astype(F32)
    return high, middle, rest - middle


def softmax_parts(query, key, value, usable):
    scores = jnp.where(usable, dot_t(query, key) * HD**-0.5, LOWEST)
    top = jnp.max(scores, axis=1, keepdims=True)
    weights = jnp.where(usable, jnp.exp(scores - top), 0.0)
    return dot(weights.astype(BF16), value), top, jnp.sum(weights, axis=1, keepdims=True)


def prepare_kernel(n, lot, *refs):
    far, info, near, (route, sems) = refs[:6], refs[6], refs[7:12], refs[12:]
    img, half = near[2].shape
    first = pl.ds(pl.multiple_of(lax.axis_index("tensor") * half, half), near[0].shape[0])
    sources = (far[0], far[1].at[first], far[2].at[first], *far[3:])
    copies = [pltpu.make_async_copy(a, b, sems.at[i]) for i, (a, b) in enumerate(zip(sources, (route, *near)))]
    for c in copies:
        c.start()
    copies[0].wait()
    pos = lax.axis_index("section")
    own = jnp.zeros((1, img), I32)
    for e in range(n):
        own = jnp.where(pos == e, route[:, e * img : (e + 1) * img], own)
    marks = own == lax.broadcasted_iota(I32, (n, img), 0)
    ones = jnp.where(marks, 1.0, 0.0).astype(BF16)
    earlier = lax.broadcasted_iota(I32, (img, img), 0) < lax.broadcasted_iota(I32, (img, img), 1)
    prefix = dot(ones, jnp.where(earlier, 1.0, 0.0).astype(BF16))
    local = jnp.sum(jnp.where(marks, prefix, 0.0), axis=0, keepdims=True).astype(I32)
    info[...] = jnp.broadcast_to(rank_of(own, n) * lot + local, info.shape)
    for c in copies[1:]:
        c.wait()


def plan_tokens(n, img, lot, page_cap, small, info, slots, bias, starts):
    route, pages, count, tail, req = small
    pos = lax.axis_index("section")
    tok, width = bias.shape
    blocks = tok // PAGE
    lanes = lax.broadcasted_iota(I32, (1, n * lot), 1)
    source, inner = section_of(lanes // lot, n), lanes % lot
    fits = jnp.zeros((1, n * lot), I32)
    offset = jnp.zeros((1, n * lot), I32)
    for e in range(n):
        here = (route[:, e * img : (e + 1) * img] == pos).astype(I32)
        arriving = jnp.sum(here, axis=1, keepdims=True)
        fits = fits + jnp.where(source == e, arriving, 0)
        offset = offset + jnp.where(source > e, arriving, 0)
    info[...] = jnp.broadcast_to(jnp.where(inner < fits, offset + inner, -1), info.shape)
    total = jnp.int32(0)
    for r in range(n):
        starts[r] = total
        total = total + count[r]
    token = lax.broadcasted_iota(I32, (1, tok), 1) + pos * tok
    token_slot = jnp.full((1, tok), -1, I32)
    for b in range(n):
        r = req[b]
        first = starts[r] * PAGE
        last = first + (count[r] - 1) * PAGE + tail[r]
        token_slot = jnp.where((token >= first) & (token < last), b, token_slot)
    member = section_of(lax.broadcasted_iota(I32, (1, width), 1) // (width // n), n)
    bias[...] = jnp.where(row_to_column(token_slot.astype(F32)) == member.astype(F32), 0.0, LOWEST)
    for g in range(blocks):
        holder = pages[0, pos * blocks + g]
        slot = page_rank_of(holder, n) * page_cap
        for e in range(g):
            slot = slot + (pages[0, pos * blocks + e] == holder).astype(I32)
        slots[g] = slot


def scale_of(near, far):
    sums = jnp.sum(squares_of(near) + squares_of(far), axis=1, keepdims=True)
    return lax.rsqrt(sums / (2.0 * near.shape[1]) + EPS)


def normed_rows(rows, c, step, scale, gain):
    return (rows[:, c : c + step].astype(F32) * scale * gain).astype(BF16)


def add_part(total, at, normed, w, begin):
    part = dot(normed, w)
    columns = slice(at, at + part.shape[1])
    if begin:
        total[:, columns] = part
    else:
        total[:, columns] += part


def vis_kernel(n, lot, sizes, step, *refs):
    near, far, gain, query, key_held, value_held, w_key, w_value, info, out, key_rest, value_rest, total, sems = refs
    img, half = near.shape
    kvw = w_key.shape[1]
    me = lax.axis_index("tensor")
    held = key_held.shape[0]
    loads = {}
    at = held
    for size in sizes:
        side = me if at < half else 1 - me
        source = pl.ds(pl.multiple_of(side * half + at % half, size), size)
        number = 2 * len(loads)
        loads[at] = [
            pltpu.make_async_copy(w.at[source], kept.at[at - held : at - held + size], sems.at[number + i])
            for i, (w, kept) in enumerate(((w_key, key_rest), (w_value, value_rest)))
        ]
        for copy in loads[at]:
            copy.start()
        at += size
    scale = scale_of(near, far)
    for at in range(0, 2 * half, step):
        for copy in loads.get(at, ()):
            copy.wait()
        rows, side = (near, me) if at < half else (far, 1 - me)
        weights, w_at = ((key_held, value_held), at) if at < held else ((key_rest, value_rest), at - held)
        c = at % half
        columns = pl.ds(pl.multiple_of(side * half + c, step), step)
        normed = normed_rows(rows, c, step, scale, gain[:, columns])
        for w, col in zip(weights, (0, kvw)):
            add_part(total, col, normed, w[w_at : w_at + step, :], at == 0)
    slot = lax.broadcasted_iota(I32, (n * lot, img), 0)
    chosen = jnp.where(slot == info[0:1, :img], 1.0, 0.0).astype(BF16)
    packed = dot(chosen, total[...].astype(BF16)).astype(BF16)
    q_lots = out.shape[1] - lot
    for k in range(n):
        for j in range(query.shape[0] // q_lots):
            out[k, :q_lots, j * HD : (j + 1) * HD] = query[j * q_lots : (j + 1) * q_lots, :]
        out[k, q_lots:, :] = packed[k * lot : (k + 1) * lot, :]


def put_page(out, page_cap, slot, rows):
    chunk = page_cap * PAGE
    for h in range(rows.shape[1] // HD):
        at = pl.ds(pl.multiple_of((slot % page_cap) * PAGE + h * chunk, PAGE), PAGE)
        out[slot // page_cap, at, :] = rows[:, h * HD : (h + 1) * HD]


def text_kernel(n, img, lot, load, step, page_cap, *refs):
    (near_far, far, gain, w_key_far, w_value_far), small_far, refs = refs[:5], refs[5:10], refs[10:]
    (out, bias, base, info, slots), (near, w_key, w_value, total, starts, sems), small = refs[:5], refs[5:11], refs[11:]
    half = near.shape[1]
    kvw = w_key.shape[1]
    me = lax.axis_index("tensor")
    first = pltpu.make_async_copy(near_far, near, sems.at[0])
    first.start()
    used = sems.shape[0] - len(small)
    lists = [pltpu.make_async_copy(a, b, sems.at[used + i]) for i, (a, b) in enumerate(zip(small_far, small))]
    for copy in lists:
        copy.start()
    loads = []
    for side in (me, 1 - me):
        for c in range(0, half, load):
            at = len(loads) * load
            columns = pl.ds(pl.multiple_of(side * half + c, load), load)
            pair = [
                pltpu.make_async_copy(w.at[columns], held.at[at : at + load], sems.at[2 * len(loads) + i])
                for i, (w, held) in enumerate(((w_key_far, w_key), (w_value_far, w_value)), 1)
            ]
            for copy in pair:
                copy.start()
            loads.append(pair)
    sums = squares_of(far)
    for copy in lists:
        copy.wait()
    plan_tokens(n, img, lot, page_cap, small, info, slots, bias, starts)
    first.wait()
    sums = jnp.sum(squares_of(near) + sums, axis=1, keepdims=True)
    scale = lax.rsqrt(sums / (2.0 * half) + EPS)
    for i, pair in enumerate(loads):
        for copy in pair:
            copy.wait()
        for at in range(i * load, (i + 1) * load, step):
            rows, side = (near, me) if at < half else (far, 1 - me)
            c = at % half
            columns = pl.ds(pl.multiple_of(side * half + c, step), step)
            normed = normed_rows(rows, c, step, scale, gain[:, columns])
            for w, col in ((w_key, 0), (w_value, kvw)):
                add_part(total, col, normed, w[at : at + step, :], at == 0)
    out[...] = total[...].astype(BF16)
    base[...] = jnp.zeros(base.shape, BF16)
    tok = near.shape[0]
    for g in range(tok // PAGE):
        put_page(base, page_cap, slots[g], out[g * PAGE : (g + 1) * PAGE, :])


def attend_kernel(n, cap, lot, page_cap, kv_heads, slots, info, kv_text, arrived, bias, base, sent, own, *scratch):
    out, mixed, held, rows_held, sems = scratch
    order = [page_section_of(k, n) for k in range(n)]
    rank = rank_of(lax.axis_index("section"), n)
    tok = kv_text.shape[0]
    kvw = kv_heads * HD
    q_lots = arrived.shape[1] - lot
    reach = min(tok, n * cap)
    hit = lax.broadcasted_iota(I32, (reach, n * lot), 0) == info[0:1, :]
    hot = jnp.where(hit, 1.0, 0.0)
    covered = jnp.sum(hot, axis=1, keepdims=True) > 0.0
    incoming = jnp.concatenate([arrived[k, q_lots:, :] for k in range(n)], axis=0)
    placed = dot(hot.astype(BF16), incoming)
    mixed[...] = jnp.where(covered, placed, kv_text[:reach, :].astype(F32)).astype(BF16)
    groups = arrived.shape[2] // HD // kv_heads
    rows = groups * q_lots
    pages = base.shape[1]
    out[:, :pages, :] = base[...]
    for g in range(reach // PAGE):
        put_page(out, page_cap, slots[g], mixed[g * PAGE : (g + 1) * PAGE, :])
    first = pltpu.make_async_copy(out.at[:, :pages, :], sent.at[:, :pages, :], sems.at[0])
    first.start()
    for g in range(kv_heads):
        query = jnp.concatenate(
            [
                arrived[k, :q_lots, (g * groups + j) * HD : (g * groups + j + 1) * HD]
                for k in range(n)
                for j in range(groups)
            ],
            axis=0,
        )
        cols = slice(g * HD, (g + 1) * HD)
        vcols = slice(kvw + g * HD, kvw + (g + 1) * HD)
        key = jnp.concatenate([mixed[:, cols], kv_text[reach:, cols]], axis=0)
        value = jnp.concatenate([mixed[:, vcols], kv_text[reach:, vcols]], axis=0)
        scores = dot_t(key, query) * HD**-0.5 + bias[...]
        top = jnp.max(scores, axis=0, keepdims=True)
        weights = jnp.exp(scores - top)
        rows_held[g : g + 1, :] = top
        rows_held[kv_heads + g : kv_heads + g + 1, :] = jnp.sum(weights, axis=0, keepdims=True)
        numerator = lax.dot_general(
            weights.astype(BF16), value, (((0,), (0,)), ((), ())), preferred_element_type=F32
        )
        held[g * n * rows : (g + 1) * n * rows, :] = numerator
        own[g * rows : (g + 1) * rows, :] = held[pl.ds(pl.multiple_of((g * n + rank) * rows, rows), rows), :]
        numerator = numerator.astype(BF16)
        for k in range(n):
            to = order.index(section_of(k, n))
            out[to, pages + g * rows : pages + (g + 1) * rows, :] = numerator[k * rows : (k + 1) * rows, :]
    stat_rows = 2 * kv_heads
    share = HD // rows
    window = pl.ds(pl.multiple_of(rank // share * HD, HD), HD)
    own[kv_heads * rows : kv_heads * rows + stat_rows, :] = rows_held[:stat_rows, window]
    blank = jnp.zeros((PAGE - 3 * stat_rows, HD), F32)
    for w in range(-(-n // share)):
        stats = rows_held[:stat_rows, w * HD : (w + 1) * HD]
        lines = jnp.concatenate([*split_three(stats), blank], axis=0).astype(BF16)
        for k in range(w * share, min(n, (w + 1) * share)):
            out[order.index(section_of(k, n)), pages + kv_heads * rows :, :] = lines
    last = pltpu.make_async_copy(out.at[:, pages:, :], sent.at[:, pages:, :], sems.at[1])
    last.start()
    first.wait()
    last.wait()


def pick_column(row, rows, start):
    shape = (rows, HD)
    chosen = lax.broadcasted_iota(I32, shape, 1) == lax.broadcasted_iota(I32, shape, 0) + start
    return jnp.sum(jnp.where(chosen, row, 0.0), axis=1, keepdims=True)


def combine(pieces, highest):
    numerator, total = 0.0, 0.0
    for rows, top, weight in pieces:
        scale = jnp.exp(top - highest)
        numerator = numerator + rows * scale
        total = total + weight * scale
    return numerator, total


def fresh_kernel(n, kv_heads, steps, query, key, value, own, mine):
    rows = query.shape[0] // kv_heads
    every = kv_heads * rows
    start = rank_of(lax.axis_index("section"), n) % (HD // rows) * rows
    row = lax.broadcasted_iota(I32, (rows, steps), 0)
    causal = lax.broadcasted_iota(I32, (rows, steps), 1) <= row % steps
    tops, totals = [], []
    for g in range(kv_heads):
        cols = slice(g * HD, (g + 1) * HD)
        at = slice(g * rows, (g + 1) * rows)
        fresh = softmax_parts(query[at, :], key[:, cols], value[:, cols], causal)
        share = (
            own[at, :],
            pick_column(own[every + g : every + g + 1, :], rows, start),
            pick_column(own[every + kv_heads + g : every + kv_heads + g + 1, :], rows, start),
        )
        highest = jnp.maximum(fresh[1], share[1])
        numerator, total = combine((fresh, share), highest)
        mine[at, :] = numerator
        tops.append(highest)
        totals.append(total)
    line = column_to_row(jnp.concatenate(tops + totals, axis=0))
    mine[every:, :] = jnp.broadcast_to(line, (STAT, line.shape[1]))


def finish_kernel(kv_heads, steps, page_cap, shares, mine, attended, keys, values):
    n = shares.shape[0]
    pos = lax.axis_index("section")
    every = mine.shape[0] - STAT
    rows = every // kv_heads
    start = rank_of(pos, n) % (HD // rows) * rows
    chunk = page_cap * PAGE
    halves = keys.shape[2] // HD
    for k in range(n):
        for i, out in enumerate((keys, values)):
            for h in range(halves):
                part = i * halves + h
                out[page_section_of(k, n), :, h * HD : (h + 1) * HD] = shares[k, part * chunk : (part + 1) * chunk, :]
    pages = 2 * halves * chunk
    stats = row_to_column(mine[every : every + 1, :])
    lines = []
    for k in range(n):
        three = shares[k, pages + every :, :].astype(F32)
        size = 2 * kv_heads
        lines.append(three[:size] + three[size : 2 * size] + three[2 * size : 3 * size])
    for g in range(kv_heads):
        at = slice(g * rows, (g + 1) * rows)
        pieces = [(mine[at, :], stats[at], stats[every + g * rows : every + (g + 1) * rows])]
        for k in range(n):
            away = pos != page_section_of(k, n)
            top = jnp.where(away, pick_column(lines[k][g : g + 1], rows, start), LOWEST)
            weight = jnp.where(away, pick_column(lines[k][kv_heads + g : kv_heads + g + 1], rows, start), 0.0)
            share = shares[k, pages + g * rows : pages + (g + 1) * rows, :].astype(F32)
            pieces.append((share, top, weight))
        highest = pieces[0][1]
        for p in pieces[1:]:
            highest = jnp.maximum(highest, p[1])
        numerator, total = combine(pieces, highest)
        result = (numerator / total).astype(BF16)
        for h in range(rows // steps):
            to = (g * rows // steps + h) * HD
            attended[0, :, to : to + HD] = result[h * steps : (h + 1) * steps, :]


def body(
    text_rows,
    vis_rows,
    img_route,
    norm_gain,
    w_key,
    w_value,
    page_count,
    tail_len,
    page_dest,
    dec_req,
    dec_query,
    dec_key,
    dec_value,
):
    n = lax.axis_size("section")
    tok, half = text_rows.shape
    img = vis_rows.shape[0]
    kvw = w_key.shape[1]
    kv_heads = kvw // HD
    _, steps, q_width = dec_query.shape
    heads = q_width // HD
    q_rows = heads * steps
    blocks = tok // PAGE
    cap = max(2, (2 * img + n - 1) // n)
    page_cap = max(1, (blocks + n - 1) // n)

    def across(array):
        return lax.ppermute(array, "tensor", [(0, 1), (1, 0)])

    def exchange(array, section_at):
        order = [[section_at(rank, n) for rank in range(n)]]
        return lax.all_to_all(array, "section", split_axis=0, concat_axis=0, tiled=True, axis_index_groups=order)

    def remote(array):
        return pltpu.with_memory_space_constraint(array, pltpu.HBM)

    def local(array):
        return pltpu.with_memory_space_constraint(array, pltpu.VMEM)

    vis_far = across(vis_rows)
    text_far = across(text_rows)
    query = dec_query.reshape(steps, heads, HD).transpose(1, 0, 2).reshape(q_rows, HD)

    lot = -(-cap // PAGE) * PAGE
    q_lots = q_rows * HD // (2 * kvw)
    gain = norm_gain.reshape(1, 2 * half)
    load = min(2048, half)
    step = min(1024, load // 2)
    kept = load + load // 2
    arguments = (img_route.T, w_key, w_value, vis_rows, gain, query)
    info, key_held, value_held, vis_near, gain_near, query_near = call(
        lambda *refs: prepare_kernel(n, lot, *refs),
        (
            jax.ShapeDtypeStruct((STAT, img), I32),
            pltpu.VMEM((kept, kvw), BF16),
            pltpu.VMEM((kept, kvw), BF16),
            *[pltpu.VMEM(a.shape, a.dtype) for a in arguments[3:]],
        ),
        [ANY] * len(arguments),
        (VM,) * 6,
        [pltpu.VMEM((1, n * img), I32), pltpu.SemaphoreType.DMA((len(arguments),))],
        flops=1 << 20,
        traffic=2 * 2 * half * 2 * kvw * 2,
    )(*[remote(a) for a in arguments])

    left = 2 * half - kept
    sizes = [half - kept, *[load] * (half // load - 1), *[load // 2] * 2]
    packed = call(
        lambda *refs: vis_kernel(n, lot, sizes, step, *refs),
        pltpu.VMEM((n, q_lots + lot, 2 * kvw), BF16),
        [VM] * 6 + [ANY] * 2 + [VM],
        VM,
        [
            pltpu.VMEM((left, kvw), BF16),
            pltpu.VMEM((left, kvw), BF16),
            pltpu.VMEM((img, 2 * kvw), F32),
            pltpu.SemaphoreType.DMA((2 * len(sizes),)),
        ],
        flops=64 * img * 2 * half * 2 * kvw,
        traffic=2 * img * 2 * half + 8 * half * kvw,
    )(
        local(vis_near),
        vis_far,
        local(gain_near),
        local(query_near),
        local(key_held),
        local(value_held),
        remote(w_key),
        remote(w_value),
        info,
    )
    arrived = exchange(packed, section_of)

    block = page_cap * PAGE * 2 * kv_heads + q_rows + PAGE
    lists = (img_route.T, page_dest.T, page_count, tail_len, dec_req)
    kv_text, bias, base, info, slots = call(
        lambda *refs: text_kernel(n, img, lot, load, step, page_cap, *refs),
        (
            jax.ShapeDtypeStruct((tok, 2 * kvw), BF16),
            jax.ShapeDtypeStruct((tok, n * q_rows // kv_heads), F32),
            jax.ShapeDtypeStruct((n, block - q_rows - PAGE, HD), BF16),
            jax.ShapeDtypeStruct((STAT, n * lot), I32),
            jax.ShapeDtypeStruct((blocks,), I32),
        ),
        [ANY, VM, VM] + [ANY] * 7,
        (VM, VM, VM, VM, SM),
        [
            pltpu.VMEM((tok, half), BF16),
            pltpu.VMEM(w_key.shape, BF16),
            pltpu.VMEM(w_value.shape, BF16),
            pltpu.VMEM((tok, 2 * kvw), F32),
            pltpu.SMEM((n,), I32),
            pltpu.SemaphoreType.DMA((1 + 4 * half // load + len(lists),)),
            *[(pltpu.VMEM if i == 0 else pltpu.SMEM)(a.shape, a.dtype) for i, a in enumerate(lists)],
        ],
        limit=24,
        flops=2 * tok * 2 * half * 2 * kvw,
        traffic=2 * tok * 2 * half + 8 * half * kvw,
    )(remote(text_rows), text_far, remote(gain), remote(w_key), remote(w_value), *[remote(a) for a in lists])

    sent, own = call(
        lambda *refs: attend_kernel(n, cap, lot, page_cap, kv_heads, *refs),
        (
            jax.ShapeDtypeStruct((n, block, HD), BF16),
            jax.ShapeDtypeStruct((q_rows + STAT, HD), F32),
        ),
        [SM] + [VM] * 5,
        (ANY, VM),
        [
            pltpu.VMEM((n, block, HD), BF16),
            pltpu.VMEM((min(tok, n * cap), 2 * kvw), BF16),
            pltpu.VMEM((n * q_rows, HD), F32),
            pltpu.VMEM((STAT, n * q_rows // kv_heads), F32),
            pltpu.SemaphoreType.DMA((2,)),
        ],
        flops=4 * n * q_rows * tok * HD,
        traffic=n * (q_rows + STAT) * HD * 4,
    )(slots, info, kv_text, arrived, bias, base)
    shares = exchange(sent, page_section_of)

    mine = call(
        lambda *refs: fresh_kernel(n, kv_heads, steps, *refs),
        jax.ShapeDtypeStruct((q_rows + STAT, HD), F32),
        [VM] * 4,
        VM,
        flops=1 << 20,
        traffic=1 << 18,
    )(remote(query), remote(dec_key[0]), remote(dec_value[0]), own)

    slots_here = n * page_cap
    attended, cache_key, cache_value = call(
        lambda *refs: finish_kernel(kv_heads, steps, page_cap, *refs),
        (
            jax.ShapeDtypeStruct(dec_query.shape, BF16),
            jax.ShapeDtypeStruct((n, page_cap * PAGE, kvw), BF16),
            jax.ShapeDtypeStruct((n, page_cap * PAGE, kvw), BF16),
        ),
        [VM, VM],
        (VM, VM, VM),
        traffic=4 * tok * 2 * kvw,
    )(shares, mine)
    return (
        attended,
        cache_key.reshape(slots_here, PAGE, kvw),
        cache_value.reshape(slots_here, PAGE, kvw),
    )


def solution(mesh):
    return jax.shard_map(
        body,
        mesh=mesh,
        in_specs=(
            P(("groups", "section"), "tensor"),
            P(("groups", "section"), "tensor"),
            P("groups", None),
            P(),
            P(None, "tensor"),
            P(None, "tensor"),
            P("groups"),
            P("groups"),
            P("groups", None),
            P("groups"),
            P(("groups", "section"), None, "tensor"),
            P(("groups", "section"), None, "tensor"),
            P(("groups", "section"), None, "tensor"),
        ),
        out_specs=(
            P(("groups", "section"), None, "tensor"),
            P(("groups", "section"), None, "tensor"),
            P(("groups", "section"), None, "tensor"),
        ),
        check_vma=False,
    )
```

```python
import jax
import jax.numpy as jnp
from jax import lax
from jax.experimental import pallas as pl
from jax.experimental.pallas import tpu as pltpu
from jax.sharding import PartitionSpec as P

HD = 128
PAGE = 16
LOWEST = -1e30
EPS = 1e-06
STAT = 8
F32 = jnp.float32
BF16 = jnp.bfloat16
I32 = jnp.int32

VM = pl.BlockSpec(memory_space=pltpu.VMEM)
SM = pl.BlockSpec(memory_space=pltpu.SMEM)
ANY = pl.BlockSpec(memory_space=pl.ANY)
MIB = 1 << 20


def call(kernel, out_shape, in_specs, out_specs, scratch=(), limit=16, flops=0, traffic=0):
    return pl.pallas_call(
        kernel,
        out_shape=out_shape,
        in_specs=in_specs,
        out_specs=out_specs,
        scratch_shapes=list(scratch),
        compiler_params=pltpu.CompilerParams(vmem_limit_bytes=limit * MIB),
        cost_estimate=pl.CostEstimate(flops=flops, bytes_accessed=traffic, transcendentals=0),
    )


def rank_of(section, n):
    return jnp.where(section < n // 2, n - 2 - 2 * section, 2 * section - n + 1)


def section_of(rank, n):
    return n // 2 - 1 - rank // 2 + rank % 2 * (rank // 2 * 2 + 1)


def page_rank_of(section, n):
    z, y, length = section // 2, section % 2, n // 2
    return y * length + (2 * length - z - n // 4) % length


def page_section_of(rank, n):
    length = n // 2
    return 2 * (length - 1 - (rank % length + n // 4 - 1) % length) + rank // length


def dot(a, b):
    return jnp.dot(a, b, preferred_element_type=F32)


def dot_t(a, b):
    return lax.dot_general(a, b, (((1,), (1,)), ((), ())), preferred_element_type=F32)


def diagonal(shape):
    return lax.broadcasted_iota(I32, shape, 0) == lax.broadcasted_iota(I32, shape, 1)


def column_to_row(column):
    rows = column.shape[0]
    return jnp.sum(jnp.where(diagonal((rows, rows)), column, 0.0), axis=0, keepdims=True)


def row_to_column(row):
    lanes = row.shape[1]
    return jnp.sum(jnp.where(diagonal((lanes, lanes)), row, 0.0), axis=1, keepdims=True)


def squares_of(rows):
    total = jnp.zeros((rows.shape[0], HD), F32)
    for c in range(0, rows.shape[1], HD):
        wide = rows[:, c : c + HD].astype(F32)
        total = total + wide * wide
    return total


def split_three(values):
    high = values.astype(BF16).astype(F32)
    rest = values - high
    middle = rest.astype(BF16).astype(F32)
    return high, middle, rest - middle


def softmax_parts(query, key, value, usable):
    scores = jnp.where(usable, dot_t(query, key) * HD**-0.5, LOWEST)
    top = jnp.max(scores, axis=1, keepdims=True)
    weights = jnp.where(usable, jnp.exp(scores - top), 0.0)
    return dot(weights.astype(BF16), value), top, jnp.sum(weights, axis=1, keepdims=True)


def prepare_kernel(n, lot, *refs):
    far, info, near, (route, sems) = refs[:6], refs[6], refs[7:12], refs[12:]
    img, half = near[2].shape
    first = pl.ds(pl.multiple_of(lax.axis_index("tensor") * half, half), near[0].shape[0])
    sources = (far[0], far[1].at[first], far[2].at[first], *far[3:])
    copies = [pltpu.make_async_copy(a, b, sems.at[i]) for i, (a, b) in enumerate(zip(sources, (route, *near)))]
    for c in copies:
        c.start()
    copies[0].wait()
    pos = lax.axis_index("section")
    own = jnp.zeros((1, img), I32)
    for e in range(n):
        own = jnp.where(pos == e, route[:, e * img : (e + 1) * img], own)
    marks = own == lax.broadcasted_iota(I32, (n, img), 0)
    ones = jnp.where(marks, 1.0, 0.0).astype(BF16)
    earlier = lax.broadcasted_iota(I32, (img, img), 0) < lax.broadcasted_iota(I32, (img, img), 1)
    prefix = dot(ones, jnp.where(earlier, 1.0, 0.0).astype(BF16))
    local = jnp.sum(jnp.where(marks, prefix, 0.0), axis=0, keepdims=True).astype(I32)
    info[...] = jnp.broadcast_to(rank_of(own, n) * lot + local, info.shape)
    for c in copies[1:]:
        c.wait()


def plan_tokens(n, img, lot, page_cap, small, info, slots, bias, starts):
    route, pages, count, tail, req = small
    pos = lax.axis_index("section")
    tok, width = bias.shape
    blocks = tok // PAGE
    lanes = lax.broadcasted_iota(I32, (1, n * lot), 1)
    source, inner = section_of(lanes // lot, n), lanes % lot
    fits = jnp.zeros((1, n * lot), I32)
    offset = jnp.zeros((1, n * lot), I32)
    for e in range(n):
        here = (route[:, e * img : (e + 1) * img] == pos).astype(I32)
        arriving = jnp.sum(here, axis=1, keepdims=True)
        fits = fits + jnp.where(source == e, arriving, 0)
        offset = offset + jnp.where(source > e, arriving, 0)
    info[...] = jnp.broadcast_to(jnp.where(inner < fits, offset + inner, -1), info.shape)
    total = jnp.int32(0)
    for r in range(n):
        starts[r] = total
        total = total + count[r]
    token = lax.broadcasted_iota(I32, (1, tok), 1) + pos * tok
    token_slot = jnp.full((1, tok), -1, I32)
    for b in range(n):
        r = req[b]
        first = starts[r] * PAGE
        last = first + (count[r] - 1) * PAGE + tail[r]
        token_slot = jnp.where((token >= first) & (token < last), b, token_slot)
    member = section_of(lax.broadcasted_iota(I32, (1, width), 1) // (width // n), n)
    bias[...] = jnp.where(row_to_column(token_slot.astype(F32)) == member.astype(F32), 0.0, LOWEST)
    for g in range(blocks):
        holder = pages[0, pos * blocks + g]
        slot = page_rank_of(holder, n) * page_cap
        for e in range(g):
            slot = slot + (pages[0, pos * blocks + e] == holder).astype(I32)
        slots[g] = slot


def scale_of(near, far):
    sums = jnp.sum(squares_of(near) + squares_of(far), axis=1, keepdims=True)
    return lax.rsqrt(sums / (2.0 * near.shape[1]) + EPS)


def normed_rows(rows, c, step, scale, gain):
    return (rows[:, c : c + step].astype(F32) * scale * gain).astype(BF16)


def add_part(total, at, normed, w, begin):
    part = dot(normed, w)
    columns = slice(at, at + part.shape[1])
    if begin:
        total[:, columns] = part
    else:
        total[:, columns] += part


def vis_kernel(n, lot, sizes, step, *refs):
    near, far, gain, query, key_held, value_held, w_key, w_value, info, out, key_rest, value_rest, total, sems = refs
    img, half = near.shape
    kvw = w_key.shape[1]
    me = lax.axis_index("tensor")
    held = key_held.shape[0]
    loads = {}
    at = held
    for size in sizes:
        side = me if at < half else 1 - me
        source = pl.ds(pl.multiple_of(side * half + at % half, size), size)
        number = 2 * len(loads)
        loads[at] = [
            pltpu.make_async_copy(w.at[source], kept.at[at - held : at - held + size], sems.at[number + i])
            for i, (w, kept) in enumerate(((w_key, key_rest), (w_value, value_rest)))
        ]
        for copy in loads[at]:
            copy.start()
        at += size
    scale = scale_of(near, far)
    for at in range(0, 2 * half, step):
        for copy in loads.get(at, ()):
            copy.wait()
        rows, side = (near, me) if at < half else (far, 1 - me)
        weights, w_at = ((key_held, value_held), at) if at < held else ((key_rest, value_rest), at - held)
        c = at % half
        columns = pl.ds(pl.multiple_of(side * half + c, step), step)
        normed = normed_rows(rows, c, step, scale, gain[:, columns])
        for w, col in zip(weights, (0, kvw)):
            add_part(total, col, normed, w[w_at : w_at + step, :], at == 0)
    slot = lax.broadcasted_iota(I32, (n * lot, img), 0)
    chosen = jnp.where(slot == info[0:1, :img], 1.0, 0.0).astype(BF16)
    packed = dot(chosen, total[...].astype(BF16)).astype(BF16)
    q_lots = out.shape[1] - lot
    for k in range(n):
        for j in range(query.shape[0] // q_lots):
            out[k, :q_lots, j * HD : (j + 1) * HD] = query[j * q_lots : (j + 1) * q_lots, :]
        out[k, q_lots:, :] = packed[k * lot : (k + 1) * lot, :]


def put_page(out, page_cap, slot, rows):
    chunk = page_cap * PAGE
    for h in range(rows.shape[1] // HD):
        at = pl.ds(pl.multiple_of((slot % page_cap) * PAGE + h * chunk, PAGE), PAGE)
        out[slot // page_cap, at, :] = rows[:, h * HD : (h + 1) * HD]


def text_kernel(n, img, lot, load, step, page_cap, *refs):
    (near_far, far, gain, w_key_far, w_value_far), small_far, refs = refs[:5], refs[5:10], refs[10:]
    (out, bias, base, info, slots), (near, w_key, w_value, total, starts, sems), small = refs[:5], refs[5:11], refs[11:]
    half = near.shape[1]
    kvw = w_key.shape[1]
    me = lax.axis_index("tensor")
    first = pltpu.make_async_copy(near_far, near, sems.at[0])
    first.start()
    used = sems.shape[0] - len(small)
    lists = [pltpu.make_async_copy(a, b, sems.at[used + i]) for i, (a, b) in enumerate(zip(small_far, small))]
    for copy in lists:
        copy.start()
    loads = []
    for side in (me, 1 - me):
        for c in range(0, half, load):
            at = len(loads) * load
            columns = pl.ds(pl.multiple_of(side * half + c, load), load)
            pair = [
                pltpu.make_async_copy(w.at[columns], held.at[at : at + load], sems.at[2 * len(loads) + i])
                for i, (w, held) in enumerate(((w_key_far, w_key), (w_value_far, w_value)), 1)
            ]
            for copy in pair:
                copy.start()
            loads.append(pair)
    sums = squares_of(far)
    for copy in lists:
        copy.wait()
    plan_tokens(n, img, lot, page_cap, small, info, slots, bias, starts)
    first.wait()
    sums = jnp.sum(squares_of(near) + sums, axis=1, keepdims=True)
    scale = lax.rsqrt(sums / (2.0 * half) + EPS)
    for i, pair in enumerate(loads):
        for copy in pair:
            copy.wait()
        for at in range(i * load, (i + 1) * load, step):
            rows, side = (near, me) if at < half else (far, 1 - me)
            c = at % half
            columns = pl.ds(pl.multiple_of(side * half + c, step), step)
            normed = normed_rows(rows, c, step, scale, gain[:, columns])
            for w, col in ((w_key, 0), (w_value, kvw)):
                add_part(total, col, normed, w[at : at + step, :], at == 0)
    out[...] = total[...].astype(BF16)
    base[...] = jnp.zeros(base.shape, BF16)
    tok = near.shape[0]
    for g in range(tok // PAGE):
        put_page(base, page_cap, slots[g], out[g * PAGE : (g + 1) * PAGE, :])


def attend_kernel(n, cap, lot, page_cap, kv_heads, slots, info, kv_text, arrived, bias, base, sent, own, *scratch):
    out, mixed, held, rows_held, sems = scratch
    order = [page_section_of(k, n) for k in range(n)]
    rank = rank_of(lax.axis_index("section"), n)
    tok = kv_text.shape[0]
    kvw = kv_heads * HD
    q_lots = arrived.shape[1] - lot
    reach = min(tok, n * cap)
    hit = lax.broadcasted_iota(I32, (reach, n * lot), 0) == info[0:1, :]
    hot = jnp.where(hit, 1.0, 0.0)
    covered = jnp.sum(hot, axis=1, keepdims=True) > 0.0
    incoming = jnp.concatenate([arrived[k, q_lots:, :] for k in range(n)], axis=0)
    placed = dot(hot.astype(BF16), incoming)
    mixed[...] = jnp.where(covered, placed, kv_text[:reach, :].astype(F32)).astype(BF16)
    groups = arrived.shape[2] // HD // kv_heads
    rows = groups * q_lots
    pages = base.shape[1]
    out[:, :pages, :] = base[...]
    for g in range(reach // PAGE):
        put_page(out, page_cap, slots[g], mixed[g * PAGE : (g + 1) * PAGE, :])
    first = pltpu.make_async_copy(out.at[:, :pages, :], sent.at[:, :pages, :], sems.at[0])
    first.start()
    for g in range(kv_heads):
        query = jnp.concatenate(
            [
                arrived[k, :q_lots, (g * groups + j) * HD : (g * groups + j + 1) * HD]
                for k in range(n)
                for j in range(groups)
            ],
            axis=0,
        )
        cols = slice(g * HD, (g + 1) * HD)
        vcols = slice(kvw + g * HD, kvw + (g + 1) * HD)
        key = jnp.concatenate([mixed[:, cols], kv_text[reach:, cols]], axis=0)
        value = jnp.concatenate([mixed[:, vcols], kv_text[reach:, vcols]], axis=0)
        scores = dot_t(key, query) * HD**-0.5 + bias[...]
        top = jnp.max(scores, axis=0, keepdims=True)
        weights = jnp.exp(scores - top)
        rows_held[g : g + 1, :] = top
        rows_held[kv_heads + g : kv_heads + g + 1, :] = jnp.sum(weights, axis=0, keepdims=True)
        numerator = lax.dot_general(
            weights.astype(BF16), value, (((0,), (0,)), ((), ())), preferred_element_type=F32
        )
        held[g * n * rows : (g + 1) * n * rows, :] = numerator
        own[g * rows : (g + 1) * rows, :] = held[pl.ds(pl.multiple_of((g * n + rank) * rows, rows), rows), :]
        numerator = numerator.astype(BF16)
        for k in range(n):
            to = order.index(section_of(k, n))
            out[to, pages + g * rows : pages + (g + 1) * rows, :] = numerator[k * rows : (k + 1) * rows, :]
    stat_rows = 2 * kv_heads
    share = HD // rows
    window = pl.ds(pl.multiple_of(rank // share * HD, HD), HD)
    own[kv_heads * rows : kv_heads * rows + stat_rows, :] = rows_held[:stat_rows, window]
    blank = jnp.zeros((PAGE - 3 * stat_rows, HD), F32)
    for w in range(-(-n // share)):
        stats = rows_held[:stat_rows, w * HD : (w + 1) * HD]
        lines = jnp.concatenate([*split_three(stats), blank], axis=0).astype(BF16)
        for k in range(w * share, min(n, (w + 1) * share)):
            out[order.index(section_of(k, n)), pages + kv_heads * rows :, :] = lines
    last = pltpu.make_async_copy(out.at[:, pages:, :], sent.at[:, pages:, :], sems.at[1])
    last.start()
    first.wait()
    last.wait()


def pick_column(row, rows, start):
    shape = (rows, HD)
    chosen = lax.broadcasted_iota(I32, shape, 1) == lax.broadcasted_iota(I32, shape, 0) + start
    return jnp.sum(jnp.where(chosen, row, 0.0), axis=1, keepdims=True)


def combine(pieces, highest):
    numerator, total = 0.0, 0.0
    for rows, top, weight in pieces:
        scale = jnp.exp(top - highest)
        numerator = numerator + rows * scale
        total = total + weight * scale
    return numerator, total


def fresh_kernel(n, kv_heads, steps, query, key, value, own, mine):
    rows = query.shape[0] // kv_heads
    every = kv_heads * rows
    start = rank_of(lax.axis_index("section"), n) % (HD // rows) * rows
    row = lax.broadcasted_iota(I32, (rows, steps), 0)
    causal = lax.broadcasted_iota(I32, (rows, steps), 1) <= row % steps
    tops, totals = [], []
    for g in range(kv_heads):
        cols = slice(g * HD, (g + 1) * HD)
        at = slice(g * rows, (g + 1) * rows)
        fresh = softmax_parts(query[at, :], key[:, cols], value[:, cols], causal)
        share = (
            own[at, :],
            pick_column(own[every + g : every + g + 1, :], rows, start),
            pick_column(own[every + kv_heads + g : every + kv_heads + g + 1, :], rows, start),
        )
        highest = jnp.maximum(fresh[1], share[1])
        numerator, total = combine((fresh, share), highest)
        mine[at, :] = numerator
        tops.append(highest)
        totals.append(total)
    line = column_to_row(jnp.concatenate(tops + totals, axis=0))
    mine[every:, :] = jnp.broadcast_to(line, (STAT, line.shape[1]))


def finish_kernel(kv_heads, steps, page_cap, shares, mine, attended, keys, values):
    n = shares.shape[0]
    pos = lax.axis_index("section")
    every = mine.shape[0] - STAT
    rows = every // kv_heads
    start = rank_of(pos, n) % (HD // rows) * rows
    chunk = page_cap * PAGE
    halves = keys.shape[2] // HD
    for k in range(n):
        for i, out in enumerate((keys, values)):
            for h in range(halves):
                part = i * halves + h
                out[page_section_of(k, n), :, h * HD : (h + 1) * HD] = shares[k, part * chunk : (part + 1) * chunk, :]
    pages = 2 * halves * chunk
    stats = row_to_column(mine[every : every + 1, :])
    lines = []
    for k in range(n):
        three = shares[k, pages + every :, :].astype(F32)
        size = 2 * kv_heads
        lines.append(three[:size] + three[size : 2 * size] + three[2 * size : 3 * size])
    for g in range(kv_heads):
        at = slice(g * rows, (g + 1) * rows)
        pieces = [(mine[at, :], stats[at], stats[every + g * rows : every + (g + 1) * rows])]
        for k in range(n):
            away = pos != page_section_of(k, n)
            top = jnp.where(away, pick_column(lines[k][g : g + 1], rows, start), LOWEST)
            weight = jnp.where(away, pick_column(lines[k][kv_heads + g : kv_heads + g + 1], rows, start), 0.0)
            share = shares[k, pages + g * rows : pages + (g + 1) * rows, :].astype(F32)
            pieces.append((share, top, weight))
        highest = pieces[0][1]
        for p in pieces[1:]:
            highest = jnp.maximum(highest, p[1])
        numerator, total = combine(pieces, highest)
        result = (numerator / total).astype(BF16)
        for h in range(rows // steps):
            to = (g * rows // steps + h) * HD
            attended[0, :, to : to + HD] = result[h * steps : (h + 1) * steps, :]


def body(
    text_rows,
    vis_rows,
    img_route,
    norm_gain,
    w_key,
    w_value,
    page_count,
    tail_len,
    page_dest,
    dec_req,
    dec_query,
    dec_key,
    dec_value,
):
    n = lax.axis_size("section")
    tok, half = text_rows.shape
    img = vis_rows.shape[0]
    kvw = w_key.shape[1]
    kv_heads = kvw // HD
    _, steps, q_width = dec_query.shape
    heads = q_width // HD
    q_rows = heads * steps
    blocks = tok // PAGE
    cap = max(2, (2 * img + n - 1) // n)
    page_cap = max(1, (blocks + n - 1) // n)

    def across(array):
        return lax.ppermute(array, "tensor", [(0, 1), (1, 0)])

    def exchange(array, section_at):
        order = [[section_at(rank, n) for rank in range(n)]]
        return lax.all_to_all(array, "section", split_axis=0, concat_axis=0, tiled=True, axis_index_groups=order)

    def remote(array):
        return pltpu.with_memory_space_constraint(array, pltpu.HBM)

    def local(array):
        return pltpu.with_memory_space_constraint(array, pltpu.VMEM)

    vis_far = across(vis_rows)
    text_far = across(text_rows)
    query = dec_query.reshape(steps, heads, HD).transpose(1, 0, 2).reshape(q_rows, HD)

    lot = -(-cap // PAGE) * PAGE
    q_lots = q_rows * HD // (2 * kvw)
    gain = norm_gain.reshape(1, 2 * half)
    load = min(2048, half)
    step = min(1024, load // 2)
    kept = half
    arguments = (img_route.T, w_key, w_value, vis_rows, gain, query)
    info, key_held, value_held, vis_near, gain_near, query_near = call(
        lambda *refs: prepare_kernel(n, lot, *refs),
        (
            jax.ShapeDtypeStruct((STAT, img), I32),
            pltpu.VMEM((kept, kvw), BF16),
            pltpu.VMEM((kept, kvw), BF16),
            *[pltpu.VMEM(a.shape, a.dtype) for a in arguments[3:]],
        ),
        [ANY] * len(arguments),
        (VM,) * 6,
        [pltpu.VMEM((1, n * img), I32), pltpu.SemaphoreType.DMA((len(arguments),))],
        flops=1 << 20,
        traffic=2 * 2 * half * 2 * kvw * 2,
    )(*[remote(a) for a in arguments])

    left = 2 * half - kept
    sizes = [*[load] * (half // load - 1), *[load // 2] * 2]
    packed = call(
        lambda *refs: vis_kernel(n, lot, sizes, step, *refs),
        pltpu.VMEM((n, q_lots + lot, 2 * kvw), BF16),
        [VM] * 6 + [ANY] * 2 + [VM],
        VM,
        [
            pltpu.VMEM((left, kvw), BF16),
            pltpu.VMEM((left, kvw), BF16),
            pltpu.VMEM((img, 2 * kvw), F32),
            pltpu.SemaphoreType.DMA((2 * len(sizes),)),
        ],
        flops=64 * img * 2 * half * 2 * kvw,
        traffic=2 * img * 2 * half + 8 * half * kvw,
    )(
        local(vis_near),
        vis_far,
        local(gain_near),
        local(query_near),
        local(key_held),
        local(value_held),
        remote(w_key),
        remote(w_value),
        info,
    )
    arrived = exchange(packed, section_of)

    block = page_cap * PAGE * 2 * kv_heads + q_rows + PAGE
    lists = (img_route.T, page_dest.T, page_count, tail_len, dec_req)
    kv_text, bias, base, info, slots = call(
        lambda *refs: text_kernel(n, img, lot, load, step, page_cap, *refs),
        (
            jax.ShapeDtypeStruct((tok, 2 * kvw), BF16),
            jax.ShapeDtypeStruct((tok, n * q_rows // kv_heads), F32),
            jax.ShapeDtypeStruct((n, block - q_rows - PAGE, HD), BF16),
            jax.ShapeDtypeStruct((STAT, n * lot), I32),
            jax.ShapeDtypeStruct((blocks,), I32),
        ),
        [ANY, VM, VM] + [ANY] * 7,
        (VM, VM, VM, VM, SM),
        [
            pltpu.VMEM((tok, half), BF16),
            pltpu.VMEM(w_key.shape, BF16),
            pltpu.VMEM(w_value.shape, BF16),
            pltpu.VMEM((tok, 2 * kvw), F32),
            pltpu.SMEM((n,), I32),
            pltpu.SemaphoreType.DMA((1 + 4 * half // load + len(lists),)),
            *[(pltpu.VMEM if i == 0 else pltpu.SMEM)(a.shape, a.dtype) for i, a in enumerate(lists)],
        ],
        limit=24,
        flops=2 * tok * 2 * half * 2 * kvw,
        traffic=2 * tok * 2 * half + 8 * half * kvw,
    )(remote(text_rows), text_far, remote(gain), remote(w_key), remote(w_value), *[remote(a) for a in lists])

    sent, own = call(
        lambda *refs: attend_kernel(n, cap, lot, page_cap, kv_heads, *refs),
        (
            jax.ShapeDtypeStruct((n, block, HD), BF16),
            jax.ShapeDtypeStruct((q_rows + STAT, HD), F32),
        ),
        [SM] + [VM] * 5,
        (ANY, VM),
        [
            pltpu.VMEM((n, block, HD), BF16),
            pltpu.VMEM((min(tok, n * cap), 2 * kvw), BF16),
            pltpu.VMEM((n * q_rows, HD), F32),
            pltpu.VMEM((STAT, n * q_rows // kv_heads), F32),
            pltpu.SemaphoreType.DMA((2,)),
        ],
        flops=4 * n * q_rows * tok * HD,
        traffic=n * (q_rows + STAT) * HD * 4,
    )(slots, info, kv_text, arrived, bias, base)
    shares = exchange(sent, page_section_of)

    mine = call(
        lambda *refs: fresh_kernel(n, kv_heads, steps, *refs),
        jax.ShapeDtypeStruct((q_rows + STAT, HD), F32),
        [VM] * 4,
        VM,
        flops=1 << 20,
        traffic=1 << 18,
    )(remote(query), remote(dec_key[0]), remote(dec_value[0]), own)

    slots_here = n * page_cap
    attended, cache_key, cache_value = call(
        lambda *refs: finish_kernel(kv_heads, steps, page_cap, *refs),
        (
            jax.ShapeDtypeStruct(dec_query.shape, BF16),
            jax.ShapeDtypeStruct((n, page_cap * PAGE, kvw), BF16),
            jax.ShapeDtypeStruct((n, page_cap * PAGE, kvw), BF16),
        ),
        [VM, VM],
        (VM, VM, VM),
        traffic=4 * tok * 2 * kvw,
    )(shares, mine)
    return (
        attended,
        cache_key.reshape(slots_here, PAGE, kvw),
        cache_value.reshape(slots_here, PAGE, kvw),
    )


def solution(mesh):
    return jax.shard_map(
        body,
        mesh=mesh,
        in_specs=(
            P(("groups", "section"), "tensor"),
            P(("groups", "section"), "tensor"),
            P("groups", None),
            P(),
            P(None, "tensor"),
            P(None, "tensor"),
            P("groups"),
            P("groups"),
            P("groups", None),
            P("groups"),
            P(("groups", "section"), None, "tensor"),
            P(("groups", "section"), None, "tensor"),
            P(("groups", "section"), None, "tensor"),
        ),
        out_specs=(
            P(("groups", "section"), None, "tensor"),
            P(("groups", "section"), None, "tensor"),
            P(("groups", "section"), None, "tensor"),
        ),
        check_vma=False,
    )
```

```python
import jax
import jax.numpy as jnp
from jax import lax
from jax.experimental import pallas as pl
from jax.experimental.pallas import tpu as pltpu
from jax.sharding import PartitionSpec as P

HD = 128
PAGE = 16
LOWEST = -1e30
EPS = 1e-06
STAT = 8
F32 = jnp.float32
BF16 = jnp.bfloat16
I32 = jnp.int32

VM = pl.BlockSpec(memory_space=pltpu.VMEM)
SM = pl.BlockSpec(memory_space=pltpu.SMEM)
ANY = pl.BlockSpec(memory_space=pl.ANY)
MIB = 1 << 20


def call(kernel, out_shape, in_specs, out_specs, scratch=(), limit=16, flops=0, traffic=0):
    return pl.pallas_call(
        kernel,
        out_shape=out_shape,
        in_specs=in_specs,
        out_specs=out_specs,
        scratch_shapes=list(scratch),
        compiler_params=pltpu.CompilerParams(vmem_limit_bytes=limit * MIB),
        cost_estimate=pl.CostEstimate(flops=flops, bytes_accessed=traffic, transcendentals=0),
    )


def rank_of(section, n):
    return jnp.where(section < n // 2, n - 2 - 2 * section, 2 * section - n + 1)


def section_of(rank, n):
    return n // 2 - 1 - rank // 2 + rank % 2 * (rank // 2 * 2 + 1)


def page_rank_of(section, n):
    z, y, length = section // 2, section % 2, n // 2
    return y * length + (2 * length - z - n // 4) % length


def page_section_of(rank, n):
    length = n // 2
    return 2 * (length - 1 - (rank % length + n // 4 - 1) % length) + rank // length


def dot(a, b):
    return jnp.dot(a, b, preferred_element_type=F32)


def dot_t(a, b):
    return lax.dot_general(a, b, (((1,), (1,)), ((), ())), preferred_element_type=F32)


def diagonal(shape):
    return lax.broadcasted_iota(I32, shape, 0) == lax.broadcasted_iota(I32, shape, 1)


def column_to_row(column):
    rows = column.shape[0]
    return jnp.sum(jnp.where(diagonal((rows, rows)), column, 0.0), axis=0, keepdims=True)


def row_to_column(row):
    lanes = row.shape[1]
    return jnp.sum(jnp.where(diagonal((lanes, lanes)), row, 0.0), axis=1, keepdims=True)


def squares_of(rows):
    total = jnp.zeros((rows.shape[0], HD), F32)
    for c in range(0, rows.shape[1], HD):
        wide = rows[:, c : c + HD].astype(F32)
        total = total + wide * wide
    return total


def split_three(values):
    high = values.astype(BF16).astype(F32)
    rest = values - high
    middle = rest.astype(BF16).astype(F32)
    return high, middle, rest - middle


def softmax_parts(query, key, value, usable):
    scores = jnp.where(usable, dot_t(query, key) * HD**-0.5, LOWEST)
    top = jnp.max(scores, axis=1, keepdims=True)
    weights = jnp.where(usable, jnp.exp(scores - top), 0.0)
    return dot(weights.astype(BF16), value), top, jnp.sum(weights, axis=1, keepdims=True)


def prepare_kernel(n, lot, *refs):
    far, info, near, (route, sems) = refs[:6], refs[6], refs[7:12], refs[12:]
    img, half = near[2].shape
    first = pl.ds(pl.multiple_of(lax.axis_index("tensor") * half, half), near[0].shape[0])
    sources = (far[0], far[1].at[first], far[2].at[first], *far[3:])
    copies = [pltpu.make_async_copy(a, b, sems.at[i]) for i, (a, b) in enumerate(zip(sources, (route, *near)))]
    for c in copies:
        c.start()
    copies[0].wait()
    pos = lax.axis_index("section")
    own = jnp.zeros((1, img), I32)
    for e in range(n):
        own = jnp.where(pos == e, route[:, e * img : (e + 1) * img], own)
    marks = own == lax.broadcasted_iota(I32, (n, img), 0)
    ones = jnp.where(marks, 1.0, 0.0).astype(BF16)
    earlier = lax.broadcasted_iota(I32, (img, img), 0) < lax.broadcasted_iota(I32, (img, img), 1)
    prefix = dot(ones, jnp.where(earlier, 1.0, 0.0).astype(BF16))
    local = jnp.sum(jnp.where(marks, prefix, 0.0), axis=0, keepdims=True).astype(I32)
    info[...] = jnp.broadcast_to(rank_of(own, n) * lot + local, info.shape)
    for c in copies[1:]:
        c.wait()


def plan_tokens(n, img, lot, page_cap, small, info, slots, bias, starts):
    route, pages, count, tail, req = small
    pos = lax.axis_index("section")
    tok, width = bias.shape
    blocks = tok // PAGE
    lanes = lax.broadcasted_iota(I32, (1, n * lot), 1)
    source, inner = section_of(lanes // lot, n), lanes % lot
    fits = jnp.zeros((1, n * lot), I32)
    offset = jnp.zeros((1, n * lot), I32)
    for e in range(n):
        here = (route[:, e * img : (e + 1) * img] == pos).astype(I32)
        arriving = jnp.sum(here, axis=1, keepdims=True)
        fits = fits + jnp.where(source == e, arriving, 0)
        offset = offset + jnp.where(source > e, arriving, 0)
    info[...] = jnp.broadcast_to(jnp.where(inner < fits, offset + inner, -1), info.shape)
    total = jnp.int32(0)
    for r in range(n):
        starts[r] = total
        total = total + count[r]
    token = lax.broadcasted_iota(I32, (1, tok), 1) + pos * tok
    token_slot = jnp.full((1, tok), -1, I32)
    for b in range(n):
        r = req[b]
        first = starts[r] * PAGE
        last = first + (count[r] - 1) * PAGE + tail[r]
        token_slot = jnp.where((token >= first) & (token < last), b, token_slot)
    member = section_of(lax.broadcasted_iota(I32, (1, width), 1) // (width // n), n)
    bias[...] = jnp.where(row_to_column(token_slot.astype(F32)) == member.astype(F32), 0.0, LOWEST)
    for g in range(blocks):
        holder = pages[0, pos * blocks + g]
        slot = page_rank_of(holder, n) * page_cap
        for e in range(g):
            slot = slot + (pages[0, pos * blocks + e] == holder).astype(I32)
        slots[g] = slot


def scale_of(near, far):
    sums = jnp.sum(squares_of(near) + squares_of(far), axis=1, keepdims=True)
    return lax.rsqrt(sums / (2.0 * near.shape[1]) + EPS)


def normed_rows(rows, c, step, scale, gain):
    return (rows[:, c : c + step].astype(F32) * scale * gain).astype(BF16)


def add_part(total, at, normed, w, begin):
    part = dot(normed, w)
    columns = slice(at, at + part.shape[1])
    if begin:
        total[:, columns] = part
    else:
        total[:, columns] += part


def vis_kernel(n, lot, sizes, step, *refs):
    near, far, gain, query, key_held, value_held, w_key, w_value, info, out, key_rest, value_rest, total, sems = refs
    img, half = near.shape
    kvw = w_key.shape[1]
    me = lax.axis_index("tensor")
    held = key_held.shape[0]
    loads = {}
    at = held
    for size in sizes:
        side = me if at < half else 1 - me
        source = pl.ds(pl.multiple_of(side * half + at % half, size), size)
        number = 2 * len(loads)
        loads[at] = [
            pltpu.make_async_copy(w.at[source], kept.at[at - held : at - held + size], sems.at[number + i])
            for i, (w, kept) in enumerate(((w_key, key_rest), (w_value, value_rest)))
        ]
        for copy in loads[at]:
            copy.start()
        at += size
    scale = scale_of(near, far)
    for at in range(0, 2 * half, step):
        for copy in loads.get(at, ()):
            copy.wait()
        rows, side = (near, me) if at < half else (far, 1 - me)
        weights, w_at = ((key_held, value_held), at) if at < held else ((key_rest, value_rest), at - held)
        c = at % half
        columns = pl.ds(pl.multiple_of(side * half + c, step), step)
        normed = normed_rows(rows, c, step, scale, gain[:, columns])
        for w, col in zip(weights, (0, kvw)):
            add_part(total, col, normed, w[w_at : w_at + step, :], at == 0)
    slot = lax.broadcasted_iota(I32, (n * lot, img), 0)
    chosen = jnp.where(slot == info[0:1, :img], 1.0, 0.0).astype(BF16)
    packed = dot(chosen, total[...].astype(BF16)).astype(BF16)
    q_lots = out.shape[1] - lot
    for k in range(n):
        for j in range(query.shape[0] // q_lots):
            out[k, :q_lots, j * HD : (j + 1) * HD] = query[j * q_lots : (j + 1) * q_lots, :]
        out[k, q_lots:, :] = packed[k * lot : (k + 1) * lot, :]


def put_page(out, page_cap, slot, rows):
    chunk = page_cap * PAGE
    for h in range(rows.shape[1] // HD):
        at = pl.ds(pl.multiple_of((slot % page_cap) * PAGE + h * chunk, PAGE), PAGE)
        out[slot // page_cap, at, :] = rows[:, h * HD : (h + 1) * HD]


def text_kernel(n, img, lot, load, step, page_cap, *refs):
    (near_far, far, gain, w_key_far, w_value_far), small_far, refs = refs[:5], refs[5:10], refs[10:]
    (out, bias, base, info, slots), (near, w_key, w_value, total, starts, sems), small = refs[:5], refs[5:11], refs[11:]
    half = near.shape[1]
    kvw = w_key.shape[1]
    me = lax.axis_index("tensor")
    first = pltpu.make_async_copy(near_far, near, sems.at[0])
    first.start()
    used = sems.shape[0] - len(small)
    lists = [pltpu.make_async_copy(a, b, sems.at[used + i]) for i, (a, b) in enumerate(zip(small_far, small))]
    for copy in lists:
        copy.start()
    loads = []
    for side in (me, 1 - me):
        for c in range(0, half, load):
            at = len(loads) * load
            columns = pl.ds(pl.multiple_of(side * half + c, load), load)
            pair = [
                pltpu.make_async_copy(w.at[columns], held.at[at : at + load], sems.at[2 * len(loads) + i])
                for i, (w, held) in enumerate(((w_key_far, w_key), (w_value_far, w_value)), 1)
            ]
            for copy in pair:
                copy.start()
            loads.append(pair)
    sums = squares_of(far)
    for copy in lists:
        copy.wait()
    plan_tokens(n, img, lot, page_cap, small, info, slots, bias, starts)
    first.wait()
    sums = jnp.sum(squares_of(near) + sums, axis=1, keepdims=True)
    scale = lax.rsqrt(sums / (2.0 * half) + EPS)
    for i, pair in enumerate(loads):
        for copy in pair:
            copy.wait()
        for at in range(i * load, (i + 1) * load, step):
            rows, side = (near, me) if at < half else (far, 1 - me)
            c = at % half
            columns = pl.ds(pl.multiple_of(side * half + c, step), step)
            normed = normed_rows(rows, c, step, scale, gain[:, columns])
            for w, col in ((w_key, 0), (w_value, kvw)):
                add_part(total, col, normed, w[at : at + step, :], at == 0)
    out[...] = total[...].astype(BF16)
    base[...] = jnp.zeros(base.shape, BF16)
    tok = near.shape[0]
    for g in range(tok // PAGE):
        put_page(base, page_cap, slots[g], out[g * PAGE : (g + 1) * PAGE, :])


def attend_kernel(n, cap, lot, page_cap, kv_heads, slots, info, kv_text, arrived, bias, base, sent, own, *scratch):
    out, mixed, rows_held, sems = scratch
    order = [page_section_of(k, n) for k in range(n)]
    rank = rank_of(lax.axis_index("section"), n)
    tok = kv_text.shape[0]
    kvw = kv_heads * HD
    q_lots = arrived.shape[1] - lot
    reach = min(tok, n * cap)
    hit = lax.broadcasted_iota(I32, (reach, n * lot), 0) == info[0:1, :]
    hot = jnp.where(hit, 1.0, 0.0)
    covered = jnp.sum(hot, axis=1, keepdims=True) > 0.0
    incoming = jnp.concatenate([arrived[k, q_lots:, :] for k in range(n)], axis=0)
    placed = dot(hot.astype(BF16), incoming)
    mixed[...] = jnp.where(covered, placed, kv_text[:reach, :].astype(F32)).astype(BF16)
    groups = arrived.shape[2] // HD // kv_heads
    rows = groups * q_lots
    pages = base.shape[1]
    out[:, :pages, :] = base[...]
    for g in range(reach // PAGE):
        put_page(out, page_cap, slots[g], mixed[g * PAGE : (g + 1) * PAGE, :])
    first = pltpu.make_async_copy(out.at[:, :pages, :], sent.at[:, :pages, :], sems.at[0])
    first.start()
    for g in range(kv_heads):
        query = jnp.concatenate(
            [
                arrived[k, :q_lots, (g * groups + j) * HD : (g * groups + j + 1) * HD]
                for k in range(n)
                for j in range(groups)
            ],
            axis=0,
        )
        cols = slice(g * HD, (g + 1) * HD)
        vcols = slice(kvw + g * HD, kvw + (g + 1) * HD)
        key = jnp.concatenate([mixed[:, cols], kv_text[reach:, cols]], axis=0)
        value = jnp.concatenate([mixed[:, vcols], kv_text[reach:, vcols]], axis=0)
        scores = dot_t(key, query) * HD**-0.5 + bias[...]
        top = jnp.max(scores, axis=0, keepdims=True)
        weights = jnp.exp(scores - top)
        rows_held[g : g + 1, :] = top
        rows_held[kv_heads + g : kv_heads + g + 1, :] = jnp.sum(weights, axis=0, keepdims=True)
        numerator = lax.dot_general(
            weights.astype(BF16), value, (((0,), (0,)), ((), ())), preferred_element_type=F32
        )
        numerator = numerator.astype(BF16)
        for k in range(n):
            to = order.index(section_of(k, n))
            out[to, pages + g * rows : pages + (g + 1) * rows, :] = numerator[k * rows : (k + 1) * rows, :]
    mine = page_rank_of(lax.axis_index("section"), n)
    own[: kv_heads * rows, :] = out[mine, pages : pages + kv_heads * rows, :].astype(F32)
    stat_rows = 2 * kv_heads
    share = HD // rows
    window = pl.ds(pl.multiple_of(rank // share * HD, HD), HD)
    own[kv_heads * rows : kv_heads * rows + stat_rows, :] = rows_held[:stat_rows, window]
    blank = jnp.zeros((PAGE - 3 * stat_rows, HD), F32)
    for w in range(-(-n // share)):
        stats = rows_held[:stat_rows, w * HD : (w + 1) * HD]
        lines = jnp.concatenate([*split_three(stats), blank], axis=0).astype(BF16)
        for k in range(w * share, min(n, (w + 1) * share)):
            out[order.index(section_of(k, n)), pages + kv_heads * rows :, :] = lines
    last = pltpu.make_async_copy(out.at[:, pages:, :], sent.at[:, pages:, :], sems.at[1])
    last.start()
    first.wait()
    last.wait()


def pick_column(row, rows, start):
    shape = (rows, HD)
    chosen = lax.broadcasted_iota(I32, shape, 1) == lax.broadcasted_iota(I32, shape, 0) + start
    return jnp.sum(jnp.where(chosen, row, 0.0), axis=1, keepdims=True)


def combine(pieces, highest):
    numerator, total = 0.0, 0.0
    for rows, top, weight in pieces:
        scale = jnp.exp(top - highest)
        numerator = numerator + rows * scale
        total = total + weight * scale
    return numerator, total


def fresh_kernel(n, kv_heads, steps, query, key, value, own, mine):
    rows = query.shape[0] // kv_heads
    every = kv_heads * rows
    start = rank_of(lax.axis_index("section"), n) % (HD // rows) * rows
    row = lax.broadcasted_iota(I32, (rows, steps), 0)
    causal = lax.broadcasted_iota(I32, (rows, steps), 1) <= row % steps
    tops, totals = [], []
    for g in range(kv_heads):
        cols = slice(g * HD, (g + 1) * HD)
        at = slice(g * rows, (g + 1) * rows)
        fresh = softmax_parts(query[at, :], key[:, cols], value[:, cols], causal)
        share = (
            own[at, :],
            pick_column(own[every + g : every + g + 1, :], rows, start),
            pick_column(own[every + kv_heads + g : every + kv_heads + g + 1, :], rows, start),
        )
        highest = jnp.maximum(fresh[1], share[1])
        numerator, total = combine((fresh, share), highest)
        mine[at, :] = numerator
        tops.append(highest)
        totals.append(total)
    line = column_to_row(jnp.concatenate(tops + totals, axis=0))
    mine[every:, :] = jnp.broadcast_to(line, (STAT, line.shape[1]))


def finish_kernel(kv_heads, steps, page_cap, shares, mine, attended, keys, values):
    n = shares.shape[0]
    pos = lax.axis_index("section")
    every = mine.shape[0] - STAT
    rows = every // kv_heads
    start = rank_of(pos, n) % (HD // rows) * rows
    chunk = page_cap * PAGE
    halves = keys.shape[2] // HD
    for k in range(n):
        for i, out in enumerate((keys, values)):
            for h in range(halves):
                part = i * halves + h
                out[page_section_of(k, n), :, h * HD : (h + 1) * HD] = shares[k, part * chunk : (part + 1) * chunk, :]
    pages = 2 * halves * chunk
    stats = row_to_column(mine[every : every + 1, :])
    lines = []
    for k in range(n):
        three = shares[k, pages + every :, :].astype(F32)
        size = 2 * kv_heads
        lines.append(three[:size] + three[size : 2 * size] + three[2 * size : 3 * size])
    for g in range(kv_heads):
        at = slice(g * rows, (g + 1) * rows)
        pieces = [(mine[at, :], stats[at], stats[every + g * rows : every + (g + 1) * rows])]
        for k in range(n):
            away = pos != page_section_of(k, n)
            top = jnp.where(away, pick_column(lines[k][g : g + 1], rows, start), LOWEST)
            weight = jnp.where(away, pick_column(lines[k][kv_heads + g : kv_heads + g + 1], rows, start), 0.0)
            share = shares[k, pages + g * rows : pages + (g + 1) * rows, :].astype(F32)
            pieces.append((share, top, weight))
        highest = pieces[0][1]
        for p in pieces[1:]:
            highest = jnp.maximum(highest, p[1])
        numerator, total = combine(pieces, highest)
        result = (numerator / total).astype(BF16)
        for h in range(rows // steps):
            to = (g * rows // steps + h) * HD
            attended[0, :, to : to + HD] = result[h * steps : (h + 1) * steps, :]


def body(
    text_rows,
    vis_rows,
    img_route,
    norm_gain,
    w_key,
    w_value,
    page_count,
    tail_len,
    page_dest,
    dec_req,
    dec_query,
    dec_key,
    dec_value,
):
    n = lax.axis_size("section")
    tok, half = text_rows.shape
    img = vis_rows.shape[0]
    kvw = w_key.shape[1]
    kv_heads = kvw // HD
    _, steps, q_width = dec_query.shape
    heads = q_width // HD
    q_rows = heads * steps
    blocks = tok // PAGE
    cap = max(2, (2 * img + n - 1) // n)
    page_cap = max(1, (blocks + n - 1) // n)

    def across(array):
        return lax.ppermute(array, "tensor", [(0, 1), (1, 0)])

    def exchange(array, section_at):
        order = [[section_at(rank, n) for rank in range(n)]]
        return lax.all_to_all(array, "section", split_axis=0, concat_axis=0, tiled=True, axis_index_groups=order)

    def remote(array):
        return pltpu.with_memory_space_constraint(array, pltpu.HBM)

    def local(array):
        return pltpu.with_memory_space_constraint(array, pltpu.VMEM)

    vis_far = across(vis_rows)
    text_far = across(text_rows)
    query = dec_query.reshape(steps, heads, HD).transpose(1, 0, 2).reshape(q_rows, HD)

    lot = -(-cap // PAGE) * PAGE
    q_lots = q_rows * HD // (2 * kvw)
    gain = norm_gain.reshape(1, 2 * half)
    load = min(2048, half)
    step = min(1024, load // 2)
    kept = load + load // 2
    arguments = (img_route.T, w_key, w_value, vis_rows, gain, query)
    info, key_held, value_held, vis_near, gain_near, query_near = call(
        lambda *refs: prepare_kernel(n, lot, *refs),
        (
            jax.ShapeDtypeStruct((STAT, img), I32),
            pltpu.VMEM((kept, kvw), BF16),
            pltpu.VMEM((kept, kvw), BF16),
            *[pltpu.VMEM(a.shape, a.dtype) for a in arguments[3:]],
        ),
        [ANY] * len(arguments),
        (VM,) * 6,
        [pltpu.VMEM((1, n * img), I32), pltpu.SemaphoreType.DMA((len(arguments),))],
        flops=1 << 20,
        traffic=2 * 2 * half * 2 * kvw * 2,
    )(*[remote(a) for a in arguments])

    left = 2 * half - kept
    sizes = [half - kept, *[load] * (half // load - 1), *[load // 2] * 2]
    packed = call(
        lambda *refs: vis_kernel(n, lot, sizes, step, *refs),
        pltpu.VMEM((n, q_lots + lot, 2 * kvw), BF16),
        [VM] * 6 + [ANY] * 2 + [VM],
        VM,
        [
            pltpu.VMEM((left, kvw), BF16),
            pltpu.VMEM((left, kvw), BF16),
            pltpu.VMEM((img, 2 * kvw), F32),
            pltpu.SemaphoreType.DMA((2 * len(sizes),)),
        ],
        flops=64 * img * 2 * half * 2 * kvw,
        traffic=2 * img * 2 * half + 8 * half * kvw,
    )(
        local(vis_near),
        vis_far,
        local(gain_near),
        local(query_near),
        local(key_held),
        local(value_held),
        remote(w_key),
        remote(w_value),
        info,
    )
    arrived = exchange(packed, section_of)

    block = page_cap * PAGE * 2 * kv_heads + q_rows + PAGE
    lists = (img_route.T, page_dest.T, page_count, tail_len, dec_req)
    kv_text, bias, base, info, slots = call(
        lambda *refs: text_kernel(n, img, lot, load, step, page_cap, *refs),
        (
            jax.ShapeDtypeStruct((tok, 2 * kvw), BF16),
            jax.ShapeDtypeStruct((tok, n * q_rows // kv_heads), F32),
            jax.ShapeDtypeStruct((n, block - q_rows - PAGE, HD), BF16),
            jax.ShapeDtypeStruct((STAT, n * lot), I32),
            jax.ShapeDtypeStruct((blocks,), I32),
        ),
        [ANY, VM, VM] + [ANY] * 7,
        (VM, VM, VM, VM, SM),
        [
            pltpu.VMEM((tok, half), BF16),
            pltpu.VMEM(w_key.shape, BF16),
            pltpu.VMEM(w_value.shape, BF16),
            pltpu.VMEM((tok, 2 * kvw), F32),
            pltpu.SMEM((n,), I32),
            pltpu.SemaphoreType.DMA((1 + 4 * half // load + len(lists),)),
            *[(pltpu.VMEM if i == 0 else pltpu.SMEM)(a.shape, a.dtype) for i, a in enumerate(lists)],
        ],
        limit=24,
        flops=2 * tok * 2 * half * 2 * kvw,
        traffic=2 * tok * 2 * half + 8 * half * kvw,
    )(remote(text_rows), text_far, remote(gain), remote(w_key), remote(w_value), *[remote(a) for a in lists])

    sent, own = call(
        lambda *refs: attend_kernel(n, cap, lot, page_cap, kv_heads, *refs),
        (
            jax.ShapeDtypeStruct((n, block, HD), BF16),
            jax.ShapeDtypeStruct((q_rows + STAT, HD), F32),
        ),
        [SM] + [VM] * 5,
        (ANY, VM),
        [
            pltpu.VMEM((n, block, HD), BF16),
            pltpu.VMEM((min(tok, n * cap), 2 * kvw), BF16),
            pltpu.VMEM((STAT, n * q_rows // kv_heads), F32),
            pltpu.SemaphoreType.DMA((2,)),
        ],
        flops=4 * n * q_rows * tok * HD,
        traffic=n * (q_rows + STAT) * HD * 4,
    )(slots, info, kv_text, arrived, bias, base)
    shares = exchange(sent, page_section_of)

    mine = call(
        lambda *refs: fresh_kernel(n, kv_heads, steps, *refs),
        jax.ShapeDtypeStruct((q_rows + STAT, HD), F32),
        [VM] * 4,
        VM,
        flops=1 << 20,
        traffic=1 << 18,
    )(remote(query), remote(dec_key[0]), remote(dec_value[0]), own)

    slots_here = n * page_cap
    attended, cache_key, cache_value = call(
        lambda *refs: finish_kernel(kv_heads, steps, page_cap, *refs),
        (
            jax.ShapeDtypeStruct(dec_query.shape, BF16),
            jax.ShapeDtypeStruct((n, page_cap * PAGE, kvw), BF16),
            jax.ShapeDtypeStruct((n, page_cap * PAGE, kvw), BF16),
        ),
        [VM, VM],
        (VM, VM, VM),
        traffic=4 * tok * 2 * kvw,
    )(shares, mine)
    return (
        attended,
        cache_key.reshape(slots_here, PAGE, kvw),
        cache_value.reshape(slots_here, PAGE, kvw),
    )


def solution(mesh):
    return jax.shard_map(
        body,
        mesh=mesh,
        in_specs=(
            P(("groups", "section"), "tensor"),
            P(("groups", "section"), "tensor"),
            P("groups", None),
            P(),
            P(None, "tensor"),
            P(None, "tensor"),
            P("groups"),
            P("groups"),
            P("groups", None),
            P("groups"),
            P(("groups", "section"), None, "tensor"),
            P(("groups", "section"), None, "tensor"),
            P(("groups", "section"), None, "tensor"),
        ),
        out_specs=(
            P(("groups", "section"), None, "tensor"),
            P(("groups", "section"), None, "tensor"),
            P(("groups", "section"), None, "tensor"),
        ),
        check_vma=False,
    )
```

```python
import jax
import jax.numpy as jnp
from jax import lax
from jax.experimental import pallas as pl
from jax.experimental.pallas import tpu as pltpu
from jax.sharding import PartitionSpec as P

HD = 128
PAGE = 16
LOWEST = -1e30
EPS = 1e-06
STAT = 8
F32 = jnp.float32
BF16 = jnp.bfloat16
I32 = jnp.int32

VM = pl.BlockSpec(memory_space=pltpu.VMEM)
SM = pl.BlockSpec(memory_space=pltpu.SMEM)
ANY = pl.BlockSpec(memory_space=pl.ANY)
MIB = 1 << 20


def call(kernel, out_shape, in_specs, out_specs, scratch=(), limit=16, flops=0, traffic=0):
    return pl.pallas_call(
        kernel,
        out_shape=out_shape,
        in_specs=in_specs,
        out_specs=out_specs,
        scratch_shapes=list(scratch),
        compiler_params=pltpu.CompilerParams(vmem_limit_bytes=limit * MIB),
        cost_estimate=pl.CostEstimate(flops=flops, bytes_accessed=traffic, transcendentals=0),
    )


def rank_of(section, n):
    return jnp.where(section < n // 2, n - 2 - 2 * section, 2 * section - n + 1)


def section_of(rank, n):
    return n // 2 - 1 - rank // 2 + rank % 2 * (rank // 2 * 2 + 1)


def page_rank_of(section, n):
    z, y, length = section // 2, section % 2, n // 2
    return y * length + (2 * length - z - n // 4) % length


def page_section_of(rank, n):
    length = n // 2
    return 2 * (length - 1 - (rank % length + n // 4 - 1) % length) + rank // length


def dot(a, b):
    return jnp.dot(a, b, preferred_element_type=F32)


def dot_t(a, b):
    return lax.dot_general(a, b, (((1,), (1,)), ((), ())), preferred_element_type=F32)


def diagonal(shape):
    return lax.broadcasted_iota(I32, shape, 0) == lax.broadcasted_iota(I32, shape, 1)


def column_to_row(column):
    rows = column.shape[0]
    return jnp.sum(jnp.where(diagonal((rows, rows)), column, 0.0), axis=0, keepdims=True)


def row_to_column(row):
    lanes = row.shape[1]
    return jnp.sum(jnp.where(diagonal((lanes, lanes)), row, 0.0), axis=1, keepdims=True)


def squares_of(rows):
    total = jnp.zeros((rows.shape[0], HD), F32)
    for c in range(0, rows.shape[1], HD):
        wide = rows[:, c : c + HD].astype(F32)
        total = total + wide * wide
    return total


def split_three(values):
    high = values.astype(BF16).astype(F32)
    rest = values - high
    middle = rest.astype(BF16).astype(F32)
    return high, middle, rest - middle


def softmax_parts(query, key, value, usable):
    scores = jnp.where(usable, dot_t(query, key) * HD**-0.5, LOWEST)
    top = jnp.max(scores, axis=1, keepdims=True)
    weights = jnp.where(usable, jnp.exp(scores - top), 0.0)
    return dot(weights.astype(BF16), value), top, jnp.sum(weights, axis=1, keepdims=True)


def prepare_kernel(n, lot, *refs):
    far, info, near, (route, sems) = refs[:6], refs[6], refs[7:12], refs[12:]
    img, half = near[2].shape
    first = pl.ds(pl.multiple_of(lax.axis_index("tensor") * half, half), near[0].shape[0])
    sources = (far[0], far[1].at[first], far[2].at[first], *far[3:])
    copies = [pltpu.make_async_copy(a, b, sems.at[i]) for i, (a, b) in enumerate(zip(sources, (route, *near)))]
    for c in copies:
        c.start()
    copies[0].wait()
    pos = lax.axis_index("section")
    own = jnp.zeros((1, img), I32)
    for e in range(n):
        own = jnp.where(pos == e, route[:, e * img : (e + 1) * img], own)
    marks = own == lax.broadcasted_iota(I32, (n, img), 0)
    ones = jnp.where(marks, 1.0, 0.0).astype(BF16)
    earlier = lax.broadcasted_iota(I32, (img, img), 0) < lax.broadcasted_iota(I32, (img, img), 1)
    prefix = dot(ones, jnp.where(earlier, 1.0, 0.0).astype(BF16))
    local = jnp.sum(jnp.where(marks, prefix, 0.0), axis=0, keepdims=True).astype(I32)
    info[...] = jnp.broadcast_to(rank_of(own, n) * lot + local, info.shape)
    for c in copies[1:]:
        c.wait()


def plan_tokens(n, img, lot, page_cap, small, info, slots, bias, starts):
    route, pages, count, tail, req = small
    pos = lax.axis_index("section")
    tok, width = bias.shape
    blocks = tok // PAGE
    lanes = lax.broadcasted_iota(I32, (1, n * lot), 1)
    source, inner = section_of(lanes // lot, n), lanes % lot
    fits = jnp.zeros((1, n * lot), I32)
    offset = jnp.zeros((1, n * lot), I32)
    for e in range(n):
        here = (route[:, e * img : (e + 1) * img] == pos).astype(I32)
        arriving = jnp.sum(here, axis=1, keepdims=True)
        fits = fits + jnp.where(source == e, arriving, 0)
        offset = offset + jnp.where(source > e, arriving, 0)
    info[...] = jnp.broadcast_to(jnp.where(inner < fits, offset + inner, -1), info.shape)
    total = jnp.int32(0)
    for r in range(n):
        starts[r] = total
        total = total + count[r]
    token = lax.broadcasted_iota(I32, (1, tok), 1) + pos * tok
    token_slot = jnp.full((1, tok), -1, I32)
    for b in range(n):
        r = req[b]
        first = starts[r] * PAGE
        last = first + (count[r] - 1) * PAGE + tail[r]
        token_slot = jnp.where((token >= first) & (token < last), b, token_slot)
    member = section_of(lax.broadcasted_iota(I32, (1, width), 1) // (width // n), n)
    bias[...] = jnp.where(row_to_column(token_slot.astype(F32)) == member.astype(F32), 0.0, LOWEST)
    for g in range(blocks):
        holder = pages[0, pos * blocks + g]
        slot = page_rank_of(holder, n) * page_cap
        for e in range(g):
            slot = slot + (pages[0, pos * blocks + e] == holder).astype(I32)
        slots[g] = slot


def scale_of(near, far):
    sums = jnp.sum(squares_of(near) + squares_of(far), axis=1, keepdims=True)
    return lax.rsqrt(sums / (2.0 * near.shape[1]) + EPS)


def normed_rows(rows, c, step, scale, gain):
    return (rows[:, c : c + step].astype(F32) * scale * gain).astype(BF16)


def add_part(total, at, normed, w, begin):
    part = dot(normed, w)
    columns = slice(at, at + part.shape[1])
    if begin:
        total[:, columns] = part
    else:
        total[:, columns] += part


def vis_kernel(n, lot, sizes, step, *refs):
    near, far, gain, query, key_held, value_held, w_key, w_value, info, out, key_rest, value_rest, total, sems = refs
    img, half = near.shape
    kvw = w_key.shape[1]
    me = lax.axis_index("tensor")
    held = key_held.shape[0]
    loads = {}
    at = held
    for size in sizes:
        side = me if at < half else 1 - me
        source = pl.ds(pl.multiple_of(side * half + at % half, size), size)
        number = 2 * len(loads)
        loads[at] = [
            pltpu.make_async_copy(w.at[source], kept.at[at - held : at - held + size], sems.at[number + i])
            for i, (w, kept) in enumerate(((w_key, key_rest), (w_value, value_rest)))
        ]
        for copy in loads[at]:
            copy.start()
        at += size
    scale = scale_of(near, far)
    for at in range(0, 2 * half, step):
        for copy in loads.get(at, ()):
            copy.wait()
        rows, side = (near, me) if at < half else (far, 1 - me)
        weights, w_at = ((key_held, value_held), at) if at < held else ((key_rest, value_rest), at - held)
        c = at % half
        columns = pl.ds(pl.multiple_of(side * half + c, step), step)
        normed = normed_rows(rows, c, step, scale, gain[:, columns])
        for w, col in zip(weights, (0, kvw)):
            add_part(total, col, normed, w[w_at : w_at + step, :], at == 0)
    slot = lax.broadcasted_iota(I32, (n * lot, img), 0)
    chosen = jnp.where(slot == info[0:1, :img], 1.0, 0.0).astype(BF16)
    packed = dot(chosen, total[...].astype(BF16)).astype(BF16)
    q_lots = out.shape[1] - lot
    for k in range(n):
        for j in range(query.shape[0] // q_lots):
            out[k, :q_lots, j * HD : (j + 1) * HD] = query[j * q_lots : (j + 1) * q_lots, :]
        out[k, q_lots:, :] = packed[k * lot : (k + 1) * lot, :]


def put_page(out, page_cap, slot, rows):
    chunk = page_cap * PAGE
    for h in range(rows.shape[1] // HD):
        at = pl.ds(pl.multiple_of((slot % page_cap) * PAGE + h * chunk, PAGE), PAGE)
        out[slot // page_cap, at, :] = rows[:, h * HD : (h + 1) * HD]


def text_kernel(n, img, lot, load, step, page_cap, *refs):
    (near_far, far, gain, w_key_far, w_value_far), small_far, refs = refs[:5], refs[5:10], refs[10:]
    (out, bias, base, info, slots), (near, w_key, w_value, total, starts, sems), small = refs[:5], refs[5:11], refs[11:]
    half = near.shape[1]
    kvw = w_key.shape[1]
    me = lax.axis_index("tensor")
    first = pltpu.make_async_copy(near_far, near, sems.at[0])
    first.start()
    used = sems.shape[0] - len(small)
    lists = [pltpu.make_async_copy(a, b, sems.at[used + i]) for i, (a, b) in enumerate(zip(small_far, small))]
    for copy in lists:
        copy.start()
    loads = []
    for side in (me, 1 - me):
        for c in range(0, half, load):
            at = len(loads) * load
            columns = pl.ds(pl.multiple_of(side * half + c, load), load)
            pair = [
                pltpu.make_async_copy(w.at[columns], held.at[at : at + load], sems.at[2 * len(loads) + i])
                for i, (w, held) in enumerate(((w_key_far, w_key), (w_value_far, w_value)), 1)
            ]
            for copy in pair:
                copy.start()
            loads.append(pair)
    sums = squares_of(far)
    for copy in lists:
        copy.wait()
    plan_tokens(n, img, lot, page_cap, small, info, slots, bias, starts)
    first.wait()
    sums = jnp.sum(squares_of(near) + sums, axis=1, keepdims=True)
    scale = lax.rsqrt(sums / (2.0 * half) + EPS)
    for i, pair in enumerate(loads):
        for copy in pair:
            copy.wait()
        for at in range(i * load, (i + 1) * load, step):
            rows, side = (near, me) if at < half else (far, 1 - me)
            c = at % half
            columns = pl.ds(pl.multiple_of(side * half + c, step), step)
            normed = normed_rows(rows, c, step, scale, gain[:, columns])
            for w, col in ((w_key, 0), (w_value, kvw)):
                add_part(total, col, normed, w[at : at + step, :], at == 0)
    out[...] = total[...].astype(BF16)
    base[...] = jnp.zeros(base.shape, BF16)
    tok = near.shape[0]
    for g in range(tok // PAGE):
        put_page(base, page_cap, slots[g], out[g * PAGE : (g + 1) * PAGE, :])


def attend_kernel(n, cap, lot, page_cap, kv_heads, slots, info, kv_text, arrived, bias, base, sent, own, *scratch):
    out, mixed, held, rows_held, sems = scratch
    order = [page_section_of(k, n) for k in range(n)]
    rank = rank_of(lax.axis_index("section"), n)
    tok = kv_text.shape[0]
    kvw = kv_heads * HD
    q_lots = arrived.shape[1] - lot
    reach = min(tok, n * cap)
    hit = lax.broadcasted_iota(I32, (reach, n * lot), 0) == info[0:1, :]
    hot = jnp.where(hit, 1.0, 0.0)
    covered = jnp.sum(hot, axis=1, keepdims=True) > 0.0
    incoming = jnp.concatenate([arrived[k, q_lots:, :] for k in range(n)], axis=0)
    placed = dot(hot.astype(BF16), incoming)
    mixed[...] = jnp.where(covered, placed, kv_text[:reach, :].astype(F32)).astype(BF16)
    groups = arrived.shape[2] // HD // kv_heads
    rows = groups * q_lots
    pages = base.shape[1]
    out[:, :pages, :] = base[...]
    for g in range(reach // PAGE):
        put_page(out, page_cap, slots[g], mixed[g * PAGE : (g + 1) * PAGE, :])
    first = pltpu.make_async_copy(out.at[:, :pages, :], sent.at[:, :pages, :], sems.at[0])
    first.start()
    for g in range(kv_heads):
        query = jnp.concatenate(
            [
                arrived[k, :q_lots, (g * groups + j) * HD : (g * groups + j + 1) * HD]
                for k in range(n)
                for j in range(groups)
            ],
            axis=0,
        )
        cols = slice(g * HD, (g + 1) * HD)
        vcols = slice(kvw + g * HD, kvw + (g + 1) * HD)
        key = jnp.concatenate([mixed[:, cols], kv_text[reach:, cols]], axis=0)
        value = jnp.concatenate([mixed[:, vcols], kv_text[reach:, vcols]], axis=0)
        scores = dot_t(key, query) * HD**-0.5 + bias[...]
        top = jnp.max(scores, axis=0, keepdims=True)
        weights = jnp.exp(scores - top)
        rows_held[g : g + 1, :] = top
        rows_held[kv_heads + g : kv_heads + g + 1, :] = jnp.sum(weights, axis=0, keepdims=True)
        numerator = lax.dot_general(
            weights.astype(BF16), value, (((0,), (0,)), ((), ())), preferred_element_type=F32
        )
        held[g * n * rows : (g + 1) * n * rows, :] = numerator
        own[g * rows : (g + 1) * rows, :] = held[pl.ds(pl.multiple_of((g * n + rank) * rows, rows), rows), :]
        numerator = numerator.astype(BF16)
        for k in range(n):
            to = order.index(section_of(k, n))
            out[to, pages + g * rows : pages + (g + 1) * rows, :] = numerator[k * rows : (k + 1) * rows, :]
    stat_rows = 2 * kv_heads
    share = HD // rows
    window = pl.ds(pl.multiple_of(rank // share * HD, HD), HD)
    own[kv_heads * rows : kv_heads * rows + stat_rows, :] = rows_held[:stat_rows, window]
    blank = jnp.zeros((PAGE - 3 * stat_rows, HD), F32)
    for w in range(-(-n // share)):
        stats = rows_held[:stat_rows, w * HD : (w + 1) * HD]
        lines = jnp.concatenate([*split_three(stats), blank], axis=0).astype(BF16)
        for k in range(w * share, min(n, (w + 1) * share)):
            out[order.index(section_of(k, n)), pages + kv_heads * rows :, :] = lines
    last = pltpu.make_async_copy(out.at[:, pages:, :], sent.at[:, pages:, :], sems.at[1])
    last.start()
    first.wait()
    last.wait()


def pick_column(row, rows, start):
    shape = (rows, HD)
    chosen = lax.broadcasted_iota(I32, shape, 1) == lax.broadcasted_iota(I32, shape, 0) + start
    return jnp.sum(jnp.where(chosen, row, 0.0), axis=1, keepdims=True)


def combine(pieces, highest):
    numerator, total = 0.0, 0.0
    for rows, top, weight in pieces:
        scale = jnp.exp(top - highest)
        numerator = numerator + rows * scale
        total = total + weight * scale
    return numerator, total


def fresh_kernel(n, kv_heads, steps, query, key, value, own, mine):
    rows = query.shape[0] // kv_heads
    every = kv_heads * rows
    start = rank_of(lax.axis_index("section"), n) % (HD // rows) * rows
    row = lax.broadcasted_iota(I32, (rows, steps), 0)
    causal = lax.broadcasted_iota(I32, (rows, steps), 1) <= row % steps
    tops, totals = [], []
    for g in range(kv_heads):
        cols = slice(g * HD, (g + 1) * HD)
        at = slice(g * rows, (g + 1) * rows)
        fresh = softmax_parts(query[at, :], key[:, cols], value[:, cols], causal)
        share = (
            own[at, :],
            pick_column(own[every + g : every + g + 1, :], rows, start),
            pick_column(own[every + kv_heads + g : every + kv_heads + g + 1, :], rows, start),
        )
        highest = jnp.maximum(fresh[1], share[1])
        numerator, total = combine((fresh, share), highest)
        mine[at, :] = numerator
        tops.append(highest)
        totals.append(total)
    line = column_to_row(jnp.concatenate(tops + totals, axis=0))
    mine[every:, :] = jnp.broadcast_to(line, (STAT, line.shape[1]))


def finish_kernel(kv_heads, steps, page_cap, shares, mine, attended, keys, values):
    n = shares.shape[0]
    pos = lax.axis_index("section")
    every = mine.shape[0] - STAT
    rows = every // kv_heads
    start = rank_of(pos, n) % (HD // rows) * rows
    chunk = page_cap * PAGE
    halves = keys.shape[2] // HD
    for k in range(n):
        for i, out in enumerate((keys, values)):
            for h in range(halves):
                part = i * halves + h
                out[page_section_of(k, n), :, h * HD : (h + 1) * HD] = shares[k, part * chunk : (part + 1) * chunk, :]
    pages = 2 * halves * chunk
    stats = row_to_column(mine[every : every + 1, :])
    lines = []
    for k in range(n):
        three = shares[k, pages + every :, :].astype(F32)
        size = 2 * kv_heads
        lines.append(three[:size] + three[size : 2 * size] + three[2 * size : 3 * size])
    for g in range(kv_heads):
        at = slice(g * rows, (g + 1) * rows)
        pieces = [(mine[at, :], stats[at], stats[every + g * rows : every + (g + 1) * rows])]
        for k in range(n):
            away = pos != page_section_of(k, n)
            top = jnp.where(away, pick_column(lines[k][g : g + 1], rows, start), LOWEST)
            weight = jnp.where(away, pick_column(lines[k][kv_heads + g : kv_heads + g + 1], rows, start), 0.0)
            share = shares[k, pages + g * rows : pages + (g + 1) * rows, :].astype(F32)
            pieces.append((share, top, weight))
        highest = pieces[0][1]
        for p in pieces[1:]:
            highest = jnp.maximum(highest, p[1])
        numerator, total = combine(pieces, highest)
        result = (numerator / total).astype(BF16)
        for h in range(rows // steps):
            to = (g * rows // steps + h) * HD
            attended[0, :, to : to + HD] = result[h * steps : (h + 1) * steps, :]


def body(
    text_rows,
    vis_rows,
    img_route,
    norm_gain,
    w_key,
    w_value,
    page_count,
    tail_len,
    page_dest,
    dec_req,
    dec_query,
    dec_key,
    dec_value,
):
    n = lax.axis_size("section")
    tok, half = text_rows.shape
    img = vis_rows.shape[0]
    kvw = w_key.shape[1]
    kv_heads = kvw // HD
    _, steps, q_width = dec_query.shape
    heads = q_width // HD
    q_rows = heads * steps
    blocks = tok // PAGE
    cap = max(2, (2 * img + n - 1) // n)
    page_cap = max(1, (blocks + n - 1) // n)

    def across(array):
        return lax.ppermute(array, "tensor", [(0, 1), (1, 0)])

    def exchange(array, section_at):
        order = [[section_at(rank, n) for rank in range(n)]]
        return lax.all_to_all(array, "section", split_axis=0, concat_axis=0, tiled=True, axis_index_groups=order)

    def remote(array):
        return pltpu.with_memory_space_constraint(array, pltpu.HBM)

    def local(array):
        return pltpu.with_memory_space_constraint(array, pltpu.VMEM)

    vis_far = across(vis_rows)
    text_far = across(text_rows)
    query = dec_query.reshape(steps, heads, HD).transpose(1, 0, 2).reshape(q_rows, HD)

    lot = -(-cap // PAGE) * PAGE
    q_lots = q_rows * HD // (2 * kvw)
    gain = norm_gain.reshape(1, 2 * half)
    load = min(2048, half)
    step = min(1024, load // 2)
    kept = load
    arguments = (img_route.T, w_key, w_value, vis_rows, gain, query)
    info, key_held, value_held, vis_near, gain_near, query_near = call(
        lambda *refs: prepare_kernel(n, lot, *refs),
        (
            jax.ShapeDtypeStruct((STAT, img), I32),
            pltpu.VMEM((kept, kvw), BF16),
            pltpu.VMEM((kept, kvw), BF16),
            *[pltpu.VMEM(a.shape, a.dtype) for a in arguments[3:]],
        ),
        [ANY] * len(arguments),
        (VM,) * 6,
        [pltpu.VMEM((1, n * img), I32), pltpu.SemaphoreType.DMA((len(arguments),))],
        flops=1 << 20,
        traffic=2 * 2 * half * 2 * kvw * 2,
    )(*[remote(a) for a in arguments])

    left = 2 * half - kept
    sizes = [half - kept, *[load] * (half // load - 1), *[load // 2] * 2]
    packed = call(
        lambda *refs: vis_kernel(n, lot, sizes, step, *refs),
        pltpu.VMEM((n, q_lots + lot, 2 * kvw), BF16),
        [VM] * 6 + [ANY] * 2 + [VM],
        VM,
        [
            pltpu.VMEM((left, kvw), BF16),
            pltpu.VMEM((left, kvw), BF16),
            pltpu.VMEM((img, 2 * kvw), F32),
            pltpu.SemaphoreType.DMA((2 * len(sizes),)),
        ],
        flops=64 * img * 2 * half * 2 * kvw,
        traffic=2 * img * 2 * half + 8 * half * kvw,
    )(
        local(vis_near),
        vis_far,
        local(gain_near),
        local(query_near),
        local(key_held),
        local(value_held),
        remote(w_key),
        remote(w_value),
        info,
    )
    arrived = exchange(packed, section_of)

    block = page_cap * PAGE * 2 * kv_heads + q_rows + PAGE
    lists = (img_route.T, page_dest.T, page_count, tail_len, dec_req)
    kv_text, bias, base, info, slots = call(
        lambda *refs: text_kernel(n, img, lot, load, step, page_cap, *refs),
        (
            jax.ShapeDtypeStruct((tok, 2 * kvw), BF16),
            jax.ShapeDtypeStruct((tok, n * q_rows // kv_heads), F32),
            jax.ShapeDtypeStruct((n, block - q_rows - PAGE, HD), BF16),
            jax.ShapeDtypeStruct((STAT, n * lot), I32),
            jax.ShapeDtypeStruct((blocks,), I32),
        ),
        [ANY, VM, VM] + [ANY] * 7,
        (VM, VM, VM, VM, SM),
        [
            pltpu.VMEM((tok, half), BF16),
            pltpu.VMEM(w_key.shape, BF16),
            pltpu.VMEM(w_value.shape, BF16),
            pltpu.VMEM((tok, 2 * kvw), F32),
            pltpu.SMEM((n,), I32),
            pltpu.SemaphoreType.DMA((1 + 4 * half // load + len(lists),)),
            *[(pltpu.VMEM if i == 0 else pltpu.SMEM)(a.shape, a.dtype) for i, a in enumerate(lists)],
        ],
        limit=24,
        flops=2 * tok * 2 * half * 2 * kvw,
        traffic=2 * tok * 2 * half + 8 * half * kvw,
    )(remote(text_rows), text_far, remote(gain), remote(w_key), remote(w_value), *[remote(a) for a in lists])

    sent, own = call(
        lambda *refs: attend_kernel(n, cap, lot, page_cap, kv_heads, *refs),
        (
            jax.ShapeDtypeStruct((n, block, HD), BF16),
            jax.ShapeDtypeStruct((q_rows + STAT, HD), F32),
        ),
        [SM] + [VM] * 5,
        (ANY, VM),
        [
            pltpu.VMEM((n, block, HD), BF16),
            pltpu.VMEM((min(tok, n * cap), 2 * kvw), BF16),
            pltpu.VMEM((n * q_rows, HD), F32),
            pltpu.VMEM((STAT, n * q_rows // kv_heads), F32),
            pltpu.SemaphoreType.DMA((2,)),
        ],
        flops=4 * n * q_rows * tok * HD,
        traffic=n * (q_rows + STAT) * HD * 4,
    )(slots, info, kv_text, arrived, bias, base)
    shares = exchange(sent, page_section_of)

    mine = call(
        lambda *refs: fresh_kernel(n, kv_heads, steps, *refs),
        jax.ShapeDtypeStruct((q_rows + STAT, HD), F32),
        [VM] * 4,
        VM,
        flops=1 << 20,
        traffic=1 << 18,
    )(remote(query), remote(dec_key[0]), remote(dec_value[0]), own)

    slots_here = n * page_cap
    attended, cache_key, cache_value = call(
        lambda *refs: finish_kernel(kv_heads, steps, page_cap, *refs),
        (
            jax.ShapeDtypeStruct(dec_query.shape, BF16),
            jax.ShapeDtypeStruct((n, page_cap * PAGE, kvw), BF16),
            jax.ShapeDtypeStruct((n, page_cap * PAGE, kvw), BF16),
        ),
        [VM, VM],
        (VM, VM, VM),
        traffic=4 * tok * 2 * kvw,
    )(shares, mine)
    return (
        attended,
        cache_key.reshape(slots_here, PAGE, kvw),
        cache_value.reshape(slots_here, PAGE, kvw),
    )


def solution(mesh):
    return jax.shard_map(
        body,
        mesh=mesh,
        in_specs=(
            P(("groups", "section"), "tensor"),
            P(("groups", "section"), "tensor"),
            P("groups", None),
            P(),
            P(None, "tensor"),
            P(None, "tensor"),
            P("groups"),
            P("groups"),
            P("groups", None),
            P("groups"),
            P(("groups", "section"), None, "tensor"),
            P(("groups", "section"), None, "tensor"),
            P(("groups", "section"), None, "tensor"),
        ),
        out_specs=(
            P(("groups", "section"), None, "tensor"),
            P(("groups", "section"), None, "tensor"),
            P(("groups", "section"), None, "tensor"),
        ),
        check_vma=False,
    )
```
